32 devices in a mesh: ctx: 16 (over z, y, x), head: 2 (over core).
Axes of the slice: x: 2, y: 2, z: 4, core: 2. Of those that a mesh axis runs over, the one named last changes fastest.
Arguments:
- hidden: bfloat16 [2048, 2048], P(('ctx', 'head')), may hold values from -6 to 6
- w_query: bfloat16 [2048, 2048], P(None, 'head'), may hold values from -0.125 to 0.125
- w_key: bfloat16 [2048, 256], P(None, 'head'), may hold values from -0.125 to 0.125
- w_value: bfloat16 [2048, 256], P(None, 'head'), may hold values from -0.125 to 0.125
- w_dir: bfloat16 [2048, 256], P(None, 'head'), may hold values from -0.125 to 0.125
- u_rate: bfloat16 [2, 2048], P('head'), may hold values from -0.125 to 0.125
- rate_bias: float32 [2], P('head'), may hold values from 5 to 7
- q_gain: float32 [128], replicated, may hold values from 0.8 to 12
- k_gain: float32 [128], replicated, may hold values from 0.8 to 12
- w_out: bfloat16 [2048, 2048], P('head'), may hold values from -0.1875 to 0.1875
- block_mask: int32 [16, 16], P('ctx'), may hold values from 0 to 1, as said below
Outputs:
- layer_out: bfloat16 [2048, 2048], P(('ctx', 'head'))
The draws below stay inside these ranges and needn't reach their ends.
Inputs may be any that keep to these rules, and one draw needn't show every extreme that they name: block_mask[I, J] is 1 only where J < I; each row holds at most 4 ones, and row 15 holds exactly 4.
All inputs are finite; a program needn't handle non-finite values.
Results may differ from the reference program's by a relative error of at most 0.01045.
Values may be sent and summed in bfloat16 or wider, within the bound.
No kernel may reach another device: no remote copies, remote signals or barrier semaphores. Data moves between devices by JAX's collectives and lax.ppermute only.
A program may use at most 128 MiB of HBM per device.

```python
import math
import jax
import jax.numpy as jnp
from jax import lax

D = 2048
HD = 128
KVH = 2
GROUP = 8
SEG = 128
QH = 16
NB = 16
TOKENS = 2048
MOSTB = 4


def channel_gains(key, stream):
    uniform_base = jax.random.uniform(jax.random.fold_in(key, stream), (HD,), jnp.float32)
    gain_values = 0.8 * jnp.exp(uniform_base * jnp.log(3.0 / 0.8))
    return gain_values


def draw_q_gain(key, part):
    return channel_gains(key, 5)


def draw_k_gain(key, part):
    return channel_gains(key, 9)


def draw_block_mask(key, part):
    first_key, second_key = jax.random.split(jax.random.fold_in(key, 31))
    third_key = jax.random.fold_in(key, 47)
    rows_index = jnp.arange(NB, dtype=jnp.int32)
    halvings = jax.random.randint(first_key, (NB,), 0, 6, dtype=jnp.int32)
    wanted = jnp.maximum(jnp.right_shift(jnp.full((NB,), MOSTB, jnp.int32), halvings), 1)
    wanted = jnp.where(rows_index == NB - 1, MOSTB, wanted)
    counts = jnp.minimum(wanted, rows_index)
    earlier = rows_index[None, :] < rows_index[:, None]
    scores = jax.random.randint(second_key, (NB, NB), 0, 1 << 20, dtype=jnp.int32) * NB + rows_index[None, :]
    favoured = jax.random.randint(third_key, (NB,), 0, 2, dtype=jnp.int32)
    far_column = rows_index - NB // 2
    pick_far = (rows_index[None, :] == far_column[:, None]) & (favoured[:, None] == 1) & (far_column[:, None] >= 0)
    scores = jnp.where(pick_far, jnp.int32(-1), scores)
    scores = jnp.where(earlier, scores, jnp.int32(1 << 30))
    rank_of = jnp.argsort(jnp.argsort(scores, axis=1, stable=True), axis=1, stable=True)
    return (earlier & (rank_of < counts[:, None])).astype(jnp.int32)


def shard_levels(rng, shape, cuts, least, high):
    loudness, own = 1.0, jax.random.fold_in(rng, 6)
    for position, shards_of in cuts:
        draws = jnp.exp(jax.random.uniform(jax.random.fold_in(own, position), (shards_of,), jnp.float32, least / len(cuts), high / len(cuts)))
        loudness = loudness * jnp.repeat(draws, shape[position] // shards_of).reshape([-1 if axis == position else 1 for axis in range(len(shape))])
    return loudness


def gaussian(own_key, dims, spread, most, cuts=(), held_as=jnp.bfloat16):
    level = shard_levels(own_key, dims, cuts, -0.22, 0.18) if cuts else 1.0
    drawn = jax.random.normal(own_key, dims, jnp.float32) * spread * level
    return jnp.minimum(jnp.maximum(drawn, -most), most).astype(held_as)


def setup_inputs(seed: int = 0) -> dict:
    seeds = jax.random.split(jax.random.key(seed), 12)
    hidden = gaussian(seeds[0], (TOKENS, D), 1.0, 6.0, ((0, 32),))
    w_query = gaussian(seeds[1], (D, QH * HD), D ** -0.5, 0.125, ((1, 2),))
    w_key = gaussian(seeds[2], (D, KVH * HD), D ** -0.5, 0.125, ((1, 2),))
    w_value = gaussian(seeds[3], (D, KVH * HD), D ** -0.5, 0.125, ((1, 2),))
    w_dir = gaussian(seeds[4], (D, KVH * HD), D ** -0.5, 0.125, ((1, 2),))
    u_rate = gaussian(seeds[5], (KVH, D), D ** -0.5, 0.125, ((0, 2),))
    rate_bias = jnp.clip(5.0 + 2.0 * jax.random.uniform(seeds[6], (KVH,), jnp.float32) ** shard_levels(seeds[6], (KVH,), ((0, 2),), -0.2, 0.2), 5.0, 7.0)
    q_gain = draw_q_gain(jax.random.fold_in(seeds[11], 71), 0)
    k_gain = draw_k_gain(jax.random.fold_in(seeds[11], 71), 0)
    w_out = gaussian(seeds[9], (QH * HD, D), (QH * HD // 2) ** -0.5, 0.1875, ((0, 2),))
    block_mask = draw_block_mask(jax.random.fold_in(seeds[11], 71), 0)
    return {"hidden": hidden, "w_query": w_query, "w_key": w_key, "w_value": w_value, "w_dir": w_dir, "u_rate": u_rate, "rate_bias": rate_bias, "q_gain": q_gain, "k_gain": k_gain, "w_out": w_out, "block_mask": block_mask}


HIGHEST = lax.Precision.HIGHEST
EPSILON = 1e-06
NEGATIVE = -1e+30

def rms_scaled(values_in, gain):
    return values_in * lax.rsqrt(lax.optimization_barrier(jnp.mean(values_in * values_in, axis=-1, keepdims=True)) + EPSILON) * gain

def segment_terms(seg_rows, query_cols, key_cols, value_cols, dir_cols, rate_vector, rate_offset, q_gain, k_gain):
    tokens_here = seg_rows.shape[0]
    head_size = key_cols.shape[1]
    groups = query_cols.shape[1] // head_size
    scaling = 1.0 / math.sqrt(head_size)
    queries = jnp.dot(seg_rows.astype(jnp.float32), query_cols.astype(jnp.float32), preferred_element_type=jnp.float32)
    queries = queries.reshape(tokens_here, groups, head_size).transpose(1, 0, 2).reshape(groups * tokens_here, head_size)
    queries = rms_scaled(queries, q_gain)
    key_rows = rms_scaled(jnp.dot(seg_rows.astype(jnp.float32), key_cols.astype(jnp.float32), preferred_element_type=jnp.float32), k_gain)
    value_rows = jnp.dot(seg_rows.astype(jnp.float32), value_cols.astype(jnp.float32), preferred_element_type=jnp.float32).astype(jnp.bfloat16)
    raw_dirs = jnp.dot(seg_rows.astype(jnp.float32), dir_cols.astype(jnp.float32), preferred_element_type=jnp.float32)
    directions = raw_dirs * lax.rsqrt(lax.optimization_barrier(jnp.sum(raw_dirs * raw_dirs, axis=-1, keepdims=True)) + EPSILON)
    rate_values = 2.0 * jax.nn.sigmoid(jnp.dot(seg_rows.astype(jnp.float32), rate_vector.astype(jnp.float32), preferred_element_type=jnp.float32) + rate_offset)
    positions = jnp.arange(tokens_here, dtype=jnp.int32)
    strictly_below = positions[:, None] > positions[None, :]
    up_to = jnp.tile(positions[:, None] >= positions[None, :], (groups, 1))
    gram_matrix = jnp.dot(directions, directions.T, precision=HIGHEST)
    lower_unit = jnp.eye(tokens_here, dtype=directions.dtype) + jnp.where(strictly_below, rate_values[:, None] * gram_matrix, 0.0)
    solved = lax.linalg.triangular_solve(lower_unit, rate_values[:, None] * directions, left_side=True, lower=True, unit_diagonal=True)
    crossing = jnp.where(strictly_below, jnp.dot(directions, key_rows.T, precision=HIGHEST), 0.0)
    coefficients = lax.linalg.triangular_solve(lower_unit, rate_values[:, None] * crossing, left_side=True, lower=True, unit_diagonal=True)
    exit_keys = key_rows - jnp.dot(coefficients.T, directions, precision=HIGHEST)
    product = jnp.eye(head_size, dtype=directions.dtype) - jnp.dot(directions.T, solved, precision=HIGHEST)
    reach_terms = jnp.where(up_to, jnp.dot(queries, directions.T, precision=HIGHEST), 0.0)
    moved_queries = (queries - jnp.dot(reach_terms, solved, precision=HIGHEST)).astype(jnp.bfloat16)
    own_scores = (jnp.dot(queries, key_rows.T, precision=HIGHEST) - jnp.dot(reach_terms, coefficients, precision=HIGHEST)) * scaling
    own_scores = jnp.where(up_to, own_scores, NEGATIVE)
    return (moved_queries, own_scores, exit_keys, value_rows, product)

def reference(hidden, w_query, w_key, w_value, w_dir, u_rate, rate_bias, q_gain, k_gain, w_out, block_mask):
    segments = NB
    scaling = 1.0 / math.sqrt(HD)
    blocks_index = jnp.arange(segments, dtype=jnp.int32)
    head_outputs = []
    for kv_head in range(KVH):
        query_cols = w_query[:, kv_head * GROUP * HD:(kv_head + 1) * GROUP * HD]
        key_cols = w_key[:, kv_head * HD:(kv_head + 1) * HD]
        value_cols = w_value[:, kv_head * HD:(kv_head + 1) * HD]
        dir_cols = w_dir[:, kv_head * HD:(kv_head + 1) * HD]
        rate_vector = u_rate[kv_head]
        rate_offset = rate_bias[kv_head]

        def per_segment(seg_rows):
            return segment_terms(seg_rows, query_cols, key_cols, value_cols, dir_cols, rate_vector, rate_offset, q_gain, k_gain)
        moved_queries, own_scores, exit_keys, value_rows, products = lax.map(per_segment, hidden.reshape(segments, SEG, D))

        def advance(buffer, seg_index):
            allowed = (block_mask[seg_index] > 0) & (blocks_index < seg_index)
            ranking = jnp.where(allowed, 0, 1) * segments + blocks_index
            chosen = jnp.argsort(ranking)[:MOSTB]
            usable = jnp.repeat(allowed[chosen], SEG)
            key_sel = buffer.reshape(segments, SEG, HD)[chosen].reshape(MOSTB * SEG, HD).astype(jnp.bfloat16)
            value_sel = value_rows[chosen].reshape(MOSTB * SEG, HD)
            scores = jnp.dot(moved_queries[seg_index].astype(jnp.float32), key_sel.T.astype(jnp.float32), preferred_element_type=jnp.float32) * scaling
            scores = jnp.where(usable[None, :], scores, NEGATIVE)
            local_scores = own_scores[seg_index]
            peak_score = jnp.maximum(lax.optimization_barrier(jnp.max(scores, axis=1)), lax.optimization_barrier(jnp.max(local_scores, axis=1)))
            far_exp = jnp.exp(scores - peak_score[:, None])
            near_exp = jnp.exp(local_scores - peak_score[:, None])
            total_weight = lax.optimization_barrier(jnp.sum(far_exp, axis=1)) + lax.optimization_barrier(jnp.sum(near_exp, axis=1))
            weighted = jnp.dot(far_exp.astype(jnp.bfloat16).astype(jnp.float32), value_sel.astype(jnp.float32), preferred_element_type=jnp.float32)
            weighted = weighted + jnp.dot(near_exp.astype(jnp.bfloat16).astype(jnp.float32), value_rows[seg_index].astype(jnp.float32), preferred_element_type=jnp.float32)
            attended = (weighted / total_weight[:, None]).astype(jnp.bfloat16)
            buffer = jnp.dot(buffer, products[seg_index].T, precision=HIGHEST)
            buffer = lax.dynamic_update_slice(buffer, exit_keys[seg_index], ((seg_index * SEG).astype(jnp.int32), jnp.int32(0)))
            return (buffer, attended)
        start_buffer = jnp.zeros((segments * SEG, HD), jnp.float32)
        _, attended_all = lax.scan(advance, start_buffer, blocks_index)
        attended_all = attended_all.reshape(segments, GROUP, SEG, HD).transpose(0, 2, 1, 3).reshape(segments * SEG, GROUP * HD)
        head_outputs.append(attended_all)
    joined = jnp.concatenate(head_outputs, axis=1)
    return jnp.dot(joined.astype(jnp.float32), w_out.astype(jnp.float32), preferred_element_type=jnp.float32).astype(jnp.bfloat16)
```

```python
import math

import jax
import jax.numpy as jnp
from jax import lax
from jax.sharding import PartitionSpec as P

HD = 128
SEG = 128


HIGHEST = lax.Precision.HIGHEST
EPSILON = 1e-06
NEGATIVE = -1e30


def rms_scaled(values_in, gain):
    return (
        values_in
        * lax.rsqrt(jnp.mean(values_in * values_in, axis=-1, keepdims=True) + EPSILON)
        * gain
    )


def segment_terms(
    seg_rows, query_cols, key_cols, value_cols, dir_cols, rate_vector, rate_offset, q_gain, k_gain
):
    tokens_here = seg_rows.shape[0]
    head_size = key_cols.shape[1]
    groups = query_cols.shape[1] // head_size
    scaling = 1.0 / math.sqrt(head_size)
    queries = jnp.dot(seg_rows, query_cols, preferred_element_type=jnp.float32)
    queries = (
        queries.reshape(tokens_here, groups, head_size)
        .transpose(1, 0, 2)
        .reshape(groups * tokens_here, head_size)
    )
    queries = rms_scaled(queries, q_gain)
    key_rows = rms_scaled(jnp.dot(seg_rows, key_cols, preferred_element_type=jnp.float32), k_gain)
    value_rows = jnp.dot(seg_rows, value_cols, preferred_element_type=jnp.float32).astype(
        jnp.bfloat16
    )
    raw_dirs = jnp.dot(seg_rows, dir_cols, preferred_element_type=jnp.float32)
    directions = raw_dirs * lax.rsqrt(
        jnp.sum(raw_dirs * raw_dirs, axis=-1, keepdims=True) + EPSILON
    )
    rate_values = 2.0 * jax.nn.sigmoid(
        jnp.dot(seg_rows, rate_vector, preferred_element_type=jnp.float32) + rate_offset
    )
    positions = jnp.arange(tokens_here, dtype=jnp.int32)
    strictly_below = positions[:, None] > positions[None, :]
    up_to = jnp.tile(positions[:, None] >= positions[None, :], (groups, 1))
    gram_matrix = jnp.dot(directions, directions.T, precision=HIGHEST)
    lower_unit = jnp.eye(tokens_here, dtype=directions.dtype) + jnp.where(
        strictly_below, rate_values[:, None] * gram_matrix, 0.0
    )
    solved = lax.linalg.triangular_solve(
        lower_unit,
        rate_values[:, None] * directions,
        left_side=True,
        lower=True,
        unit_diagonal=True,
    )
    crossing = jnp.where(strictly_below, jnp.dot(directions, key_rows.T, precision=HIGHEST), 0.0)
    coefficients = lax.linalg.triangular_solve(
        lower_unit, rate_values[:, None] * crossing, left_side=True, lower=True, unit_diagonal=True
    )
    exit_keys = key_rows - jnp.dot(coefficients.T, directions, precision=HIGHEST)
    product = jnp.eye(head_size, dtype=directions.dtype) - jnp.dot(
        directions.T, solved, precision=HIGHEST
    )
    reach_terms = jnp.where(up_to, jnp.dot(queries, directions.T, precision=HIGHEST), 0.0)
    moved_queries = (queries - jnp.dot(reach_terms, solved, precision=HIGHEST)).astype(jnp.bfloat16)
    own_scores = (
        jnp.dot(queries, key_rows.T, precision=HIGHEST)
        - jnp.dot(reach_terms, coefficients, precision=HIGHEST)
    ) * scaling
    own_scores = jnp.where(up_to, own_scores, NEGATIVE)
    return (moved_queries, own_scores, exit_keys, value_rows, product)


def attend_blocks(moved_queries, key_blocks, value_blocks, usable, running):
    block_total, tokens_here, head_size = key_blocks.shape
    scaling = 1.0 / math.sqrt(head_size)
    per_step = math.gcd(block_total, max(1, 1024 // tokens_here))
    steps_total = block_total // per_step
    key_groups = key_blocks.reshape(steps_total, per_step * tokens_here, head_size)
    value_groups = value_blocks.reshape(steps_total, per_step * tokens_here, head_size)
    keep_groups = jnp.repeat(usable, tokens_here).reshape(steps_total, per_step * tokens_here)

    def advance(carried, pieces):
        peak_score, total_weight, weighted = carried
        group_keys, group_values, group_keep = pieces
        scores = (
            lax.dot_general(
                moved_queries,
                group_keys,
                (((1,), (1,)), ((), ())),
                preferred_element_type=jnp.float32,
            )
            * scaling
        )
        scores = jnp.where(group_keep[None, :], scores, NEGATIVE)
        new_peak = jnp.maximum(peak_score, jnp.max(scores, axis=1))
        fading = jnp.exp(peak_score - new_peak)
        expo_weights = jnp.exp(scores - new_peak[:, None])
        total_weight = total_weight * fading + jnp.sum(expo_weights, axis=1)
        weighted = weighted * fading[:, None] + jnp.dot(
            expo_weights.astype(jnp.bfloat16), group_values, preferred_element_type=jnp.float32
        )
        return ((new_peak, total_weight, weighted), None)

    running, _ = lax.scan(advance, running, (key_groups, value_groups, keep_groups))
    return running


def body(
    hidden, w_query, w_key, w_value, w_dir, u_rate, rate_bias, q_gain, k_gain, w_out, block_mask
):
    seg_rows = lax.all_gather(hidden, "head", axis=0, tiled=True)
    moved_queries, own_scores, exit_keys, value_rows, product = segment_terms(
        seg_rows, w_query, w_key, w_value, w_dir, u_rate[0], rate_bias[0], q_gain, k_gain
    )
    segments = lax.axis_size("ctx")
    position = lax.axis_index("ctx")
    mask_row = block_mask[0]
    most_blocks = segments // 4
    slots = jnp.arange(segments, dtype=jnp.int32)
    value_blocks = lax.all_gather(value_rows, "ctx")
    products = lax.all_gather(product, "ctx")
    key_blocks = lax.all_gather(exit_keys, "ctx")
    allowed = (mask_row > 0) & (slots < position)
    ranking = jnp.where(allowed, 0, 1) * segments + slots
    chosen = jnp.argsort(ranking)[:most_blocks]
    allowed = allowed[chosen]

    def extend(crossed, step):
        segment = jnp.maximum(position - 1 - step, 0)
        return jnp.dot(crossed, products[segment], precision=HIGHEST), crossed

    _, crossings = lax.scan(
        extend, jnp.eye(HD, dtype=jnp.float32), jnp.arange(segments - 1, dtype=jnp.int32)
    )
    crossings = crossings[jnp.clip(position - 1 - chosen, 0, segments - 2)]
    key_blocks = jnp.einsum(
        "bij,btj->bti", crossings, key_blocks[chosen], precision=HIGHEST
    ).astype(jnp.bfloat16)
    value_blocks = value_blocks[chosen]
    local_peak = jnp.max(own_scores, axis=1)
    near_exp = jnp.exp(own_scores - local_peak[:, None])
    running = (
        local_peak,
        jnp.sum(near_exp, axis=1),
        jnp.dot(near_exp.astype(jnp.bfloat16), value_rows, preferred_element_type=jnp.float32),
    )
    running = attend_blocks(moved_queries, key_blocks, value_blocks, allowed, running)
    attended = (running[2] / running[1][:, None]).astype(jnp.bfloat16)
    groups = attended.shape[0] // SEG
    attended = attended.reshape(groups, SEG, HD).transpose(1, 0, 2).reshape(SEG, groups * HD)
    partial = jnp.dot(attended, w_out, preferred_element_type=jnp.float32).astype(jnp.bfloat16)
    core = lax.axis_index("head")
    half = SEG // lax.axis_size("head")
    away = lax.dynamic_slice_in_dim(partial, (1 - core) * half, half)
    kept = lax.dynamic_slice_in_dim(partial, core * half, half)
    return kept + lax.ppermute(away, "head", [(0, 1), (1, 0)])


def solution(mesh):
    in_specs = (
        P(("ctx", "head"), None),
        P(None, "head"),
        P(None, "head"),
        P(None, "head"),
        P(None, "head"),
        P("head", None),
        P("head"),
        P(),
        P(),
        P("head", None),
        P("ctx", None),
    )
    out_specs = P(("ctx", "head"), None)
    return jax.shard_map(body, mesh=mesh, in_specs=in_specs, out_specs=out_specs, check_vma=False)
```

```python
import functools
import math

import jax
import jax.numpy as jnp
from jax import lax
from jax.experimental import pallas as pl
from jax.experimental.pallas import tpu as pltpu
from jax.sharding import PartitionSpec as P

EPSILON = 1e-06
NEGATIVE = -1e30
F32 = jnp.float32
BF16 = jnp.bfloat16
VMEM_LIMIT = 48 * 1024 * 1024


def call(kernel, out_shape, args, in_specs=None, scratch=(), flops=0, moved=0):
    vmem = pl.BlockSpec(memory_space=pltpu.VMEM)
    return pl.pallas_call(
        kernel,
        out_shape=out_shape,
        in_specs=in_specs or [vmem] * len(args),
        out_specs=jax.tree.map(lambda _: vmem, out_shape),
        scratch_shapes=list(scratch),
        compiler_params=pltpu.CompilerParams(vmem_limit_bytes=VMEM_LIMIT),
        cost_estimate=pl.CostEstimate(flops=flops, bytes_accessed=moved, transcendentals=0),
    )(*args)


def shaped(shape, dtype):
    return jax.ShapeDtypeStruct(shape, dtype)


def split(value):
    high = value.astype(BF16)
    return high, (value - high.astype(F32)).astype(BF16)


def dot3(left, right, left_dim=1, right_dim=0):
    left_high, left_low = split(left)
    right_high, right_low = split(right)
    return lax.dot_general(
        jnp.concatenate([left_high, left_high, left_low], axis=left_dim),
        jnp.concatenate([right_high, right_low, right_high], axis=right_dim),
        (((left_dim,), (right_dim,)), ((), ())),
        preferred_element_type=F32,
    )


def iota2(shape):
    return lax.broadcasted_iota(jnp.int32, shape, 0), lax.broadcasted_iota(jnp.int32, shape, 1)


def project_kernel(rows_ref, key_ref, value_ref, dir_ref, rate_ref, bias_ref, gain_ref,
                   kn_ref, val_ref, dirs_ref, rates_ref):
    rows = rows_ref[...]
    keys = jnp.dot(rows, key_ref[...], preferred_element_type=F32)
    kn_ref[...] = (
        keys * lax.rsqrt(jnp.mean(keys * keys, axis=-1, keepdims=True) + EPSILON) * gain_ref[...]
    )
    raw = jnp.dot(rows, dir_ref[...], preferred_element_type=F32)
    dirs_ref[...] = raw * lax.rsqrt(jnp.sum(raw * raw, axis=-1, keepdims=True) + EPSILON)
    vector = jnp.broadcast_to(rate_ref[...], (16, rows.shape[1]))
    logits = lax.dot_general(rows, vector, (((1,), (1,)), ((), ())), preferred_element_type=F32)
    rates_ref[...] = 2.0 * jax.nn.sigmoid(logits[:, :1] + bias_ref[0])
    val_ref[...] = jnp.dot(rows, value_ref[...], preferred_element_type=F32).astype(BF16)


def solve_kernel(kn_ref, dirs_ref, rates_ref, exit_ref, turn_ref, coeff_ref, solved_ref):
    kn, dirs, rates = kn_ref[...], dirs_ref[...], rates_ref[...]
    tokens, size = dirs.shape
    rows, cols = iota2((tokens, tokens))
    below = rows > cols
    grams = dot3(dirs, jnp.concatenate([dirs, kn], axis=0), 1, 1)
    lower = jnp.where(below, rates * grams[:, :tokens], 0.0)
    crossing = jnp.where(below, rates * grams[:, tokens:], 0.0)
    block = 8
    inverse = jnp.where(rows == cols, 1.0, 0.0).astype(F32)
    first = rows - rows % block
    for step in range(block - 1):
        column = jnp.sum(jnp.where(cols == first + step, lower, 0.0), axis=1, keepdims=True)
        pivot = inverse.reshape(tokens // block, block, tokens)[:, step : step + 1, :]
        pivot = jnp.broadcast_to(pivot, (tokens // block, block, tokens)).reshape(tokens, tokens)
        inverse = inverse - column * pivot
    while block < tokens:
        corner = (
            (rows // (2 * block) == cols // (2 * block))
            & (rows % (2 * block) >= block)
            & (cols % (2 * block) < block)
        )
        inverse = inverse - dot3(dot3(inverse, jnp.where(corner, lower, 0.0)), inverse)
        block *= 2
    both = dot3(inverse, jnp.concatenate([crossing, rates * dirs], axis=1))
    coeff_ref[...] = both[:, :tokens]
    solved_ref[...] = both[:, tokens:]
    crossed = dot3(both, dirs, 0, 0)
    exit_ref[...] = kn - crossed[:tokens]
    heads, lanes = iota2((size, size))
    turn_ref[...] = jnp.where(heads == lanes, 1.0, 0.0) - crossed[tokens:]


def query_kernel(rows_ref, weight_ref, gain_ref, kn_ref, dirs_ref, coeff_ref, solved_ref, val_ref,
                 moved_ref, weighted_ref, peak_ref, total_ref):
    tokens, size = kn_ref.shape
    heads = moved_ref.shape[0]
    raw = jnp.dot(rows_ref[...], weight_ref[...], preferred_element_type=F32)
    raw = jnp.concatenate([raw[:, h * size : (h + 1) * size] for h in range(heads)], axis=0)
    queries = raw * lax.rsqrt(jnp.mean(raw * raw, axis=-1, keepdims=True) + EPSILON) * gain_ref[...]
    seen = dot3(queries, jnp.concatenate([kn_ref[...], dirs_ref[...]], axis=0), 1, 1)
    rows, cols = iota2((heads * tokens, tokens))
    up_to = rows % tokens >= cols
    reach = jnp.where(up_to, seen[:, tokens:], 0.0)
    taken = dot3(reach, jnp.concatenate([coeff_ref[...], solved_ref[...]], axis=1))
    scores = (seen[:, :tokens] - taken[:, :tokens]) * (1.0 / math.sqrt(size))
    scores = jnp.where(up_to, scores, NEGATIVE)
    moved = (queries - taken[:, tokens:]).astype(BF16)
    peak = jnp.max(scores, axis=1, keepdims=True)
    weights = jnp.exp(scores - peak)
    total = jnp.sum(weights, axis=1, keepdims=True)
    weighted = jnp.dot(weights.astype(BF16), val_ref[...], preferred_element_type=F32)
    for h in range(heads):
        part = slice(h * tokens, (h + 1) * tokens)
        moved_ref[h] = moved[part]
        weighted_ref[h] = weighted[part]
        peak_ref[h] = peak[part]
        total_ref[h] = total[part]


def leave_kernel(member_ref, exit_ref, turns_ref, near_ref, last_ref, whole_ref, starts_ref):
    member = member_ref[0]
    size = exit_ref.shape[1]
    group = turns_ref.shape[0]
    own = exit_ref[...]
    heads, lanes = iota2((size, size))
    product = jnp.where(heads == lanes, 1.0, 0.0).astype(F32)
    keys = own
    for index in range(group):
        near_ref[index] = keys.astype(BF16)
        starts_ref[:, index * size : (index + 1) * size] = product
        turn = turns_ref[index]
        product = dot3(product, turn) if index else turn
        keys = jnp.where(index > member, dot3(keys, turn), own)
    last_ref[...] = keys
    whole_ref[...] = product


def arrive_kernel(count, *refs):
    lasts, wholes = refs[:count], refs[count : 2 * count - 1]
    starts_ref, far_ref = refs[2 * count - 1 :]
    tokens, size = lasts[0].shape
    brought = [lasts[0][...]]
    product = None
    for index in range(1, count):
        whole = wholes[index - 1][...]
        product = whole if product is None else dot3(whole, product)
        brought.append(dot3(lasts[index][...], product))
    keys = jnp.concatenate(brought, axis=0)
    for member in range(far_ref.shape[0]):
        start = starts_ref[:, member * size : (member + 1) * size]
        far_ref[member] = (dot3(keys, start) if member else keys).astype(BF16)


def attend_kernel(most, position_ref, mask_ref, near_ref, far_ref, val_ref, moved_ref, weighted_ref,
                  peak_ref, total_ref, out_hbm, away_ref, kept_ref,
                  chosen_ref, keys_ref, vals_ref, attended_ref, run_w, run_p, run_t, out_ref, out_sem):
    out_copy = pltpu.make_async_copy(out_hbm, out_ref, out_sem)
    out_copy.start()
    place, core = position_ref[0], position_ref[1]
    group = near_ref.shape[0]
    heads, tokens, size = moved_ref.shape
    segments = mask_ref.shape[0]
    scaling = 1.0 / math.sqrt(size)
    mine, member = place // group, place % group

    def pick(segment, count):
        @pl.when((mask_ref[segment] > 0) & (segment < place) & (count < most))
        def _():
            chosen_ref[count] = segment

        return count + ((mask_ref[segment] > 0) & (segment < place)).astype(jnp.int32)

    for slot in range(most):
        chosen_ref[slot] = 0
    found = lax.fori_loop(0, segments, pick, jnp.int32(0))
    chunk = keys_ref.shape[0] // tokens
    run_w[...] = weighted_ref[...]
    run_p[...] = peak_ref[...]
    run_t[...] = total_ref[...]
    lanes = lax.broadcasted_iota(jnp.int32, (tokens, chunk * tokens), 1)

    @pl.loop(0, most // chunk)
    def _(turn):
        for slot in range(chunk):
            segment = chosen_ref[turn * chunk + slot]
            whose, distance = segment % group, mine - segment // group
            before = pl.multiple_of(jnp.maximum(distance - 1, 0) * tokens, tokens)
            far = far_ref[whose, pl.ds(before, tokens), :]
            keys_ref[slot * tokens : (slot + 1) * tokens, :] = jnp.where(
                distance > 0, far, near_ref[whose]
            )
            vals_ref[slot * tokens : (slot + 1) * tokens, :] = val_ref[
                whose, pl.ds(pl.multiple_of(distance * tokens, tokens), tokens), :
            ]
        keep = lanes < (found - turn * chunk) * tokens
        keys, vals = keys_ref[...], vals_ref[...]
        for head in range(heads):
            scores = lax.dot_general(
                moved_ref[head], keys, (((1,), (1,)), ((), ())), preferred_element_type=F32
            )
            scores = jnp.where(keep, scores * scaling, NEGATIVE)
            peak = run_p[head]
            new_peak = jnp.maximum(peak, jnp.max(scores, axis=1, keepdims=True))
            fading = jnp.exp(peak - new_peak)
            weights = jnp.exp(scores - new_peak)
            run_p[head] = new_peak
            run_t[head] = run_t[head] * fading + jnp.sum(weights, axis=1, keepdims=True)
            run_w[head] = run_w[head] * fading + jnp.dot(
                weights.astype(BF16), vals, preferred_element_type=F32
            )

    for head in range(heads):
        attended_ref[:, head * size : (head + 1) * size] = (run_w[head] / run_t[head]).astype(BF16)
    out_copy.wait()
    half = kept_ref.shape[0]
    weight = out_ref[...]
    for ref, which in ((away_ref, 1 - core), (kept_ref, core)):
        rows = attended_ref[pl.ds(pl.multiple_of(which * half, half), half), :]
        ref[...] = jnp.dot(rows, weight, preferred_element_type=F32).astype(BF16)


def body(
    hidden, w_query, w_key, w_value, w_dir, u_rate, rate_bias, q_gain, k_gain, w_out, block_mask
):
    segments = lax.axis_size("ctx")
    position = lax.axis_index("ctx")
    core = lax.axis_index("head")
    group = max(d for d in range(1, math.isqrt(segments) + 1) if segments % d == 0)
    groups = segments // group
    members = [[g * group + m for m in range(group)] for g in range(groups)]
    seg_rows = lax.all_gather(hidden, "head", axis=0, tiled=True)
    tokens, width = seg_rows.shape
    size = w_key.shape[1]
    heads = w_query.shape[1] // size
    smem = pl.BlockSpec(memory_space=pltpu.SMEM)
    vmem = pl.BlockSpec(memory_space=pltpu.VMEM)
    square = shaped((tokens, size), F32)

    def within_group(parts):
        return lax.all_to_all(parts, "ctx", 0, 0, axis_index_groups=members)

    def to_later_group(value, distance):
        step = distance * group
        return lax.ppermute(value, "ctx", [(s, s + step) for s in range(segments - step)])

    kn, val, dirs, rates = call(
        project_kernel,
        (square, shaped((tokens, size), BF16), square, shaped((tokens, 1), F32)),
        (seg_rows, w_key, w_value, w_dir, u_rate, rate_bias, k_gain.reshape(1, size)),
        in_specs=[vmem] * 5 + [smem, vmem],
        flops=6 * tokens * width * size,
        moved=8 * width * size,
    )
    vals = jnp.concatenate([val] + [to_later_group(val, d) for d in range(1, groups)], axis=0)
    vals = within_group(jnp.broadcast_to(vals[None], (group,) + vals.shape))
    exit_keys, turn, coeff, solved = call(
        solve_kernel, (square, shaped((size, size), F32), square, square), (kn, dirs, rates),
        flops=40 * tokens**3 * 3, moved=10**6,
    )
    turns = within_group(jnp.broadcast_to(turn[None], (group, size, size)))
    pair = math.gcd(heads, 2)
    blocks = pl.BlockSpec((pair, tokens, size), lambda i: (i, 0, 0))
    thin = pl.BlockSpec((pair, tokens, 1), lambda i: (i, 0, 0))
    moved, weighted, peak, total = pl.pallas_call(
        query_kernel,
        grid=(heads // pair,),
        in_specs=[vmem, pl.BlockSpec((width, pair * size), lambda i: (0, i))] + [vmem] * 6,
        out_specs=(blocks, blocks, thin, thin),
        out_shape=(
            shaped((heads, tokens, size), BF16),
            shaped((heads, tokens, size), F32),
            shaped((heads, tokens, 1), F32),
            shaped((heads, tokens, 1), F32),
        ),
        compiler_params=pltpu.CompilerParams(vmem_limit_bytes=VMEM_LIMIT),
        cost_estimate=pl.CostEstimate(
            flops=4 * tokens * width * heads * size, bytes_accessed=8 * width * heads * size,
            transcendentals=0,
        ),
    )(seg_rows, w_query, q_gain.reshape(1, size), kn, dirs, coeff, solved, val)
    near, last, whole, starts = call(
        leave_kernel,
        (
            shaped((group, tokens, size), BF16),
            square,
            shaped((size, size), F32),
            shaped((size, group * size), F32),
        ),
        ((position % group).reshape(1).astype(jnp.int32), exit_keys, turns),
        in_specs=[smem, vmem, vmem],
        flops=12 * group * size**3,
        moved=10**6,
    )
    wholes = [to_later_group(whole, d) for d in range(1, groups - 1)]
    lasts = [to_later_group(last, d) for d in range(1, groups)]
    near = within_group(near)
    far = call(
        functools.partial(arrive_kernel, groups - 1),
        shaped((group, (groups - 1) * tokens, size), BF16),
        tuple(lasts + wholes + [starts]),
        flops=6 * groups * group * size**3,
        moved=10**6,
    )
    far = within_group(far)
    most = segments // 4
    chunk = math.gcd(most, 4)
    width_out = w_out.shape[1]
    half = tokens // lax.axis_size("head")
    away, kept = call(
        functools.partial(attend_kernel, most),
        (shaped((half, width_out), BF16), shaped((half, width_out), BF16)),
        (
            jnp.stack([position, core]).astype(jnp.int32),
            block_mask[0], near, far, vals, moved, weighted, peak, total, w_out,
        ),
        in_specs=[smem] * 2 + [vmem] * 7 + [pl.BlockSpec(memory_space=pl.ANY)],
        scratch=(
            pltpu.SMEM((most,), jnp.int32),
            pltpu.VMEM((chunk * tokens, size), BF16),
            pltpu.VMEM((chunk * tokens, size), BF16),
            pltpu.VMEM((tokens, heads * size), BF16),
            pltpu.VMEM((heads, tokens, size), F32),
            pltpu.VMEM((heads, tokens, 1), F32),
            pltpu.VMEM((heads, tokens, 1), F32),
            pltpu.VMEM(w_out.shape, BF16),
            pltpu.SemaphoreType.DMA,
        ),
        flops=2 * tokens * width_out * heads * size,
        moved=4 * 10**6,
    )
    return kept + lax.ppermute(away, "head", [(0, 1), (1, 0)])


def solution(mesh):
    in_specs = (
        P(("ctx", "head"), None),
        P(None, "head"),
        P(None, "head"),
        P(None, "head"),
        P(None, "head"),
        P("head", None),
        P("head"),
        P(),
        P(),
        P("head", None),
        P("ctx", None),
    )
    out_specs = P(("ctx", "head"), None)
    return jax.shard_map(body, mesh=mesh, in_specs=in_specs, out_specs=out_specs, check_vma=False)
```

```python
import functools
import math

import jax
import jax.numpy as jnp
from jax import lax
from jax.experimental import pallas as pl
from jax.experimental.pallas import tpu as pltpu
from jax.sharding import PartitionSpec as P

EPSILON = 1e-06
NEGATIVE = -1e30
F32 = jnp.float32
BF16 = jnp.bfloat16
MIB = 1024 * 1024


def call(kernel, out_shape, args, in_specs=None, scratch=(), flops=0, moved=0, limit=6):
    vmem = pl.BlockSpec(memory_space=pltpu.VMEM)
    return pl.pallas_call(
        kernel,
        out_shape=out_shape,
        in_specs=in_specs or [vmem] * len(args),
        out_specs=jax.tree.map(lambda _: vmem, out_shape),
        scratch_shapes=list(scratch),
        compiler_params=pltpu.CompilerParams(vmem_limit_bytes=limit * MIB),
        cost_estimate=pl.CostEstimate(flops=flops, bytes_accessed=moved, transcendentals=0),
    )(*args)


def shaped(shape, dtype):
    return jax.ShapeDtypeStruct(shape, dtype)


def split(value):
    high = value.astype(BF16)
    return high, (value - high.astype(F32)).astype(BF16)


def dot3(left, right, left_dim=1, right_dim=0):
    left_high, left_low = split(left)
    right_high, right_low = split(right)
    return lax.dot_general(
        jnp.concatenate([left_high, left_high, left_low], axis=left_dim),
        jnp.concatenate([right_high, right_low, right_high], axis=right_dim),
        (((left_dim,), (right_dim,)), ((), ())),
        preferred_element_type=F32,
    )


def iota2(shape):
    return lax.broadcasted_iota(jnp.int32, shape, 0), lax.broadcasted_iota(jnp.int32, shape, 1)


def merge_inverse(lower, rows, cols):
    tokens = lower.shape[0]
    block = 8
    inverse = jnp.where(rows == cols, 1.0, 0.0).astype(F32)
    first = rows - rows % block
    for step in range(block - 1):
        column = jnp.sum(jnp.where(cols == first + step, lower, 0.0), axis=1, keepdims=True)
        pivot = inverse.reshape(tokens // block, block, tokens)[:, step : step + 1, :]
        pivot = jnp.broadcast_to(pivot, (tokens // block, block, tokens)).reshape(tokens, tokens)
        inverse = inverse - column * pivot
    while block < tokens:
        corner = (
            (rows // (2 * block) == cols // (2 * block))
            & (rows % (2 * block) >= block)
            & (cols % (2 * block) < block)
        )
        inverse = inverse - dot3(dot3(inverse, jnp.where(corner, lower, 0.0)), inverse)
        block *= 2
    return inverse


def prepare_kernel(core_ref, mine_ref, other_ref, key_ref, value_ref, dir_ref, rate_ref, bias_ref,
                   gain_ref, rows_ref, kn_ref, val_ref, dirs_ref, coeff_ref, solved_ref, exit_ref,
                   turns_ref):
    core = core_ref[0]
    half = mine_ref.shape[0]
    rows_ref[pl.ds(pl.multiple_of(core * half, half), half), :] = mine_ref[...]
    rows_ref[pl.ds(pl.multiple_of((1 - core) * half, half), half), :] = other_ref[...]
    seg = rows_ref[...]
    keys = jnp.dot(seg, key_ref[...], preferred_element_type=F32)
    kn = keys * lax.rsqrt(jnp.mean(keys * keys, axis=-1, keepdims=True) + EPSILON) * gain_ref[...]
    raw = jnp.dot(seg, dir_ref[...], preferred_element_type=F32)
    dirs = raw * lax.rsqrt(jnp.sum(raw * raw, axis=-1, keepdims=True) + EPSILON)
    vector = jnp.broadcast_to(rate_ref[...], (16, seg.shape[1]))
    logits = lax.dot_general(seg, vector, (((1,), (1,)), ((), ())), preferred_element_type=F32)
    rates = 2.0 * jax.nn.sigmoid(logits[:, :1] + bias_ref[0])
    val_ref[...] = jnp.dot(seg, value_ref[...], preferred_element_type=F32).astype(BF16)
    kn_ref[...] = kn
    dirs_ref[...] = dirs
    tokens, size = dirs.shape
    rows, cols = iota2((tokens, tokens))
    below = rows > cols
    grams = dot3(dirs, jnp.concatenate([dirs, kn], axis=0), 1, 1)
    lower = jnp.where(below, rates * grams[:, :tokens], 0.0)
    crossing = jnp.where(below, rates * grams[:, tokens:], 0.0)
    inverse = merge_inverse(lower, rows, cols)
    both = dot3(inverse, jnp.concatenate([crossing, rates * dirs], axis=1))
    coeff_ref[...] = both[:, :tokens]
    solved_ref[...] = both[:, tokens:]
    crossed = dot3(both, dirs, 0, 0)
    exit_ref[...] = kn - crossed[:tokens]
    heads, lanes = iota2((size, size))
    turn = jnp.where(heads == lanes, 1.0, 0.0) - crossed[tokens:]
    for member in range(turns_ref.shape[0]):
        turns_ref[member] = turn


def leave_kernel(member_ref, exit_ref, val_ref, turns_ref, long_ref, short_ref, starts_ref):
    member = member_ref[0]
    tokens, size = exit_ref.shape
    group = turns_ref.shape[0]
    own = exit_ref[...]
    keys = own
    product = None
    heads, lanes = iota2((size, size))
    starts_ref[:, :size] = jnp.where(heads == lanes, 1.0, 0.0)
    for index in range(group):
        turn = turns_ref[index]
        product = turn if product is None else dot3(product, turn)
        if index:
            keys = jnp.where(index > member, dot3(keys, turn), own)
        if index < group - 1:
            starts_ref[:, (index + 1) * size : (index + 2) * size] = product
    high, low = split(keys)
    for ref in (long_ref, short_ref):
        ref[:tokens] = high
        ref[tokens : 2 * tokens] = low
        ref[2 * tokens : 3 * tokens] = val_ref[...]
    high, low = split(product)
    long_ref[3 * tokens : 3 * tokens + size] = high
    long_ref[3 * tokens + size :] = low


def query_kernel(member_ref, rows_ref, weight_ref, gain_ref, kn_ref, dirs_ref, coeff_ref,
                 solved_ref, val_ref, exit_ref, turns_ref, after_ref,
                 moved_ref, weighted_ref, peak_ref, total_ref, near_ref):
    tokens, size = kn_ref.shape
    heads = moved_ref.shape[0]

    @pl.when(pl.program_id(0) == 0)
    def _():
        member = member_ref[0]
        keys = exit_ref[...]
        for index in range(near_ref.shape[0]):
            if index > 1:
                keys = jnp.where(index - 1 > member, dot3(keys, turns_ref[index - 1]), exit_ref[...])
            near_ref[index, :tokens] = keys.astype(BF16)
            near_ref[index, tokens:] = val_ref[...]

    raw = jnp.dot(rows_ref[...], weight_ref[...], preferred_element_type=F32)
    raw = jnp.concatenate([raw[:, h * size : (h + 1) * size] for h in range(heads)], axis=0)
    queries = raw * lax.rsqrt(jnp.mean(raw * raw, axis=-1, keepdims=True) + EPSILON) * gain_ref[...]
    seen = dot3(queries, jnp.concatenate([kn_ref[...], dirs_ref[...]], axis=0), 1, 1)
    rows, cols = iota2((heads * tokens, tokens))
    up_to = rows % tokens >= cols
    reach = jnp.where(up_to, seen[:, tokens:], 0.0)
    taken = dot3(reach, jnp.concatenate([coeff_ref[...], solved_ref[...]], axis=1))
    scores = (seen[:, :tokens] - taken[:, :tokens]) * (1.0 / math.sqrt(size))
    scores = jnp.where(up_to, scores, NEGATIVE)
    moved = (queries - taken[:, tokens:]).astype(BF16)
    peak = jnp.max(scores, axis=1, keepdims=True)
    weights = jnp.exp(scores - peak)
    total = jnp.sum(weights, axis=1, keepdims=True)
    weighted = jnp.dot(weights.astype(BF16), val_ref[...], preferred_element_type=F32)
    for h in range(heads):
        part = slice(h * tokens, (h + 1) * tokens)
        moved_ref[h] = moved[part]
        weighted_ref[h] = weighted[part]
        peak_ref[h] = peak[part]
        total_ref[h] = total[part]


def arrive_kernel(count, tokens, *refs):
    arrived, starts_ref, far_ref = refs[:count], refs[count], refs[-1]
    size = starts_ref.shape[0]
    product = None
    brought = []
    for index in range(count):
        ref = arrived[index]
        keys = ref[:tokens].astype(F32) + ref[tokens : 2 * tokens].astype(F32)
        if index:
            before = arrived[index - 1]
            whole = before[3 * tokens : 3 * tokens + size].astype(F32)
            whole = whole + before[3 * tokens + size :].astype(F32)
            product = whole if product is None else dot3(whole, product)
            keys = dot3(keys, product)
        brought.append(keys)
    keys = jnp.concatenate(brought, axis=0)
    split_at = count * tokens
    for member in range(far_ref.shape[0]):
        start = starts_ref[:, member * size : (member + 1) * size]
        far_ref[member, :split_at] = (dot3(keys, start) if member else keys).astype(BF16)
        for index in range(count):
            far_ref[member, split_at + index * tokens : split_at + (index + 1) * tokens] = arrived[
                index
            ][2 * tokens : 3 * tokens]


def attend_kernel(most, position_ref, mask_ref, near_ref, far_ref, moved_ref, weighted_ref, peak_ref,
                  total_ref, out_hbm, away_ref, kept_ref,
                  chosen_ref, keys_ref, vals_ref, attended_ref, run_w, run_p, run_t, out_ref, out_sem):
    out_copy = pltpu.make_async_copy(out_hbm, out_ref, out_sem)
    out_copy.start()
    place, core = position_ref[0], position_ref[1]
    group = near_ref.shape[0]
    heads, tokens, size = moved_ref.shape
    segments = mask_ref.shape[0]
    scaling = 1.0 / math.sqrt(size)
    mine, member = place // group, place % group

    def pick(segment, count):
        @pl.when((mask_ref[segment] > 0) & (segment < place) & (count < most))
        def _():
            chosen_ref[count] = segment

        return count + ((mask_ref[segment] > 0) & (segment < place)).astype(jnp.int32)

    for slot in range(most):
        chosen_ref[slot] = 0
    found = lax.fori_loop(0, segments, pick, jnp.int32(0))
    chunk = keys_ref.shape[0] // tokens
    run_w[...] = weighted_ref[...]
    run_p[...] = peak_ref[...]
    run_t[...] = total_ref[...]
    lanes = lax.broadcasted_iota(jnp.int32, (tokens, chunk * tokens), 1)

    @pl.loop(0, most // chunk)
    def _(turn):
        for slot in range(chunk):
            segment = chosen_ref[turn * chunk + slot]
            whose, distance = segment % group, mine - segment // group
            before = jnp.maximum(distance - 1, 0) * tokens
            part = slice(slot * tokens, (slot + 1) * tokens)
            for ref, at, offset in ((keys_ref, 0, 0), (vals_ref, tokens, far_ref.shape[1] // 2)):
                far = far_ref[whose, pl.ds(pl.multiple_of(offset + before, tokens), tokens), :]
                ref[part, :] = jnp.where(distance > 0, far, near_ref[whose, at : at + tokens, :])
        keep = lanes < (found - turn * chunk) * tokens
        keys, vals = keys_ref[...], vals_ref[...]
        for head in range(heads):
            scores = lax.dot_general(
                moved_ref[head], keys, (((1,), (1,)), ((), ())), preferred_element_type=F32
            )
            scores = jnp.where(keep, scores * scaling, NEGATIVE)
            peak = run_p[head]
            new_peak = jnp.maximum(peak, jnp.max(scores, axis=1, keepdims=True))
            fading = jnp.exp(peak - new_peak)
            weights = jnp.exp(scores - new_peak)
            run_p[head] = new_peak
            run_t[head] = run_t[head] * fading + jnp.sum(weights, axis=1, keepdims=True)
            run_w[head] = run_w[head] * fading + jnp.dot(
                weights.astype(BF16), vals, preferred_element_type=F32
            )

    half = kept_ref.shape[0]
    for head in range(heads):
        done = (run_w[head] / run_t[head]).astype(BF16)
        for index in range(tokens // half):
            at = jnp.where(index == core, half, 0)
            attended_ref[pl.ds(pl.multiple_of(at, half), half), head * size : (head + 1) * size] = (
                done[index * half : (index + 1) * half]
            )
    out_copy.wait()
    result = jnp.dot(attended_ref[...], out_ref[...], preferred_element_type=F32).astype(BF16)
    away_ref[...] = result[:half]
    kept_ref[...] = result[half:]


def body(
    hidden, w_query, w_key, w_value, w_dir, u_rate, rate_bias, q_gain, k_gain, w_out, block_mask
):
    segments = lax.axis_size("ctx")
    position = lax.axis_index("ctx")
    core = lax.axis_index("head")
    group = max(d for d in range(1, math.isqrt(segments) + 1) if segments % d == 0)
    groups = segments // group
    members = [[g * group + m for m in range(group)] for g in range(groups)]
    other = lax.ppermute(hidden, "head", [(0, 1), (1, 0)])
    half, width = hidden.shape
    tokens = half * lax.axis_size("head")
    size = w_key.shape[1]
    heads = w_query.shape[1] // size
    smem = pl.BlockSpec(memory_space=pltpu.SMEM)
    vmem = pl.BlockSpec(memory_space=pltpu.VMEM)
    anywhere = pl.BlockSpec(memory_space=pl.ANY)
    square = shaped((tokens, size), F32)
    member = (position % group).reshape(1).astype(jnp.int32)

    def within_group(parts):
        return lax.all_to_all(parts, "ctx", 0, 0, axis_index_groups=members)

    def to_later_group(value, distance):
        step = distance * group
        return lax.ppermute(value, "ctx", [(s, s + step) for s in range(segments - step)])

    rows, kn, val, dirs, coeff, solved, exit_keys, turns = call(
        prepare_kernel,
        (
            shaped((tokens, width), BF16), square, shaped((tokens, size), BF16), square, square,
            square, square, shaped((group, size, size), F32),
        ),
        (
            core.reshape(1).astype(jnp.int32), hidden, other, w_key, w_value, w_dir, u_rate,
            rate_bias, k_gain.reshape(1, size),
        ),
        in_specs=[smem] + [vmem] * 6 + [smem, vmem],
        flops=6 * tokens * width * size,
        moved=8 * width * size,
    )
    turns = within_group(turns)
    long, short, starts = call(
        leave_kernel,
        (
            shaped((3 * tokens + 2 * size, size), BF16),
            shaped((3 * tokens, size), BF16),
            shaped((size, group * size), F32),
        ),
        (member, exit_keys, val, turns),
        in_specs=[smem, vmem, vmem, vmem],
        flops=12 * group * size**3,
        moved=10**6,
    )
    arrived = [
        to_later_group(long if d < groups - 1 else short, d) for d in range(1, groups)
    ]
    pair = math.gcd(heads, 2)
    blocks = pl.BlockSpec((pair, tokens, size), lambda i: (i, 0, 0))
    thin = pl.BlockSpec((pair, tokens, 1), lambda i: (i, 0, 0))
    moved, weighted, peak, total, near = pl.pallas_call(
        query_kernel,
        grid=(heads // pair,),
        in_specs=[smem, vmem, pl.BlockSpec((width, pair * size), lambda i: (0, i))]
        + [vmem] * 8
        + [anywhere],
        out_specs=(
            blocks, blocks, thin, thin,
            pl.BlockSpec((group, 2 * tokens, size), lambda i: (0, 0, 0)),
        ),
        out_shape=(
            shaped((heads, tokens, size), BF16),
            shaped((heads, tokens, size), F32),
            shaped((heads, tokens, 1), F32),
            shaped((heads, tokens, 1), F32),
            shaped((group, 2 * tokens, size), BF16),
        ),
        compiler_params=pltpu.CompilerParams(vmem_limit_bytes=12 * MIB),
        cost_estimate=pl.CostEstimate(
            flops=4 * tokens * width * heads * size, bytes_accessed=8 * width * heads * size,
            transcendentals=0,
        ),
    )(
        member, rows, w_query, q_gain.reshape(1, size), kn, dirs, coeff, solved, val, exit_keys,
        turns, starts,
    )
    near = within_group(near)
    far = call(
        functools.partial(arrive_kernel, groups - 1, tokens),
        shaped((group, 2 * (groups - 1) * tokens, size), BF16),
        tuple(arrived + [starts, peak]),
        in_specs=[vmem] * groups + [anywhere],
        flops=6 * groups * group * size**3,
        moved=10**6,
        limit=8 + group * groups // 4,
    )
    far = within_group(far)
    most = segments // 4
    chunk = math.gcd(most, 4)
    width_out = w_out.shape[1]
    away, kept = call(
        functools.partial(attend_kernel, most),
        (shaped((half, width_out), BF16), shaped((half, width_out), BF16)),
        (
            jnp.stack([position, core]).astype(jnp.int32),
            block_mask[0], near, far, moved, weighted, peak, total, w_out,
        ),
        in_specs=[smem] * 2 + [vmem] * 6 + [anywhere],
        scratch=(
            pltpu.SMEM((most,), jnp.int32),
            pltpu.VMEM((chunk * tokens, size), BF16),
            pltpu.VMEM((chunk * tokens, size), BF16),
            pltpu.VMEM((tokens, heads * size), BF16),
            pltpu.VMEM((heads, tokens, size), F32),
            pltpu.VMEM((heads, tokens, 1), F32),
            pltpu.VMEM((heads, tokens, 1), F32),
            pltpu.VMEM(w_out.shape, BF16),
            pltpu.SemaphoreType.DMA,
        ),
        flops=2 * tokens * width_out * heads * size,
        moved=4 * 10**6,
        limit=14 + group * groups // 4,
    )
    return kept + lax.ppermute(away, "head", [(0, 1), (1, 0)])


def solution(mesh):
    in_specs = (
        P(("ctx", "head"), None),
        P(None, "head"),
        P(None, "head"),
        P(None, "head"),
        P(None, "head"),
        P("head", None),
        P("head"),
        P(),
        P(),
        P("head", None),
        P("ctx", None),
    )
    out_specs = P(("ctx", "head"), None)
    return jax.shard_map(body, mesh=mesh, in_specs=in_specs, out_specs=out_specs, check_vma=False)
```

```python
import functools
import math

import jax
import jax.numpy as jnp
from jax import lax
from jax.experimental import pallas as pl
from jax.experimental.pallas import tpu as pltpu
from jax.sharding import PartitionSpec as P

EPSILON = 1e-06
NEGATIVE = -1e30
F32 = jnp.float32
BF16 = jnp.bfloat16
MIB = 1024 * 1024


def call(kernel, out_shape, args, in_specs=None, scratch=(), flops=0, moved=0, limit=6):
    vmem = pl.BlockSpec(memory_space=pltpu.VMEM)
    return pl.pallas_call(
        kernel,
        out_shape=out_shape,
        in_specs=in_specs or [vmem] * len(args),
        out_specs=jax.tree.map(lambda _: vmem, out_shape),
        scratch_shapes=list(scratch),
        compiler_params=pltpu.CompilerParams(vmem_limit_bytes=limit * MIB),
        cost_estimate=pl.CostEstimate(flops=flops, bytes_accessed=moved, transcendentals=0),
    )(*args)


def target_of(member, step, group):
    return member ^ step if group & (group - 1) == 0 else (member + step) % group


def source_of(member, step, group):
    return member ^ step if group & (group - 1) == 0 else (member + group - step) % group


def in_hbm(array):
    return pltpu.with_memory_space_constraint(array, pltpu.HBM)


def shaped(shape, dtype):
    return jax.ShapeDtypeStruct(shape, dtype)


def split(value):
    high = value.astype(BF16)
    return high, (value - high.astype(F32)).astype(BF16)


def dot3(left, right, left_dim=1, right_dim=0):
    left_high, left_low = split(left)
    right_high, right_low = split(right)
    return lax.dot_general(
        jnp.concatenate([left_high, left_high, left_low], axis=left_dim),
        jnp.concatenate([right_high, right_low, right_high], axis=right_dim),
        (((left_dim,), (right_dim,)), ((), ())),
        preferred_element_type=F32,
    )


def iota2(shape):
    return lax.broadcasted_iota(jnp.int32, shape, 0), lax.broadcasted_iota(jnp.int32, shape, 1)


def merge_inverse(lower, rows, cols):
    tokens = lower.shape[0]
    block = 8
    inverse = jnp.where(rows == cols, 1.0, 0.0).astype(F32)
    first = rows - rows % block
    for step in range(block - 1):
        column = jnp.sum(jnp.where(cols == first + step, lower, 0.0), axis=1, keepdims=True)
        pivot = inverse.reshape(tokens // block, block, tokens)[:, step : step + 1, :]
        pivot = jnp.broadcast_to(pivot, (tokens // block, block, tokens)).reshape(tokens, tokens)
        inverse = inverse - column * pivot
    while block < tokens:
        corner = (
            (rows // (2 * block) == cols // (2 * block))
            & (rows % (2 * block) >= block)
            & (cols % (2 * block) < block)
        )
        inverse = inverse - dot3(dot3(inverse, jnp.where(corner, lower, 0.0)), inverse)
        block *= 2
    return inverse


def load_kernel(size, key_hbm, dir_hbm, value_hbm, rate_hbm, key_gain_hbm,
                query_gain_hbm, mine_hbm, weight_ref, rate_ref, key_gain_ref, query_gain_ref,
                mine_ref, sems):
    pairs = [
        (hbm, weight_ref.at[:, index * size : (index + 1) * size])
        for index, hbm in enumerate((key_hbm, dir_hbm, value_hbm))
    ]
    pairs += [(rate_hbm, rate_ref), (key_gain_hbm, key_gain_ref)]
    pairs += [(query_gain_hbm, query_gain_ref), (mine_hbm, mine_ref)]
    copies = [pltpu.make_async_copy(*pair, sems.at[n]) for n, pair in enumerate(pairs)]
    for copy in copies:
        copy.start()
    for copy in copies:
        copy.wait()


def prepare_kernel(place_ref, mine_ref, other_ref, weight_ref, rate_ref, bias_ref, gain_ref,
                   rows_ref, kn_ref, val_ref, dirs_ref, coeff_ref, solved_ref, exit_ref, turn_ref):
    core = place_ref[1]
    half = mine_ref.shape[0]
    rows_ref[pl.ds(pl.multiple_of(core * half, half), half), :] = mine_ref[...]
    rows_ref[pl.ds(pl.multiple_of((1 - core) * half, half), half), :] = other_ref[...]
    seg = rows_ref[...]
    size = turn_ref.shape[0]
    raw = jnp.dot(seg, weight_ref[...], preferred_element_type=F32)
    keys, raw, vals = raw[:, :size], raw[:, size : 2 * size], raw[:, 2 * size :]
    kn = keys * lax.rsqrt(jnp.mean(keys * keys, axis=-1, keepdims=True) + EPSILON) * gain_ref[...]
    dirs = raw * lax.rsqrt(jnp.sum(raw * raw, axis=-1, keepdims=True) + EPSILON)
    vector = jnp.broadcast_to(rate_ref[...], (16, seg.shape[1]))
    logits = lax.dot_general(seg, vector, (((1,), (1,)), ((), ())), preferred_element_type=F32)
    rates = 2.0 * jax.nn.sigmoid(logits[:, :1] + bias_ref[0])
    val_ref[...] = vals.astype(BF16)
    kn_ref[...] = kn
    dirs_ref[...] = dirs
    tokens, size = dirs.shape
    rows, cols = iota2((tokens, tokens))
    below = rows > cols
    grams = dot3(dirs, jnp.concatenate([dirs, kn], axis=0), 1, 1)
    lower = jnp.where(below, rates * grams[:, :tokens], 0.0)
    crossing = jnp.where(below, rates * grams[:, tokens:], 0.0)
    inverse = merge_inverse(lower, rows, cols)
    both = dot3(inverse, jnp.concatenate([crossing, rates * dirs], axis=1))
    coeff_ref[...] = both[:, :tokens]
    solved_ref[...] = both[:, tokens:]
    crossed = dot3(both, dirs, 0, 0)
    exit_ref[...] = kn - crossed[:tokens]
    heads, lanes = iota2((size, size))
    turn_ref[...] = jnp.where(heads == lanes, 1.0, 0.0) - crossed[tokens:]


def leave_kernel(group, place_ref, exit_ref, val_ref, *refs):
    turn_refs, (long_ref, short_ref, starts_ref) = refs[:group], refs[group : group + 3]
    near_refs, (turns_ref, seen_ref) = refs[group + 3 : -2], refs[-2:]
    member = place_ref[0] % group
    tokens, size = exit_ref.shape
    for step in range(group):
        turns_ref[source_of(member, step, group)] = turn_refs[step][...]
    own = exit_ref[...]
    keys = own
    product = None
    heads, lanes = iota2((size, size))
    starts_ref[0] = jnp.where(heads == lanes, 1.0, 0.0)
    for index in range(group):
        seen_ref[index] = keys.astype(BF16)
        turn = turns_ref[index]
        product = turn if product is None else dot3(product, turn)
        if index:
            keys = jnp.where(index > member, dot3(keys, turn), own)
        if index < group - 1:
            starts_ref[index + 1] = product
    high, low = split(keys)
    for ref in (long_ref, short_ref):
        ref[:tokens] = high
        ref[tokens : 2 * tokens] = low
        ref[2 * tokens : 3 * tokens] = val_ref[...]
    high, low = split(product)
    long_ref[3 * tokens : 3 * tokens + size] = high
    long_ref[3 * tokens + size :] = low
    for step in range(1, group):
        near_refs[step - 1][:tokens] = seen_ref[target_of(member, step, group)]
        near_refs[step - 1][tokens:] = val_ref[...]


def query_kernel(rows_ref, weight_hbm, gain_ref, kn_ref, dirs_ref, coeff_ref, solved_ref, val_ref,
                 moved_ref, weighted_ref, peak_ref, total_ref, weight_ref, sems):
    tokens, size = kn_ref.shape
    heads = moved_ref.shape[0]
    pieces = weight_ref.shape[0]
    wide = weight_ref.shape[2]
    copies = [
        pltpu.make_async_copy(
            weight_hbm.at[:, n * wide : (n + 1) * wide], weight_ref.at[n], sems.at[n]
        )
        for n in range(pieces)
    ]
    for copy in copies:
        copy.start()
    across = jnp.concatenate([kn_ref[...], dirs_ref[...]], axis=0)
    into = jnp.concatenate([coeff_ref[...], solved_ref[...]], axis=1)
    together = math.gcd(pieces, 2)
    for turn in range(pieces // together):
        parts = []
        for n in range(turn * together, (turn + 1) * together):
            copies[n].wait()
            raw = jnp.dot(rows_ref[...], weight_ref[n], preferred_element_type=F32)
            parts += [raw[:, at : at + size] for at in range(0, wide, size)]
        count = len(parts)
        raw = jnp.concatenate(parts, axis=0)
        queries = (
            raw * lax.rsqrt(jnp.mean(raw * raw, axis=-1, keepdims=True) + EPSILON) * gain_ref[...]
        )
        seen = dot3(queries, across, 1, 1)
        rows, cols = iota2((count * tokens, tokens))
        up_to = rows % tokens >= cols
        reach = jnp.where(up_to, seen[:, tokens:], 0.0)
        taken = dot3(reach, into)
        scores = (seen[:, :tokens] - taken[:, :tokens]) * (1.0 / math.sqrt(size))
        scores = jnp.where(up_to, scores, NEGATIVE)
        moved = (queries - taken[:, tokens:]).astype(BF16)
        peak = jnp.max(scores, axis=1, keepdims=True)
        weights = jnp.exp(scores - peak)
        total = jnp.sum(weights, axis=1, keepdims=True)
        weighted = jnp.dot(weights.astype(BF16), val_ref[...], preferred_element_type=F32)
        for h in range(count):
            part = slice(h * tokens, (h + 1) * tokens)
            head = turn * count + h
            moved_ref[head] = moved[part]
            weighted_ref[head] = weighted[part]
            peak_ref[head] = peak[part]
            total_ref[head] = total[part]


def arrive_kernel(count, group, tokens, place_ref, *refs):
    arrived, starts_ref = refs[:count], refs[count]
    far_refs = refs[-group:]
    member = place_ref[0] % group
    size = starts_ref.shape[1]
    product = None
    brought = []
    for index in range(count):
        ref = arrived[index]
        keys = ref[:tokens].astype(F32) + ref[tokens : 2 * tokens].astype(F32)
        if index:
            before = arrived[index - 1]
            whole = before[3 * tokens : 3 * tokens + size].astype(F32)
            whole = whole + before[3 * tokens + size :].astype(F32)
            product = whole if product is None else dot3(whole, product)
            keys = dot3(keys, product)
        brought.append(keys)
    keys = jnp.concatenate(brought, axis=0)
    split_at = count * tokens
    for step in range(group):
        start = starts_ref[target_of(member, step, group)]
        far_refs[step][:split_at] = dot3(keys, start).astype(BF16)
        for index in range(count):
            far_refs[step][split_at + index * tokens : split_at + (index + 1) * tokens] = arrived[
                index
            ][2 * tokens : 3 * tokens]


def attend_kernel(most, group, place_ref, mask_ref, *refs):
    near_refs, far_refs = refs[: group - 1], refs[group - 1 : 2 * group - 1]
    (moved_ref, weighted_ref, peak_ref, total_ref, out_hbm, away_ref, kept_ref, chosen_ref,
     keys_ref, vals_ref, attended_ref, out_ref, sems, *state) = refs[2 * group - 1 :]
    pieces, _, wide = out_ref.shape
    copies = [
        pltpu.make_async_copy(
            out_hbm.at[:, n * wide : (n + 1) * wide], out_ref.at[n], sems.at[n]
        )
        for n in range(pieces)
    ]
    for copy in copies:
        copy.start()
    place, core = place_ref[0], place_ref[1]
    heads, tokens, size = moved_ref.shape
    segments = mask_ref.shape[0]
    scaling = 1.0 / math.sqrt(size)
    mine, member = place // group, place % group

    def pick(segment, count):
        wanted = (mask_ref[segment] > 0) & (segment < place)

        @pl.when(wanted & (count < most))
        def _():
            chosen_ref[count] = segment

        return count + wanted.astype(jnp.int32)

    found = lax.fori_loop(0, segments, pick, jnp.int32(0))
    chunk = keys_ref.shape[0] // tokens
    lanes = lax.broadcasted_iota(jnp.int32, (tokens, chunk * tokens), 1)

    def collect(turn):
        for slot in range(chunk):
            part = slice(slot * tokens, (slot + 1) * tokens)
            index = turn * chunk + slot
            used = index < found
            segment = jnp.where(used, chosen_ref[index], 0)
            whose, distance = segment % group, mine - segment // group
            before = jnp.maximum(distance - 1, 0) * tokens

            @pl.when(jnp.logical_not(used))
            def _():
                keys_ref[part, :] = jnp.zeros((tokens, size), BF16)
                vals_ref[part, :] = jnp.zeros((tokens, size), BF16)

            for step in range(group):
                here = used & (whose == source_of(member, step, group))

                @pl.when(here & (distance > 0))
                def _():
                    far = far_refs[step]
                    middle = far.shape[0] // 2
                    keys_ref[part, :] = far[pl.ds(pl.multiple_of(before, tokens), tokens), :]
                    vals_ref[part, :] = far[
                        pl.ds(pl.multiple_of(middle + before, tokens), tokens), :
                    ]

                if step:

                    @pl.when(here & (distance == 0))
                    def _():
                        keys_ref[part, :] = near_refs[step - 1][:tokens]
                        vals_ref[part, :] = near_refs[step - 1][tokens:]

    def advance(head, turn, peak, total, weighted):
        scores = lax.dot_general(
            moved_ref[head], keys_ref[...], (((1,), (1,)), ((), ())), preferred_element_type=F32
        )
        scores = jnp.where(lanes < (found - turn * chunk) * tokens, scores * scaling, NEGATIVE)
        new_peak = jnp.maximum(peak, jnp.max(scores, axis=1, keepdims=True))
        fading = jnp.exp(peak - new_peak)
        weights = jnp.exp(scores - new_peak)
        total = total * fading + jnp.sum(weights, axis=1, keepdims=True)
        weighted = weighted * fading + jnp.dot(
            weights.astype(BF16), vals_ref[...], preferred_element_type=F32
        )
        return new_peak, total, weighted

    half = kept_ref.shape[0]

    def finish(head, total, weighted):
        done = (weighted / total).astype(BF16)
        for index in range(tokens // half):
            at = pl.multiple_of(jnp.where(index == core, half, 0), half)
            attended_ref[pl.ds(at, half), head * size : (head + 1) * size] = done[
                index * half : (index + 1) * half
            ]

    turns = most // chunk
    if turns == 1:
        collect(0)
        for head in range(heads):
            _, total, weighted = advance(
                head, 0, peak_ref[head], total_ref[head], weighted_ref[head]
            )
            finish(head, total, weighted)
    else:
        run_p, run_t, run_w = state
        run_p[...], run_t[...], run_w[...] = peak_ref[...], total_ref[...], weighted_ref[...]

        @pl.loop(0, turns)
        def _(turn):
            collect(turn)
            for head in range(heads):
                run_p[head], run_t[head], run_w[head] = advance(
                    head, turn, run_p[head], run_t[head], run_w[head]
                )

        for head in range(heads):
            finish(head, run_t[head], run_w[head])
    for n in range(pieces):
        copies[n].wait()
        result = jnp.dot(attended_ref[...], out_ref[n], preferred_element_type=F32).astype(BF16)
        away_ref[:, n * wide : (n + 1) * wide] = result[:half]
        kept_ref[:, n * wide : (n + 1) * wide] = result[half:]


def body(
    hidden, w_query, w_key, w_value, w_dir, u_rate, rate_bias, q_gain, k_gain, w_out, block_mask
):
    segments = lax.axis_size("ctx")
    position = lax.axis_index("ctx")
    core = lax.axis_index("head")
    group = max(d for d in range(1, math.isqrt(segments) + 1) if segments % d == 0)
    groups = segments // group
    other = lax.ppermute(hidden, "head", [(0, 1), (1, 0)])
    half, width = hidden.shape
    tokens = half * lax.axis_size("head")
    size = w_key.shape[1]
    heads = w_query.shape[1] // size
    smem = pl.BlockSpec(memory_space=pltpu.SMEM)
    vmem = pl.BlockSpec(memory_space=pltpu.VMEM)
    hbm = pl.BlockSpec(memory_space=pltpu.HBM)
    anywhere = pl.BlockSpec(memory_space=pl.ANY)
    square = shaped((tokens, size), F32)
    place = jnp.stack([position, core]).astype(jnp.int32)

    def to_member(value, step):
        pairs = [
            (s, s - s % group + target_of(s % group, step, group)) for s in range(segments)
        ]
        return lax.ppermute(value, "ctx", pairs)

    def to_later_group(value, distance):
        step = distance * group
        return lax.ppermute(value, "ctx", [(s, s + step) for s in range(segments - step)])

    weights, rate_row, key_gain, query_gain, mine = call(
        functools.partial(load_kernel, size),
        (
            shaped((width, 3 * size), BF16), shaped((1, width), BF16), shaped((1, size), F32),
            shaped((1, size), F32), shaped((half, width), BF16),
        ),
        tuple(
            in_hbm(array)
            for array in (
                w_key, w_dir, w_value, u_rate, k_gain.reshape(1, size), q_gain.reshape(1, size),
                hidden,
            )
        ),
        in_specs=[hbm] * 7,
        scratch=(pltpu.SemaphoreType.DMA((7,)),),
        moved=12 * width * size,
    )
    rows, kn, val, dirs, coeff, solved, exit_keys, turn = call(
        prepare_kernel,
        (
            shaped((tokens, width), BF16), square, shaped((tokens, size), BF16), square, square,
            square, square, shaped((size, size), F32),
        ),
        (place, mine, other, weights, rate_row, rate_bias, key_gain),
        in_specs=[smem] + [vmem] * 4 + [smem, vmem],
        flops=6 * tokens * width * size,
        moved=8 * width * size,
    )
    turns = [turn] + [to_member(turn, step) for step in range(1, group)]
    long, short, starts, *near = call(
        functools.partial(leave_kernel, group),
        [
            shaped((3 * tokens + 2 * size, size), BF16),
            shaped((3 * tokens, size), BF16),
            shaped((group, size, size), F32),
        ]
        + [shaped((2 * tokens, size), BF16)] * (group - 1),
        (place, exit_keys, val, *turns),
        in_specs=[smem] + [vmem] * (2 + group),
        scratch=(
            pltpu.VMEM((group, size, size), F32),
            pltpu.VMEM((group, tokens, size), BF16),
        ),
        flops=12 * group * size**3,
        moved=10**6,
    )
    arrived = [
        to_later_group(long if d < groups - 1 else short, d) for d in range(1, groups)
    ]
    near = [to_member(near[step - 1], step) for step in range(1, group)]
    pieces = math.gcd(heads, 4)
    moved, weighted, peak, total = call(
        query_kernel,
        (
            shaped((heads, tokens, size), BF16),
            shaped((heads, tokens, size), F32),
            shaped((heads, tokens, 1), F32),
            shaped((heads, tokens, 1), F32),
        ),
        (rows, in_hbm(w_query), query_gain, kn, dirs, coeff, solved, val),
        in_specs=[vmem, hbm] + [vmem] * 6,
        scratch=(
            pltpu.VMEM((pieces, width, w_query.shape[1] // pieces), BF16),
            pltpu.SemaphoreType.DMA((pieces,)),
        ),
        flops=4 * tokens * width * heads * size,
        moved=8 * width * heads * size,
        limit=16,
    )
    far = call(
        functools.partial(arrive_kernel, groups - 1, group, tokens),
        [shaped((2 * (groups - 1) * tokens, size), BF16)] * group,
        (place, *arrived, starts, *near),
        in_specs=[smem] + [vmem] * groups + [anywhere] * (group - 1),
        flops=6 * groups * group * size**3,
        moved=10**6,
        limit=8 + group * groups // 4,
    )
    far = [far[0]] + [to_member(far[step], step) for step in range(1, group)]
    most = segments // 4
    chunk = math.gcd(most, 4)
    width_out = w_out.shape[1]
    pieces = math.gcd(width_out // size, 4)
    scratch = [
        pltpu.SMEM((most,), jnp.int32),
        pltpu.VMEM((chunk * tokens, size), BF16),
        pltpu.VMEM((chunk * tokens, size), BF16),
        pltpu.VMEM((tokens, heads * size), BF16),
        pltpu.VMEM((pieces, heads * size, width_out // pieces), BF16),
        pltpu.SemaphoreType.DMA((pieces,)),
    ]
    if most > chunk:
        scratch += [pltpu.VMEM((heads, tokens, 1), F32)] * 2
        scratch += [pltpu.VMEM((heads, tokens, size), F32)]
    away, kept = call(
        functools.partial(attend_kernel, most, group),
        [shaped((half, width_out), BF16)] * 2,
        (place, block_mask[0], *near, *far, moved, weighted, peak, total, in_hbm(w_out)),
        in_specs=[smem] * 2 + [vmem] * (2 * group - 1 + 4) + [hbm],
        scratch=scratch,
        flops=2 * tokens * width_out * heads * size,
        moved=4 * 10**6,
        limit=16 + group * groups // 4,
    )
    return kept + lax.ppermute(away, "head", [(0, 1), (1, 0)])


def solution(mesh):
    in_specs = (
        P(("ctx", "head"), None),
        P(None, "head"),
        P(None, "head"),
        P(None, "head"),
        P(None, "head"),
        P("head", None),
        P("head"),
        P(),
        P(),
        P("head", None),
        P("ctx", None),
    )
    out_specs = P(("ctx", "head"), None)
    return jax.shard_map(body, mesh=mesh, in_specs=in_specs, out_specs=out_specs, check_vma=False)
```

```python
import functools
import math

import jax
import jax.numpy as jnp
from jax import lax
from jax.experimental import pallas as pl
from jax.experimental.pallas import tpu as pltpu
from jax.sharding import PartitionSpec as P

EPSILON = 1e-06
NEGATIVE = -1e30
F32 = jnp.float32
BF16 = jnp.bfloat16
MIB = 1024 * 1024


def call(kernel, out_shape, args, in_specs=None, scratch=(), flops=0, moved=0, limit=6):
    vmem = pl.BlockSpec(memory_space=pltpu.VMEM)
    return pl.pallas_call(
        kernel,
        out_shape=out_shape,
        in_specs=in_specs or [vmem] * len(args),
        out_specs=jax.tree.map(lambda _: vmem, out_shape),
        scratch_shapes=list(scratch),
        compiler_params=pltpu.CompilerParams(vmem_limit_bytes=limit * MIB),
        cost_estimate=pl.CostEstimate(flops=flops, bytes_accessed=moved, transcendentals=0),
    )(*args)


def target_of(member, step, group):
    return member ^ step if group & (group - 1) == 0 else (member + step) % group


def source_of(member, step, group):
    return member ^ step if group & (group - 1) == 0 else (member + group - step) % group


def in_hbm(array):
    return pltpu.with_memory_space_constraint(array, pltpu.HBM)


def shaped(shape, dtype):
    return jax.ShapeDtypeStruct(shape, dtype)


def split(value):
    high = value.astype(BF16)
    return high, (value - high.astype(F32)).astype(BF16)


def dot3(left, right, left_dim=1, right_dim=0):
    left_high, left_low = split(left)
    right_high, right_low = split(right)
    return lax.dot_general(
        jnp.concatenate([left_high, left_high, left_low], axis=left_dim),
        jnp.concatenate([right_high, right_low, right_high], axis=right_dim),
        (((left_dim,), (right_dim,)), ((), ())),
        preferred_element_type=F32,
    )


def iota2(shape):
    return lax.broadcasted_iota(jnp.int32, shape, 0), lax.broadcasted_iota(jnp.int32, shape, 1)


def merge_inverse(lower, rows, cols):
    tokens = lower.shape[0]
    block = 8
    inverse = jnp.where(rows == cols, 1.0, 0.0).astype(F32)
    first = rows - rows % block
    for step in range(block - 1):
        column = jnp.sum(jnp.where(cols == first + step, lower, 0.0), axis=1, keepdims=True)
        pivot = inverse.reshape(tokens // block, block, tokens)[:, step : step + 1, :]
        pivot = jnp.broadcast_to(pivot, (tokens // block, block, tokens)).reshape(tokens, tokens)
        inverse = inverse - column * pivot
    while block < tokens:
        corner = (
            (rows // (2 * block) == cols // (2 * block))
            & (rows % (2 * block) >= block)
            & (cols % (2 * block) < block)
        )
        inverse = inverse - dot3(dot3(inverse, jnp.where(corner, lower, 0.0)), inverse)
        block *= 2
    return inverse


def load_kernel(size, key_hbm, dir_hbm, value_hbm, rate_hbm, key_gain_hbm,
                query_gain_hbm, mine_hbm, weight_ref, rate_ref, key_gain_ref, query_gain_ref,
                mine_ref, sems):
    pairs = [
        (hbm, weight_ref.at[:, index * size : (index + 1) * size])
        for index, hbm in enumerate((key_hbm, dir_hbm, value_hbm))
    ]
    pairs += [(rate_hbm, rate_ref), (key_gain_hbm, key_gain_ref)]
    pairs += [(query_gain_hbm, query_gain_ref), (mine_hbm, mine_ref)]
    copies = [pltpu.make_async_copy(*pair, sems.at[n]) for n, pair in enumerate(pairs)]
    for copy in copies:
        copy.start()
    for copy in copies:
        copy.wait()


def prepare_kernel(place_ref, mine_ref, other_ref, weight_ref, rate_ref, bias_ref, gain_ref,
                   rows_ref, kn_ref, val_ref, dirs_ref, coeff_ref, solved_ref, exit_ref, turn_ref):
    core = place_ref[1]
    half = mine_ref.shape[0]
    rows_ref[pl.ds(pl.multiple_of(core * half, half), half), :] = mine_ref[...]
    rows_ref[pl.ds(pl.multiple_of((1 - core) * half, half), half), :] = other_ref[...]
    seg = rows_ref[...]
    size = turn_ref.shape[0]
    raw = jnp.dot(seg, weight_ref[...], preferred_element_type=F32)
    keys, raw, vals = raw[:, :size], raw[:, size : 2 * size], raw[:, 2 * size :]
    kn = keys * lax.rsqrt(jnp.mean(keys * keys, axis=-1, keepdims=True) + EPSILON) * gain_ref[...]
    dirs = raw * lax.rsqrt(jnp.sum(raw * raw, axis=-1, keepdims=True) + EPSILON)
    vector = jnp.broadcast_to(rate_ref[...], (16, seg.shape[1]))
    logits = lax.dot_general(seg, vector, (((1,), (1,)), ((), ())), preferred_element_type=F32)
    rates = 2.0 * jax.nn.sigmoid(logits[:, :1] + bias_ref[0])
    val_ref[...] = vals.astype(BF16)
    kn_ref[...] = kn
    dirs_ref[...] = dirs
    tokens, size = dirs.shape
    rows, cols = iota2((tokens, tokens))
    below = rows > cols
    grams = dot3(dirs, jnp.concatenate([dirs, kn], axis=0), 1, 1)
    lower = jnp.where(below, rates * grams[:, :tokens], 0.0)
    crossing = jnp.where(below, rates * grams[:, tokens:], 0.0)
    inverse = merge_inverse(lower, rows, cols)
    both = dot3(inverse, jnp.concatenate([crossing, rates * dirs], axis=1))
    coeff_ref[...] = both[:, :tokens]
    solved_ref[...] = both[:, tokens:]
    crossed = dot3(both, dirs, 0, 0)
    exit_ref[...] = kn - crossed[:tokens]
    heads, lanes = iota2((size, size))
    turn_ref[...] = jnp.where(heads == lanes, 1.0, 0.0) - crossed[tokens:]


def in_order(place_ref, turn_refs, turns_ref):
    group = len(turn_refs)
    member = place_ref[0] % group
    for step in range(group):
        turns_ref[source_of(member, step, group)] = turn_refs[step][...]
    return member


def leave_kernel(group, place_ref, exit_ref, *refs):
    turn_refs, (long_ref, short_ref, starts_ref, turns_ref) = refs[:group], refs[group:]
    member = in_order(place_ref, turn_refs, turns_ref)
    tokens, size = exit_ref.shape
    own = exit_ref[...]
    keys = own
    product = None
    heads, lanes = iota2((size, size))
    starts_ref[0] = jnp.where(heads == lanes, 1.0, 0.0)
    for index in range(group):
        turn = turns_ref[index]
        product = turn if product is None else dot3(product, turn)
        if index:
            keys = jnp.where(index > member, dot3(keys, turn), own)
        if index < group - 1:
            starts_ref[index + 1] = product
    high, low = split(keys)
    for ref in (long_ref, short_ref):
        ref[:tokens] = high
        ref[tokens : 2 * tokens] = low
    high, low = split(product)
    long_ref[2 * tokens : 2 * tokens + size] = high
    long_ref[2 * tokens + size :] = low


def bundle_kernel(group, place_ref, exit_ref, after_ref, *refs):
    turn_refs, val_refs = refs[:group], refs[group : -group - 2]
    bundle_refs, (turns_ref, seen_ref) = refs[-group - 2 : -2], refs[-2:]
    member = in_order(place_ref, turn_refs, turns_ref)
    tokens, size = exit_ref.shape
    keys = exit_ref[...]
    for index in range(group):
        if index > 1:
            keys = jnp.where(index - 1 > member, dot3(keys, turns_ref[index - 1]), exit_ref[...])
        seen_ref[index] = keys.astype(BF16)
    for step in range(group):
        bundle_refs[step][:tokens] = seen_ref[target_of(member, step, group)]
        for index, ref in enumerate(val_refs):
            bundle_refs[step][(index + 1) * tokens : (index + 2) * tokens] = ref[...]


def query_kernel(first, rows_ref, weight_hbm, gain_ref, kn_ref, dirs_ref, coeff_ref, solved_ref, val_ref,
                 moved_ref, weighted_ref, peak_ref, total_ref, weight_ref, sems):
    tokens, size = kn_ref.shape
    heads = moved_ref.shape[0]
    pieces = weight_ref.shape[0]
    wide = weight_ref.shape[2]
    copies = [
        pltpu.make_async_copy(
            weight_hbm.at[:, first + n * wide : first + (n + 1) * wide], weight_ref.at[n], sems.at[n]
        )
        for n in range(pieces)
    ]
    for copy in copies:
        copy.start()
    across = jnp.concatenate([kn_ref[...], dirs_ref[...]], axis=0)
    into = jnp.concatenate([coeff_ref[...], solved_ref[...]], axis=1)
    together = math.gcd(pieces, 2)
    for turn in range(pieces // together):
        parts = []
        for n in range(turn * together, (turn + 1) * together):
            copies[n].wait()
            raw = jnp.dot(rows_ref[...], weight_ref[n], preferred_element_type=F32)
            parts += [raw[:, at : at + size] for at in range(0, wide, size)]
        count = len(parts)
        raw = jnp.concatenate(parts, axis=0)
        queries = (
            raw * lax.rsqrt(jnp.mean(raw * raw, axis=-1, keepdims=True) + EPSILON) * gain_ref[...]
        )
        seen = dot3(queries, across, 1, 1)
        rows, cols = iota2((count * tokens, tokens))
        up_to = rows % tokens >= cols
        reach = jnp.where(up_to, seen[:, tokens:], 0.0)
        taken = dot3(reach, into)
        scores = (seen[:, :tokens] - taken[:, :tokens]) * (1.0 / math.sqrt(size))
        scores = jnp.where(up_to, scores, NEGATIVE)
        moved = (queries - taken[:, tokens:]).astype(BF16)
        peak = jnp.max(scores, axis=1, keepdims=True)
        weights = jnp.exp(scores - peak)
        total = jnp.sum(weights, axis=1, keepdims=True)
        weighted = jnp.dot(weights.astype(BF16), val_ref[...], preferred_element_type=F32)
        for h in range(count):
            part = slice(h * tokens, (h + 1) * tokens)
            head = turn * count + h
            moved_ref[head] = moved[part]
            weighted_ref[head] = weighted[part]
            peak_ref[head] = peak[part]
            total_ref[head] = total[part]


def arrive_kernel(count, group, tokens, place_ref, *refs):
    arrived, starts_ref = refs[:count], refs[count]
    far_refs = refs[-group:]
    member = place_ref[0] % group
    size = starts_ref.shape[1]
    product = None
    brought = []
    for index in range(count):
        ref = arrived[index]
        keys = ref[:tokens].astype(F32) + ref[tokens : 2 * tokens].astype(F32)
        if index:
            before = arrived[index - 1]
            whole = before[2 * tokens : 2 * tokens + size].astype(F32)
            whole = whole + before[2 * tokens + size :].astype(F32)
            product = whole if product is None else dot3(whole, product)
            keys = dot3(keys, product)
        brought.append(keys)
    keys = jnp.concatenate(brought, axis=0)
    for step in range(group):
        start = starts_ref[target_of(member, step, group)]
        far_refs[step][...] = dot3(keys, start).astype(BF16)


def attend_kernel(most, group, place_ref, mask_ref, *refs):
    bundle_refs, far_refs = refs[:group], refs[group : 2 * group]
    parts = (len(refs) - 2 * group - 9) // 4
    owns, refs = [refs[2 * group + 4 * n : 2 * group + 4 * n + 4] for n in range(parts)], refs[
        2 * group + 4 * parts :
    ]
    (out_hbm, away_ref, kept_ref, chosen_ref, keys_ref, vals_ref, attended_ref, out_ref,
     sems) = refs
    pieces, _, wide = out_ref.shape
    copies = [
        pltpu.make_async_copy(
            out_hbm.at[:, n * wide : (n + 1) * wide], out_ref.at[n], sems.at[n]
        )
        for n in range(pieces)
    ]
    for copy in copies:
        copy.start()
    place, core = place_ref[0], place_ref[1]
    heads, tokens, size = owns[0][0].shape
    segments = mask_ref.shape[0]
    scaling = 1.0 / math.sqrt(size)
    mine, member = place // group, place % group

    def pick(segment, count):
        wanted = (mask_ref[segment] > 0) & (segment < place)

        @pl.when(wanted & (count < most))
        def _():
            chosen_ref[count] = segment

        return count + wanted.astype(jnp.int32)

    found = lax.fori_loop(0, segments, pick, jnp.int32(0))
    chunk = keys_ref.shape[0] // tokens
    lanes = lax.broadcasted_iota(jnp.int32, (heads * tokens, chunk * tokens), 1)

    def collect(turn):
        for slot in range(chunk):
            part = slice(slot * tokens, (slot + 1) * tokens)
            index = turn * chunk + slot
            used = index < found
            segment = jnp.where(used, chosen_ref[index], 0)
            whose, distance = segment % group, mine - segment // group
            before = pl.multiple_of(jnp.maximum(distance - 1, 0) * tokens, tokens)

            @pl.when(jnp.logical_not(used))
            def _():
                keys_ref[part, :] = jnp.zeros((tokens, size), BF16)
                vals_ref[part, :] = jnp.zeros((tokens, size), BF16)

            for step in range(group):
                here = used & (whose == source_of(member, step, group))

                @pl.when(here)
                def _():
                    after = pl.multiple_of((distance + 1) * tokens, tokens)
                    vals_ref[part, :] = bundle_refs[step][pl.ds(after, tokens), :]

                @pl.when(here & (distance > 0))
                def _():
                    keys_ref[part, :] = far_refs[step][pl.ds(before, tokens), :]

                @pl.when(here & (distance == 0))
                def _():
                    keys_ref[part, :] = bundle_refs[step][:tokens]

    def advance(moved, turn, peak, total, weighted):
        scores = lax.dot_general(
            moved, keys_ref[...], (((1,), (1,)), ((), ())), preferred_element_type=F32
        )
        scores = jnp.where(lanes < (found - turn * chunk) * tokens, scores * scaling, NEGATIVE)
        new_peak = jnp.maximum(peak, jnp.max(scores, axis=1, keepdims=True))
        fading = jnp.exp(peak - new_peak)
        weights = jnp.exp(scores - new_peak)
        total = total * fading + jnp.sum(weights, axis=1, keepdims=True)
        weighted = weighted * fading + jnp.dot(
            weights.astype(BF16), vals_ref[...], preferred_element_type=F32
        )
        return new_peak, total, weighted

    half = kept_ref.shape[0]
    turns = most // chunk
    if turns == 1:
        collect(0)
    for number, (moved_ref, weighted_ref, peak_ref, total_ref) in enumerate(owns):
        moved = moved_ref[...].reshape(heads * tokens, size)
        state = (
            peak_ref[...].reshape(heads * tokens, 1),
            total_ref[...].reshape(heads * tokens, 1),
            weighted_ref[...].reshape(heads * tokens, size),
        )
        if turns == 1:
            _, total, weighted = advance(moved, 0, *state)
        else:

            def step_of(turn, state, moved=moved):
                collect(turn)
                return advance(moved, turn, *state)

            _, total, weighted = lax.fori_loop(0, turns, step_of, state)
        done = (weighted * (1.0 / total)).astype(BF16)
        for h in range(heads):
            columns = slice((number * heads + h) * size, (number * heads + h + 1) * size)
            for index in range(tokens // half):
                at = pl.multiple_of(jnp.where(index == core, half, 0), half)
                attended_ref[pl.ds(at, half), columns] = done[
                    h * tokens + index * half : h * tokens + (index + 1) * half
                ]
    for n in range(pieces):
        copies[n].wait()
        result = jnp.dot(attended_ref[...], out_ref[n], preferred_element_type=F32).astype(BF16)
        away_ref[:, n * wide : (n + 1) * wide] = result[:half]
        kept_ref[:, n * wide : (n + 1) * wide] = result[half:]


def body(
    hidden, w_query, w_key, w_value, w_dir, u_rate, rate_bias, q_gain, k_gain, w_out, block_mask
):
    segments = lax.axis_size("ctx")
    position = lax.axis_index("ctx")
    core = lax.axis_index("head")
    group = max(d for d in range(1, math.isqrt(segments) + 1) if segments % d == 0)
    groups = segments // group
    other = lax.ppermute(hidden, "head", [(0, 1), (1, 0)])
    half, width = hidden.shape
    tokens = half * lax.axis_size("head")
    size = w_key.shape[1]
    heads = w_query.shape[1] // size
    smem = pl.BlockSpec(memory_space=pltpu.SMEM)
    vmem = pl.BlockSpec(memory_space=pltpu.VMEM)
    hbm = pl.BlockSpec(memory_space=pltpu.HBM)
    anywhere = pl.BlockSpec(memory_space=pl.ANY)
    square = shaped((tokens, size), F32)
    place = jnp.stack([position, core]).astype(jnp.int32)

    def to_member(value, step):
        pairs = [
            (s, s - s % group + target_of(s % group, step, group)) for s in range(segments)
        ]
        return lax.ppermute(value, "ctx", pairs)

    def to_later_group(value, distance):
        step = distance * group
        return lax.ppermute(value, "ctx", [(s, s + step) for s in range(segments - step)])

    weights, rate_row, key_gain, query_gain, mine = call(
        functools.partial(load_kernel, size),
        (
            shaped((width, 3 * size), BF16), shaped((1, width), BF16), shaped((1, size), F32),
            shaped((1, size), F32), shaped((half, width), BF16),
        ),
        tuple(
            in_hbm(array)
            for array in (
                w_key, w_dir, w_value, u_rate, k_gain.reshape(1, size), q_gain.reshape(1, size),
                hidden,
            )
        ),
        in_specs=[hbm] * 7,
        scratch=(pltpu.SemaphoreType.DMA((7,)),),
        moved=12 * width * size,
    )
    rows, kn, val, dirs, coeff, solved, exit_keys, turn = call(
        prepare_kernel,
        (
            shaped((tokens, width), BF16), square, shaped((tokens, size), BF16), square, square,
            square, square, shaped((size, size), F32),
        ),
        (place, mine, other, weights, rate_row, rate_bias, key_gain),
        in_specs=[smem] + [vmem] * 4 + [smem, vmem],
        flops=6 * tokens * width * size,
        moved=8 * width * size,
    )
    turns = [turn] + [to_member(turn, step) for step in range(1, group)]
    line = [val] + [to_later_group(val, d) for d in range(1, groups)]
    long, short, starts = call(
        functools.partial(leave_kernel, group),
        [
            shaped((2 * tokens + 2 * size, size), BF16),
            shaped((2 * tokens, size), BF16),
            shaped((group, size, size), F32),
        ],
        (place, exit_keys, *turns),
        in_specs=[smem] + [vmem] * (1 + group),
        scratch=(pltpu.VMEM((group, size, size), F32),),
        flops=12 * group * size**3,
        moved=10**6,
    )
    arrived = [
        to_later_group(long if d < groups - 1 else short, d) for d in range(1, groups)
    ]
    bundle = call(
        functools.partial(bundle_kernel, group),
        [shaped(((1 + groups) * tokens, size), BF16)] * group,
        (place, exit_keys, starts, *turns, *line),
        in_specs=[smem, vmem, anywhere] + [vmem] * (group + groups),
        scratch=(
            pltpu.VMEM((group, size, size), F32),
            pltpu.VMEM((group, tokens, size), BF16),
        ),
        flops=12 * group * size**3,
        moved=10**6,
        limit=8 + group * groups // 4,
    )
    bundle = [bundle[0]] + [to_member(bundle[step], step) for step in range(1, group)]
    calls = math.gcd(heads, 2)
    each = heads // calls
    pieces = math.gcd(each, 2)
    owns = [
        call(
            functools.partial(query_kernel, number * each * size),
            (
                shaped((each, tokens, size), BF16),
                shaped((each, tokens, size), F32),
                shaped((each, tokens, 1), F32),
                shaped((each, tokens, 1), F32),
            ),
            (rows, in_hbm(w_query), query_gain, kn, dirs, coeff, solved, val),
            in_specs=[vmem, hbm] + [vmem] * 6,
            scratch=(
                pltpu.VMEM((pieces, width, each * size // pieces), BF16),
                pltpu.SemaphoreType.DMA((pieces,)),
            ),
            flops=4 * tokens * width * each * size,
            moved=8 * width * each * size,
            limit=12,
        )
        for number in range(calls)
    ]
    far = call(
        functools.partial(arrive_kernel, groups - 1, group, tokens),
        [shaped(((groups - 1) * tokens, size), BF16)] * group,
        (place, *arrived, starts, owns[0][2]),
        in_specs=[smem] + [vmem] * groups + [anywhere],
        flops=6 * groups * group * size**3,
        moved=10**6,
        limit=8 + group * groups // 4,
    )
    far = [far[0]] + [to_member(far[step], step) for step in range(1, group)]
    most = segments // 4
    chunk = math.gcd(most, 4)
    width_out = w_out.shape[1]
    pieces = math.gcd(width_out // size, 4)
    scratch = [
        pltpu.SMEM((most,), jnp.int32),
        pltpu.VMEM((chunk * tokens, size), BF16),
        pltpu.VMEM((chunk * tokens, size), BF16),
        pltpu.VMEM((tokens, heads * size), BF16),
        pltpu.VMEM((pieces, heads * size, width_out // pieces), BF16),
        pltpu.SemaphoreType.DMA((pieces,)),
    ]
    away, kept = call(
        functools.partial(attend_kernel, most, group),
        [shaped((half, width_out), BF16)] * 2,
        (
            place, block_mask[0], *bundle, *far, *(array for own in owns for array in own),
            in_hbm(w_out),
        ),
        in_specs=[smem] * 2 + [vmem] * (2 * group + 4 * calls) + [hbm],
        scratch=scratch,
        flops=2 * tokens * width_out * heads * size,
        moved=4 * 10**6,
        limit=20 + group * groups // 4,
    )
    return kept + lax.ppermute(away, "head", [(0, 1), (1, 0)])


def solution(mesh):
    in_specs = (
        P(("ctx", "head"), None),
        P(None, "head"),
        P(None, "head"),
        P(None, "head"),
        P(None, "head"),
        P("head", None),
        P("head"),
        P(),
        P(),
        P("head", None),
        P("ctx", None),
    )
    out_specs = P(("ctx", "head"), None)
    return jax.shard_map(body, mesh=mesh, in_specs=in_specs, out_specs=out_specs, check_vma=False)
```

```python
import functools
import math

import jax
import jax.numpy as jnp
from jax import lax
from jax.experimental import pallas as pl
from jax.experimental.pallas import tpu as pltpu
from jax.sharding import PartitionSpec as P

EPSILON = 1e-06
NEGATIVE = -1e30
F32 = jnp.float32
BF16 = jnp.bfloat16
MIB = 1024 * 1024


def call(kernel, out_shape, args, in_specs=None, out_specs=None, scratch=(), flops=0, moved=0, limit=6):
    vmem = pl.BlockSpec(memory_space=pltpu.VMEM)
    return pl.pallas_call(
        kernel,
        out_shape=out_shape,
        in_specs=in_specs or [vmem] * len(args),
        out_specs=out_specs or jax.tree.map(lambda _: vmem, out_shape),
        scratch_shapes=list(scratch),
        compiler_params=pltpu.CompilerParams(vmem_limit_bytes=limit * MIB),
        cost_estimate=pl.CostEstimate(flops=flops, bytes_accessed=moved, transcendentals=0),
    )(*args)


def target_of(member, step, group):
    return member ^ step if group & (group - 1) == 0 else (member + step) % group


def source_of(member, step, group):
    return member ^ step if group & (group - 1) == 0 else (member + group - step) % group


def in_hbm(array):
    return pltpu.with_memory_space_constraint(array, pltpu.HBM)


def shaped(shape, dtype):
    return jax.ShapeDtypeStruct(shape, dtype)


def split(value):
    high = value.astype(BF16)
    return high, (value - high.astype(F32)).astype(BF16)


def dot3(left, right, left_dim=1, right_dim=0):
    left_high, left_low = split(left)
    right_high, right_low = split(right)
    return lax.dot_general(
        jnp.concatenate([left_high, left_high, left_low], axis=left_dim),
        jnp.concatenate([right_high, right_low, right_high], axis=right_dim),
        (((left_dim,), (right_dim,)), ((), ())),
        preferred_element_type=F32,
    )


def iota2(shape):
    return lax.broadcasted_iota(jnp.int32, shape, 0), lax.broadcasted_iota(jnp.int32, shape, 1)


def merge_inverse(lower, rows, cols):
    tokens = lower.shape[0]
    block = 8
    inverse = jnp.where(rows == cols, 1.0, 0.0).astype(F32)
    first = rows - rows % block
    for step in range(block - 1):
        column = jnp.sum(jnp.where(cols == first + step, lower, 0.0), axis=1, keepdims=True)
        pivot = inverse.reshape(tokens // block, block, tokens)[:, step : step + 1, :]
        pivot = jnp.broadcast_to(pivot, (tokens // block, block, tokens)).reshape(tokens, tokens)
        inverse = inverse - column * pivot
    while block < tokens:
        corner = (
            (rows // (2 * block) == cols // (2 * block))
            & (rows % (2 * block) >= block)
            & (cols % (2 * block) < block)
        )
        inverse = inverse - dot3(dot3(inverse, jnp.where(corner, lower, 0.0)), inverse)
        block *= 2
    return inverse


def load_kernel(size, key_hbm, dir_hbm, value_hbm, rate_hbm, key_gain_hbm,
                query_gain_hbm, mine_hbm, weight_ref, rate_ref, key_gain_ref, query_gain_ref,
                mine_ref, sems):
    pairs = [
        (hbm, weight_ref.at[:, index * size : (index + 1) * size])
        for index, hbm in enumerate((key_hbm, dir_hbm, value_hbm))
    ]
    pairs += [(rate_hbm, rate_ref), (key_gain_hbm, key_gain_ref)]
    pairs += [(query_gain_hbm, query_gain_ref), (mine_hbm, mine_ref)]
    copies = [pltpu.make_async_copy(*pair, sems.at[n]) for n, pair in enumerate(pairs)]
    for copy in copies:
        copy.start()
    for copy in copies:
        copy.wait()


def prepare_kernel(place_ref, mine_ref, other_ref, weight_ref, rate_ref, bias_ref, gain_ref,
                   rows_ref, kn_ref, val_ref, dirs_ref, coeff_ref, solved_ref, exit_ref, turn_ref):
    core = place_ref[1]
    half = mine_ref.shape[0]
    rows_ref[pl.ds(pl.multiple_of(core * half, half), half), :] = mine_ref[...]
    rows_ref[pl.ds(pl.multiple_of((1 - core) * half, half), half), :] = other_ref[...]
    seg = rows_ref[...]
    size = turn_ref.shape[0]
    raw = jnp.dot(seg, weight_ref[...], preferred_element_type=F32)
    keys, raw, vals = raw[:, :size], raw[:, size : 2 * size], raw[:, 2 * size :]
    kn = keys * lax.rsqrt(jnp.mean(keys * keys, axis=-1, keepdims=True) + EPSILON) * gain_ref[...]
    dirs = raw * lax.rsqrt(jnp.sum(raw * raw, axis=-1, keepdims=True) + EPSILON)
    vector = jnp.broadcast_to(rate_ref[...], (16, seg.shape[1]))
    logits = lax.dot_general(seg, vector, (((1,), (1,)), ((), ())), preferred_element_type=F32)
    rates = 2.0 * jax.nn.sigmoid(logits[:, :1] + bias_ref[0])
    val_ref[...] = vals.astype(BF16)
    kn_ref[...] = kn
    dirs_ref[...] = dirs
    tokens, size = dirs.shape
    rows, cols = iota2((tokens, tokens))
    below = rows > cols
    grams = dot3(dirs, jnp.concatenate([dirs, kn], axis=0), 1, 1)
    lower = jnp.where(below, rates * grams[:, :tokens], 0.0)
    crossing = jnp.where(below, rates * grams[:, tokens:], 0.0)
    inverse = merge_inverse(lower, rows, cols)
    both = dot3(inverse, jnp.concatenate([crossing, rates * dirs], axis=1))
    coeff_ref[...] = both[:, :tokens]
    solved_ref[...] = both[:, tokens:]
    crossed = dot3(both, dirs, 0, 0)
    exit_ref[...] = kn - crossed[:tokens]
    heads, lanes = iota2((size, size))
    turn_ref[...] = jnp.where(heads == lanes, 1.0, 0.0) - crossed[tokens:]


def in_order(place_ref, turn_refs, turns_ref):
    group = len(turn_refs)
    member = place_ref[0] % group
    for step in range(group):
        turns_ref[source_of(member, step, group)] = turn_refs[step][...]
    return member


def leave_kernel(group, place_ref, exit_ref, *refs):
    turn_refs, (leave_ref, starts_ref, turns_ref) = refs[:group], refs[group:]
    member = in_order(place_ref, turn_refs, turns_ref)
    tokens, size = exit_ref.shape
    own = exit_ref[...]
    keys = own
    product = None
    heads, lanes = iota2((size, size))
    starts_ref[0] = jnp.where(heads == lanes, 1.0, 0.0)
    for index in range(group):
        turn = turns_ref[index]
        product = turn if product is None else dot3(product, turn)
        if index:
            keys = jnp.where(index > member, dot3(keys, turn), own)
        if index < group - 1:
            starts_ref[index + 1] = product
    high, low = split(keys)
    leave_ref[:tokens] = high
    leave_ref[tokens : 2 * tokens] = low
    high, low = split(product)
    leave_ref[2 * tokens : 2 * tokens + size] = high
    leave_ref[2 * tokens + size :] = low


def bundle_kernel(group, place_ref, mask_ref, exit_ref, after_ref, *refs):
    groups = len(refs) - 2 * group - 3
    turn_refs, val_refs = refs[:group], refs[group : group + groups]
    bundle_refs, (table_ref, turns_ref, seen_ref) = refs[-group - 3 : -3], refs[-3:]
    member = in_order(place_ref, turn_refs, turns_ref)
    place = place_ref[0]
    mine = place // group
    most = (table_ref.shape[0] - 1) // 2
    for slot in range(most):
        table_ref[2 * slot] = 0
        table_ref[2 * slot + 1] = mine
    segments = mask_ref.shape[0]

    def pick(segment, count):
        wanted = (mask_ref[segment] > 0) & (segment < place) & (count < most)

        @pl.when(wanted)
        def _():
            table_ref[2 * count] = target_of(segment % group, member, group) if (
                group & (group - 1) == 0
            ) else (member + group - segment % group) % group
            table_ref[2 * count + 1] = segment // group

        return count + wanted.astype(jnp.int32)

    table_ref[2 * most] = lax.fori_loop(0, segments, pick, jnp.int32(0))
    tokens, size = exit_ref.shape
    keys = exit_ref[...]
    for index in range(group):
        if index > 1:
            keys = jnp.where(index - 1 > member, dot3(keys, turns_ref[index - 1]), exit_ref[...])
        seen_ref[index] = keys.astype(BF16)
    for step in range(group):
        bundle_refs[step][:tokens] = seen_ref[target_of(member, step, group)]
        for way in range(groups):
            at = (source_of(mine, way, groups) + 1) * tokens
            bundle_refs[step][pl.ds(pl.multiple_of(at, tokens), tokens), :] = val_refs[way][...]


def query_kernel(first, rows_ref, weight_hbm, gain_ref, kn_ref, dirs_ref, coeff_ref, solved_ref, val_ref,
                 moved_ref, weighted_ref, peak_ref, total_ref, weight_ref, sems):
    tokens, size = kn_ref.shape
    heads = moved_ref.shape[0]
    pieces = weight_ref.shape[0]
    wide = weight_ref.shape[2]
    copies = [
        pltpu.make_async_copy(
            weight_hbm.at[:, first + n * wide : first + (n + 1) * wide], weight_ref.at[n], sems.at[n]
        )
        for n in range(pieces)
    ]
    for copy in copies:
        copy.start()
    across = jnp.concatenate([kn_ref[...], dirs_ref[...]], axis=0)
    into = jnp.concatenate([coeff_ref[...], solved_ref[...]], axis=1)
    together = math.gcd(pieces, 2)
    for turn in range(pieces // together):
        parts = []
        for n in range(turn * together, (turn + 1) * together):
            copies[n].wait()
            raw = jnp.dot(rows_ref[...], weight_ref[n], preferred_element_type=F32)
            parts += [raw[:, at : at + size] for at in range(0, wide, size)]
        count = len(parts)
        raw = jnp.concatenate(parts, axis=0)
        queries = (
            raw * lax.rsqrt(jnp.mean(raw * raw, axis=-1, keepdims=True) + EPSILON) * gain_ref[...]
        )
        seen = dot3(queries, across, 1, 1)
        rows, cols = iota2((count * tokens, tokens))
        up_to = rows % tokens >= cols
        reach = jnp.where(up_to, seen[:, tokens:], 0.0)
        taken = dot3(reach, into)
        scores = (seen[:, :tokens] - taken[:, :tokens]) * (1.0 / math.sqrt(size))
        scores = jnp.where(up_to, scores, NEGATIVE)
        moved = (queries - taken[:, tokens:]).astype(BF16)
        peak = jnp.max(scores, axis=1, keepdims=True)
        weights = jnp.exp(scores - peak)
        total = jnp.sum(weights, axis=1, keepdims=True)
        weighted = jnp.dot(weights.astype(BF16), val_ref[...], preferred_element_type=F32)
        for h in range(count):
            part = slice(h * tokens, (h + 1) * tokens)
            head = turn * count + h
            moved_ref[head] = moved[part]
            weighted_ref[head] = weighted[part]
            peak_ref[head] = peak[part]
            total_ref[head] = total[part]


def arrive_kernel(groups, group, tokens, place_ref, *refs):
    arrived, starts_ref = refs[:groups], refs[groups]
    far_refs, (keys_ref, whole_ref) = refs[-group - 2 : -2], refs[-2:]
    mine, member = place_ref[0] // group, place_ref[0] % group
    size = starts_ref.shape[1]
    for step in range(groups):
        index = source_of(mine, step, groups)
        ref = arrived[step]
        keys_ref[index] = ref[:tokens].astype(F32) + ref[tokens : 2 * tokens].astype(F32)
        whole = ref[2 * tokens : 2 * tokens + size].astype(F32)
        whole_ref[index] = whole + ref[2 * tokens + size :].astype(F32)
    brought = [keys_ref[groups - 2]]
    product = None
    for index in range(groups - 3, -1, -1):
        keys, whole = keys_ref[index], whole_ref[index + 1]
        if product is not None:
            whole = jnp.where(index + 2 < mine, dot3(whole, product), whole)
        product = whole
        brought.append(jnp.where(index + 1 < mine, dot3(keys, product), keys))
    keys = jnp.concatenate(brought[::-1], axis=0)
    for step in range(group):
        start = starts_ref[target_of(member, step, group)]
        far_refs[step][...] = dot3(keys, start).astype(BF16)


def attend_kernel(group, place_ref, table_ref, *refs):
    bundle_refs, far_refs = refs[:group], refs[group : 2 * group]
    parts = (len(refs) - 2 * group - 8) // 4
    owns, refs = [refs[2 * group + 4 * n : 2 * group + 4 * n + 4] for n in range(parts)], refs[
        2 * group + 4 * parts :
    ]
    out_hbm, away_ref, kept_ref, keys_ref, vals_ref, attended_ref, out_ref, sems = refs
    pieces, _, wide = out_ref.shape
    copies = [
        pltpu.make_async_copy(
            out_hbm.at[:, n * wide : (n + 1) * wide], out_ref.at[n], sems.at[n]
        )
        for n in range(pieces)
    ]
    for copy in copies:
        copy.start()
    core = place_ref[1]
    mine = place_ref[0] // group
    most = (table_ref.shape[0] - 1) // 2
    found = table_ref[2 * most]
    heads, tokens, size = owns[0][0].shape
    earlier = far_refs[0].shape[0] // tokens
    scaling = 1.0 / math.sqrt(size)
    chunk = keys_ref.shape[0] // tokens
    lanes = lax.broadcasted_iota(jnp.int32, (tokens, chunk * tokens), 1)

    def collect(turn):
        for slot in range(chunk):
            part = slice(slot * tokens, (slot + 1) * tokens)
            step, source = table_ref[2 * (turn * chunk + slot)], table_ref[2 * (turn * chunk + slot) + 1]
            before = pl.multiple_of(jnp.minimum(source, earlier - 1) * tokens, tokens)
            after = pl.multiple_of((source + 1) * tokens, tokens)
            for number in range(group):

                @pl.when(step == number)
                def _():
                    vals_ref[part, :] = bundle_refs[number][pl.ds(after, tokens), :]
                    keys_ref[part, :] = jnp.where(
                        source < mine,
                        far_refs[number][pl.ds(before, tokens), :],
                        bundle_refs[number][:tokens],
                    )

    def advance(moved, turn, peak, total, weighted):
        scores = lax.dot_general(
            moved, keys_ref[...], (((1,), (1,)), ((), ())), preferred_element_type=F32
        )
        scores = jnp.where(lanes < (found - turn * chunk) * tokens, scores * scaling, NEGATIVE)
        new_peak = jnp.maximum(peak, jnp.max(scores, axis=1, keepdims=True))
        fading = jnp.exp(peak - new_peak)
        weights = jnp.exp(scores - new_peak)
        total = total * fading + jnp.sum(weights, axis=1, keepdims=True)
        weighted = weighted * fading + jnp.dot(
            weights.astype(BF16), vals_ref[...], preferred_element_type=F32
        )
        return new_peak, total, weighted

    half = kept_ref.shape[0]
    turns = most // chunk
    if turns == 1:
        collect(0)
    for number in range(parts * heads):
        moved_ref, weighted_ref, peak_ref, total_ref = owns[number // heads]
        h = number % heads
        state = (peak_ref[h], total_ref[h], weighted_ref[h])
        if turns == 1:
            _, total, weighted = advance(moved_ref[h], 0, *state)
        else:

            def step_of(turn, state, moved_ref=moved_ref, h=h):
                collect(turn)
                return advance(moved_ref[h], turn, *state)

            _, total, weighted = lax.fori_loop(0, turns, step_of, state)
        done = (weighted * (1.0 / total)).astype(BF16)
        for index in range(tokens // half):
            at = pl.multiple_of(jnp.where(index == core, half, 0), half)
            attended_ref[pl.ds(at, half), number * size : (number + 1) * size] = done[
                index * half : (index + 1) * half
            ]
    for n in range(pieces):
        copies[n].wait()
        result = jnp.dot(attended_ref[...], out_ref[n], preferred_element_type=F32).astype(BF16)
        away_ref[:, n * wide : (n + 1) * wide] = result[:half]
        kept_ref[:, n * wide : (n + 1) * wide] = result[half:]


def body(
    hidden, w_query, w_key, w_value, w_dir, u_rate, rate_bias, q_gain, k_gain, w_out, block_mask
):
    segments = lax.axis_size("ctx")
    position = lax.axis_index("ctx")
    core = lax.axis_index("head")
    group = max(d for d in range(1, math.isqrt(segments) + 1) if segments % d == 0)
    groups = segments // group
    other = lax.ppermute(hidden, "head", [(0, 1), (1, 0)])
    half, width = hidden.shape
    tokens = half * lax.axis_size("head")
    size = w_key.shape[1]
    heads = w_query.shape[1] // size
    smem = pl.BlockSpec(memory_space=pltpu.SMEM)
    vmem = pl.BlockSpec(memory_space=pltpu.VMEM)
    hbm = pl.BlockSpec(memory_space=pltpu.HBM)
    anywhere = pl.BlockSpec(memory_space=pl.ANY)
    square = shaped((tokens, size), F32)
    place = jnp.stack([position, core]).astype(jnp.int32)

    def swapped(values, count, pairs_of):
        out = [values[0]] * count
        for step in range(count - 1, 0, -1):
            out[step] = lax.ppermute(values[step], "ctx", pairs_of(step))
        return out

    def within_group(values):
        return swapped(values, group, lambda step: [
            (s, s - s % group + target_of(s % group, step, group)) for s in range(segments)
        ])

    def along_line(values):
        return swapped(values, groups, lambda step: [
            (s, s % group + group * target_of(s // group, step, groups)) for s in range(segments)
        ])

    weights, rate_row, key_gain, query_gain, mine = call(
        functools.partial(load_kernel, size),
        (
            shaped((width, 3 * size), BF16), shaped((1, width), BF16), shaped((1, size), F32),
            shaped((1, size), F32), shaped((half, width), BF16),
        ),
        tuple(
            in_hbm(array)
            for array in (
                w_key, w_dir, w_value, u_rate, k_gain.reshape(1, size), q_gain.reshape(1, size),
                hidden,
            )
        ),
        in_specs=[hbm] * 7,
        scratch=(pltpu.SemaphoreType.DMA((7,)),),
        moved=12 * width * size,
    )
    rows, kn, val, dirs, coeff, solved, exit_keys, turn = call(
        prepare_kernel,
        (
            shaped((tokens, width), BF16), square, shaped((tokens, size), BF16), square, square,
            square, square, shaped((size, size), F32),
        ),
        (place, mine, other, weights, rate_row, rate_bias, key_gain),
        in_specs=[smem] + [vmem] * 4 + [smem, vmem],
        flops=6 * tokens * width * size,
        moved=8 * width * size,
    )
    turns = within_group([turn] * group)
    line = along_line([val] * groups)
    leaving, starts = call(
        functools.partial(leave_kernel, group),
        [
            shaped((2 * tokens + 2 * size, size), BF16),
            shaped((group, size, size), F32),
        ],
        (place, exit_keys, *turns),
        in_specs=[smem] + [vmem] * (1 + group),
        scratch=(pltpu.VMEM((group, size, size), F32),),
        flops=12 * group * size**3,
        moved=10**6,
    )
    arrived = along_line([leaving] * groups)
    *bundle, table = call(
        functools.partial(bundle_kernel, group),
        [shaped(((1 + groups) * tokens, size), BF16)] * group
        + [shaped((2 * (segments // 4) + 1,), jnp.int32)],
        (place, block_mask[0], exit_keys, starts, *turns, *line),
        in_specs=[smem, smem, vmem, anywhere] + [vmem] * (group + groups),
        out_specs=[vmem] * group + [smem],
        scratch=(
            pltpu.VMEM((group, size, size), F32),
            pltpu.VMEM((group, tokens, size), BF16),
        ),
        flops=12 * group * size**3,
        moved=10**6,
        limit=8 + group * groups // 4,
    )
    bundle = within_group(bundle)
    calls = math.gcd(heads, 2)
    each = heads // calls
    pieces = math.gcd(each, 2)
    owns = [
        call(
            functools.partial(query_kernel, number * each * size),
            (
                shaped((each, tokens, size), BF16),
                shaped((each, tokens, size), F32),
                shaped((each, tokens, 1), F32),
                shaped((each, tokens, 1), F32),
            ),
            (rows, in_hbm(w_query), query_gain, kn, dirs, coeff, solved, val),
            in_specs=[vmem, hbm] + [vmem] * 6,
            scratch=(
                pltpu.VMEM((pieces, width, each * size // pieces), BF16),
                pltpu.SemaphoreType.DMA((pieces,)),
            ),
            flops=4 * tokens * width * each * size,
            moved=8 * width * each * size,
            limit=12,
        )
        for number in range(calls)
    ]
    far = call(
        functools.partial(arrive_kernel, groups, group, tokens),
        [shaped(((groups - 1) * tokens, size), BF16)] * group,
        (place, *arrived, starts, owns[0][2]),
        in_specs=[smem] + [vmem] * (groups + 1) + [anywhere],
        scratch=(
            pltpu.VMEM((groups, tokens, size), F32),
            pltpu.VMEM((groups, size, size), F32),
        ),
        flops=6 * groups * group * size**3,
        moved=10**6,
        limit=8 + group * groups // 4,
    )
    far = within_group(far)
    most = segments // 4
    chunk = math.gcd(most, 4)
    width_out = w_out.shape[1]
    pieces = math.gcd(width_out // size, 4)
    scratch = [
        pltpu.VMEM((chunk * tokens, size), BF16),
        pltpu.VMEM((chunk * tokens, size), BF16),
        pltpu.VMEM((tokens, heads * size), BF16),
        pltpu.VMEM((pieces, heads * size, width_out // pieces), BF16),
        pltpu.SemaphoreType.DMA((pieces,)),
    ]
    away, kept = call(
        functools.partial(attend_kernel, group),
        [shaped((half, width_out), BF16)] * 2,
        (
            place, table, *bundle, *far, *(array for own in owns for array in own),
            in_hbm(w_out),
        ),
        in_specs=[smem] * 2 + [vmem] * (2 * group + 4 * calls) + [hbm],
        scratch=scratch,
        flops=2 * tokens * width_out * heads * size,
        moved=4 * 10**6,
        limit=20 + group * groups // 4,
    )
    return kept + lax.ppermute(away, "head", [(0, 1), (1, 0)])


def solution(mesh):
    in_specs = (
        P(("ctx", "head"), None),
        P(None, "head"),
        P(None, "head"),
        P(None, "head"),
        P(None, "head"),
        P("head", None),
        P("head"),
        P(),
        P(),
        P("head", None),
        P("ctx", None),
    )
    out_specs = P(("ctx", "head"), None)
    return jax.shard_map(body, mesh=mesh, in_specs=in_specs, out_specs=out_specs, check_vma=False)
```

```python
import functools
import math

import jax
import jax.numpy as jnp
from jax import lax
from jax.experimental import pallas as pl
from jax.experimental.pallas import tpu as pltpu
from jax.sharding import PartitionSpec as P

EPSILON = 1e-06
NEGATIVE = -1e30
F32 = jnp.float32
BF16 = jnp.bfloat16
MIB = 1024 * 1024


def call(kernel, out_shape, args, in_specs=None, out_specs=None, scratch=(), flops=0, moved=0, limit=6):
    vmem = pl.BlockSpec(memory_space=pltpu.VMEM)
    return pl.pallas_call(
        kernel,
        out_shape=out_shape,
        in_specs=in_specs or [vmem] * len(args),
        out_specs=out_specs or jax.tree.map(lambda _: vmem, out_shape),
        scratch_shapes=list(scratch),
        compiler_params=pltpu.CompilerParams(vmem_limit_bytes=limit * MIB),
        cost_estimate=pl.CostEstimate(flops=flops, bytes_accessed=moved, transcendentals=0),
    )(*args)


def target_of(member, step, group):
    return member ^ step if group & (group - 1) == 0 else (member + step) % group


def source_of(member, step, group):
    return member ^ step if group & (group - 1) == 0 else (member + group - step) % group


def in_hbm(array):
    return pltpu.with_memory_space_constraint(array, pltpu.HBM)


def shaped(shape, dtype):
    return jax.ShapeDtypeStruct(shape, dtype)


def split(value):
    high = value.astype(BF16)
    return high, (value - high.astype(F32)).astype(BF16)


def dot3(left, right, left_dim=1, right_dim=0):
    left_high, left_low = split(left)
    right_high, right_low = split(right)
    return lax.dot_general(
        jnp.concatenate([left_high, left_high, left_low], axis=left_dim),
        jnp.concatenate([right_high, right_low, right_high], axis=right_dim),
        (((left_dim,), (right_dim,)), ((), ())),
        preferred_element_type=F32,
    )


def iota2(shape):
    return lax.broadcasted_iota(jnp.int32, shape, 0), lax.broadcasted_iota(jnp.int32, shape, 1)


def merge_inverse(lower, rows, cols):
    tokens = lower.shape[0]
    block = 8
    inverse = jnp.where(rows == cols, 1.0, 0.0).astype(F32)
    first = rows - rows % block
    for step in range(block - 1):
        column = jnp.sum(jnp.where(cols == first + step, lower, 0.0), axis=1, keepdims=True)
        pivot = inverse.reshape(tokens // block, block, tokens)[:, step : step + 1, :]
        pivot = jnp.broadcast_to(pivot, (tokens // block, block, tokens)).reshape(tokens, tokens)
        inverse = inverse - column * pivot
    while block < tokens:
        corner = (
            (rows // (2 * block) == cols // (2 * block))
            & (rows % (2 * block) >= block)
            & (cols % (2 * block) < block)
        )
        inverse = inverse - dot3(dot3(inverse, jnp.where(corner, lower, 0.0)), inverse)
        block *= 2
    return inverse


def load_kernel(size, key_hbm, dir_hbm, value_hbm, rate_hbm, key_gain_hbm,
                query_gain_hbm, mine_hbm, weight_ref, rate_ref, key_gain_ref, query_gain_ref,
                mine_ref, sems):
    pairs = [
        (hbm, weight_ref.at[:, index * size : (index + 1) * size])
        for index, hbm in enumerate((key_hbm, dir_hbm, value_hbm))
    ]
    pairs += [(rate_hbm, rate_ref), (key_gain_hbm, key_gain_ref)]
    pairs += [(query_gain_hbm, query_gain_ref), (mine_hbm, mine_ref)]
    copies = [pltpu.make_async_copy(*pair, sems.at[n]) for n, pair in enumerate(pairs)]
    for copy in copies:
        copy.start()
    for copy in copies:
        copy.wait()


def prepare_kernel(place_ref, mine_ref, other_ref, weight_ref, rate_ref, bias_ref, gain_ref,
                   rows_ref, kn_ref, val_ref, dirs_ref, coeff_ref, solved_ref, exit_ref, turn_ref):
    core = place_ref[1]
    half = mine_ref.shape[0]
    rows_ref[pl.ds(pl.multiple_of(core * half, half), half), :] = mine_ref[...]
    rows_ref[pl.ds(pl.multiple_of((1 - core) * half, half), half), :] = other_ref[...]
    seg = rows_ref[...]
    size = turn_ref.shape[0]
    raw = jnp.dot(seg, weight_ref[...], preferred_element_type=F32)
    keys, raw, vals = raw[:, :size], raw[:, size : 2 * size], raw[:, 2 * size :]
    kn = keys * lax.rsqrt(jnp.mean(keys * keys, axis=-1, keepdims=True) + EPSILON) * gain_ref[...]
    dirs = raw * lax.rsqrt(jnp.sum(raw * raw, axis=-1, keepdims=True) + EPSILON)
    vector = jnp.broadcast_to(rate_ref[...], (16, seg.shape[1]))
    logits = lax.dot_general(seg, vector, (((1,), (1,)), ((), ())), preferred_element_type=F32)
    rates = 2.0 * jax.nn.sigmoid(logits[:, :1] + bias_ref[0])
    val_ref[...] = vals.astype(BF16)
    kn_ref[...] = kn
    dirs_ref[...] = dirs
    tokens, size = dirs.shape
    rows, cols = iota2((tokens, tokens))
    below = rows > cols
    grams = dot3(dirs, jnp.concatenate([dirs, kn], axis=0), 1, 1)
    lower = jnp.where(below, rates * grams[:, :tokens], 0.0)
    crossing = jnp.where(below, rates * grams[:, tokens:], 0.0)
    inverse = merge_inverse(lower, rows, cols)
    both = dot3(inverse, jnp.concatenate([crossing, rates * dirs], axis=1))
    coeff_ref[...] = both[:, :tokens]
    solved_ref[...] = both[:, tokens:]
    crossed = dot3(both, dirs, 0, 0)
    exit_ref[...] = kn - crossed[:tokens]
    heads, lanes = iota2((size, size))
    turn_ref[...] = jnp.where(heads == lanes, 1.0, 0.0) - crossed[tokens:]


def in_order(place_ref, turn_refs, turns_ref):
    group = len(turn_refs)
    member = place_ref[0] % group
    for step in range(group):
        turns_ref[source_of(member, step, group)] = turn_refs[group - 1 - step][...]
    return member


def leave_kernel(group, place_ref, exit_ref, *refs):
    turn_refs, (leave_ref, starts_ref, turns_ref) = refs[:group], refs[group:]
    member = in_order(place_ref, turn_refs, turns_ref)
    tokens, size = exit_ref.shape
    own = exit_ref[...]
    keys = own
    product = None
    heads, lanes = iota2((size, size))
    starts_ref[0] = jnp.where(heads == lanes, 1.0, 0.0)
    for index in range(group):
        turn = turns_ref[index]
        product = turn if product is None else dot3(product, turn)
        if index:
            keys = jnp.where(index > member, dot3(keys, turn), own)
        if index < group - 1:
            starts_ref[index + 1] = product
    high, low = split(keys)
    leave_ref[:tokens] = high
    leave_ref[tokens : 2 * tokens] = low
    high, low = split(product)
    leave_ref[2 * tokens : 2 * tokens + size] = high
    leave_ref[2 * tokens + size :] = low


def bundle_kernel(group, place_ref, mask_ref, exit_ref, after_ref, *refs):
    groups = len(refs) - 2 * group - 4
    turn_refs, val_refs, line_ref = refs[:group], refs[group : group + groups], refs[group + groups]
    near_refs, (table_ref, turns_ref, seen_ref) = refs[-group - 3 : -3], refs[-3:]
    member = in_order(place_ref, turn_refs, turns_ref)
    place = place_ref[0]
    mine = place // group
    most = (table_ref.shape[0] - 1) // 2
    for slot in range(most):
        table_ref[2 * slot] = 0
        table_ref[2 * slot + 1] = mine
    segments = mask_ref.shape[0]

    def pick(segment, count):
        wanted = (mask_ref[segment] > 0) & (segment < place) & (count < most)

        @pl.when(wanted)
        def _():
            table_ref[2 * count] = target_of(segment % group, member, group) if (
                group & (group - 1) == 0
            ) else (member + group - segment % group) % group
            table_ref[2 * count + 1] = segment // group

        return count + wanted.astype(jnp.int32)

    table_ref[2 * most] = lax.fori_loop(0, segments, pick, jnp.int32(0))
    tokens, size = exit_ref.shape
    keys = exit_ref[...]
    for index in range(group):
        if index > 1:
            keys = jnp.where(index - 1 > member, dot3(keys, turns_ref[index - 1]), exit_ref[...])
        seen_ref[index] = keys.astype(BF16)
    for step in range(group):
        near_refs[step][...] = seen_ref[target_of(member, step, group)]
    for way in range(groups):
        at = pl.multiple_of(source_of(mine, way, groups) * tokens, tokens)
        line_ref[pl.ds(at, tokens), :] = val_refs[groups - 1 - way][...]


def query_kernel(first, rows_ref, weight_hbm, gain_ref, kn_ref, dirs_ref, coeff_ref, solved_ref, val_ref,
                 moved_ref, weighted_ref, peak_ref, total_ref, weight_ref, sems):
    tokens, size = kn_ref.shape
    heads = moved_ref.shape[0]
    pieces = weight_ref.shape[0]
    wide = weight_ref.shape[2]
    copies = [
        pltpu.make_async_copy(
            weight_hbm.at[:, first + n * wide : first + (n + 1) * wide], weight_ref.at[n], sems.at[n]
        )
        for n in range(pieces)
    ]
    for copy in copies:
        copy.start()
    across = jnp.concatenate([kn_ref[...], dirs_ref[...]], axis=0)
    into = jnp.concatenate([coeff_ref[...], solved_ref[...]], axis=1)
    together = math.gcd(pieces, 2)
    for turn in range(pieces // together):
        parts = []
        for n in range(turn * together, (turn + 1) * together):
            copies[n].wait()
            raw = jnp.dot(rows_ref[...], weight_ref[n], preferred_element_type=F32)
            parts += [raw[:, at : at + size] for at in range(0, wide, size)]
        count = len(parts)
        raw = jnp.concatenate(parts, axis=0)
        queries = (
            raw * lax.rsqrt(jnp.mean(raw * raw, axis=-1, keepdims=True) + EPSILON) * gain_ref[...]
        )
        seen = dot3(queries, across, 1, 1)
        rows, cols = iota2((count * tokens, tokens))
        up_to = rows % tokens >= cols
        reach = jnp.where(up_to, seen[:, tokens:], 0.0)
        taken = dot3(reach, into)
        scores = (seen[:, :tokens] - taken[:, :tokens]) * (1.0 / math.sqrt(size))
        scores = jnp.where(up_to, scores, NEGATIVE)
        moved = (queries - taken[:, tokens:]).astype(BF16)
        peak = jnp.max(scores, axis=1, keepdims=True)
        weights = jnp.exp(scores - peak)
        total = jnp.sum(weights, axis=1, keepdims=True)
        weighted = jnp.dot(weights.astype(BF16), val_ref[...], preferred_element_type=F32)
        for h in range(count):
            part = slice(h * tokens, (h + 1) * tokens)
            head = turn * count + h
            moved_ref[head] = moved[part]
            weighted_ref[head] = weighted[part]
            peak_ref[head] = peak[part]
            total_ref[head] = total[part]


def arrive_kernel(groups, group, tokens, place_ref, *refs):
    arrived, starts_ref, near_refs = refs[:groups], refs[groups], refs[groups + 1 :]
    far_refs, (keys_ref, whole_ref) = refs[-group - 2 : -2], refs[-2:]
    mine, member = place_ref[0] // group, place_ref[0] % group
    size = starts_ref.shape[1]
    for step in range(groups):
        index = source_of(mine, step, groups)
        ref = arrived[groups - 1 - step]
        keys_ref[index] = ref[:tokens].astype(F32) + ref[tokens : 2 * tokens].astype(F32)
        whole = ref[2 * tokens : 2 * tokens + size].astype(F32)
        whole_ref[index] = whole + ref[2 * tokens + size :].astype(F32)
    brought = [keys_ref[groups - 2]]
    product = None
    for index in range(groups - 3, -1, -1):
        keys, whole = keys_ref[index], whole_ref[index + 1]
        if product is not None:
            whole = jnp.where(index + 2 < mine, dot3(whole, product), whole)
        product = whole
        brought.append(jnp.where(index + 1 < mine, dot3(keys, product), keys))
    keys = jnp.concatenate(brought[::-1], axis=0)
    for step in range(group):
        start = starts_ref[target_of(member, step, group)]
        far_refs[step][: (groups - 1) * tokens] = dot3(keys, start).astype(BF16)
        far_refs[step][(groups - 1) * tokens :] = near_refs[step][...]


def attend_kernel(group, place_ref, table_ref, *refs):
    far_refs, line_refs = refs[:group][::-1], refs[group : 2 * group][::-1]
    parts = (len(refs) - 2 * group - 8) // 4
    owns, refs = [refs[2 * group + 4 * n : 2 * group + 4 * n + 4] for n in range(parts)], refs[
        2 * group + 4 * parts :
    ]
    out_hbm, away_ref, kept_ref, keys_ref, vals_ref, attended_ref, out_ref, sems = refs
    pieces, _, wide = out_ref.shape
    copies = [
        pltpu.make_async_copy(
            out_hbm.at[:, n * wide : (n + 1) * wide], out_ref.at[n], sems.at[n]
        )
        for n in range(pieces)
    ]
    for copy in copies:
        copy.start()
    core = place_ref[1]
    mine = place_ref[0] // group
    most = (table_ref.shape[0] - 1) // 2
    found = table_ref[2 * most]
    heads, tokens, size = owns[0][0].shape
    groups = far_refs[0].shape[0] // tokens
    scaling = 1.0 / math.sqrt(size)
    chunk = keys_ref.shape[0] // tokens
    lanes = lax.broadcasted_iota(jnp.int32, (tokens, chunk * tokens), 1)

    def collect(turn):
        for slot in range(chunk):
            part = slice(slot * tokens, (slot + 1) * tokens)
            step, source = table_ref[2 * (turn * chunk + slot)], table_ref[2 * (turn * chunk + slot) + 1]
            before = jnp.where(source < mine, source, groups - 1)
            before = pl.multiple_of(before * tokens, tokens)
            after = pl.multiple_of(source * tokens, tokens)
            for number in range(group):

                @pl.when(step == number)
                def _():
                    vals_ref[part, :] = line_refs[number][pl.ds(after, tokens), :]
                    keys_ref[part, :] = far_refs[number][pl.ds(before, tokens), :]

    def advance(moved, turn, peak, total, weighted):
        scores = lax.dot_general(
            moved, keys_ref[...], (((1,), (1,)), ((), ())), preferred_element_type=F32
        )
        scores = jnp.where(lanes < (found - turn * chunk) * tokens, scores * scaling, NEGATIVE)
        new_peak = jnp.maximum(peak, jnp.max(scores, axis=1, keepdims=True))
        fading = jnp.exp(peak - new_peak)
        weights = jnp.exp(scores - new_peak)
        total = total * fading + jnp.sum(weights, axis=1, keepdims=True)
        weighted = weighted * fading + jnp.dot(
            weights.astype(BF16), vals_ref[...], preferred_element_type=F32
        )
        return new_peak, total, weighted

    half = kept_ref.shape[0]
    turns = most // chunk
    if turns == 1:
        collect(0)
    for number in range(parts * heads):
        moved_ref, weighted_ref, peak_ref, total_ref = owns[number // heads]
        h = number % heads
        state = (peak_ref[h], total_ref[h], weighted_ref[h])
        if turns == 1:
            _, total, weighted = advance(moved_ref[h], 0, *state)
        else:

            def step_of(turn, state, moved_ref=moved_ref, h=h):
                collect(turn)
                return advance(moved_ref[h], turn, *state)

            _, total, weighted = lax.fori_loop(0, turns, step_of, state)
        done = (weighted * (1.0 / total)).astype(BF16)
        for index in range(tokens // half):
            at = pl.multiple_of(jnp.where(index == core, half, 0), half)
            attended_ref[pl.ds(at, half), number * size : (number + 1) * size] = done[
                index * half : (index + 1) * half
            ]
    for n in range(pieces):
        copies[n].wait()
        result = jnp.dot(attended_ref[...], out_ref[n], preferred_element_type=F32).astype(BF16)
        away_ref[:, n * wide : (n + 1) * wide] = result[:half]
        kept_ref[:, n * wide : (n + 1) * wide] = result[half:]


def body(
    hidden, w_query, w_key, w_value, w_dir, u_rate, rate_bias, q_gain, k_gain, w_out, block_mask
):
    segments = lax.axis_size("ctx")
    position = lax.axis_index("ctx")
    core = lax.axis_index("head")
    group = max(d for d in range(1, math.isqrt(segments) + 1) if segments % d == 0)
    groups = segments // group
    other = lax.ppermute(hidden, "head", [(0, 1), (1, 0)])
    half, width = hidden.shape
    tokens = half * lax.axis_size("head")
    size = w_key.shape[1]
    heads = w_query.shape[1] // size
    smem = pl.BlockSpec(memory_space=pltpu.SMEM)
    vmem = pl.BlockSpec(memory_space=pltpu.VMEM)
    hbm = pl.BlockSpec(memory_space=pltpu.HBM)
    anywhere = pl.BlockSpec(memory_space=pl.ANY)
    square = shaped((tokens, size), F32)
    place = jnp.stack([position, core]).astype(jnp.int32)

    def swapped(values, count, pairs_of):
        out = [values[0]] * count
        for step in range(count - 1, 0, -1):
            out[step] = lax.ppermute(values[step], "ctx", pairs_of(step))
        return out

    def within_group(values):
        return swapped(values, group, lambda step: [
            (s, s - s % group + target_of(s % group, step, group)) for s in range(segments)
        ])

    def along_line(values):
        return swapped(values, groups, lambda step: [
            (s, s % group + group * target_of(s // group, step, groups)) for s in range(segments)
        ])

    weights, rate_row, key_gain, query_gain, mine = call(
        functools.partial(load_kernel, size),
        (
            shaped((width, 3 * size), BF16), shaped((1, width), BF16), shaped((1, size), F32),
            shaped((1, size), F32), shaped((half, width), BF16),
        ),
        tuple(
            in_hbm(array)
            for array in (
                w_key, w_dir, w_value, u_rate, k_gain.reshape(1, size), q_gain.reshape(1, size),
                hidden,
            )
        ),
        in_specs=[hbm] * 7,
        scratch=(pltpu.SemaphoreType.DMA((7,)),),
        moved=12 * width * size,
    )
    rows, kn, val, dirs, coeff, solved, exit_keys, turn = call(
        prepare_kernel,
        (
            shaped((tokens, width), BF16), square, shaped((tokens, size), BF16), square, square,
            square, square, shaped((size, size), F32),
        ),
        (place, mine, other, weights, rate_row, rate_bias, key_gain),
        in_specs=[smem] + [vmem] * 4 + [smem, vmem],
        flops=6 * tokens * width * size,
        moved=8 * width * size,
    )
    turns = within_group([turn] * group)
    line = along_line([val] * groups)
    leaving, starts = call(
        functools.partial(leave_kernel, group),
        [
            shaped((2 * tokens + 2 * size, size), BF16),
            shaped((group, size, size), F32),
        ],
        (place, exit_keys, *turns[::-1]),
        in_specs=[smem] + [vmem] * (1 + group),
        scratch=(pltpu.VMEM((group, size, size), F32),),
        flops=12 * group * size**3,
        moved=10**6,
    )
    arrived = along_line([leaving] * groups)
    values, *near, table = call(
        functools.partial(bundle_kernel, group),
        [shaped((groups * tokens, size), BF16)]
        + [shaped((tokens, size), BF16)] * group
        + [shaped((2 * (segments // 4) + 1,), jnp.int32)],
        (place, block_mask[0], exit_keys, starts, *turns[::-1], *line[::-1]),
        in_specs=[smem, smem, vmem, anywhere] + [vmem] * (group + groups),
        out_specs=[vmem] * (1 + group) + [smem],
        scratch=(
            pltpu.VMEM((group, size, size), F32),
            pltpu.VMEM((group, tokens, size), BF16),
        ),
        flops=12 * group * size**3,
        moved=10**6,
        limit=8 + group * groups // 4,
    )
    values = within_group([values] * group)
    calls = math.gcd(heads, 2)
    each = heads // calls
    pieces = math.gcd(each, 2)
    owns = [
        call(
            functools.partial(query_kernel, number * each * size),
            (
                shaped((each, tokens, size), BF16),
                shaped((each, tokens, size), F32),
                shaped((each, tokens, 1), F32),
                shaped((each, tokens, 1), F32),
            ),
            (rows, in_hbm(w_query), query_gain, kn, dirs, coeff, solved, val),
            in_specs=[vmem, hbm] + [vmem] * 6,
            scratch=(
                pltpu.VMEM((pieces, width, each * size // pieces), BF16),
                pltpu.SemaphoreType.DMA((pieces,)),
            ),
            flops=4 * tokens * width * each * size,
            moved=8 * width * each * size,
            limit=12,
        )
        for number in range(calls)
    ]
    far = call(
        functools.partial(arrive_kernel, groups, group, tokens),
        [shaped((groups * tokens, size), BF16)] * group,
        (place, *arrived[::-1], starts, *near, owns[0][2]),
        in_specs=[smem] + [vmem] * (groups + 1 + group) + [anywhere],
        scratch=(
            pltpu.VMEM((groups, tokens, size), F32),
            pltpu.VMEM((groups, size, size), F32),
        ),
        flops=6 * groups * group * size**3,
        moved=10**6,
        limit=8 + group * groups // 4,
    )
    far = within_group(far)
    most = segments // 4
    chunk = math.gcd(most, 4)
    width_out = w_out.shape[1]
    pieces = math.gcd(width_out // size, 4)
    scratch = [
        pltpu.VMEM((chunk * tokens, size), BF16),
        pltpu.VMEM((chunk * tokens, size), BF16),
        pltpu.VMEM((tokens, heads * size), BF16),
        pltpu.VMEM((pieces, heads * size, width_out // pieces), BF16),
        pltpu.SemaphoreType.DMA((pieces,)),
    ]
    away, kept = call(
        functools.partial(attend_kernel, group),
        [shaped((half, width_out), BF16)] * 2,
        (
            place, table, *far[::-1], *values[::-1], *(array for own in owns for array in own),
            in_hbm(w_out),
        ),
        in_specs=[smem] * 2 + [vmem] * (2 * group + 4 * calls) + [hbm],
        scratch=scratch,
        flops=2 * tokens * width_out * heads * size,
        moved=4 * 10**6,
        limit=20 + group * groups // 4,
    )
    return kept + lax.ppermute(away, "head", [(0, 1), (1, 0)])


def solution(mesh):
    in_specs = (
        P(("ctx", "head"), None),
        P(None, "head"),
        P(None, "head"),
        P(None, "head"),
        P(None, "head"),
        P("head", None),
        P("head"),
        P(),
        P(),
        P("head", None),
        P("ctx", None),
    )
    out_specs = P(("ctx", "head"), None)
    return jax.shard_map(body, mesh=mesh, in_specs=in_specs, out_specs=out_specs, check_vma=False)
```

```python
import functools
import math

import jax
import jax.numpy as jnp
from jax import lax
from jax.experimental import pallas as pl
from jax.experimental.pallas import tpu as pltpu
from jax.sharding import PartitionSpec as P

EPSILON = 1e-06
NEGATIVE = -1e30
F32 = jnp.float32
BF16 = jnp.bfloat16
MIB = 1024 * 1024


def call(kernel, out_shape, args, in_specs=None, out_specs=None, scratch=(), flops=0, moved=0, limit=6):
    vmem = pl.BlockSpec(memory_space=pltpu.VMEM)
    return pl.pallas_call(
        kernel,
        out_shape=out_shape,
        in_specs=in_specs or [vmem] * len(args),
        out_specs=out_specs or jax.tree.map(lambda _: vmem, out_shape),
        scratch_shapes=list(scratch),
        compiler_params=pltpu.CompilerParams(vmem_limit_bytes=limit * MIB),
        cost_estimate=pl.CostEstimate(flops=flops, bytes_accessed=moved, transcendentals=0),
    )(*args)


def target_of(member, step, group):
    return member ^ step if group & (group - 1) == 0 else (member + step) % group


def source_of(member, step, group):
    return member ^ step if group & (group - 1) == 0 else (member + group - step) % group


def in_hbm(array):
    return pltpu.with_memory_space_constraint(array, pltpu.HBM)


def shaped(shape, dtype):
    return jax.ShapeDtypeStruct(shape, dtype)


def split(value):
    high = value.astype(BF16)
    return high, (value - high.astype(F32)).astype(BF16)


def dot3(left, right, left_dim=1, right_dim=0):
    left_high, left_low = split(left)
    right_high, right_low = split(right)
    return lax.dot_general(
        jnp.concatenate([left_high, left_high, left_low], axis=left_dim),
        jnp.concatenate([right_high, right_low, right_high], axis=right_dim),
        (((left_dim,), (right_dim,)), ((), ())),
        preferred_element_type=F32,
    )


def iota2(shape):
    return lax.broadcasted_iota(jnp.int32, shape, 0), lax.broadcasted_iota(jnp.int32, shape, 1)


def merge_inverse(lower, rows, cols):
    tokens = lower.shape[0]
    block = 8
    inverse = jnp.where(rows == cols, 1.0, 0.0).astype(F32)
    first = rows - rows % block
    for step in range(block - 1):
        column = jnp.sum(jnp.where(cols == first + step, lower, 0.0), axis=1, keepdims=True)
        pivot = inverse.reshape(tokens // block, block, tokens)[:, step : step + 1, :]
        pivot = jnp.broadcast_to(pivot, (tokens // block, block, tokens)).reshape(tokens, tokens)
        inverse = inverse - column * pivot
    while block < tokens:
        corner = (
            (rows // (2 * block) == cols // (2 * block))
            & (rows % (2 * block) >= block)
            & (cols % (2 * block) < block)
        )
        inverse = inverse - dot3(dot3(inverse, jnp.where(corner, lower, 0.0)), inverse)
        block *= 2
    return inverse


def load_kernel(size, key_hbm, dir_hbm, value_hbm, rate_hbm, key_gain_hbm,
                query_gain_hbm, mine_hbm, weight_ref, rate_ref, key_gain_ref, query_gain_ref,
                mine_ref, sems):
    pairs = [
        (hbm, weight_ref.at[:, index * size : (index + 1) * size])
        for index, hbm in enumerate((key_hbm, dir_hbm, value_hbm))
    ]
    pairs += [(rate_hbm, rate_ref), (key_gain_hbm, key_gain_ref)]
    pairs += [(query_gain_hbm, query_gain_ref), (mine_hbm, mine_ref)]
    copies = [pltpu.make_async_copy(*pair, sems.at[n]) for n, pair in enumerate(pairs)]
    for copy in copies:
        copy.start()
    for copy in copies:
        copy.wait()


def prepare_kernel(core_ref, mine_ref, other_ref, weight_ref, rate_ref, bias_ref, gain_ref,
                   rows_ref, kn_ref, val_ref, dirs_ref, coeff_ref, solved_ref, exit_ref, turn_ref):
    core = core_ref[0]
    half = mine_ref.shape[0]
    rows_ref[pl.ds(pl.multiple_of(core * half, half), half), :] = mine_ref[...]
    rows_ref[pl.ds(pl.multiple_of((1 - core) * half, half), half), :] = other_ref[...]
    seg = rows_ref[...]
    size = turn_ref.shape[0]
    raw = jnp.dot(seg, weight_ref[...], preferred_element_type=F32)
    keys, raw, vals = raw[:, :size], raw[:, size : 2 * size], raw[:, 2 * size :]
    kn = keys * lax.rsqrt(jnp.mean(keys * keys, axis=-1, keepdims=True) + EPSILON) * gain_ref[...]
    dirs = raw * lax.rsqrt(jnp.sum(raw * raw, axis=-1, keepdims=True) + EPSILON)
    vector = jnp.broadcast_to(rate_ref[...], (16, seg.shape[1]))
    logits = lax.dot_general(seg, vector, (((1,), (1,)), ((), ())), preferred_element_type=F32)
    rates = 2.0 * jax.nn.sigmoid(logits[:, :1] + bias_ref[0])
    val_ref[...] = vals.astype(BF16)
    kn_ref[...] = kn
    dirs_ref[...] = dirs
    tokens, size = dirs.shape
    rows, cols = iota2((tokens, tokens))
    below = rows > cols
    grams = dot3(dirs, jnp.concatenate([dirs, kn], axis=0), 1, 1)
    lower = jnp.where(below, rates * grams[:, :tokens], 0.0)
    crossing = jnp.where(below, rates * grams[:, tokens:], 0.0)
    inverse = merge_inverse(lower, rows, cols)
    both = dot3(inverse, jnp.concatenate([crossing, rates * dirs], axis=1))
    coeff_ref[...] = both[:, :tokens]
    solved_ref[...] = both[:, tokens:]
    crossed = dot3(both, dirs, 0, 0)
    exit_ref[...] = kn - crossed[:tokens]
    heads, lanes = iota2((size, size))
    turn_ref[...] = jnp.where(heads == lanes, 1.0, 0.0) - crossed[tokens:]


def leave_kernel(group, place_ref, exit_ref, *refs):
    turn_refs, (leave_ref, starts_ref) = refs[:group], refs[group : group + 2]
    near_refs, (turns_ref, seen_ref) = refs[group + 2 : -2], refs[-2:]
    member = place_ref[0] % group
    tokens, size = exit_ref.shape
    for step in range(group):
        turns_ref[source_of(member, step, group)] = turn_refs[group - 1 - step][...]
    own = exit_ref[...]
    keys = own
    product = None
    heads, lanes = iota2((size, size))
    starts_ref[0] = jnp.where(heads == lanes, 1.0, 0.0)
    for index in range(group):
        seen_ref[index] = keys.astype(BF16)
        turn = turns_ref[index]
        product = turn if product is None else dot3(product, turn)
        if index:
            keys = jnp.where(index > member, dot3(keys, turn), own)
        if index < group - 1:
            starts_ref[index + 1] = product
    high, low = split(keys)
    leave_ref[:tokens] = high
    leave_ref[tokens : 2 * tokens] = low
    high, low = split(product)
    leave_ref[2 * tokens : 2 * tokens + size] = high
    leave_ref[2 * tokens + size :] = low
    for step in range(group):
        near_refs[step][...] = seen_ref[target_of(member, step, group)]


def word_of(slot, segments):
    bits = segments.bit_length()
    per_word = 31 // bits
    return slot // per_word, bits * (slot % per_word), (1 << bits) - 1


def bundle_kernel(group, groups, most, place_ref, mask_ref, after_ref, *refs):
    val_refs, (line_ref, table_ref) = refs[:groups], refs[groups:]
    place = place_ref[0]
    mine = place // group
    segments = mask_ref.shape[0]
    for word in range(table_ref.shape[0]):
        table_ref[word] = 0

    def pick(segment, count):
        wanted = (mask_ref[segment] > 0) & (segment < place) & (count < most)
        word, shift, _ = word_of(count, segments)

        @pl.when(wanted)
        def _():
            table_ref[word] = table_ref[word] | ((segment + 1) << shift)

        return count + wanted.astype(jnp.int32)

    lax.fori_loop(0, segments, pick, jnp.int32(0))
    tokens = val_refs[0].shape[0]
    for way in range(groups):
        at = pl.multiple_of(source_of(mine, way, groups) * tokens, tokens)
        line_ref[pl.ds(at, tokens), :] = val_refs[groups - 1 - way][...]


def query_kernel(first, rows_ref, weight_hbm, gain_ref, kn_ref, dirs_ref, coeff_ref, solved_ref, val_ref,
                 moved_ref, weighted_ref, peak_ref, total_ref, weight_ref, sems):
    tokens, size = kn_ref.shape
    heads = moved_ref.shape[0]
    pieces = weight_ref.shape[0]
    wide = weight_ref.shape[2]
    copies = [
        pltpu.make_async_copy(
            weight_hbm.at[:, first + n * wide : first + (n + 1) * wide], weight_ref.at[n], sems.at[n]
        )
        for n in range(pieces)
    ]
    for copy in copies:
        copy.start()
    across = jnp.concatenate([kn_ref[...], dirs_ref[...]], axis=0)
    into = jnp.concatenate([coeff_ref[...], solved_ref[...]], axis=1)
    together = math.gcd(pieces, 2)
    for turn in range(pieces // together):
        parts = []
        for n in range(turn * together, (turn + 1) * together):
            copies[n].wait()
            raw = jnp.dot(rows_ref[...], weight_ref[n], preferred_element_type=F32)
            parts += [raw[:, at : at + size] for at in range(0, wide, size)]
        count = len(parts)
        raw = jnp.concatenate(parts, axis=0)
        queries = (
            raw * lax.rsqrt(jnp.mean(raw * raw, axis=-1, keepdims=True) + EPSILON) * gain_ref[...]
        )
        seen = dot3(queries, across, 1, 1)
        rows, cols = iota2((count * tokens, tokens))
        up_to = rows % tokens >= cols
        reach = jnp.where(up_to, seen[:, tokens:], 0.0)
        taken = dot3(reach, into)
        scores = (seen[:, :tokens] - taken[:, :tokens]) * (1.0 / math.sqrt(size))
        scores = jnp.where(up_to, scores, NEGATIVE)
        moved = (queries - taken[:, tokens:]).astype(BF16)
        peak = jnp.max(scores, axis=1, keepdims=True)
        weights = jnp.exp(scores - peak)
        total = jnp.sum(weights, axis=1, keepdims=True)
        weighted = jnp.dot(weights.astype(BF16), val_ref[...], preferred_element_type=F32)
        for h in range(count):
            part = slice(h * tokens, (h + 1) * tokens)
            head = turn * count + h
            moved_ref[head] = moved[part]
            weighted_ref[head] = weighted[part]
            peak_ref[head] = peak[part]
            total_ref[head] = total[part]


def arrive_kernel(groups, group, tokens, place_ref, *refs):
    arrived, starts_ref, near_refs = refs[:groups], refs[groups], refs[groups + 1 :]
    far_refs, (keys_ref, whole_ref) = refs[-group - 2 : -2], refs[-2:]
    mine, member = place_ref[0] // group, place_ref[0] % group
    size = starts_ref.shape[1]
    for step in range(groups):
        index = source_of(mine, step, groups)
        ref = arrived[groups - 1 - step]
        keys_ref[index] = ref[:tokens].astype(F32) + ref[tokens : 2 * tokens].astype(F32)
        whole = ref[2 * tokens : 2 * tokens + size].astype(F32)
        whole_ref[index] = whole + ref[2 * tokens + size :].astype(F32)
    brought = [keys_ref[groups - 2]]
    product = None
    for index in range(groups - 3, -1, -1):
        keys, whole = keys_ref[index], whole_ref[index + 1]
        if product is not None:
            whole = jnp.where(index + 2 < mine, dot3(whole, product), whole)
        product = whole
        brought.append(jnp.where(index + 1 < mine, dot3(keys, product), keys))
    keys = jnp.concatenate(brought[::-1], axis=0)
    for step in range(group):
        start = starts_ref[target_of(member, step, group)]
        far_refs[step][: (groups - 1) * tokens] = dot3(keys, start).astype(BF16)
        far_refs[step][(groups - 1) * tokens :] = near_refs[step][...]


def attend_kernel(group, segments, most, place_ref, core_ref, table_ref, *refs):
    far_refs, line_refs = refs[:group][::-1], refs[group : 2 * group][::-1]
    parts = (len(refs) - 2 * group - 8) // 4
    owns, refs = [refs[2 * group + 4 * n : 2 * group + 4 * n + 4] for n in range(parts)], refs[
        2 * group + 4 * parts :
    ]
    out_hbm, away_ref, kept_ref, keys_ref, vals_ref, attended_ref, out_ref, sems = refs
    pieces, _, wide = out_ref.shape
    copies = [
        pltpu.make_async_copy(
            out_hbm.at[:, n * wide : (n + 1) * wide], out_ref.at[n], sems.at[n]
        )
        for n in range(pieces)
    ]
    for copy in copies:
        copy.start()
    core = core_ref[0]
    mine, member = place_ref[0] // group, place_ref[0] % group
    heads, tokens, size = owns[0][0].shape
    groups = far_refs[0].shape[0] // tokens
    scaling = 1.0 / math.sqrt(size)
    chunk = keys_ref.shape[0] // tokens
    lanes = lax.broadcasted_iota(jnp.int32, (tokens, chunk * tokens), 1)

    def collect(turn):
        found = jnp.int32(0)
        for slot in range(chunk):
            part = slice(slot * tokens, (slot + 1) * tokens)
            word, shift, ones = word_of(turn * chunk + slot, segments)
            code = (table_ref[word] >> shift) & ones
            found = found + (code > 0).astype(jnp.int32)
            segment = jnp.maximum(code - 1, 0)
            whose, source = segment % group, segment // group
            before = jnp.where(source < mine, source, groups - 1)
            before = pl.multiple_of(before * tokens, tokens)
            after = pl.multiple_of(source * tokens, tokens)
            for number in range(group):

                @pl.when(whose == source_of(member, number, group))
                def _():
                    vals_ref[part, :] = line_refs[number][pl.ds(after, tokens), :]
                    keys_ref[part, :] = far_refs[number][pl.ds(before, tokens), :]

        return found * tokens

    def advance(moved, kept, peak, total, weighted):
        scores = lax.dot_general(
            moved, keys_ref[...], (((1,), (1,)), ((), ())), preferred_element_type=F32
        )
        scores = jnp.where(lanes < kept, scores * scaling, NEGATIVE)
        new_peak = jnp.maximum(peak, jnp.max(scores, axis=1, keepdims=True))
        fading = jnp.exp(peak - new_peak)
        weights = jnp.exp(scores - new_peak)
        total = total * fading + jnp.sum(weights, axis=1, keepdims=True)
        weighted = weighted * fading + jnp.dot(
            weights.astype(BF16), vals_ref[...], preferred_element_type=F32
        )
        return new_peak, total, weighted

    half = kept_ref.shape[0]
    turns = most // chunk
    if turns == 1:
        kept = collect(0)
    for number in range(parts * heads):
        moved_ref, weighted_ref, peak_ref, total_ref = owns[number // heads]
        h = number % heads
        state = (peak_ref[h], total_ref[h], weighted_ref[h])
        if turns == 1:
            _, total, weighted = advance(moved_ref[h], kept, *state)
        else:

            def step_of(turn, state, moved_ref=moved_ref, h=h):
                return advance(moved_ref[h], collect(turn), *state)

            _, total, weighted = lax.fori_loop(0, turns, step_of, state)
        done = (weighted * (1.0 / total)).astype(BF16)
        for index in range(tokens // half):
            at = pl.multiple_of(jnp.where(index == core, half, 0), half)
            attended_ref[pl.ds(at, half), number * size : (number + 1) * size] = done[
                index * half : (index + 1) * half
            ]
    for n in range(pieces):
        copies[n].wait()
        result = jnp.dot(attended_ref[...], out_ref[n], preferred_element_type=F32).astype(BF16)
        away_ref[:, n * wide : (n + 1) * wide] = result[:half]
        kept_ref[:, n * wide : (n + 1) * wide] = result[half:]


def body(
    hidden, w_query, w_key, w_value, w_dir, u_rate, rate_bias, q_gain, k_gain, w_out, block_mask
):
    segments = lax.axis_size("ctx")
    place = lax.axis_index("ctx").astype(jnp.int32).reshape(1)
    core = lax.axis_index("head").astype(jnp.int32).reshape(1)
    group = max(d for d in range(1, math.isqrt(segments) + 1) if segments % d == 0)
    groups = segments // group
    other = lax.ppermute(hidden, "head", [(0, 1), (1, 0)])
    half, width = hidden.shape
    tokens = half * lax.axis_size("head")
    size = w_key.shape[1]
    heads = w_query.shape[1] // size
    smem = pl.BlockSpec(memory_space=pltpu.SMEM)
    vmem = pl.BlockSpec(memory_space=pltpu.VMEM)
    hbm = pl.BlockSpec(memory_space=pltpu.HBM)
    anywhere = pl.BlockSpec(memory_space=pl.ANY)
    square = shaped((tokens, size), F32)

    def swapped(values, count, pairs_of):
        out = [values[0]] * count
        for step in range(count - 1, 0, -1):
            out[step] = lax.ppermute(values[step], "ctx", pairs_of(step))
        return out

    def within_group(values):
        return swapped(values, group, lambda step: [
            (s, s - s % group + target_of(s % group, step, group)) for s in range(segments)
        ])

    def along_line(values):
        return swapped(values, groups, lambda step: [
            (s, s % group + group * target_of(s // group, step, groups)) for s in range(segments)
        ])

    weights, rate_row, key_gain, query_gain, mine = call(
        functools.partial(load_kernel, size),
        (
            shaped((width, 3 * size), BF16), shaped((1, width), BF16), shaped((1, size), F32),
            shaped((1, size), F32), shaped((half, width), BF16),
        ),
        tuple(
            in_hbm(array)
            for array in (
                w_key, w_dir, w_value, u_rate, k_gain.reshape(1, size), q_gain.reshape(1, size),
                hidden,
            )
        ),
        in_specs=[hbm] * 7,
        scratch=(pltpu.SemaphoreType.DMA((7,)),),
        moved=12 * width * size,
    )
    rows, kn, val, dirs, coeff, solved, exit_keys, turn = call(
        prepare_kernel,
        (
            shaped((tokens, width), BF16), square, shaped((tokens, size), BF16), square, square,
            square, square, shaped((size, size), F32),
        ),
        (core, mine, other, weights, rate_row, rate_bias, key_gain),
        in_specs=[smem] + [vmem] * 4 + [smem, vmem],
        flops=6 * tokens * width * size,
        moved=8 * width * size,
    )
    turns = within_group([turn] * group)
    line = along_line([val] * groups)
    leaving, starts, *near = call(
        functools.partial(leave_kernel, group),
        [
            shaped((2 * tokens + 2 * size, size), BF16),
            shaped((group, size, size), F32),
        ]
        + [shaped((tokens, size), BF16)] * group,
        (place, exit_keys, *turns[::-1]),
        in_specs=[smem] + [vmem] * (1 + group),
        scratch=(
            pltpu.VMEM((group, size, size), F32),
            pltpu.VMEM((group, tokens, size), BF16),
        ),
        flops=12 * group * size**3,
        moved=10**6,
    )
    arrived = along_line([leaving] * groups)
    most = segments // 4
    values, table = call(
        functools.partial(bundle_kernel, group, groups, most),
        [
            shaped((groups * tokens, size), BF16),
            shaped((word_of(most - 1, segments)[0] + 1,), jnp.int32),
        ],
        (place, block_mask[0], starts, *line[::-1]),
        in_specs=[smem, smem, anywhere] + [vmem] * groups,
        out_specs=[vmem, smem],
        moved=10**6,
        limit=8 + group * groups // 4,
    )
    values = within_group([values] * group)
    calls = 1
    each = heads // calls
    pieces = math.gcd(each, 4)
    owns = [
        call(
            functools.partial(query_kernel, number * each * size),
            (
                shaped((each, tokens, size), BF16),
                shaped((each, tokens, size), F32),
                shaped((each, tokens, 1), F32),
                shaped((each, tokens, 1), F32),
            ),
            (rows, in_hbm(w_query), query_gain, kn, dirs, coeff, solved, val),
            in_specs=[vmem, hbm] + [vmem] * 6,
            scratch=(
                pltpu.VMEM((pieces, width, each * size // pieces), BF16),
                pltpu.SemaphoreType.DMA((pieces,)),
            ),
            flops=4 * tokens * width * each * size,
            moved=8 * width * each * size,
            limit=16,
        )
        for number in range(calls)
    ]
    far = call(
        functools.partial(arrive_kernel, groups, group, tokens),
        [shaped((groups * tokens, size), BF16)] * group,
        (place, *arrived[::-1], starts, *near),
        in_specs=[smem] + [vmem] * (groups + 1 + group),
        scratch=(
            pltpu.VMEM((groups, tokens, size), F32),
            pltpu.VMEM((groups, size, size), F32),
        ),
        flops=6 * groups * group * size**3,
        moved=10**6,
        limit=8 + group * groups // 4,
    )
    far = within_group(far)
    chunk = math.gcd(most, 4)
    width_out = w_out.shape[1]
    pieces = math.gcd(width_out // size, 4)
    scratch = [
        pltpu.VMEM((chunk * tokens, size), BF16),
        pltpu.VMEM((chunk * tokens, size), BF16),
        pltpu.VMEM((tokens, heads * size), BF16),
        pltpu.VMEM((pieces, heads * size, width_out // pieces), BF16),
        pltpu.SemaphoreType.DMA((pieces,)),
    ]
    away, kept = call(
        functools.partial(attend_kernel, group, segments, most),
        [shaped((half, width_out), BF16)] * 2,
        (
            place, core, table, *far[::-1], *values[::-1], *(array for own in owns for array in own),
            in_hbm(w_out),
        ),
        in_specs=[smem] * 3 + [vmem] * (2 * group + 4 * calls) + [hbm],
        scratch=scratch,
        flops=2 * tokens * width_out * heads * size,
        moved=4 * 10**6,
        limit=20 + group * groups // 4,
    )
    return kept + lax.ppermute(away, "head", [(0, 1), (1, 0)])


def solution(mesh):
    in_specs = (
        P(("ctx", "head"), None),
        P(None, "head"),
        P(None, "head"),
        P(None, "head"),
        P(None, "head"),
        P("head", None),
        P("head"),
        P(),
        P(),
        P("head", None),
        P("ctx", None),
    )
    out_specs = P(("ctx", "head"), None)
    return jax.shard_map(body, mesh=mesh, in_specs=in_specs, out_specs=out_specs, check_vma=False)
```

```python
import functools
import math

import jax
import jax.numpy as jnp
from jax import lax
from jax.experimental import pallas as pl
from jax.experimental.pallas import tpu as pltpu
from jax.sharding import PartitionSpec as P

EPSILON = 1e-06
NEGATIVE = -1e30
LOG2E = math.log2(math.e)
F32 = jnp.float32
BF16 = jnp.bfloat16
MIB = 1024 * 1024


def call(kernel, out_shape, args, in_specs=None, out_specs=None, scratch=(), flops=0, moved=0, limit=6):
    vmem = pl.BlockSpec(memory_space=pltpu.VMEM)
    return pl.pallas_call(
        kernel,
        out_shape=out_shape,
        in_specs=in_specs or [vmem] * len(args),
        out_specs=out_specs or jax.tree.map(lambda _: vmem, out_shape),
        scratch_shapes=list(scratch),
        compiler_params=pltpu.CompilerParams(vmem_limit_bytes=limit * MIB),
        cost_estimate=pl.CostEstimate(flops=flops, bytes_accessed=moved, transcendentals=0),
    )(*args)


def target_of(member, step, group):
    return member ^ step if group & (group - 1) == 0 else (member + step) % group


def source_of(member, step, group):
    return member ^ step if group & (group - 1) == 0 else (member + group - step) % group


def in_hbm(array):
    return pltpu.with_memory_space_constraint(array, pltpu.HBM)


def step_between(member, source, group):
    return member ^ source if group & (group - 1) == 0 else (member + group - source) % group


def shaped(shape, dtype):
    return jax.ShapeDtypeStruct(shape, dtype)


def split(value):
    high = value.astype(BF16)
    return high, (value - high.astype(F32)).astype(BF16)


def dot3(left, right, left_dim=1, right_dim=0):
    left_high, left_low = split(left)
    right_high, right_low = split(right)
    return lax.dot_general(
        jnp.concatenate([left_high, left_high, left_low], axis=left_dim),
        jnp.concatenate([right_high, right_low, right_high], axis=right_dim),
        (((left_dim,), (right_dim,)), ((), ())),
        preferred_element_type=F32,
    )


def iota2(shape):
    return lax.broadcasted_iota(jnp.int32, shape, 0), lax.broadcasted_iota(jnp.int32, shape, 1)


def merge_inverse(lower, rows, cols):
    tokens = lower.shape[0]
    block = 8
    inverse = jnp.where(rows == cols, 1.0, 0.0).astype(F32)
    first = rows - rows % block
    for step in range(block - 1):
        column = jnp.sum(jnp.where(cols == first + step, lower, 0.0), axis=1, keepdims=True)
        pivot = inverse.reshape(tokens // block, block, tokens)[:, step : step + 1, :]
        pivot = jnp.broadcast_to(pivot, (tokens // block, block, tokens)).reshape(tokens, tokens)
        inverse = inverse - column * pivot
    while block < tokens:
        corner = (
            (rows // (2 * block) == cols // (2 * block))
            & (rows % (2 * block) >= block)
            & (cols % (2 * block) < block)
        )
        inverse = inverse - dot3(dot3(inverse, jnp.where(corner, lower, 0.0)), inverse)
        block *= 2
    return inverse


def load_kernel(size, key_hbm, dir_hbm, value_hbm, rate_hbm, key_gain_hbm,
                query_gain_hbm, mine_hbm, weight_ref, rate_ref, key_gain_ref, query_gain_ref,
                mine_ref, sems):
    pairs = [
        (hbm, weight_ref.at[:, index * size : (index + 1) * size])
        for index, hbm in enumerate((key_hbm, dir_hbm, value_hbm))
    ]
    pairs += [(rate_hbm, rate_ref), (key_gain_hbm, key_gain_ref)]
    pairs += [(query_gain_hbm, query_gain_ref), (mine_hbm, mine_ref)]
    copies = [pltpu.make_async_copy(*pair, sems.at[n]) for n, pair in enumerate(pairs)]
    for copy in copies:
        copy.start()
    for copy in copies:
        copy.wait()


def prepare_kernel(core_ref, mine_ref, other_ref, weight_ref, rate_ref, bias_ref, gain_ref,
                   rows_ref, kn_ref, val_ref, dirs_ref, coeff_ref, solved_ref, exit_ref, turn_ref):
    core = core_ref[0]
    half = mine_ref.shape[0]
    rows_ref[pl.ds(pl.multiple_of(core * half, half), half), :] = mine_ref[...]
    rows_ref[pl.ds(pl.multiple_of((1 - core) * half, half), half), :] = other_ref[...]
    seg = rows_ref[...]
    size = turn_ref.shape[1]
    raw = jnp.dot(seg, weight_ref[...], preferred_element_type=F32)
    keys, raw, vals = raw[:, :size], raw[:, size : 2 * size], raw[:, 2 * size :]
    kn = keys * lax.rsqrt(jnp.mean(keys * keys, axis=-1, keepdims=True) + EPSILON) * gain_ref[...]
    dirs = raw * lax.rsqrt(jnp.sum(raw * raw, axis=-1, keepdims=True) + EPSILON)
    vector = jnp.broadcast_to(rate_ref[...], (16, seg.shape[1]))
    logits = lax.dot_general(seg, vector, (((1,), (1,)), ((), ())), preferred_element_type=F32)
    rates = 2.0 * jax.nn.sigmoid(logits[:, :1] + bias_ref[0])
    val_ref[...] = vals.astype(BF16)
    kn_ref[...] = kn
    dirs_ref[...] = dirs
    tokens, size = dirs.shape
    rows, cols = iota2((tokens, tokens))
    below = rows > cols
    grams = dot3(dirs, jnp.concatenate([dirs, kn], axis=0), 1, 1)
    lower = jnp.where(below, rates * grams[:, :tokens], 0.0)
    crossing = jnp.where(below, rates * grams[:, tokens:], 0.0)
    inverse = merge_inverse(lower, rows, cols)
    both = dot3(inverse, jnp.concatenate([crossing, rates * dirs], axis=1))
    coeff_ref[...] = both[:, :tokens]
    solved_ref[...] = both[:, tokens:]
    crossed = dot3(both, dirs, 0, 0)
    exit_ref[...] = kn - crossed[:tokens]
    heads, lanes = iota2((size, size))
    high, low = split(jnp.where(heads == lanes, 1.0, 0.0) - crossed[tokens:])
    turn_ref[:size] = high
    turn_ref[size : 2 * size] = low
    turn_ref[2 * size :] = vals.astype(BF16)


def leave_kernel(group, place_ref, exit_ref, *refs):
    turn_refs, (leave_ref, starts_ref) = refs[:group], refs[group : group + 2]
    near_refs, (turns_ref, seen_ref) = refs[group + 2 : -2], refs[-2:]
    member = place_ref[0] % group
    tokens, size = exit_ref.shape
    for step in range(group):
        ref = turn_refs[group - 1 - step]
        turns_ref[source_of(member, step, group)] = ref[:size].astype(F32) + ref[
            size : 2 * size
        ].astype(F32)
    own = exit_ref[...]
    keys = own
    product = None
    heads, lanes = iota2((size, size))
    starts_ref[0] = jnp.where(heads == lanes, 1.0, 0.0)
    for index in range(group):
        seen_ref[index] = keys.astype(BF16)
        turn = turns_ref[index]
        product = turn if product is None else dot3(product, turn)
        if index:
            keys = jnp.where(index > member, dot3(keys, turn), own)
        if index < group - 1:
            starts_ref[index + 1] = product
    high, low = split(keys)
    leave_ref[:tokens] = high
    leave_ref[tokens : 2 * tokens] = low
    leave_ref[2 * tokens :] = product.astype(BF16)
    for step in range(group):
        near_refs[step][...] = seen_ref[target_of(member, step, group)]


def word_of(slot, segments):
    bits = segments.bit_length()
    per_word = 31 // bits
    return slot // per_word, bits * (slot % per_word), (1 << bits) - 1


def bundle_kernel(group, groups, most, place_ref, mask_ref, after_ref, *refs):
    val_refs, (line_ref, table_ref) = refs[: groups - 1], refs[groups - 1 :]
    place = place_ref[0]
    segments = mask_ref.shape[0]
    for word in range(table_ref.shape[0]):
        table_ref[word] = 0

    def pick(segment, count):
        wanted = (mask_ref[segment] > 0) & (segment < place) & (count < most)
        word, shift, _ = word_of(count, segments)

        @pl.when(wanted)
        def _():
            table_ref[word] = table_ref[word] | ((segment + 1) << shift)

        return count + wanted.astype(jnp.int32)

    lax.fori_loop(0, segments, pick, jnp.int32(0))
    tokens = val_refs[0].shape[0]
    for way in range(1, groups):
        line_ref[(way - 1) * tokens : way * tokens] = val_refs[groups - 1 - way][...]


def query_kernel(rows_ref, weight_ref, gain_ref, kn_ref, dirs_ref, coeff_ref, solved_ref, val_ref,
                 moved_ref, weighted_ref, peak_ref, total_ref):
    tokens, size = kn_ref.shape
    heads = moved_ref.shape[0]
    across = jnp.concatenate([kn_ref[...], dirs_ref[...]], axis=0)
    into = jnp.concatenate([coeff_ref[...], solved_ref[...]], axis=1)
    count = math.gcd(heads, 4)
    for turn in range(heads // count):
        wide = slice(turn * count * size, (turn + 1) * count * size)
        raw = jnp.dot(rows_ref[...], weight_ref[:, wide], preferred_element_type=F32)
        parts = [raw[:, at : at + size] for at in range(0, count * size, size)]
        raw = jnp.concatenate(parts, axis=0)
        queries = (
            raw * lax.rsqrt(jnp.mean(raw * raw, axis=-1, keepdims=True) + EPSILON) * gain_ref[...]
        )
        seen = dot3(queries, across, 1, 1)
        rows, cols = iota2((count * tokens, tokens))
        up_to = rows % tokens >= cols
        reach = jnp.where(up_to, seen[:, tokens:], 0.0)
        taken = dot3(reach, into)
        scores = (seen[:, :tokens] - taken[:, :tokens]) * (LOG2E / math.sqrt(size))
        scores = jnp.where(up_to, scores, NEGATIVE)
        moved = (queries - taken[:, tokens:]).astype(BF16)
        peak = jnp.max(scores, axis=1, keepdims=True)
        weights = jnp.exp2(scores - peak)
        total = jnp.sum(weights, axis=1, keepdims=True)
        weighted = jnp.dot(weights.astype(BF16), val_ref[...], preferred_element_type=F32)
        for h in range(count):
            part = slice(h * tokens, (h + 1) * tokens)
            head = turn * count + h
            moved_ref[head] = moved[part]
            weighted_ref[head] = weighted[part]
            peak_ref[head] = peak[part]
            total_ref[head] = total[part]


def arrive_kernel(groups, group, tokens, place_ref, *refs):
    arrived, starts_ref, near_refs = refs[:groups], refs[groups], refs[groups + 1 :]
    far_refs, (keys_ref, whole_ref) = refs[-group - 2 : -2], refs[-2:]
    mine, member = place_ref[0] // group, place_ref[0] % group
    size = starts_ref.shape[1]
    for step in range(groups):
        index = source_of(mine, step, groups)
        ref = arrived[groups - 1 - step]
        keys_ref[index] = ref[:tokens].astype(F32) + ref[tokens : 2 * tokens].astype(F32)
        whole_ref[index] = ref[2 * tokens :].astype(F32)
    brought = [keys_ref[groups - 2]]
    product = None
    for index in range(groups - 3, -1, -1):
        keys, whole = keys_ref[index], whole_ref[index + 1]
        if product is not None:
            whole = jnp.where(index + 2 < mine, dot3(whole, product), whole)
        product = whole
        brought.append(jnp.where(index + 1 < mine, dot3(keys, product), keys))
    keys = jnp.concatenate(brought[::-1], axis=0)
    for step in range(group):
        start = starts_ref[target_of(member, step, group)]
        far_refs[step][: (groups - 1) * tokens] = dot3(keys, start).astype(BF16)
        far_refs[step][(groups - 1) * tokens :] = near_refs[step][...]


def attend_kernel(group, segments, most, place_ref, core_ref, table_ref, *refs):
    far_refs, line_refs = refs[:group][::-1], refs[group : 2 * group][::-1]
    turn_refs = refs[2 * group : 3 * group][::-1]
    (moved_ref, weighted_ref, peak_ref, total_ref, out_ref, away_ref, kept_ref, keys_ref, vals_ref,
     attended_ref) = refs[3 * group :]
    core = core_ref[0]
    mine, member = place_ref[0] // group, place_ref[0] % group
    heads, tokens, size = moved_ref.shape
    groups = far_refs[0].shape[0] // tokens
    scaling = LOG2E / math.sqrt(size)
    chunk = keys_ref.shape[0] // tokens
    lanes = lax.broadcasted_iota(jnp.int32, (1, chunk * tokens), 1)

    def collect(turn):
        found = jnp.int32(0)
        for slot in range(chunk):
            part = slice(slot * tokens, (slot + 1) * tokens)
            word, shift, ones = word_of(turn * chunk + slot, segments)
            code = (table_ref[word] >> shift) & ones
            found = found + (code > 0).astype(jnp.int32)
            segment = jnp.maximum(code - 1, 0)
            whose, source = segment % group, segment // group
            before = jnp.where(source < mine, source, groups - 1)
            before = pl.multiple_of(before * tokens, tokens)
            after = jnp.maximum(step_between(mine, source, groups) - 1, 0)
            after = pl.multiple_of(after * tokens, tokens)
            for number in range(group):

                @pl.when(whose == source_of(member, number, group))
                def _():
                    vals_ref[part, :] = jnp.where(
                        source < mine,
                        line_refs[number][pl.ds(after, tokens), :],
                        turn_refs[number][2 * size :],
                    )
                    keys_ref[part, :] = far_refs[number][pl.ds(before, tokens), :]

        return jnp.where(lanes < found * tokens, 0.0, NEGATIVE)

    def advance(moved, bias, peak, total, weighted):
        scores = lax.dot_general(
            moved, keys_ref[...], (((1,), (1,)), ((), ())), preferred_element_type=F32
        )
        scores = scores * scaling + bias
        new_peak = jnp.maximum(peak, jnp.max(scores, axis=1, keepdims=True))
        fading = jnp.exp2(peak - new_peak)
        weights = jnp.exp2(scores - new_peak)
        total = total * fading + jnp.sum(weights, axis=1, keepdims=True)
        weighted = weighted * fading + jnp.dot(
            weights.astype(BF16), vals_ref[...], preferred_element_type=F32
        )
        return new_peak, total, weighted

    half = kept_ref.shape[0]
    turns = most // chunk
    if turns == 1:
        bias = collect(0)
    for head in range(heads):
        state = (peak_ref[head], total_ref[head], weighted_ref[head])
        if turns == 1:
            _, total, weighted = advance(moved_ref[head], bias, *state)
        else:

            def step_of(turn, state, head=head):
                return advance(moved_ref[head], collect(turn), *state)

            _, total, weighted = lax.fori_loop(0, turns, step_of, state)
        done = (weighted * (1.0 / total)).astype(BF16)
        for index in range(tokens // half):
            at = pl.multiple_of(jnp.where(index == core, half, 0), half)
            attended_ref[pl.ds(at, half), head * size : (head + 1) * size] = done[
                index * half : (index + 1) * half
            ]
    wide = math.gcd(out_ref.shape[1], 4 * size)
    for at in range(0, out_ref.shape[1], wide):
        part = slice(at, at + wide)
        result = jnp.dot(attended_ref[...], out_ref[:, part], preferred_element_type=F32)
        result = result.astype(BF16)
        away_ref[:, part] = result[:half]
        kept_ref[:, part] = result[half:]


def body(
    hidden, w_query, w_key, w_value, w_dir, u_rate, rate_bias, q_gain, k_gain, w_out, block_mask
):
    segments = lax.axis_size("ctx")
    place = lax.axis_index("ctx").astype(jnp.int32).reshape(1)
    core = lax.axis_index("head").astype(jnp.int32).reshape(1)
    group = max(d for d in range(1, math.isqrt(segments) + 1) if segments % d == 0)
    groups = segments // group
    other = lax.ppermute(hidden, "head", [(0, 1), (1, 0)])
    half, width = hidden.shape
    tokens = half * lax.axis_size("head")
    size = w_key.shape[1]
    heads = w_query.shape[1] // size
    smem = pl.BlockSpec(memory_space=pltpu.SMEM)
    vmem = pl.BlockSpec(memory_space=pltpu.VMEM)
    hbm = pl.BlockSpec(memory_space=pltpu.HBM)
    anywhere = pl.BlockSpec(memory_space=pl.ANY)
    square = shaped((tokens, size), F32)

    def swapped(values, count, pairs_of):
        out = [values[0]] * count
        for step in range(count - 1, 0, -1):
            out[step] = lax.ppermute(values[step], "ctx", pairs_of(step))
        return out

    def within_group(values):
        return swapped(values, group, lambda step: [
            (s, s - s % group + target_of(s % group, step, group)) for s in range(segments)
        ])

    def along_line(values):
        return swapped(values, groups, lambda step: [
            (s, s % group + group * target_of(s // group, step, groups)) for s in range(segments)
        ])

    weights, rate_row, key_gain, query_gain, mine = call(
        functools.partial(load_kernel, size),
        (
            shaped((width, 3 * size), BF16), shaped((1, width), BF16), shaped((1, size), F32),
            shaped((1, size), F32), shaped((half, width), BF16),
        ),
        tuple(
            in_hbm(array)
            for array in (
                w_key, w_dir, w_value, u_rate, k_gain.reshape(1, size), q_gain.reshape(1, size),
                hidden,
            )
        ),
        in_specs=[hbm] * 7,
        scratch=(pltpu.SemaphoreType.DMA((7,)),),
        moved=12 * width * size,
    )
    rows, kn, val, dirs, coeff, solved, exit_keys, turn = call(
        prepare_kernel,
        (
            shaped((tokens, width), BF16), square, shaped((tokens, size), BF16), square, square,
            square, square, shaped((2 * size + tokens, size), BF16),
        ),
        (core, mine, other, weights, rate_row, rate_bias, key_gain),
        in_specs=[smem] + [vmem] * 4 + [smem, vmem],
        flops=6 * tokens * width * size,
        moved=8 * width * size,
    )
    turns = within_group([turn] * group)
    line = along_line([val] * groups)
    leaving, starts, *near = call(
        functools.partial(leave_kernel, group),
        [
            shaped((2 * tokens + size, size), BF16),
            shaped((group, size, size), F32),
        ]
        + [shaped((tokens, size), BF16)] * group,
        (place, exit_keys, *turns[::-1]),
        in_specs=[smem] + [vmem] * (1 + group),
        scratch=(
            pltpu.VMEM((group, size, size), F32),
            pltpu.VMEM((group, tokens, size), BF16),
        ),
        flops=12 * group * size**3,
        moved=10**6,
    )
    arrived = along_line([leaving] * groups)
    most = segments // 4
    values, table = call(
        functools.partial(bundle_kernel, group, groups, most),
        [
            shaped(((groups - 1) * tokens, size), BF16),
            shaped((word_of(most - 1, segments)[0] + 1,), jnp.int32),
        ],
        (place, block_mask[0], starts, *line[:0:-1]),
        in_specs=[smem, smem, anywhere] + [vmem] * (groups - 1),
        out_specs=[vmem, smem],
        moved=10**6,
        limit=8 + group * groups // 4,
    )
    values = within_group([values] * group)
    own = call(
        query_kernel,
        (
            shaped((heads, tokens, size), BF16),
            shaped((heads, tokens, size), F32),
            shaped((heads, tokens, 1), F32),
            shaped((heads, tokens, 1), F32),
        ),
        (rows, w_query, query_gain, kn, dirs, coeff, solved, val),
        flops=4 * tokens * width * heads * size,
        moved=8 * width * heads * size,
        limit=14,
    )
    most = segments // 4
    values, table = call(
        functools.partial(bundle_kernel, group, groups, most),
        [
            shaped(((groups - 1) * tokens, size), BF16),
            shaped((word_of(most - 1, segments)[0] + 1,), jnp.int32),
        ],
        (place, block_mask[0], starts, *line[:0:-1]),
        in_specs=[smem, smem, anywhere] + [vmem] * (groups - 1),
        out_specs=[vmem, smem],
        moved=10**6,
        limit=8 + group * groups // 4,
    )
    values = within_group([values] * group)
    far = call(
        functools.partial(arrive_kernel, groups, group, tokens),
        [shaped((groups * tokens, size), BF16)] * group,
        (place, *arrived[::-1], starts, *near),
        in_specs=[smem] + [vmem] * (groups + 1 + group),
        scratch=(
            pltpu.VMEM((groups, tokens, size), F32),
            pltpu.VMEM((groups, size, size), F32),
        ),
        flops=6 * groups * group * size**3,
        moved=10**6,
        limit=8 + group * groups // 4,
    )
    far = within_group(far)
    chunk = math.gcd(most, 4)
    width_out = w_out.shape[1]
    scratch = [
        pltpu.VMEM((chunk * tokens, size), BF16),
        pltpu.VMEM((chunk * tokens, size), BF16),
        pltpu.VMEM((tokens, heads * size), BF16),
    ]
    away, kept = call(
        functools.partial(attend_kernel, group, segments, most),
        [shaped((half, width_out), BF16)] * 2,
        (place, core, table, *far[::-1], *values[::-1], *turns[::-1], *own, w_out),
        in_specs=[smem] * 3 + [vmem] * (3 * group + 5),
        scratch=scratch,
        flops=2 * tokens * width_out * heads * size,
        moved=4 * 10**6,
        limit=14 + group * groups // 4,
    )
    return kept + lax.ppermute(away, "head", [(0, 1), (1, 0)])


def solution(mesh):
    in_specs = (
        P(("ctx", "head"), None),
        P(None, "head"),
        P(None, "head"),
        P(None, "head"),
        P(None, "head"),
        P("head", None),
        P("head"),
        P(),
        P(),
        P("head", None),
        P("ctx", None),
    )
    out_specs = P(("ctx", "head"), None)
    return jax.shard_map(body, mesh=mesh, in_specs=in_specs, out_specs=out_specs, check_vma=False)
```

```python
import functools
import math

import jax
import jax.numpy as jnp
from jax import lax
from jax.experimental import pallas as pl
from jax.experimental.pallas import tpu as pltpu
from jax.sharding import PartitionSpec as P

EPSILON = 1e-06
NEGATIVE = -1e30
LOG2E = math.log2(math.e)
F32 = jnp.float32
BF16 = jnp.bfloat16
MIB = 1024 * 1024


def call(kernel, out_shape, args, in_specs=None, out_specs=None, scratch=(), flops=0, moved=0, limit=6):
    vmem = pl.BlockSpec(memory_space=pltpu.VMEM)
    return pl.pallas_call(
        kernel,
        out_shape=out_shape,
        in_specs=in_specs or [vmem] * len(args),
        out_specs=out_specs or jax.tree.map(lambda _: vmem, out_shape),
        scratch_shapes=list(scratch),
        compiler_params=pltpu.CompilerParams(vmem_limit_bytes=limit * MIB),
        cost_estimate=pl.CostEstimate(flops=flops, bytes_accessed=moved, transcendentals=0),
    )(*args)


def target_of(member, step, group):
    return member ^ step if group & (group - 1) == 0 else (member + step) % group


def source_of(member, step, group):
    return member ^ step if group & (group - 1) == 0 else (member + group - step) % group


def in_hbm(array):
    return pltpu.with_memory_space_constraint(array, pltpu.HBM)


def step_between(member, source, group):
    return member ^ source if group & (group - 1) == 0 else (member + group - source) % group


def shaped(shape, dtype):
    return jax.ShapeDtypeStruct(shape, dtype)


def split(value):
    high = value.astype(BF16)
    return high, (value - high.astype(F32)).astype(BF16)


def dot3(left, right, left_dim=1, right_dim=0):
    left_high, left_low = split(left)
    right_high, right_low = split(right)
    return lax.dot_general(
        jnp.concatenate([left_high, left_high, left_low], axis=left_dim),
        jnp.concatenate([right_high, right_low, right_high], axis=right_dim),
        (((left_dim,), (right_dim,)), ((), ())),
        preferred_element_type=F32,
    )


def iota2(shape):
    return lax.broadcasted_iota(jnp.int32, shape, 0), lax.broadcasted_iota(jnp.int32, shape, 1)


def merge_inverse(lower, rows, cols):
    tokens = lower.shape[0]
    block = 8
    inverse = jnp.where(rows == cols, 1.0, 0.0).astype(F32)
    first = rows - rows % block
    for step in range(block - 1):
        column = jnp.sum(jnp.where(cols == first + step, lower, 0.0), axis=1, keepdims=True)
        pivot = inverse.reshape(tokens // block, block, tokens)[:, step : step + 1, :]
        pivot = jnp.broadcast_to(pivot, (tokens // block, block, tokens)).reshape(tokens, tokens)
        inverse = inverse - column * pivot
    while block < tokens:
        corner = (
            (rows // (2 * block) == cols // (2 * block))
            & (rows % (2 * block) >= block)
            & (cols % (2 * block) < block)
        )
        inverse = inverse - dot3(dot3(inverse, jnp.where(corner, lower, 0.0)), inverse)
        block *= 2
    return inverse


def load_kernel(size, key_hbm, dir_hbm, value_hbm, rate_hbm, key_gain_hbm,
                query_gain_hbm, mine_hbm, weight_ref, rate_ref, key_gain_ref, query_gain_ref,
                mine_ref, sems):
    pairs = [
        (hbm, weight_ref.at[:, index * size : (index + 1) * size])
        for index, hbm in enumerate((key_hbm, dir_hbm, value_hbm))
    ]
    pairs += [(rate_hbm, rate_ref), (key_gain_hbm, key_gain_ref)]
    pairs += [(query_gain_hbm, query_gain_ref), (mine_hbm, mine_ref)]
    copies = [pltpu.make_async_copy(*pair, sems.at[n]) for n, pair in enumerate(pairs)]
    for copy in copies:
        copy.start()
    for copy in copies:
        copy.wait()


def prepare_kernel(core_ref, mine_ref, other_ref, weight_ref, rate_ref, bias_ref, gain_ref,
                   query_hbm, rows_ref, kn_ref, val_ref, dirs_ref, coeff_ref, solved_ref, exit_ref,
                   turn_ref, query_ref, sem):
    query_copy = pltpu.make_async_copy(query_hbm, query_ref, sem)
    query_copy.start()
    core = core_ref[0]
    half = mine_ref.shape[0]
    rows_ref[pl.ds(pl.multiple_of(core * half, half), half), :] = mine_ref[...]
    rows_ref[pl.ds(pl.multiple_of((1 - core) * half, half), half), :] = other_ref[...]
    seg = rows_ref[...]
    size = turn_ref.shape[1]
    raw = jnp.dot(seg, weight_ref[...], preferred_element_type=F32)
    keys, raw, vals = raw[:, :size], raw[:, size : 2 * size], raw[:, 2 * size :]
    kn = keys * lax.rsqrt(jnp.mean(keys * keys, axis=-1, keepdims=True) + EPSILON) * gain_ref[...]
    dirs = raw * lax.rsqrt(jnp.sum(raw * raw, axis=-1, keepdims=True) + EPSILON)
    vector = jnp.broadcast_to(rate_ref[...], (16, seg.shape[1]))
    logits = lax.dot_general(seg, vector, (((1,), (1,)), ((), ())), preferred_element_type=F32)
    rates = 2.0 * jax.nn.sigmoid(logits[:, :1] + bias_ref[0])
    val_ref[...] = vals.astype(BF16)
    kn_ref[...] = kn
    dirs_ref[...] = dirs
    tokens, size = dirs.shape
    rows, cols = iota2((tokens, tokens))
    below = rows > cols
    grams = dot3(dirs, jnp.concatenate([dirs, kn], axis=0), 1, 1)
    lower = jnp.where(below, rates * grams[:, :tokens], 0.0)
    crossing = jnp.where(below, rates * grams[:, tokens:], 0.0)
    inverse = merge_inverse(lower, rows, cols)
    both = dot3(inverse, jnp.concatenate([crossing, rates * dirs], axis=1))
    coeff_ref[...] = both[:, :tokens]
    solved_ref[...] = both[:, tokens:]
    crossed = dot3(both, dirs, 0, 0)
    exit_ref[...] = kn - crossed[:tokens]
    heads, lanes = iota2((size, size))
    high, low = split(jnp.where(heads == lanes, 1.0, 0.0) - crossed[tokens:])
    turn_ref[:size] = high
    turn_ref[size : 2 * size] = low
    turn_ref[2 * size :] = vals.astype(BF16)
    query_copy.wait()


def leave_kernel(group, after, place_ref, exit_ref, *refs):
    turn_refs, refs = refs[after : after + group], refs[after + group :]
    leave_ref, starts_ref = refs[:2]
    near_refs, (turns_ref, seen_ref) = refs[2:-2], refs[-2:]
    member = place_ref[0] % group
    tokens, size = exit_ref.shape
    for step in range(group):
        ref = turn_refs[group - 1 - step]
        turns_ref[source_of(member, step, group)] = ref[:size].astype(F32) + ref[
            size : 2 * size
        ].astype(F32)
    own = exit_ref[...]
    keys = own
    product = None
    heads, lanes = iota2((size, size))
    starts_ref[0] = jnp.where(heads == lanes, 1.0, 0.0)
    for index in range(group):
        seen_ref[index] = keys.astype(BF16)
        turn = turns_ref[index]
        product = turn if product is None else dot3(product, turn)
        if index:
            keys = jnp.where(index > member, dot3(keys, turn), own)
        if index < group - 1:
            starts_ref[index + 1] = product
    high, low = split(keys)
    leave_ref[:tokens] = high
    leave_ref[tokens : 2 * tokens] = low
    leave_ref[2 * tokens :] = product.astype(BF16)
    for step in range(group):
        near_refs[step][...] = seen_ref[target_of(member, step, group)]


def word_of(slot, segments):
    bits = segments.bit_length()
    per_word = 31 // bits
    return slot // per_word, bits * (slot % per_word), (1 << bits) - 1


def bundle_kernel(group, groups, most, place_ref, mask_ref, after_ref, *refs):
    val_refs, (line_ref, table_ref) = refs[: groups - 1], refs[groups - 1 :]
    place = place_ref[0]
    segments = mask_ref.shape[0]
    for word in range(table_ref.shape[0]):
        table_ref[word] = 0

    def pick(segment, count):
        wanted = (mask_ref[segment] > 0) & (segment < place) & (count < most)
        word, shift, _ = word_of(count, segments)

        @pl.when(wanted)
        def _():
            table_ref[word] = table_ref[word] | ((segment + 1) << shift)

        return count + wanted.astype(jnp.int32)

    lax.fori_loop(0, segments, pick, jnp.int32(0))
    tokens = val_refs[0].shape[0]
    for way in range(1, groups):
        line_ref[(way - 1) * tokens : way * tokens] = val_refs[groups - 1 - way][...]


def query_kernel(rows_ref, weight_ref, gain_ref, kn_ref, dirs_ref, coeff_ref, solved_ref, val_ref,
                 moved_ref, weighted_ref, peak_ref, total_ref):
    tokens, size = kn_ref.shape
    heads = moved_ref.shape[0]
    across = jnp.concatenate([kn_ref[...], dirs_ref[...]], axis=0)
    into = jnp.concatenate([coeff_ref[...], solved_ref[...]], axis=1)
    count = math.gcd(heads, 4)
    for turn in range(heads // count):
        wide = slice(turn * count * size, (turn + 1) * count * size)
        raw = jnp.dot(rows_ref[...], weight_ref[:, wide], preferred_element_type=F32)
        parts = [raw[:, at : at + size] for at in range(0, count * size, size)]
        raw = jnp.concatenate(parts, axis=0)
        queries = (
            raw * lax.rsqrt(jnp.mean(raw * raw, axis=-1, keepdims=True) + EPSILON) * gain_ref[...]
        )
        seen = dot3(queries, across, 1, 1)
        rows, cols = iota2((count * tokens, tokens))
        up_to = rows % tokens >= cols
        reach = jnp.where(up_to, seen[:, tokens:], 0.0)
        taken = dot3(reach, into)
        scores = (seen[:, :tokens] - taken[:, :tokens]) * (LOG2E / math.sqrt(size))
        scores = jnp.where(up_to, scores, NEGATIVE)
        moved = (queries - taken[:, tokens:]).astype(BF16)
        peak = jnp.max(scores, axis=1, keepdims=True)
        weights = jnp.exp2(scores - peak)
        total = jnp.sum(weights, axis=1, keepdims=True)
        weighted = jnp.dot(weights.astype(BF16), val_ref[...], preferred_element_type=F32)
        for h in range(count):
            part = slice(h * tokens, (h + 1) * tokens)
            head = turn * count + h
            moved_ref[head] = moved[part]
            weighted_ref[head] = weighted[part]
            peak_ref[head] = peak[part]
            total_ref[head] = total[part]


def arrive_kernel(groups, group, tokens, place_ref, *refs):
    arrived, starts_ref, near_refs = refs[:groups], refs[groups], refs[groups + 1 :]
    far_refs, (keys_ref, whole_ref) = refs[-group - 2 : -2], refs[-2:]
    mine, member = place_ref[0] // group, place_ref[0] % group
    size = starts_ref.shape[1]
    for step in range(groups):
        index = source_of(mine, step, groups)
        ref = arrived[groups - 1 - step]
        keys_ref[index] = ref[:tokens].astype(F32) + ref[tokens : 2 * tokens].astype(F32)
        whole_ref[index] = ref[2 * tokens :].astype(F32)
    brought = [keys_ref[groups - 2]]
    product = None
    for index in range(groups - 3, -1, -1):
        keys, whole = keys_ref[index], whole_ref[index + 1]
        if product is not None:
            whole = jnp.where(index + 2 < mine, dot3(whole, product), whole)
        product = whole
        brought.append(jnp.where(index + 1 < mine, dot3(keys, product), keys))
    keys = jnp.concatenate(brought[::-1], axis=0)
    for step in range(group):
        start = starts_ref[target_of(member, step, group)]
        far_refs[step][: (groups - 1) * tokens] = dot3(keys, start).astype(BF16)
        far_refs[step][(groups - 1) * tokens :] = near_refs[step][...]


def attend_kernel(group, segments, most, place_ref, core_ref, table_ref, *refs):
    far_refs, line_refs = refs[:group][::-1], refs[group : 2 * group][::-1]
    turn_refs = refs[2 * group : 3 * group][::-1]
    (moved_ref, weighted_ref, peak_ref, total_ref, out_ref, away_ref, kept_ref, keys_ref, vals_ref,
     attended_ref) = refs[3 * group :]
    core = core_ref[0]
    mine, member = place_ref[0] // group, place_ref[0] % group
    heads, tokens, size = moved_ref.shape
    groups = far_refs[0].shape[0] // tokens
    scaling = LOG2E / math.sqrt(size)
    chunk = keys_ref.shape[0] // tokens
    lanes = lax.broadcasted_iota(jnp.int32, (1, chunk * tokens), 1)

    def collect(turn):
        found = jnp.int32(0)
        for slot in range(chunk):
            part = slice(slot * tokens, (slot + 1) * tokens)
            word, shift, ones = word_of(turn * chunk + slot, segments)
            code = (table_ref[word] >> shift) & ones
            found = found + (code > 0).astype(jnp.int32)
            segment = jnp.maximum(code - 1, 0)
            whose, source = segment % group, segment // group
            before = jnp.where(source < mine, source, groups - 1)
            before = pl.multiple_of(before * tokens, tokens)
            after = jnp.maximum(step_between(mine, source, groups) - 1, 0)
            after = pl.multiple_of(after * tokens, tokens)
            for number in range(group):

                @pl.when(whose == source_of(member, number, group))
                def _():
                    vals_ref[part, :] = jnp.where(
                        source < mine,
                        line_refs[number][pl.ds(after, tokens), :],
                        turn_refs[number][2 * size :],
                    )
                    keys_ref[part, :] = far_refs[number][pl.ds(before, tokens), :]

        return jnp.where(lanes < found * tokens, 0.0, NEGATIVE)

    def advance(moved, bias, peak, total, weighted):
        scores = lax.dot_general(
            moved, keys_ref[...], (((1,), (1,)), ((), ())), preferred_element_type=F32
        )
        scores = scores * scaling + bias
        new_peak = jnp.maximum(peak, jnp.max(scores, axis=1, keepdims=True))
        fading = jnp.exp2(peak - new_peak)
        weights = jnp.exp2(scores - new_peak)
        total = total * fading + jnp.sum(weights, axis=1, keepdims=True)
        weighted = weighted * fading + jnp.dot(
            weights.astype(BF16), vals_ref[...], preferred_element_type=F32
        )
        return new_peak, total, weighted

    half = kept_ref.shape[0]
    turns = most // chunk
    if turns == 1:
        bias = collect(0)
    for head in range(heads):
        state = (peak_ref[head], total_ref[head], weighted_ref[head])
        if turns == 1:
            _, total, weighted = advance(moved_ref[head], bias, *state)
        else:

            def step_of(turn, state, head=head):
                return advance(moved_ref[head], collect(turn), *state)

            _, total, weighted = lax.fori_loop(0, turns, step_of, state)
        done = (weighted * (1.0 / total)).astype(BF16)
        for index in range(tokens // half):
            at = pl.multiple_of(jnp.where(index == core, half, 0), half)
            attended_ref[pl.ds(at, half), head * size : (head + 1) * size] = done[
                index * half : (index + 1) * half
            ]
    wide = math.gcd(out_ref.shape[1], 4 * size)
    for at in range(0, out_ref.shape[1], wide):
        part = slice(at, at + wide)
        result = jnp.dot(attended_ref[...], out_ref[:, part], preferred_element_type=F32)
        result = result.astype(BF16)
        away_ref[:, part] = result[:half]
        kept_ref[:, part] = result[half:]


def body(
    hidden, w_query, w_key, w_value, w_dir, u_rate, rate_bias, q_gain, k_gain, w_out, block_mask
):
    segments = lax.axis_size("ctx")
    place = lax.axis_index("ctx").astype(jnp.int32).reshape(1)
    core = lax.axis_index("head").astype(jnp.int32).reshape(1)
    group = max(d for d in range(1, math.isqrt(segments) + 1) if segments % d == 0)
    groups = segments // group
    other = lax.ppermute(hidden, "head", [(0, 1), (1, 0)])
    half, width = hidden.shape
    tokens = half * lax.axis_size("head")
    size = w_key.shape[1]
    heads = w_query.shape[1] // size
    smem = pl.BlockSpec(memory_space=pltpu.SMEM)
    vmem = pl.BlockSpec(memory_space=pltpu.VMEM)
    hbm = pl.BlockSpec(memory_space=pltpu.HBM)
    anywhere = pl.BlockSpec(memory_space=pl.ANY)
    square = shaped((tokens, size), F32)

    def swapped(values, count, pairs_of):
        out = [values[0]] * count
        for step in range(count - 1, 0, -1):
            out[step] = lax.ppermute(values[step], "ctx", pairs_of(step))
        return out

    def within_group(values):
        return swapped(values, group, lambda step: [
            (s, s - s % group + target_of(s % group, step, group)) for s in range(segments)
        ])

    def along_line(values):
        return swapped(values, groups, lambda step: [
            (s, s % group + group * target_of(s // group, step, groups)) for s in range(segments)
        ])

    weights, rate_row, key_gain, query_gain, mine = call(
        functools.partial(load_kernel, size),
        (
            shaped((width, 3 * size), BF16), shaped((1, width), BF16), shaped((1, size), F32),
            shaped((1, size), F32), shaped((half, width), BF16),
        ),
        tuple(
            in_hbm(array)
            for array in (
                w_key, w_dir, w_value, u_rate, k_gain.reshape(1, size), q_gain.reshape(1, size),
                hidden,
            )
        ),
        in_specs=[hbm] * 7,
        scratch=(pltpu.SemaphoreType.DMA((7,)),),
        moved=12 * width * size,
    )
    rows, kn, val, dirs, coeff, solved, exit_keys, turn, query_weights = call(
        prepare_kernel,
        (
            shaped((tokens, width), BF16), square, shaped((tokens, size), BF16), square, square,
            square, square, shaped((2 * size + tokens, size), BF16),
            shaped(w_query.shape, BF16),
        ),
        (core, mine, other, weights, rate_row, rate_bias, key_gain, in_hbm(w_query)),
        in_specs=[smem] + [vmem] * 4 + [smem, vmem, hbm],
        scratch=(pltpu.SemaphoreType.DMA,),
        limit=12,
        flops=6 * tokens * width * size,
        moved=8 * width * size,
    )
    turns = within_group([turn] * group)
    line = along_line([val] * groups)
    leaving, starts, *near = call(
        functools.partial(leave_kernel, group, groups - 1),
        [
            shaped((2 * tokens + size, size), BF16),
            shaped((group, size, size), F32),
        ]
        + [shaped((tokens, size), BF16)] * group,
        (place, exit_keys, *line[1:], *turns[::-1]),
        in_specs=[smem, vmem] + [anywhere] * (groups - 1) + [vmem] * group,
        scratch=(
            pltpu.VMEM((group, size, size), F32),
            pltpu.VMEM((group, tokens, size), BF16),
        ),
        flops=12 * group * size**3,
        moved=10**6,
    )
    arrived = along_line([leaving] * groups)
    most = segments // 4
    values, table = call(
        functools.partial(bundle_kernel, group, groups, most),
        [
            shaped(((groups - 1) * tokens, size), BF16),
            shaped((word_of(most - 1, segments)[0] + 1,), jnp.int32),
        ],
        (place, block_mask[0], starts, *line[:0:-1]),
        in_specs=[smem, smem, anywhere] + [vmem] * (groups - 1),
        out_specs=[vmem, smem],
        moved=10**6,
        limit=8 + group * groups // 4,
    )
    values = within_group([values] * group)
    own = call(
        query_kernel,
        (
            shaped((heads, tokens, size), BF16),
            shaped((heads, tokens, size), F32),
            shaped((heads, tokens, 1), F32),
            shaped((heads, tokens, 1), F32),
        ),
        (rows, query_weights, query_gain, kn, dirs, coeff, solved, val),
        flops=4 * tokens * width * heads * size,
        moved=8 * width * heads * size,
        limit=14,
    )
    most = segments // 4
    values, table = call(
        functools.partial(bundle_kernel, group, groups, most),
        [
            shaped(((groups - 1) * tokens, size), BF16),
            shaped((word_of(most - 1, segments)[0] + 1,), jnp.int32),
        ],
        (place, block_mask[0], starts, *line[:0:-1]),
        in_specs=[smem, smem, anywhere] + [vmem] * (groups - 1),
        out_specs=[vmem, smem],
        moved=10**6,
        limit=8 + group * groups // 4,
    )
    values = within_group([values] * group)
    far = call(
        functools.partial(arrive_kernel, groups, group, tokens),
        [shaped((groups * tokens, size), BF16)] * group,
        (place, *arrived[::-1], starts, *near),
        in_specs=[smem] + [vmem] * (groups + 1 + group),
        scratch=(
            pltpu.VMEM((groups, tokens, size), F32),
            pltpu.VMEM((groups, size, size), F32),
        ),
        flops=6 * groups * group * size**3,
        moved=10**6,
        limit=8 + group * groups // 4,
    )
    far = within_group(far)
    chunk = math.gcd(most, 4)
    width_out = w_out.shape[1]
    scratch = [
        pltpu.VMEM((chunk * tokens, size), BF16),
        pltpu.VMEM((chunk * tokens, size), BF16),
        pltpu.VMEM((tokens, heads * size), BF16),
    ]
    away, kept = call(
        functools.partial(attend_kernel, group, segments, most),
        [shaped((half, width_out), BF16)] * 2,
        (place, core, table, *far[::-1], *values[::-1], *turns[::-1], *own, w_out),
        in_specs=[smem] * 3 + [vmem] * (3 * group + 5),
        scratch=scratch,
        flops=2 * tokens * width_out * heads * size,
        moved=4 * 10**6,
        limit=14 + group * groups // 4,
    )
    return kept + lax.ppermute(away, "head", [(0, 1), (1, 0)])


def solution(mesh):
    in_specs = (
        P(("ctx", "head"), None),
        P(None, "head"),
        P(None, "head"),
        P(None, "head"),
        P(None, "head"),
        P("head", None),
        P("head"),
        P(),
        P(),
        P("head", None),
        P("ctx", None),
    )
    out_specs = P(("ctx", "head"), None)
    return jax.shard_map(body, mesh=mesh, in_specs=in_specs, out_specs=out_specs, check_vma=False)
```

```python
import functools
import math

import jax
import jax.numpy as jnp
from jax import lax
from jax.experimental import pallas as pl
from jax.experimental.pallas import tpu as pltpu
from jax.sharding import PartitionSpec as P

EPSILON = 1e-06
NEGATIVE = -1e30
LOG2E = math.log2(math.e)
F32 = jnp.float32
BF16 = jnp.bfloat16
MIB = 1024 * 1024


def call(kernel, out_shape, args, in_specs=None, out_specs=None, scratch=(), flops=0, moved=0, limit=6):
    vmem = pl.BlockSpec(memory_space=pltpu.VMEM)
    return pl.pallas_call(
        kernel,
        out_shape=out_shape,
        in_specs=in_specs or [vmem] * len(args),
        out_specs=out_specs or jax.tree.map(lambda _: vmem, out_shape),
        scratch_shapes=list(scratch),
        compiler_params=pltpu.CompilerParams(vmem_limit_bytes=limit * MIB),
        cost_estimate=pl.CostEstimate(flops=flops, bytes_accessed=moved, transcendentals=0),
    )(*args)


def target_of(member, step, group):
    return member ^ step if group & (group - 1) == 0 else (member + step) % group


def source_of(member, step, group):
    return member ^ step if group & (group - 1) == 0 else (member + group - step) % group


def in_hbm(array):
    return pltpu.with_memory_space_constraint(array, pltpu.HBM)


def step_between(member, source, group):
    return member ^ source if group & (group - 1) == 0 else (member + group - source) % group


def shaped(shape, dtype):
    return jax.ShapeDtypeStruct(shape, dtype)


def split(value):
    high = value.astype(BF16)
    return high, (value - high.astype(F32)).astype(BF16)


def dot3(left, right, left_dim=1, right_dim=0):
    left_high, left_low = split(left)
    right_high, right_low = split(right)
    return lax.dot_general(
        jnp.concatenate([left_high, left_high, left_low], axis=left_dim),
        jnp.concatenate([right_high, right_low, right_high], axis=right_dim),
        (((left_dim,), (right_dim,)), ((), ())),
        preferred_element_type=F32,
    )


def iota2(shape):
    return lax.broadcasted_iota(jnp.int32, shape, 0), lax.broadcasted_iota(jnp.int32, shape, 1)


def merge_inverse(lower, rows, cols):
    tokens = lower.shape[0]
    block = 8
    inverse = jnp.where(rows == cols, 1.0, 0.0).astype(F32)
    first = rows - rows % block
    for step in range(block - 1):
        column = jnp.sum(jnp.where(cols == first + step, lower, 0.0), axis=1, keepdims=True)
        pivot = inverse.reshape(tokens // block, block, tokens)[:, step : step + 1, :]
        pivot = jnp.broadcast_to(pivot, (tokens // block, block, tokens)).reshape(tokens, tokens)
        inverse = inverse - column * pivot
    while block < tokens:
        corner = (
            (rows // (2 * block) == cols // (2 * block))
            & (rows % (2 * block) >= block)
            & (cols % (2 * block) < block)
        )
        inverse = inverse - dot3(dot3(inverse, jnp.where(corner, lower, 0.0)), inverse)
        block *= 2
    return inverse


def load_kernel(size, key_hbm, dir_hbm, value_hbm, rate_hbm, key_gain_hbm,
                query_gain_hbm, mine_hbm, weight_ref, rate_ref, key_gain_ref, query_gain_ref,
                mine_ref, sems):
    pairs = [
        (hbm, weight_ref.at[:, index * size : (index + 1) * size])
        for index, hbm in enumerate((key_hbm, dir_hbm, value_hbm))
    ]
    pairs += [(rate_hbm, rate_ref), (key_gain_hbm, key_gain_ref)]
    pairs += [(query_gain_hbm, query_gain_ref), (mine_hbm, mine_ref)]
    copies = [pltpu.make_async_copy(*pair, sems.at[n]) for n, pair in enumerate(pairs)]
    for copy in copies:
        copy.start()
    for copy in copies:
        copy.wait()


def prepare_kernel(core_ref, mine_ref, other_ref, weight_ref, rate_ref, bias_ref, gain_ref,
                   rows_ref, kn_ref, val_ref, dirs_ref, coeff_ref, solved_ref, exit_ref, turn_ref):
    core = core_ref[0]
    half = mine_ref.shape[0]
    rows_ref[pl.ds(pl.multiple_of(core * half, half), half), :] = mine_ref[...]
    rows_ref[pl.ds(pl.multiple_of((1 - core) * half, half), half), :] = other_ref[...]
    seg = rows_ref[...]
    size = turn_ref.shape[1]
    raw = jnp.dot(seg, weight_ref[...], preferred_element_type=F32)
    keys, raw, vals = raw[:, :size], raw[:, size : 2 * size], raw[:, 2 * size :]
    kn = keys * lax.rsqrt(jnp.mean(keys * keys, axis=-1, keepdims=True) + EPSILON) * gain_ref[...]
    dirs = raw * lax.rsqrt(jnp.sum(raw * raw, axis=-1, keepdims=True) + EPSILON)
    vector = jnp.broadcast_to(rate_ref[...], (16, seg.shape[1]))
    logits = lax.dot_general(seg, vector, (((1,), (1,)), ((), ())), preferred_element_type=F32)
    rates = 2.0 * jax.nn.sigmoid(logits[:, :1] + bias_ref[0])
    val_ref[...] = vals.astype(BF16)
    kn_ref[...] = kn
    dirs_ref[...] = dirs
    tokens, size = dirs.shape
    rows, cols = iota2((tokens, tokens))
    below = rows > cols
    grams = dot3(dirs, jnp.concatenate([dirs, kn], axis=0), 1, 1)
    lower = jnp.where(below, rates * grams[:, :tokens], 0.0)
    crossing = jnp.where(below, rates * grams[:, tokens:], 0.0)
    inverse = merge_inverse(lower, rows, cols)
    both = dot3(inverse, jnp.concatenate([crossing, rates * dirs], axis=1))
    coeff_ref[...] = both[:, :tokens]
    solved_ref[...] = both[:, tokens:]
    crossed = dot3(both, dirs, 0, 0)
    exit_ref[...] = kn - crossed[:tokens]
    heads, lanes = iota2((size, size))
    high, low = split(jnp.where(heads == lanes, 1.0, 0.0) - crossed[tokens:])
    turn_ref[:size] = high
    turn_ref[size : 2 * size] = low
    turn_ref[2 * size :] = vals.astype(BF16)


def leave_kernel(group, place_ref, exit_ref, *refs):
    turn_refs, (leave_ref, starts_ref) = refs[:group], refs[group : group + 2]
    near_refs, (turns_ref, seen_ref) = refs[group + 2 : -2], refs[-2:]
    member = place_ref[0] % group
    tokens, size = exit_ref.shape
    for step in range(group):
        ref = turn_refs[group - 1 - step]
        turns_ref[source_of(member, step, group)] = ref[:size].astype(F32) + ref[
            size : 2 * size
        ].astype(F32)
    own = exit_ref[...]
    keys = own
    product = None
    heads, lanes = iota2((size, size))
    starts_ref[0] = jnp.where(heads == lanes, 1.0, 0.0)
    for index in range(group):
        seen_ref[index] = keys.astype(BF16)
        turn = turns_ref[index]
        product = turn if product is None else dot3(product, turn)
        if index:
            keys = jnp.where(index > member, dot3(keys, turn), own)
        if index < group - 1:
            starts_ref[index + 1] = product
    high, low = split(keys)
    leave_ref[:tokens] = high
    leave_ref[tokens : 2 * tokens] = low
    leave_ref[2 * tokens :] = product.astype(BF16)
    for step in range(group):
        near_refs[step][...] = seen_ref[target_of(member, step, group)]


def word_of(slot, segments):
    bits = segments.bit_length()
    per_word = 31 // bits
    return slot // per_word, bits * (slot % per_word), (1 << bits) - 1


def bundle_kernel(group, groups, most, place_ref, mask_ref, after_ref, *refs):
    val_refs, (line_ref, table_ref) = refs[: groups - 1], refs[groups - 1 :]
    place = place_ref[0]
    segments = mask_ref.shape[0]
    for word in range(table_ref.shape[0]):
        table_ref[word] = 0

    def pick(segment, count):
        wanted = (mask_ref[segment] > 0) & (segment < place) & (count < most)
        word, shift, _ = word_of(count, segments)

        @pl.when(wanted)
        def _():
            table_ref[word] = table_ref[word] | ((segment + 1) << shift)

        return count + wanted.astype(jnp.int32)

    lax.fori_loop(0, segments, pick, jnp.int32(0))
    tokens = val_refs[0].shape[0]
    for way in range(1, groups):
        line_ref[(way - 1) * tokens : way * tokens] = val_refs[groups - 1 - way][...]


def query_kernel(rows_ref, weight_hbm, gain_ref, kn_ref, dirs_ref, coeff_ref, solved_ref, val_ref,
                 moved_ref, weighted_ref, peak_ref, total_ref, weight_ref, sems):
    tokens, size = kn_ref.shape
    heads = moved_ref.shape[0]
    across = jnp.concatenate([kn_ref[...], dirs_ref[...]], axis=0)
    into = jnp.concatenate([coeff_ref[...], solved_ref[...]], axis=1)
    turns, _, wide = weight_ref.shape
    count = heads // turns
    copies = [
        pltpu.make_async_copy(
            weight_hbm.at[:, turn * wide : (turn + 1) * wide], weight_ref.at[turn], sems.at[turn]
        )
        for turn in range(turns)
    ]
    copies[0].start()
    for turn in range(turns):
        copies[turn].wait()
        if turn + 1 < turns:
            copies[turn + 1].start()
        raw = jnp.dot(rows_ref[...], weight_ref[turn], preferred_element_type=F32)
        parts = [raw[:, at : at + size] for at in range(0, count * size, size)]
        raw = jnp.concatenate(parts, axis=0)
        queries = (
            raw * lax.rsqrt(jnp.mean(raw * raw, axis=-1, keepdims=True) + EPSILON) * gain_ref[...]
        )
        seen = dot3(queries, across, 1, 1)
        rows, cols = iota2((count * tokens, tokens))
        up_to = rows % tokens >= cols
        reach = jnp.where(up_to, seen[:, tokens:], 0.0)
        taken = dot3(reach, into)
        scores = (seen[:, :tokens] - taken[:, :tokens]) * (LOG2E / math.sqrt(size))
        scores = jnp.where(up_to, scores, NEGATIVE)
        moved = (queries - taken[:, tokens:]).astype(BF16)
        peak = jnp.max(scores, axis=1, keepdims=True)
        weights = jnp.exp2(scores - peak)
        total = jnp.sum(weights, axis=1, keepdims=True)
        weighted = jnp.dot(weights.astype(BF16), val_ref[...], preferred_element_type=F32)
        for h in range(count):
            part = slice(h * tokens, (h + 1) * tokens)
            head = turn * count + h
            moved_ref[head] = moved[part]
            weighted_ref[head] = weighted[part]
            peak_ref[head] = peak[part]
            total_ref[head] = total[part]


def arrive_kernel(groups, group, tokens, place_ref, *refs):
    arrived, (brought_ref, keys_ref, whole_ref) = refs[:groups], refs[groups:]
    mine = place_ref[0] // group
    for step in range(groups):
        index = source_of(mine, step, groups)
        ref = arrived[groups - 1 - step]
        keys_ref[index] = ref[:tokens].astype(F32) + ref[tokens : 2 * tokens].astype(F32)
        whole_ref[index] = ref[2 * tokens :].astype(F32)
    brought = [keys_ref[groups - 2]]
    product = None
    for index in range(groups - 3, -1, -1):
        keys, whole = keys_ref[index], whole_ref[index + 1]
        if product is not None:
            whole = jnp.where(index + 2 < mine, dot3(whole, product), whole)
        product = whole
        brought.append(jnp.where(index + 1 < mine, dot3(keys, product), keys))
    brought_ref[...] = jnp.concatenate(brought[::-1], axis=0)


def spread_kernel(group, place_ref, *refs):
    brought_ref, starts_ref, near_refs = refs[0], refs[1], refs[2 : 2 + group]
    far_refs = refs[-group:]
    member = place_ref[0] % group
    keys = brought_ref[...]
    brought = keys.shape[0]
    for step in range(group):
        start = starts_ref[target_of(member, step, group)]
        far_refs[step][:brought] = dot3(keys, start).astype(BF16)
        far_refs[step][brought:] = near_refs[step][...]


def attend_kernel(group, segments, most, place_ref, core_ref, table_ref, *refs):
    far_refs, line_refs = refs[:group][::-1], refs[group : 2 * group][::-1]
    turn_refs = refs[2 * group : 3 * group][::-1]
    (moved_ref, weighted_ref, peak_ref, total_ref, out_ref, away_ref, kept_ref, keys_ref, vals_ref,
     attended_ref) = refs[3 * group :]
    core = core_ref[0]
    mine, member = place_ref[0] // group, place_ref[0] % group
    heads, tokens, size = moved_ref.shape
    groups = far_refs[0].shape[0] // tokens
    scaling = LOG2E / math.sqrt(size)
    chunk = keys_ref.shape[0] // tokens
    lanes = lax.broadcasted_iota(jnp.int32, (1, chunk * tokens), 1)

    def collect(turn):
        found = jnp.int32(0)
        for slot in range(chunk):
            part = slice(slot * tokens, (slot + 1) * tokens)
            word, shift, ones = word_of(turn * chunk + slot, segments)
            code = (table_ref[word] >> shift) & ones
            found = found + (code > 0).astype(jnp.int32)
            segment = jnp.maximum(code - 1, 0)
            whose, source = segment % group, segment // group
            before = jnp.where(source < mine, source, groups - 1)
            before = pl.multiple_of(before * tokens, tokens)
            after = jnp.maximum(step_between(mine, source, groups) - 1, 0)
            after = pl.multiple_of(after * tokens, tokens)
            for number in range(group):

                @pl.when(whose == source_of(member, number, group))
                def _():
                    vals_ref[part, :] = jnp.where(
                        source < mine,
                        line_refs[number][pl.ds(after, tokens), :],
                        turn_refs[number][2 * size :],
                    )
                    keys_ref[part, :] = far_refs[number][pl.ds(before, tokens), :]

        return jnp.where(lanes < found * tokens, 0.0, NEGATIVE)

    def advance(moved, bias, peak, total, weighted):
        scores = lax.dot_general(
            moved, keys_ref[...], (((1,), (1,)), ((), ())), preferred_element_type=F32
        )
        scores = scores * scaling + bias
        new_peak = jnp.maximum(peak, jnp.max(scores, axis=1, keepdims=True))
        fading = jnp.exp2(peak - new_peak)
        weights = jnp.exp2(scores - new_peak)
        total = total * fading + jnp.sum(weights, axis=1, keepdims=True)
        weighted = weighted * fading + jnp.dot(
            weights.astype(BF16), vals_ref[...], preferred_element_type=F32
        )
        return new_peak, total, weighted

    half = kept_ref.shape[0]
    turns = most // chunk
    if turns == 1:
        bias = collect(0)
    for head in range(heads):
        state = (peak_ref[head], total_ref[head], weighted_ref[head])
        if turns == 1:
            _, total, weighted = advance(moved_ref[head], bias, *state)
        else:

            def step_of(turn, state, head=head):
                return advance(moved_ref[head], collect(turn), *state)

            _, total, weighted = lax.fori_loop(0, turns, step_of, state)
        done = (weighted * (1.0 / total)).astype(BF16)
        for index in range(tokens // half):
            at = pl.multiple_of(jnp.where(index == core, half, 0), half)
            attended_ref[pl.ds(at, half), head * size : (head + 1) * size] = done[
                index * half : (index + 1) * half
            ]
    wide = math.gcd(out_ref.shape[1], 4 * size)
    for at in range(0, out_ref.shape[1], wide):
        part = slice(at, at + wide)
        result = jnp.dot(attended_ref[...], out_ref[:, part], preferred_element_type=F32)
        result = result.astype(BF16)
        away_ref[:, part] = result[:half]
        kept_ref[:, part] = result[half:]


def body(
    hidden, w_query, w_key, w_value, w_dir, u_rate, rate_bias, q_gain, k_gain, w_out, block_mask
):
    segments = lax.axis_size("ctx")
    place = lax.axis_index("ctx").astype(jnp.int32).reshape(1)
    core = lax.axis_index("head").astype(jnp.int32).reshape(1)
    group = max(d for d in range(1, math.isqrt(segments) + 1) if segments % d == 0)
    groups = segments // group
    other = lax.ppermute(hidden, "head", [(0, 1), (1, 0)])
    half, width = hidden.shape
    tokens = half * lax.axis_size("head")
    size = w_key.shape[1]
    heads = w_query.shape[1] // size
    smem = pl.BlockSpec(memory_space=pltpu.SMEM)
    vmem = pl.BlockSpec(memory_space=pltpu.VMEM)
    hbm = pl.BlockSpec(memory_space=pltpu.HBM)
    anywhere = pl.BlockSpec(memory_space=pl.ANY)
    square = shaped((tokens, size), F32)

    def swapped(values, count, pairs_of):
        out = [values[0]] * count
        for step in range(count - 1, 0, -1):
            out[step] = lax.ppermute(values[step], "ctx", pairs_of(step))
        return out

    def within_group(values):
        return swapped(values, group, lambda step: [
            (s, s - s % group + target_of(s % group, step, group)) for s in range(segments)
        ])

    def along_line(values):
        return swapped(values, groups, lambda step: [
            (s, s % group + group * target_of(s // group, step, groups)) for s in range(segments)
        ])

    weights, rate_row, key_gain, query_gain, mine = call(
        functools.partial(load_kernel, size),
        (
            shaped((width, 3 * size), BF16), shaped((1, width), BF16), shaped((1, size), F32),
            shaped((1, size), F32), shaped((half, width), BF16),
        ),
        tuple(
            in_hbm(array)
            for array in (
                w_key, w_dir, w_value, u_rate, k_gain.reshape(1, size), q_gain.reshape(1, size),
                hidden,
            )
        ),
        in_specs=[hbm] * 7,
        scratch=(pltpu.SemaphoreType.DMA((7,)),),
        moved=12 * width * size,
    )
    rows, kn, val, dirs, coeff, solved, exit_keys, turn = call(
        prepare_kernel,
        (
            shaped((tokens, width), BF16), square, shaped((tokens, size), BF16), square, square,
            square, square, shaped((2 * size + tokens, size), BF16),
        ),
        (core, mine, other, weights, rate_row, rate_bias, key_gain),
        in_specs=[smem] + [vmem] * 4 + [smem, vmem],
        flops=6 * tokens * width * size,
        moved=8 * width * size,
    )
    turns = within_group([turn] * group)
    line = along_line([val] * groups)
    leaving, starts, *near = call(
        functools.partial(leave_kernel, group),
        [
            shaped((2 * tokens + size, size), BF16),
            shaped((group, size, size), F32),
        ]
        + [shaped((tokens, size), BF16)] * group,
        (place, exit_keys, *turns[::-1]),
        in_specs=[smem] + [vmem] * (1 + group),
        scratch=(
            pltpu.VMEM((group, size, size), F32),
            pltpu.VMEM((group, tokens, size), BF16),
        ),
        flops=12 * group * size**3,
        moved=10**6,
    )
    arrived = along_line([leaving] * groups)
    most = segments // 4
    values, table = call(
        functools.partial(bundle_kernel, group, groups, most),
        [
            shaped(((groups - 1) * tokens, size), BF16),
            shaped((word_of(most - 1, segments)[0] + 1,), jnp.int32),
        ],
        (place, block_mask[0], starts, *line[:0:-1]),
        in_specs=[smem, smem, anywhere] + [vmem] * (groups - 1),
        out_specs=[vmem, smem],
        moved=10**6,
        limit=8 + group * groups // 4,
    )
    values = within_group([values] * group)
    turns_of = heads // math.gcd(heads, 4)
    own = call(
        query_kernel,
        (
            shaped((heads, tokens, size), BF16),
            shaped((heads, tokens, size), F32),
            shaped((heads, tokens, 1), F32),
            shaped((heads, tokens, 1), F32),
        ),
        (rows, in_hbm(w_query), query_gain, kn, dirs, coeff, solved, val),
        in_specs=[vmem, hbm] + [vmem] * 6,
        scratch=(
            pltpu.VMEM((turns_of, width, w_query.shape[1] // turns_of), BF16),
            pltpu.SemaphoreType.DMA((turns_of,)),
        ),
        flops=4 * tokens * width * heads * size,
        moved=8 * width * heads * size,
        limit=14,
    )
    most = segments // 4
    values, table = call(
        functools.partial(bundle_kernel, group, groups, most),
        [
            shaped(((groups - 1) * tokens, size), BF16),
            shaped((word_of(most - 1, segments)[0] + 1,), jnp.int32),
        ],
        (place, block_mask[0], starts, *line[:0:-1]),
        in_specs=[smem, smem, anywhere] + [vmem] * (groups - 1),
        out_specs=[vmem, smem],
        moved=10**6,
        limit=8 + group * groups // 4,
    )
    values = within_group([values] * group)
    (brought,) = call(
        functools.partial(arrive_kernel, groups, group, tokens),
        [shaped(((groups - 1) * tokens, size), F32)],
        (place, *arrived[::-1]),
        in_specs=[smem] + [vmem] * groups,
        scratch=(
            pltpu.VMEM((groups, tokens, size), F32),
            pltpu.VMEM((groups, size, size), F32),
        ),
        flops=6 * groups * size**3,
        moved=10**6,
        limit=8 + group * groups // 4,
    )
    far = call(
        functools.partial(spread_kernel, group),
        [shaped((groups * tokens, size), BF16)] * group,
        (place, brought, starts, *near, *values[1:]),
        in_specs=[smem] + [vmem] * (2 + group) + [anywhere] * (group - 1),
        flops=6 * groups * group * size**3,
        moved=10**6,
        limit=8 + group * groups // 4,
    )
    far = within_group(far)
    chunk = math.gcd(most, 4)
    width_out = w_out.shape[1]
    scratch = [
        pltpu.VMEM((chunk * tokens, size), BF16),
        pltpu.VMEM((chunk * tokens, size), BF16),
        pltpu.VMEM((tokens, heads * size), BF16),
    ]
    away, kept = call(
        functools.partial(attend_kernel, group, segments, most),
        [shaped((half, width_out), BF16)] * 2,
        (place, core, table, *far[::-1], *values[::-1], *turns[::-1], *own, w_out),
        in_specs=[smem] * 3 + [vmem] * (3 * group + 5),
        scratch=scratch,
        flops=2 * tokens * width_out * heads * size,
        moved=4 * 10**6,
        limit=14 + group * groups // 4,
    )
    return kept + lax.ppermute(away, "head", [(0, 1), (1, 0)])


def solution(mesh):
    in_specs = (
        P(("ctx", "head"), None),
        P(None, "head"),
        P(None, "head"),
        P(None, "head"),
        P(None, "head"),
        P("head", None),
        P("head"),
        P(),
        P(),
        P("head", None),
        P("ctx", None),
    )
    out_specs = P(("ctx", "head"), None)
    return jax.shard_map(body, mesh=mesh, in_specs=in_specs, out_specs=out_specs, check_vma=False)
```

```python
import functools
import math

import jax
import jax.numpy as jnp
from jax import lax
from jax.experimental import pallas as pl
from jax.experimental.pallas import tpu as pltpu
from jax.sharding import PartitionSpec as P

EPSILON = 1e-06
NEGATIVE = -1e30
LOG2E = math.log2(math.e)
F32 = jnp.float32
BF16 = jnp.bfloat16
MIB = 1024 * 1024


def call(kernel, out_shape, args, in_specs=None, out_specs=None, scratch=(), flops=0, moved=0, limit=6):
    vmem = pl.BlockSpec(memory_space=pltpu.VMEM)
    return pl.pallas_call(
        kernel,
        out_shape=out_shape,
        in_specs=in_specs or [vmem] * len(args),
        out_specs=out_specs or jax.tree.map(lambda _: vmem, out_shape),
        scratch_shapes=list(scratch),
        compiler_params=pltpu.CompilerParams(vmem_limit_bytes=limit * MIB),
        cost_estimate=pl.CostEstimate(flops=flops, bytes_accessed=moved, transcendentals=0),
    )(*args)


def target_of(member, step, group):
    return member ^ step if group & (group - 1) == 0 else (member + step) % group


def source_of(member, step, group):
    return member ^ step if group & (group - 1) == 0 else (member + group - step) % group


def in_hbm(array):
    return pltpu.with_memory_space_constraint(array, pltpu.HBM)


def shaped(shape, dtype):
    return jax.ShapeDtypeStruct(shape, dtype)


def split(value):
    high = value.astype(BF16)
    return high, (value - high.astype(F32)).astype(BF16)


def dot3(left, right, left_dim=1, right_dim=0):
    left_high, left_low = split(left)
    right_high, right_low = split(right)
    return lax.dot_general(
        jnp.concatenate([left_high, left_high, left_low], axis=left_dim),
        jnp.concatenate([right_high, right_low, right_high], axis=right_dim),
        (((left_dim,), (right_dim,)), ((), ())),
        preferred_element_type=F32,
    )


def iota2(shape):
    return lax.broadcasted_iota(jnp.int32, shape, 0), lax.broadcasted_iota(jnp.int32, shape, 1)


def merge_inverse(lower, rows, cols):
    tokens = lower.shape[0]
    block = 8
    inverse = jnp.where(rows == cols, 1.0, 0.0).astype(F32)
    first = rows - rows % block
    for step in range(block - 1):
        column = jnp.sum(jnp.where(cols == first + step, lower, 0.0), axis=1, keepdims=True)
        pivot = inverse.reshape(tokens // block, block, tokens)[:, step : step + 1, :]
        pivot = jnp.broadcast_to(pivot, (tokens // block, block, tokens)).reshape(tokens, tokens)
        inverse = inverse - column * pivot
    while block < tokens:
        corner = (
            (rows // (2 * block) == cols // (2 * block))
            & (rows % (2 * block) >= block)
            & (cols % (2 * block) < block)
        )
        inverse = inverse - dot3(dot3(inverse, jnp.where(corner, lower, 0.0)), inverse)
        block *= 2
    return inverse


def load_kernel(size, key_hbm, dir_hbm, value_hbm, rate_hbm, key_gain_hbm,
                query_gain_hbm, mine_hbm, weight_ref, rate_ref, key_gain_ref, query_gain_ref,
                mine_ref, sems):
    pairs = [
        (hbm, weight_ref.at[:, index * size : (index + 1) * size])
        for index, hbm in enumerate((key_hbm, dir_hbm, value_hbm))
    ]
    pairs += [(rate_hbm, rate_ref), (key_gain_hbm, key_gain_ref)]
    pairs += [(query_gain_hbm, query_gain_ref), (mine_hbm, mine_ref)]
    copies = [pltpu.make_async_copy(*pair, sems.at[n]) for n, pair in enumerate(pairs)]
    for copy in copies:
        copy.start()
    for copy in copies:
        copy.wait()


def prepare_kernel(core_ref, mine_ref, other_ref, weight_ref, rate_ref, bias_ref, gain_ref,
                   rows_ref, kn_ref, val_ref, dirs_ref, coeff_ref, solved_ref, exit_ref, turn_ref):
    core = core_ref[0]
    half = mine_ref.shape[0]
    rows_ref[pl.ds(pl.multiple_of(core * half, half), half), :] = mine_ref[...]
    rows_ref[pl.ds(pl.multiple_of((1 - core) * half, half), half), :] = other_ref[...]
    seg = rows_ref[...]
    size = turn_ref.shape[0]
    raw = jnp.dot(seg, weight_ref[...], preferred_element_type=F32)
    keys, raw, vals = raw[:, :size], raw[:, size : 2 * size], raw[:, 2 * size :]
    kn = keys * lax.rsqrt(jnp.mean(keys * keys, axis=-1, keepdims=True) + EPSILON) * gain_ref[...]
    dirs = raw * lax.rsqrt(jnp.sum(raw * raw, axis=-1, keepdims=True) + EPSILON)
    vector = jnp.broadcast_to(rate_ref[...], (16, seg.shape[1]))
    logits = lax.dot_general(seg, vector, (((1,), (1,)), ((), ())), preferred_element_type=F32)
    rates = 2.0 * jax.nn.sigmoid(logits[:, :1] + bias_ref[0])
    val_ref[...] = vals.astype(BF16)
    kn_ref[...] = kn
    dirs_ref[...] = dirs
    tokens, size = dirs.shape
    rows, cols = iota2((tokens, tokens))
    below = rows > cols
    grams = dot3(dirs, jnp.concatenate([dirs, kn], axis=0), 1, 1)
    lower = jnp.where(below, rates * grams[:, :tokens], 0.0)
    crossing = jnp.where(below, rates * grams[:, tokens:], 0.0)
    inverse = merge_inverse(lower, rows, cols)
    both = dot3(inverse, jnp.concatenate([crossing, rates * dirs], axis=1))
    coeff_ref[...] = both[:, :tokens]
    solved_ref[...] = both[:, tokens:]
    crossed = dot3(both, dirs, 0, 0)
    exit_ref[...] = kn - crossed[:tokens]
    heads, lanes = iota2((size, size))
    turn_ref[...] = jnp.where(heads == lanes, 1.0, 0.0) - crossed[tokens:]


def leave_kernel(group, place_ref, exit_ref, *refs):
    turn_refs, (leave_ref, starts_ref) = refs[:group], refs[group : group + 2]
    near_refs, (turns_ref, seen_ref) = refs[group + 2 : -2], refs[-2:]
    member = place_ref[0] % group
    tokens, size = exit_ref.shape
    for step in range(group):
        turns_ref[source_of(member, step, group)] = turn_refs[group - 1 - step][...]
    own = exit_ref[...]
    keys = own
    product = None
    heads, lanes = iota2((size, size))
    starts_ref[0] = jnp.where(heads == lanes, 1.0, 0.0)
    for index in range(group):
        seen_ref[index] = keys.astype(BF16)
        turn = turns_ref[index]
        product = turn if product is None else dot3(product, turn)
        if index:
            keys = jnp.where(index > member, dot3(keys, turn), own)
        if index < group - 1:
            starts_ref[index + 1] = product
    high, low = split(keys)
    leave_ref[:tokens] = high
    leave_ref[tokens : 2 * tokens] = low
    high, low = split(product)
    leave_ref[2 * tokens : 2 * tokens + size] = high
    leave_ref[2 * tokens + size :] = low
    for step in range(group):
        near_refs[step][...] = seen_ref[target_of(member, step, group)]


def word_of(slot, segments):
    bits = segments.bit_length()
    per_word = 31 // bits
    return slot // per_word, bits * (slot % per_word), (1 << bits) - 1


def bundle_kernel(group, groups, most, place_ref, mask_ref, after_ref, *refs):
    val_refs, (line_ref, table_ref) = refs[:groups], refs[groups:]
    place = place_ref[0]
    mine = place // group
    segments = mask_ref.shape[0]
    for word in range(table_ref.shape[0]):
        table_ref[word] = 0

    def pick(segment, count):
        wanted = (mask_ref[segment] > 0) & (segment < place) & (count < most)
        word, shift, _ = word_of(count, segments)

        @pl.when(wanted)
        def _():
            table_ref[word] = table_ref[word] | ((segment + 1) << shift)

        return count + wanted.astype(jnp.int32)

    lax.fori_loop(0, segments, pick, jnp.int32(0))
    tokens = val_refs[0].shape[0]
    for way in range(groups):
        at = pl.multiple_of(source_of(mine, way, groups) * tokens, tokens)
        line_ref[pl.ds(at, tokens), :] = val_refs[groups - 1 - way][...]


def query_kernel(rows_ref, weight_hbm, gain_ref, kn_ref, dirs_ref, coeff_ref, solved_ref, val_ref,
                 moved_ref, weighted_ref, peak_ref, total_ref, weight_ref, raw_ref, sems):
    tokens, size = kn_ref.shape
    heads = moved_ref.shape[0]
    pieces, deep, _ = weight_ref.shape
    copies = [
        pltpu.make_async_copy(
            weight_hbm.at[n * deep : (n + 1) * deep, :], weight_ref.at[n], sems.at[n]
        )
        for n in range(pieces)
    ]
    for copy in copies:
        copy.start()
    across = jnp.concatenate([kn_ref[...], dirs_ref[...]], axis=0)
    into = jnp.concatenate([coeff_ref[...], solved_ref[...]], axis=1)
    for n in range(pieces):
        copies[n].wait()
        part = jnp.dot(
            rows_ref[:, n * deep : (n + 1) * deep], weight_ref[n], preferred_element_type=F32
        )
        raw_ref[...] = raw_ref[...] + part if n else part
    count = math.gcd(heads, 4)
    for turn in range(heads // count):
        raw = jnp.concatenate(
            [
                raw_ref[:, head * size : (head + 1) * size]
                for head in range(turn * count, (turn + 1) * count)
            ],
            axis=0,
        )
        queries = (
            raw * lax.rsqrt(jnp.mean(raw * raw, axis=-1, keepdims=True) + EPSILON) * gain_ref[...]
        )
        seen = dot3(queries, across, 1, 1)
        rows, cols = iota2((count * tokens, tokens))
        up_to = rows % tokens >= cols
        reach = jnp.where(up_to, seen[:, tokens:], 0.0)
        taken = dot3(reach, into)
        scores = (seen[:, :tokens] - taken[:, :tokens]) * (LOG2E / math.sqrt(size))
        scores = jnp.where(up_to, scores, NEGATIVE)
        moved = (queries - taken[:, tokens:]).astype(BF16)
        peak = jnp.max(scores, axis=1, keepdims=True)
        weights = jnp.exp2(scores - peak)
        total = jnp.sum(weights, axis=1, keepdims=True)
        weighted = jnp.dot(weights.astype(BF16), val_ref[...], preferred_element_type=F32)
        for h in range(count):
            part = slice(h * tokens, (h + 1) * tokens)
            head = turn * count + h
            moved_ref[head] = moved[part]
            weighted_ref[head] = weighted[part]
            peak_ref[head] = peak[part]
            total_ref[head] = total[part]


def arrive_kernel(groups, group, tokens, place_ref, *refs):
    arrived, starts_ref, near_refs = refs[:groups], refs[groups], refs[groups + 1 :]
    far_refs, (keys_ref, whole_ref) = refs[-group - 2 : -2], refs[-2:]
    mine, member = place_ref[0] // group, place_ref[0] % group
    size = starts_ref.shape[1]
    for step in range(groups):
        index = source_of(mine, step, groups)
        ref = arrived[groups - 1 - step]
        keys_ref[index] = ref[:tokens].astype(F32) + ref[tokens : 2 * tokens].astype(F32)
        whole = ref[2 * tokens : 2 * tokens + size].astype(F32)
        whole_ref[index] = whole + ref[2 * tokens + size :].astype(F32)
    brought = [keys_ref[groups - 2]]
    product = None
    for index in range(groups - 3, -1, -1):
        keys, whole = keys_ref[index], whole_ref[index + 1]
        if product is not None:
            whole = jnp.where(index + 2 < mine, dot3(whole, product), whole)
        product = whole
        brought.append(jnp.where(index + 1 < mine, dot3(keys, product), keys))
    keys = jnp.concatenate(brought[::-1], axis=0)
    for step in range(group):
        start = starts_ref[target_of(member, step, group)]
        far_refs[step][: (groups - 1) * tokens] = dot3(keys, start).astype(BF16)
        far_refs[step][(groups - 1) * tokens :] = near_refs[step][...]


def attend_kernel(group, segments, most, place_ref, core_ref, table_ref, *refs):
    far_refs, line_refs = refs[:group][::-1], refs[group : 2 * group][::-1]
    (moved_ref, weighted_ref, peak_ref, total_ref, out_ref, away_ref, kept_ref, keys_ref, vals_ref,
     attended_ref) = refs[2 * group :]
    core = core_ref[0]
    mine, member = place_ref[0] // group, place_ref[0] % group
    heads, tokens, size = moved_ref.shape
    groups = far_refs[0].shape[0] // tokens
    scaling = LOG2E / math.sqrt(size)
    chunk = keys_ref.shape[0] // tokens
    lanes = lax.broadcasted_iota(jnp.int32, (1, chunk * tokens), 1)

    def collect(turn):
        found = jnp.int32(0)
        for slot in range(chunk):
            part = slice(slot * tokens, (slot + 1) * tokens)
            word, shift, ones = word_of(turn * chunk + slot, segments)
            code = (table_ref[word] >> shift) & ones
            found = found + (code > 0).astype(jnp.int32)
            segment = jnp.maximum(code - 1, 0)
            whose, source = segment % group, segment // group
            before = jnp.where(source < mine, source, groups - 1)
            before = pl.multiple_of(before * tokens, tokens)
            after = pl.multiple_of(source * tokens, tokens)
            for number in range(group):

                @pl.when(whose == source_of(member, number, group))
                def _():
                    vals_ref[part, :] = line_refs[number][pl.ds(after, tokens), :]
                    keys_ref[part, :] = far_refs[number][pl.ds(before, tokens), :]

        return jnp.where(lanes < found * tokens, 0.0, NEGATIVE)

    def advance(moved, bias, peak, total, weighted):
        scores = lax.dot_general(
            moved, keys_ref[...], (((1,), (1,)), ((), ())), preferred_element_type=F32
        )
        scores = scores * scaling + bias
        new_peak = jnp.maximum(peak, jnp.max(scores, axis=1, keepdims=True))
        fading = jnp.exp2(peak - new_peak)
        weights = jnp.exp2(scores - new_peak)
        total = total * fading + jnp.sum(weights, axis=1, keepdims=True)
        weighted = weighted * fading + jnp.dot(
            weights.astype(BF16), vals_ref[...], preferred_element_type=F32
        )
        return new_peak, total, weighted

    half = kept_ref.shape[0]
    turns = most // chunk
    if turns == 1:
        bias = collect(0)
    for head in range(heads):
        state = (peak_ref[head], total_ref[head], weighted_ref[head])
        if turns == 1:
            _, total, weighted = advance(moved_ref[head], bias, *state)
        else:

            def step_of(turn, state, head=head):
                return advance(moved_ref[head], collect(turn), *state)

            _, total, weighted = lax.fori_loop(0, turns, step_of, state)
        done = (weighted * (1.0 / total)).astype(BF16)
        for index in range(tokens // half):
            at = pl.multiple_of(jnp.where(index == core, half, 0), half)
            attended_ref[pl.ds(at, half), head * size : (head + 1) * size] = done[
                index * half : (index + 1) * half
            ]
    wide = math.gcd(out_ref.shape[1], 4 * size)
    for at in range(0, out_ref.shape[1], wide):
        part = slice(at, at + wide)
        result = jnp.dot(attended_ref[...], out_ref[:, part], preferred_element_type=F32)
        result = result.astype(BF16)
        away_ref[:, part] = result[:half]
        kept_ref[:, part] = result[half:]


def body(
    hidden, w_query, w_key, w_value, w_dir, u_rate, rate_bias, q_gain, k_gain, w_out, block_mask
):
    segments = lax.axis_size("ctx")
    place = lax.axis_index("ctx").astype(jnp.int32).reshape(1)
    core = lax.axis_index("head").astype(jnp.int32).reshape(1)
    group = max(d for d in range(1, math.isqrt(segments) + 1) if segments % d == 0)
    groups = segments // group
    other = lax.ppermute(hidden, "head", [(0, 1), (1, 0)])
    half, width = hidden.shape
    tokens = half * lax.axis_size("head")
    size = w_key.shape[1]
    heads = w_query.shape[1] // size
    smem = pl.BlockSpec(memory_space=pltpu.SMEM)
    vmem = pl.BlockSpec(memory_space=pltpu.VMEM)
    hbm = pl.BlockSpec(memory_space=pltpu.HBM)
    anywhere = pl.BlockSpec(memory_space=pl.ANY)
    square = shaped((tokens, size), F32)

    def swapped(values, count, pairs_of):
        out = [values[0]] * count
        for step in range(count - 1, 0, -1):
            out[step] = lax.ppermute(values[step], "ctx", pairs_of(step))
        return out

    def within_group(values):
        return swapped(values, group, lambda step: [
            (s, s - s % group + target_of(s % group, step, group)) for s in range(segments)
        ])

    def along_line(values):
        return swapped(values, groups, lambda step: [
            (s, s % group + group * target_of(s // group, step, groups)) for s in range(segments)
        ])

    weights, rate_row, key_gain, query_gain, mine = call(
        functools.partial(load_kernel, size),
        (
            shaped((width, 3 * size), BF16), shaped((1, width), BF16), shaped((1, size), F32),
            shaped((1, size), F32), shaped((half, width), BF16),
        ),
        tuple(
            in_hbm(array)
            for array in (
                w_key, w_dir, w_value, u_rate, k_gain.reshape(1, size), q_gain.reshape(1, size),
                hidden,
            )
        ),
        in_specs=[hbm] * 7,
        scratch=(pltpu.SemaphoreType.DMA((7,)),),
        moved=12 * width * size,
    )
    rows, kn, val, dirs, coeff, solved, exit_keys, turn = call(
        prepare_kernel,
        (
            shaped((tokens, width), BF16), square, shaped((tokens, size), BF16), square, square,
            square, square, shaped((size, size), F32),
        ),
        (core, mine, other, weights, rate_row, rate_bias, key_gain),
        in_specs=[smem] + [vmem] * 4 + [smem, vmem],
        flops=6 * tokens * width * size,
        moved=8 * width * size,
    )
    turns = within_group([turn] * group)
    line = along_line([val] * groups)
    leaving, starts, *near = call(
        functools.partial(leave_kernel, group),
        [
            shaped((2 * tokens + 2 * size, size), BF16),
            shaped((group, size, size), F32),
        ]
        + [shaped((tokens, size), BF16)] * group,
        (place, exit_keys, *turns[::-1]),
        in_specs=[smem] + [vmem] * (1 + group),
        scratch=(
            pltpu.VMEM((group, size, size), F32),
            pltpu.VMEM((group, tokens, size), BF16),
        ),
        flops=12 * group * size**3,
        moved=10**6,
    )
    arrived = along_line([leaving] * groups)
    most = segments // 4
    values, table = call(
        functools.partial(bundle_kernel, group, groups, most),
        [
            shaped((groups * tokens, size), BF16),
            shaped((word_of(most - 1, segments)[0] + 1,), jnp.int32),
        ],
        (place, block_mask[0], starts, *line[::-1]),
        in_specs=[smem, smem, anywhere] + [vmem] * groups,
        out_specs=[vmem, smem],
        moved=10**6,
        limit=8 + group * groups // 4,
    )
    values = within_group([values] * group)
    own = call(
        query_kernel,
        (
            shaped((heads, tokens, size), BF16),
            shaped((heads, tokens, size), F32),
            shaped((heads, tokens, 1), F32),
            shaped((heads, tokens, 1), F32),
        ),
        (rows, in_hbm(w_query), query_gain, kn, dirs, coeff, solved, val),
        in_specs=[vmem, hbm] + [vmem] * 6,
        scratch=(
            pltpu.VMEM((2, width // 2, w_query.shape[1]), BF16),
            pltpu.VMEM((tokens, w_query.shape[1]), F32),
            pltpu.SemaphoreType.DMA((2,)),
        ),
        flops=4 * tokens * width * heads * size,
        moved=8 * width * heads * size,
        limit=16,
    )
    far = call(
        functools.partial(arrive_kernel, groups, group, tokens),
        [shaped((groups * tokens, size), BF16)] * group,
        (place, *arrived[::-1], starts, *near),
        in_specs=[smem] + [vmem] * (groups + 1 + group),
        scratch=(
            pltpu.VMEM((groups, tokens, size), F32),
            pltpu.VMEM((groups, size, size), F32),
        ),
        flops=6 * groups * group * size**3,
        moved=10**6,
        limit=8 + group * groups // 4,
    )
    far = within_group(far)
    chunk = math.gcd(most, 4)
    width_out = w_out.shape[1]
    away, kept = call(
        functools.partial(attend_kernel, group, segments, most),
        [shaped((half, width_out), BF16)] * 2,
        (place, core, table, *far[::-1], *values[::-1], *own, w_out),
        in_specs=[smem] * 3 + [vmem] * (2 * group + 5),
        scratch=[
            pltpu.VMEM((chunk * tokens, size), BF16),
            pltpu.VMEM((chunk * tokens, size), BF16),
            pltpu.VMEM((tokens, heads * size), BF16),
        ],
        flops=2 * tokens * width_out * heads * size,
        moved=4 * 10**6,
        limit=14 + group * groups // 4,
    )
    return kept + lax.ppermute(away, "head", [(0, 1), (1, 0)])


def solution(mesh):
    in_specs = (
        P(("ctx", "head"), None),
        P(None, "head"),
        P(None, "head"),
        P(None, "head"),
        P(None, "head"),
        P("head", None),
        P("head"),
        P(),
        P(),
        P("head", None),
        P("ctx", None),
    )
    out_specs = P(("ctx", "head"), None)
    return jax.shard_map(body, mesh=mesh, in_specs=in_specs, out_specs=out_specs, check_vma=False)
```

```python
import functools
import math

import jax
import jax.numpy as jnp
from jax import lax
from jax.experimental import pallas as pl
from jax.experimental.pallas import tpu as pltpu
from jax.sharding import PartitionSpec as P

EPSILON = 1e-06
NEGATIVE = -1e30
LOG2E = math.log2(math.e)
F32 = jnp.float32
BF16 = jnp.bfloat16
MIB = 1024 * 1024


def call(kernel, out_shape, args, in_specs=None, out_specs=None, scratch=(), flops=0, moved=0, limit=6):
    vmem = pl.BlockSpec(memory_space=pltpu.VMEM)
    return pl.pallas_call(
        kernel,
        out_shape=out_shape,
        in_specs=in_specs or [vmem] * len(args),
        out_specs=out_specs or jax.tree.map(lambda _: vmem, out_shape),
        scratch_shapes=list(scratch),
        compiler_params=pltpu.CompilerParams(vmem_limit_bytes=limit * MIB),
        cost_estimate=pl.CostEstimate(flops=flops, bytes_accessed=moved, transcendentals=0),
    )(*args)


def target_of(member, step, group):
    return member ^ step if group & (group - 1) == 0 else (member + step) % group


def source_of(member, step, group):
    return member ^ step if group & (group - 1) == 0 else (member + group - step) % group


def in_hbm(array):
    return pltpu.with_memory_space_constraint(array, pltpu.HBM)


def shaped(shape, dtype):
    return jax.ShapeDtypeStruct(shape, dtype)


def split(value):
    high = value.astype(BF16)
    return high, (value - high.astype(F32)).astype(BF16)


def dot3(left, right, left_dim=1, right_dim=0):
    left_high, left_low = split(left)
    right_high, right_low = split(right)
    return lax.dot_general(
        jnp.concatenate([left_high, left_high, left_low], axis=left_dim),
        jnp.concatenate([right_high, right_low, right_high], axis=right_dim),
        (((left_dim,), (right_dim,)), ((), ())),
        preferred_element_type=F32,
    )


def iota2(shape):
    return lax.broadcasted_iota(jnp.int32, shape, 0), lax.broadcasted_iota(jnp.int32, shape, 1)


def merge_inverse(lower, rows, cols):
    tokens = lower.shape[0]
    block = 8
    inverse = jnp.where(rows == cols, 1.0, 0.0).astype(F32)
    first = rows - rows % block
    for step in range(block - 1):
        column = jnp.sum(jnp.where(cols == first + step, lower, 0.0), axis=1, keepdims=True)
        pivot = inverse.reshape(tokens // block, block, tokens)[:, step : step + 1, :]
        pivot = jnp.broadcast_to(pivot, (tokens // block, block, tokens)).reshape(tokens, tokens)
        inverse = inverse - column * pivot
    while block < tokens:
        corner = (
            (rows // (2 * block) == cols // (2 * block))
            & (rows % (2 * block) >= block)
            & (cols % (2 * block) < block)
        )
        inverse = inverse - dot3(dot3(inverse, jnp.where(corner, lower, 0.0)), inverse)
        block *= 2
    return inverse


def load_kernel(size, key_hbm, dir_hbm, value_hbm, rate_hbm, key_gain_hbm,
                query_gain_hbm, mine_hbm, weight_ref, rate_ref, key_gain_ref, query_gain_ref,
                mine_ref, sems):
    pairs = [
        (hbm, weight_ref.at[:, index * size : (index + 1) * size])
        for index, hbm in enumerate((key_hbm, dir_hbm, value_hbm))
    ]
    pairs += [(rate_hbm, rate_ref), (key_gain_hbm, key_gain_ref)]
    pairs += [(query_gain_hbm, query_gain_ref), (mine_hbm, mine_ref)]
    copies = [pltpu.make_async_copy(*pair, sems.at[n]) for n, pair in enumerate(pairs)]
    for copy in copies:
        copy.start()
    for copy in copies:
        copy.wait()


def prepare_kernel(core_ref, mine_ref, other_ref, weight_ref, rate_ref, bias_ref, gain_ref,
                   rows_ref, kn_ref, val_ref, dirs_ref, coeff_ref, solved_ref, exit_ref, turn_ref):
    core = core_ref[0]
    half = mine_ref.shape[0]
    rows_ref[pl.ds(pl.multiple_of(core * half, half), half), :] = mine_ref[...]
    rows_ref[pl.ds(pl.multiple_of((1 - core) * half, half), half), :] = other_ref[...]
    seg = rows_ref[...]
    size = turn_ref.shape[0]
    raw = jnp.dot(seg, weight_ref[...], preferred_element_type=F32)
    keys, raw, vals = raw[:, :size], raw[:, size : 2 * size], raw[:, 2 * size :]
    kn = keys * lax.rsqrt(jnp.mean(keys * keys, axis=-1, keepdims=True) + EPSILON) * gain_ref[...]
    dirs = raw * lax.rsqrt(jnp.sum(raw * raw, axis=-1, keepdims=True) + EPSILON)
    vector = jnp.broadcast_to(rate_ref[...], (16, seg.shape[1]))
    logits = lax.dot_general(seg, vector, (((1,), (1,)), ((), ())), preferred_element_type=F32)
    rates = 2.0 * jax.nn.sigmoid(logits[:, :1] + bias_ref[0])
    val_ref[...] = vals.astype(BF16)
    kn_ref[...] = kn
    dirs_ref[...] = dirs
    tokens, size = dirs.shape
    rows, cols = iota2((tokens, tokens))
    below = rows > cols
    grams = dot3(dirs, jnp.concatenate([dirs, kn], axis=0), 1, 1)
    lower = jnp.where(below, rates * grams[:, :tokens], 0.0)
    crossing = jnp.where(below, rates * grams[:, tokens:], 0.0)
    inverse = merge_inverse(lower, rows, cols)
    both = dot3(inverse, jnp.concatenate([crossing, rates * dirs], axis=1))
    coeff_ref[...] = both[:, :tokens]
    solved_ref[...] = both[:, tokens:]
    crossed = dot3(both, dirs, 0, 0)
    exit_ref[...] = kn - crossed[:tokens]
    heads, lanes = iota2((size, size))
    turn_ref[...] = jnp.where(heads == lanes, 1.0, 0.0) - crossed[tokens:]


def leave_kernel(group, place_ref, exit_ref, val_ref, *refs):
    turn_refs, (leave_ref, starts_ref) = refs[:group], refs[group : group + 2]
    near_refs, (turns_ref, seen_ref) = refs[group + 2 : -2], refs[-2:]
    member = place_ref[0] % group
    tokens, size = exit_ref.shape
    for step in range(group):
        turns_ref[source_of(member, step, group)] = turn_refs[group - 1 - step][...]
    own = exit_ref[...]
    keys = own
    product = None
    heads, lanes = iota2((size, size))
    starts_ref[0] = jnp.where(heads == lanes, 1.0, 0.0)
    for index in range(group):
        seen_ref[index] = keys.astype(BF16)
        turn = turns_ref[index]
        product = turn if product is None else dot3(product, turn)
        if index:
            keys = jnp.where(index > member, dot3(keys, turn), own)
        if index < group - 1:
            starts_ref[index + 1] = product
    leave_ref[:tokens] = keys.astype(BF16)
    leave_ref[tokens : 2 * tokens] = val_ref[...]
    leave_ref[2 * tokens :] = product.astype(BF16)
    for step in range(group):
        near_refs[step][:tokens] = seen_ref[target_of(member, step, group)]
        near_refs[step][tokens:] = val_ref[...]


def word_of(slot, segments):
    bits = segments.bit_length()
    per_word = 31 // bits
    return slot // per_word, bits * (slot % per_word), (1 << bits) - 1


def pack_table(most, place, mask_ref, table_ref):
    segments = mask_ref.shape[0]
    for word in range(table_ref.shape[0]):
        table_ref[word] = 0

    def pick(segment, count):
        wanted = (mask_ref[segment] > 0) & (segment < place) & (count < most)
        word, shift, _ = word_of(count, segments)

        @pl.when(wanted)
        def _():
            table_ref[word] = table_ref[word] | ((segment + 1) << shift)

        return count + wanted.astype(jnp.int32)

    lax.fori_loop(0, segments, pick, jnp.int32(0))


def query_kernel(most, place_ref, mask_ref, rows_ref, weight_hbm, gain_ref, kn_ref, dirs_ref,
                 coeff_ref, solved_ref, val_ref, moved_ref, weighted_ref, peak_ref, total_ref,
                 table_ref, weight_ref, raw_ref, sems):
    tokens, size = kn_ref.shape
    heads = moved_ref.shape[0]
    pieces, deep, _ = weight_ref.shape
    copies = [
        pltpu.make_async_copy(
            weight_hbm.at[n * deep : (n + 1) * deep, :], weight_ref.at[n], sems.at[n]
        )
        for n in range(pieces)
    ]
    for copy in copies:
        copy.start()
    pack_table(most, place_ref[0], mask_ref, table_ref)
    across = jnp.concatenate([kn_ref[...], dirs_ref[...]], axis=0)
    into = jnp.concatenate([coeff_ref[...], solved_ref[...]], axis=1)
    for n in range(pieces):
        copies[n].wait()
        part = jnp.dot(
            rows_ref[:, n * deep : (n + 1) * deep], weight_ref[n], preferred_element_type=F32
        )
        raw_ref[...] = raw_ref[...] + part if n else part
    count = math.gcd(heads, 4)
    for turn in range(heads // count):
        raw = jnp.concatenate(
            [
                raw_ref[:, head * size : (head + 1) * size]
                for head in range(turn * count, (turn + 1) * count)
            ],
            axis=0,
        )
        queries = (
            raw * lax.rsqrt(jnp.mean(raw * raw, axis=-1, keepdims=True) + EPSILON) * gain_ref[...]
        )
        seen = dot3(queries, across, 1, 1)
        rows, cols = iota2((count * tokens, tokens))
        up_to = rows % tokens >= cols
        reach = jnp.where(up_to, seen[:, tokens:], 0.0)
        taken = dot3(reach, into)
        scores = (seen[:, :tokens] - taken[:, :tokens]) * (LOG2E / math.sqrt(size))
        scores = jnp.where(up_to, scores, NEGATIVE)
        moved = (queries - taken[:, tokens:]).astype(BF16)
        peak = jnp.max(scores, axis=1, keepdims=True)
        weights = jnp.exp2(scores - peak)
        total = jnp.sum(weights, axis=1, keepdims=True)
        weighted = jnp.dot(weights.astype(BF16), val_ref[...], preferred_element_type=F32)
        for h in range(count):
            part = slice(h * tokens, (h + 1) * tokens)
            head = turn * count + h
            moved_ref[head] = moved[part]
            weighted_ref[head] = weighted[part]
            peak_ref[head] = peak[part]
            total_ref[head] = total[part]


def arrive_kernel(groups, group, tokens, place_ref, *refs):
    arrived, starts_ref = refs[:groups], refs[groups]
    far_refs, (keys_ref, vals_ref, whole_ref) = refs[-group - 3 : -3], refs[-3:]
    mine, member = place_ref[0] // group, place_ref[0] % group
    for step in range(groups):
        index = source_of(mine, step, groups)
        ref = arrived[groups - 1 - step]
        keys_ref[index] = ref[:tokens].astype(F32)
        vals_ref[index] = ref[tokens : 2 * tokens]
        whole_ref[index] = ref[2 * tokens :].astype(F32)
    brought = [keys_ref[groups - 2]]
    product = None
    for index in range(groups - 3, -1, -1):
        keys, whole = keys_ref[index], whole_ref[index + 1]
        if product is not None:
            whole = jnp.where(index + 2 < mine, dot3(whole, product), whole)
        product = whole
        brought.append(jnp.where(index + 1 < mine, dot3(keys, product), keys))
    keys = jnp.concatenate(brought[::-1], axis=0)
    count = (groups - 1) * tokens
    for step in range(group):
        start = starts_ref[target_of(member, step, group)]
        far_refs[step][:count] = dot3(keys, start).astype(BF16)
        for index in range(groups - 1):
            at = count + index * tokens
            far_refs[step][at : at + tokens] = vals_ref[index]


def attend_kernel(group, segments, most, place_ref, core_ref, table_ref, *refs):
    far_refs, near_refs = refs[:group][::-1], refs[group : 2 * group][::-1]
    (moved_ref, weighted_ref, peak_ref, total_ref, out_ref, away_ref, kept_ref, keys_ref, vals_ref,
     attended_ref) = refs[2 * group :]
    core = core_ref[0]
    mine, member = place_ref[0] // group, place_ref[0] % group
    heads, tokens, size = moved_ref.shape
    earlier = far_refs[0].shape[0] // (2 * tokens)
    scaling = LOG2E / math.sqrt(size)
    chunk = keys_ref.shape[0] // tokens
    lanes = lax.broadcasted_iota(jnp.int32, (1, chunk * tokens), 1)

    def collect(turn):
        found = jnp.int32(0)
        for slot in range(chunk):
            part = slice(slot * tokens, (slot + 1) * tokens)
            word, shift, ones = word_of(turn * chunk + slot, segments)
            code = (table_ref[word] >> shift) & ones
            found = found + (code > 0).astype(jnp.int32)
            segment = jnp.maximum(code - 1, 0)
            whose, source = segment % group, segment // group
            before = pl.multiple_of(jnp.minimum(source, earlier - 1) * tokens, tokens)
            after = pl.multiple_of(before + earlier * tokens, tokens)
            for number in range(group):

                @pl.when((whose == source_of(member, number, group)) & (source < mine))
                def _():
                    keys_ref[part, :] = far_refs[number][pl.ds(before, tokens), :]
                    vals_ref[part, :] = far_refs[number][pl.ds(after, tokens), :]

                @pl.when((whose == source_of(member, number, group)) & (source >= mine))
                def _():
                    keys_ref[part, :] = near_refs[number][:tokens]
                    vals_ref[part, :] = near_refs[number][tokens:]

        return jnp.where(lanes < found * tokens, 0.0, NEGATIVE)

    def advance(moved, bias, peak, total, weighted):
        scores = lax.dot_general(
            moved, keys_ref[...], (((1,), (1,)), ((), ())), preferred_element_type=F32
        )
        scores = scores * scaling + bias
        new_peak = jnp.maximum(peak, jnp.max(scores, axis=1, keepdims=True))
        fading = jnp.exp2(peak - new_peak)
        weights = jnp.exp2(scores - new_peak)
        total = total * fading + jnp.sum(weights, axis=1, keepdims=True)
        weighted = weighted * fading + jnp.dot(
            weights.astype(BF16), vals_ref[...], preferred_element_type=F32
        )
        return new_peak, total, weighted

    half = kept_ref.shape[0]
    turns = most // chunk
    if turns == 1:
        bias = collect(0)
    for head in range(heads):
        state = (peak_ref[head], total_ref[head], weighted_ref[head])
        if turns == 1:
            _, total, weighted = advance(moved_ref[head], bias, *state)
        else:

            def step_of(turn, state, head=head):
                return advance(moved_ref[head], collect(turn), *state)

            _, total, weighted = lax.fori_loop(0, turns, step_of, state)
        done = (weighted * (1.0 / total)).astype(BF16)
        for index in range(tokens // half):
            at = pl.multiple_of(jnp.where(index == core, half, 0), half)
            attended_ref[pl.ds(at, half), head * size : (head + 1) * size] = done[
                index * half : (index + 1) * half
            ]
    wide = math.gcd(out_ref.shape[1], 4 * size)
    for at in range(0, out_ref.shape[1], wide):
        part = slice(at, at + wide)
        result = jnp.dot(attended_ref[...], out_ref[:, part], preferred_element_type=F32)
        result = result.astype(BF16)
        away_ref[:, part] = result[:half]
        kept_ref[:, part] = result[half:]


def body(
    hidden, w_query, w_key, w_value, w_dir, u_rate, rate_bias, q_gain, k_gain, w_out, block_mask
):
    segments = lax.axis_size("ctx")
    place = lax.axis_index("ctx").astype(jnp.int32).reshape(1)
    core = lax.axis_index("head").astype(jnp.int32).reshape(1)
    group = max(d for d in range(1, math.isqrt(segments) + 1) if segments % d == 0)
    groups = segments // group
    other = lax.ppermute(hidden, "head", [(0, 1), (1, 0)])
    half, width = hidden.shape
    tokens = half * lax.axis_size("head")
    size = w_key.shape[1]
    heads = w_query.shape[1] // size
    smem = pl.BlockSpec(memory_space=pltpu.SMEM)
    vmem = pl.BlockSpec(memory_space=pltpu.VMEM)
    hbm = pl.BlockSpec(memory_space=pltpu.HBM)
    anywhere = pl.BlockSpec(memory_space=pl.ANY)
    square = shaped((tokens, size), F32)

    def swapped(values, count, pairs_of):
        out = [values[0]] * count
        for step in range(count - 1, 0, -1):
            out[step] = lax.ppermute(values[step], "ctx", pairs_of(step))
        return out

    def within_group(values):
        return swapped(values, group, lambda step: [
            (s, s - s % group + target_of(s % group, step, group)) for s in range(segments)
        ])

    def along_line(values):
        return swapped(values, groups, lambda step: [
            (s, s % group + group * target_of(s // group, step, groups)) for s in range(segments)
        ])

    weights, rate_row, key_gain, query_gain, mine = call(
        functools.partial(load_kernel, size),
        (
            shaped((width, 3 * size), BF16), shaped((1, width), BF16), shaped((1, size), F32),
            shaped((1, size), F32), shaped((half, width), BF16),
        ),
        tuple(
            in_hbm(array)
            for array in (
                w_key, w_dir, w_value, u_rate, k_gain.reshape(1, size), q_gain.reshape(1, size),
                hidden,
            )
        ),
        in_specs=[hbm] * 7,
        scratch=(pltpu.SemaphoreType.DMA((7,)),),
        moved=12 * width * size,
    )
    rows, kn, val, dirs, coeff, solved, exit_keys, turn = call(
        prepare_kernel,
        (
            shaped((tokens, width), BF16), square, shaped((tokens, size), BF16), square, square,
            square, square, shaped((size, size), F32),
        ),
        (core, mine, other, weights, rate_row, rate_bias, key_gain),
        in_specs=[smem] + [vmem] * 4 + [smem, vmem],
        flops=6 * tokens * width * size,
        moved=8 * width * size,
    )
    turns = within_group([turn] * group)
    leaving, starts, *near = call(
        functools.partial(leave_kernel, group),
        [
            shaped((2 * tokens + size, size), BF16),
            shaped((group, size, size), F32),
        ]
        + [shaped((2 * tokens, size), BF16)] * group,
        (place, exit_keys, val, *turns[::-1]),
        in_specs=[smem] + [vmem] * (2 + group),
        scratch=(
            pltpu.VMEM((group, size, size), F32),
            pltpu.VMEM((group, tokens, size), BF16),
        ),
        flops=12 * group * size**3,
        moved=10**6,
    )
    arrived = along_line([leaving] * groups)
    near = within_group(near)
    most = segments // 4
    *own, table = call(
        functools.partial(query_kernel, most),
        (
            shaped((heads, tokens, size), BF16),
            shaped((heads, tokens, size), F32),
            shaped((heads, tokens, 1), F32),
            shaped((heads, tokens, 1), F32),
            shaped((word_of(most - 1, segments)[0] + 1,), jnp.int32),
        ),
        (
            place, block_mask[0], rows, in_hbm(w_query), query_gain, kn, dirs, coeff, solved, val,
        ),
        in_specs=[smem, smem, vmem, hbm] + [vmem] * 6,
        out_specs=(vmem, vmem, vmem, vmem, smem),
        scratch=(
            pltpu.VMEM((2, width // 2, w_query.shape[1]), BF16),
            pltpu.VMEM((tokens, w_query.shape[1]), F32),
            pltpu.SemaphoreType.DMA((2,)),
        ),
        flops=4 * tokens * width * heads * size,
        moved=8 * width * heads * size,
        limit=16,
    )
    far = call(
        functools.partial(arrive_kernel, groups, group, tokens),
        [shaped((2 * (groups - 1) * tokens, size), BF16)] * group,
        (place, *arrived[::-1], starts, *near[1:]),
        in_specs=[smem] + [vmem] * (groups + 1) + [anywhere] * (group - 1),
        scratch=(
            pltpu.VMEM((groups, tokens, size), F32),
            pltpu.VMEM((groups, tokens, size), BF16),
            pltpu.VMEM((groups, size, size), F32),
        ),
        flops=6 * groups * group * size**3,
        moved=10**6,
        limit=8 + group * groups // 4,
    )
    far = within_group(far)
    chunk = math.gcd(most, 4)
    width_out = w_out.shape[1]
    away, kept = call(
        functools.partial(attend_kernel, group, segments, most),
        [shaped((half, width_out), BF16)] * 2,
        (place, core, table, *far[::-1], *near[::-1], *own, w_out),
        in_specs=[smem] * 3 + [vmem] * (2 * group + 5),
        scratch=[
            pltpu.VMEM((chunk * tokens, size), BF16),
            pltpu.VMEM((chunk * tokens, size), BF16),
            pltpu.VMEM((tokens, heads * size), BF16),
        ],
        flops=2 * tokens * width_out * heads * size,
        moved=4 * 10**6,
        limit=14 + group * groups // 4,
    )
    return kept + lax.ppermute(away, "head", [(0, 1), (1, 0)])


def solution(mesh):
    in_specs = (
        P(("ctx", "head"), None),
        P(None, "head"),
        P(None, "head"),
        P(None, "head"),
        P(None, "head"),
        P("head", None),
        P("head"),
        P(),
        P(),
        P("head", None),
        P("ctx", None),
    )
    out_specs = P(("ctx", "head"), None)
    return jax.shard_map(body, mesh=mesh, in_specs=in_specs, out_specs=out_specs, check_vma=False)
```

```python
import functools
import math

import jax
import jax.numpy as jnp
from jax import lax
from jax.experimental import pallas as pl
from jax.experimental.pallas import tpu as pltpu
from jax.sharding import PartitionSpec as P

EPSILON = 1e-06
NEGATIVE = -1e30
LOG2E = math.log2(math.e)
F32 = jnp.float32
BF16 = jnp.bfloat16
MIB = 1024 * 1024


def call(kernel, out_shape, args, in_specs=None, out_specs=None, scratch=(), flops=0, moved=0, limit=6):
    vmem = pl.BlockSpec(memory_space=pltpu.VMEM)
    return pl.pallas_call(
        kernel,
        out_shape=out_shape,
        in_specs=in_specs or [vmem] * len(args),
        out_specs=out_specs or jax.tree.map(lambda _: vmem, out_shape),
        scratch_shapes=list(scratch),
        compiler_params=pltpu.CompilerParams(vmem_limit_bytes=limit * MIB),
        cost_estimate=pl.CostEstimate(flops=flops, bytes_accessed=moved, transcendentals=0),
    )(*args)


def target_of(member, step, group):
    return member ^ step if group & (group - 1) == 0 else (member + step) % group


def source_of(member, step, group):
    return member ^ step if group & (group - 1) == 0 else (member + group - step) % group


def in_hbm(array):
    return pltpu.with_memory_space_constraint(array, pltpu.HBM)


def shaped(shape, dtype):
    return jax.ShapeDtypeStruct(shape, dtype)


def split(value):
    high = value.astype(BF16)
    return high, (value - high.astype(F32)).astype(BF16)


def dot3(left, right, left_dim=1, right_dim=0):
    left_high, left_low = split(left)
    right_high, right_low = split(right)
    return lax.dot_general(
        jnp.concatenate([left_high, left_high, left_low], axis=left_dim),
        jnp.concatenate([right_high, right_low, right_high], axis=right_dim),
        (((left_dim,), (right_dim,)), ((), ())),
        preferred_element_type=F32,
    )


def iota2(shape):
    return lax.broadcasted_iota(jnp.int32, shape, 0), lax.broadcasted_iota(jnp.int32, shape, 1)


def merge_inverse(lower, rows, cols):
    tokens = lower.shape[0]
    block = 16
    inverse = jnp.where(rows == cols, 1.0, 0.0).astype(F32)
    first = rows - rows % block
    for step in range(block - 1):
        column = jnp.sum(jnp.where(cols == first + step, lower, 0.0), axis=1, keepdims=True)
        pivot = inverse.reshape(tokens // block, block, tokens)[:, step : step + 1, :]
        pivot = jnp.broadcast_to(pivot, (tokens // block, block, tokens)).reshape(tokens, tokens)
        inverse = inverse - column * pivot
    while block < tokens:
        corner = (
            (rows // (2 * block) == cols // (2 * block))
            & (rows % (2 * block) >= block)
            & (cols % (2 * block) < block)
        )
        inverse = inverse - dot3(dot3(inverse, jnp.where(corner, lower, 0.0)), inverse)
        block *= 2
    return inverse


def load_kernel(size, key_hbm, dir_hbm, value_hbm, rate_hbm, key_gain_hbm,
                query_gain_hbm, mine_hbm, weight_ref, rate_ref, key_gain_ref, query_gain_ref,
                mine_ref, sems):
    pairs = [
        (hbm, weight_ref.at[:, index * size : (index + 1) * size])
        for index, hbm in enumerate((key_hbm, dir_hbm, value_hbm))
    ]
    pairs += [(rate_hbm, rate_ref), (key_gain_hbm, key_gain_ref)]
    pairs += [(query_gain_hbm, query_gain_ref), (mine_hbm, mine_ref)]
    copies = [pltpu.make_async_copy(*pair, sems.at[n]) for n, pair in enumerate(pairs)]
    for copy in copies:
        copy.start()
    for copy in copies:
        copy.wait()


def prepare_kernel(core_ref, mine_ref, other_ref, weight_ref, rate_ref, bias_ref, gain_ref,
                   rows_ref, kn_ref, val_ref, dirs_ref, coeff_ref, solved_ref, exit_ref, turn_ref):
    core = core_ref[0]
    half = mine_ref.shape[0]
    rows_ref[pl.ds(pl.multiple_of(core * half, half), half), :] = mine_ref[...]
    rows_ref[pl.ds(pl.multiple_of((1 - core) * half, half), half), :] = other_ref[...]
    seg = rows_ref[...]
    size = turn_ref.shape[0]
    raw = jnp.dot(seg, weight_ref[...], preferred_element_type=F32)
    keys, raw, vals = raw[:, :size], raw[:, size : 2 * size], raw[:, 2 * size :]
    kn = keys * lax.rsqrt(jnp.mean(keys * keys, axis=-1, keepdims=True) + EPSILON) * gain_ref[...]
    dirs = raw * lax.rsqrt(jnp.sum(raw * raw, axis=-1, keepdims=True) + EPSILON)
    vector = jnp.broadcast_to(rate_ref[...], (16, seg.shape[1]))
    logits = lax.dot_general(seg, vector, (((1,), (1,)), ((), ())), preferred_element_type=F32)
    rates = 2.0 * jax.nn.sigmoid(logits[:, :1] + bias_ref[0])
    val_ref[...] = vals.astype(BF16)
    kn_ref[...] = kn
    dirs_ref[...] = dirs
    tokens, size = dirs.shape
    rows, cols = iota2((tokens, tokens))
    below = rows > cols
    grams = dot3(dirs, jnp.concatenate([dirs, kn], axis=0), 1, 1)
    lower = jnp.where(below, rates * grams[:, :tokens], 0.0)
    crossing = jnp.where(below, rates * grams[:, tokens:], 0.0)
    inverse = merge_inverse(lower, rows, cols)
    both = dot3(inverse, jnp.concatenate([crossing, rates * dirs], axis=1))
    coeff_ref[...] = both[:, :tokens]
    solved_ref[...] = both[:, tokens:]
    crossed = dot3(both, dirs, 0, 0)
    exit_ref[...] = kn - crossed[:tokens]
    heads, lanes = iota2((size, size))
    turn_ref[...] = jnp.where(heads == lanes, 1.0, 0.0) - crossed[tokens:]


def leave_kernel(group, place_ref, exit_ref, *refs):
    turn_refs, (leave_ref, starts_ref) = refs[:group], refs[group : group + 2]
    near_refs, (turns_ref, seen_ref) = refs[group + 2 : -2], refs[-2:]
    member = place_ref[0] % group
    tokens, size = exit_ref.shape
    for step in range(group):
        turns_ref[source_of(member, step, group)] = turn_refs[group - 1 - step][...]
    own = exit_ref[...]
    keys = own
    product = None
    heads, lanes = iota2((size, size))
    starts_ref[0] = jnp.where(heads == lanes, 1.0, 0.0)
    for index in range(group):
        seen_ref[index] = keys.astype(BF16)
        turn = turns_ref[index]
        product = turn if product is None else dot3(product, turn)
        if index:
            keys = jnp.where(index > member, dot3(keys, turn), own)
        if index < group - 1:
            starts_ref[index + 1] = product
    high, low = split(keys)
    leave_ref[:tokens] = high
    leave_ref[tokens : 2 * tokens] = low
    high, low = split(product)
    leave_ref[2 * tokens : 2 * tokens + size] = high
    leave_ref[2 * tokens + size :] = low
    for step in range(group):
        near_refs[step][...] = seen_ref[target_of(member, step, group)]


def word_of(slot, segments):
    bits = segments.bit_length()
    per_word = 31 // bits
    return slot // per_word, bits * (slot % per_word), (1 << bits) - 1


def bundle_kernel(group, groups, most, place_ref, mask_ref, after_ref, *refs):
    val_refs, (line_ref, table_ref) = refs[:groups], refs[groups:]
    place = place_ref[0]
    mine = place // group
    segments = mask_ref.shape[0]
    for word in range(table_ref.shape[0]):
        table_ref[word] = 0

    def pick(segment, count):
        wanted = (mask_ref[segment] > 0) & (segment < place) & (count < most)
        word, shift, _ = word_of(count, segments)

        @pl.when(wanted)
        def _():
            table_ref[word] = table_ref[word] | ((segment + 1) << shift)

        return count + wanted.astype(jnp.int32)

    lax.fori_loop(0, segments, pick, jnp.int32(0))
    tokens = val_refs[0].shape[0]
    for way in range(groups):
        at = pl.multiple_of(source_of(mine, way, groups) * tokens, tokens)
        line_ref[pl.ds(at, tokens), :] = val_refs[groups - 1 - way][...]


def query_kernel(rows_ref, weight_hbm, gain_ref, kn_ref, dirs_ref, coeff_ref, solved_ref, val_ref,
                 moved_ref, weighted_ref, peak_ref, total_ref, weight_ref, raw_ref, sems):
    tokens, size = kn_ref.shape
    heads = moved_ref.shape[0]
    pieces, deep, _ = weight_ref.shape
    copies = [
        pltpu.make_async_copy(
            weight_hbm.at[n * deep : (n + 1) * deep, :], weight_ref.at[n], sems.at[n]
        )
        for n in range(pieces)
    ]
    for copy in copies:
        copy.start()
    across = jnp.concatenate([kn_ref[...], dirs_ref[...]], axis=0)
    into = jnp.concatenate([coeff_ref[...], solved_ref[...]], axis=1)
    for n in range(pieces):
        copies[n].wait()
        part = jnp.dot(
            rows_ref[:, n * deep : (n + 1) * deep], weight_ref[n], preferred_element_type=F32
        )
        raw_ref[...] = raw_ref[...] + part if n else part
    count = math.gcd(heads, 4)
    for turn in range(heads // count):
        raw = jnp.concatenate(
            [
                raw_ref[:, head * size : (head + 1) * size]
                for head in range(turn * count, (turn + 1) * count)
            ],
            axis=0,
        )
        queries = (
            raw * lax.rsqrt(jnp.mean(raw * raw, axis=-1, keepdims=True) + EPSILON) * gain_ref[...]
        )
        seen = dot3(queries, across, 1, 1)
        rows, cols = iota2((count * tokens, tokens))
        up_to = rows % tokens >= cols
        reach = jnp.where(up_to, seen[:, tokens:], 0.0)
        taken = dot3(reach, into)
        scores = (seen[:, :tokens] - taken[:, :tokens]) * (LOG2E / math.sqrt(size))
        scores = jnp.where(up_to, scores, NEGATIVE)
        moved = (queries - taken[:, tokens:]).astype(BF16)
        peak = jnp.max(scores, axis=1, keepdims=True)
        weights = jnp.exp2(scores - peak)
        total = jnp.sum(weights, axis=1, keepdims=True)
        weighted = jnp.dot(weights.astype(BF16), val_ref[...], preferred_element_type=F32)
        for h in range(count):
            part = slice(h * tokens, (h + 1) * tokens)
            head = turn * count + h
            moved_ref[head] = moved[part]
            weighted_ref[head] = weighted[part]
            peak_ref[head] = peak[part]
            total_ref[head] = total[part]


def arrive_kernel(groups, group, tokens, place_ref, *refs):
    arrived, starts_ref, near_refs = refs[:groups], refs[groups], refs[groups + 1 :]
    far_refs, (keys_ref, whole_ref) = refs[-group - 2 : -2], refs[-2:]
    mine, member = place_ref[0] // group, place_ref[0] % group
    size = starts_ref.shape[1]
    for step in range(groups):
        index = source_of(mine, step, groups)
        ref = arrived[groups - 1 - step]
        keys_ref[index] = ref[:tokens].astype(F32) + ref[tokens : 2 * tokens].astype(F32)
        whole = ref[2 * tokens : 2 * tokens + size].astype(F32)
        whole_ref[index] = whole + ref[2 * tokens + size :].astype(F32)
    brought = [keys_ref[groups - 2]]
    product = None
    for index in range(groups - 3, -1, -1):
        keys, whole = keys_ref[index], whole_ref[index + 1]
        if product is not None:
            whole = jnp.where(index + 2 < mine, dot3(whole, product), whole)
        product = whole
        brought.append(jnp.where(index + 1 < mine, dot3(keys, product), keys))
    keys = jnp.concatenate(brought[::-1], axis=0)
    for step in range(group):
        start = starts_ref[target_of(member, step, group)]
        far_refs[step][: (groups - 1) * tokens] = dot3(keys, start).astype(BF16)
        far_refs[step][(groups - 1) * tokens :] = near_refs[step][...]


def attend_kernel(group, segments, most, place_ref, core_ref, table_ref, *refs):
    far_refs, line_refs = refs[:group][::-1], refs[group : 2 * group][::-1]
    (moved_ref, weighted_ref, peak_ref, total_ref, out_ref, away_ref, kept_ref, keys_ref, vals_ref,
     attended_ref) = refs[2 * group :]
    core = core_ref[0]
    mine, member = place_ref[0] // group, place_ref[0] % group
    heads, tokens, size = moved_ref.shape
    groups = far_refs[0].shape[0] // tokens
    scaling = LOG2E / math.sqrt(size)
    chunk = keys_ref.shape[0] // tokens
    lanes = lax.broadcasted_iota(jnp.int32, (1, chunk * tokens), 1)

    def collect(turn):
        found = jnp.int32(0)
        for slot in range(chunk):
            part = slice(slot * tokens, (slot + 1) * tokens)
            word, shift, ones = word_of(turn * chunk + slot, segments)
            code = (table_ref[word] >> shift) & ones
            found = found + (code > 0).astype(jnp.int32)
            segment = jnp.maximum(code - 1, 0)
            whose, source = segment % group, segment // group
            before = jnp.where(source < mine, source, groups - 1)
            before = pl.multiple_of(before * tokens, tokens)
            after = pl.multiple_of(source * tokens, tokens)
            for number in range(group):

                @pl.when(whose == source_of(member, number, group))
                def _():
                    vals_ref[part, :] = line_refs[number][pl.ds(after, tokens), :]
                    keys_ref[part, :] = far_refs[number][pl.ds(before, tokens), :]

        return jnp.where(lanes < found * tokens, 0.0, NEGATIVE)

    def advance(moved, bias, peak, total, weighted):
        scores = lax.dot_general(
            moved, keys_ref[...], (((1,), (1,)), ((), ())), preferred_element_type=F32
        )
        scores = scores * scaling + bias
        new_peak = jnp.maximum(peak, jnp.max(scores, axis=1, keepdims=True))
        fading = jnp.exp2(peak - new_peak)
        weights = jnp.exp2(scores - new_peak)
        total = total * fading + jnp.sum(weights, axis=1, keepdims=True)
        weighted = weighted * fading + jnp.dot(
            weights.astype(BF16), vals_ref[...], preferred_element_type=F32
        )
        return new_peak, total, weighted

    half = kept_ref.shape[0]
    turns = most // chunk
    if turns == 1:
        bias = collect(0)
    stack = math.gcd(heads, 2)
    for first in range(0, heads, stack):
        some = slice(first, first + stack)
        moved = moved_ref[some].reshape(stack * tokens, size)
        state = (
            peak_ref[some].reshape(stack * tokens, 1),
            total_ref[some].reshape(stack * tokens, 1),
            weighted_ref[some].reshape(stack * tokens, size),
        )
        if turns == 1:
            _, total, weighted = advance(moved, bias, *state)
        else:

            def step_of(turn, state, moved=moved):
                return advance(moved, collect(turn), *state)

            _, total, weighted = lax.fori_loop(0, turns, step_of, state)
        done = (weighted * (1.0 / total)).astype(BF16)
        for head in range(first, first + stack):
            for index in range(tokens // half):
                at = pl.multiple_of(jnp.where(index == core, half, 0), half)
                row = (head - first) * tokens + index * half
                attended_ref[pl.ds(at, half), head * size : (head + 1) * size] = done[
                    row : row + half
                ]
    wide = math.gcd(out_ref.shape[1], 4 * size)
    for at in range(0, out_ref.shape[1], wide):
        part = slice(at, at + wide)
        result = jnp.dot(attended_ref[...], out_ref[:, part], preferred_element_type=F32)
        result = result.astype(BF16)
        away_ref[:, part] = result[:half]
        kept_ref[:, part] = result[half:]


def body(
    hidden, w_query, w_key, w_value, w_dir, u_rate, rate_bias, q_gain, k_gain, w_out, block_mask
):
    segments = lax.axis_size("ctx")
    place = lax.axis_index("ctx").astype(jnp.int32).reshape(1)
    core = lax.axis_index("head").astype(jnp.int32).reshape(1)
    group = max(d for d in range(1, math.isqrt(segments) + 1) if segments % d == 0)
    groups = segments // group
    other = lax.ppermute(hidden, "head", [(0, 1), (1, 0)])
    half, width = hidden.shape
    tokens = half * lax.axis_size("head")
    size = w_key.shape[1]
    heads = w_query.shape[1] // size
    smem = pl.BlockSpec(memory_space=pltpu.SMEM)
    vmem = pl.BlockSpec(memory_space=pltpu.VMEM)
    hbm = pl.BlockSpec(memory_space=pltpu.HBM)
    anywhere = pl.BlockSpec(memory_space=pl.ANY)
    square = shaped((tokens, size), F32)

    def swapped(values, count, pairs_of):
        out = [values[0]] * count
        for step in range(count - 1, 0, -1):
            out[step] = lax.ppermute(values[step], "ctx", pairs_of(step))
        return out

    def within_group(values):
        return swapped(values, group, lambda step: [
            (s, s - s % group + target_of(s % group, step, group)) for s in range(segments)
        ])

    def along_line(values):
        return swapped(values, groups, lambda step: [
            (s, s % group + group * target_of(s // group, step, groups)) for s in range(segments)
        ])

    weights, rate_row, key_gain, query_gain, mine = call(
        functools.partial(load_kernel, size),
        (
            shaped((width, 3 * size), BF16), shaped((1, width), BF16), shaped((1, size), F32),
            shaped((1, size), F32), shaped((half, width), BF16),
        ),
        tuple(
            in_hbm(array)
            for array in (
                w_key, w_dir, w_value, u_rate, k_gain.reshape(1, size), q_gain.reshape(1, size),
                hidden,
            )
        ),
        in_specs=[hbm] * 7,
        scratch=(pltpu.SemaphoreType.DMA((7,)),),
        moved=12 * width * size,
    )
    rows, kn, val, dirs, coeff, solved, exit_keys, turn = call(
        prepare_kernel,
        (
            shaped((tokens, width), BF16), square, shaped((tokens, size), BF16), square, square,
            square, square, shaped((size, size), F32),
        ),
        (core, mine, other, weights, rate_row, rate_bias, key_gain),
        in_specs=[smem] + [vmem] * 4 + [smem, vmem],
        flops=6 * tokens * width * size,
        moved=8 * width * size,
    )
    turns = within_group([turn] * group)
    line = along_line([val] * groups)
    leaving, starts, *near = call(
        functools.partial(leave_kernel, group),
        [
            shaped((2 * tokens + 2 * size, size), BF16),
            shaped((group, size, size), F32),
        ]
        + [shaped((tokens, size), BF16)] * group,
        (place, exit_keys, *turns[::-1]),
        in_specs=[smem] + [vmem] * (1 + group),
        scratch=(
            pltpu.VMEM((group, size, size), F32),
            pltpu.VMEM((group, tokens, size), BF16),
        ),
        flops=12 * group * size**3,
        moved=10**6,
    )
    arrived = along_line([leaving] * groups)
    most = segments // 4
    values, table = call(
        functools.partial(bundle_kernel, group, groups, most),
        [
            shaped((groups * tokens, size), BF16),
            shaped((word_of(most - 1, segments)[0] + 1,), jnp.int32),
        ],
        (place, block_mask[0], starts, *line[::-1]),
        in_specs=[smem, smem, anywhere] + [vmem] * groups,
        out_specs=[vmem, smem],
        moved=10**6,
        limit=8 + group * groups // 4,
    )
    values = within_group([values] * group)
    own = call(
        query_kernel,
        (
            shaped((heads, tokens, size), BF16),
            shaped((heads, tokens, size), F32),
            shaped((heads, tokens, 1), F32),
            shaped((heads, tokens, 1), F32),
        ),
        (rows, in_hbm(w_query), query_gain, kn, dirs, coeff, solved, val),
        in_specs=[vmem, hbm] + [vmem] * 6,
        scratch=(
            pltpu.VMEM((2, width // 2, w_query.shape[1]), BF16),
            pltpu.VMEM((tokens, w_query.shape[1]), F32),
            pltpu.SemaphoreType.DMA((2,)),
        ),
        flops=4 * tokens * width * heads * size,
        moved=8 * width * heads * size,
        limit=16,
    )
    far = call(
        functools.partial(arrive_kernel, groups, group, tokens),
        [shaped((groups * tokens, size), BF16)] * group,
        (place, *arrived[::-1], starts, *near),
        in_specs=[smem] + [vmem] * (groups + 1 + group),
        scratch=(
            pltpu.VMEM((groups, tokens, size), F32),
            pltpu.VMEM((groups, size, size), F32),
        ),
        flops=6 * groups * group * size**3,
        moved=10**6,
        limit=8 + group * groups // 4,
    )
    far = within_group(far)
    chunk = math.gcd(most, 4)
    width_out = w_out.shape[1]
    away, kept = call(
        functools.partial(attend_kernel, group, segments, most),
        [shaped((half, width_out), BF16)] * 2,
        (place, core, table, *far[::-1], *values[::-1], *own, w_out),
        in_specs=[smem] * 3 + [vmem] * (2 * group + 5),
        scratch=[
            pltpu.VMEM((chunk * tokens, size), BF16),
            pltpu.VMEM((chunk * tokens, size), BF16),
            pltpu.VMEM((tokens, heads * size), BF16),
        ],
        flops=2 * tokens * width_out * heads * size,
        moved=4 * 10**6,
        limit=14 + group * groups // 4,
    )
    return kept + lax.ppermute(away, "head", [(0, 1), (1, 0)])


def solution(mesh):
    in_specs = (
        P(("ctx", "head"), None),
        P(None, "head"),
        P(None, "head"),
        P(None, "head"),
        P(None, "head"),
        P("head", None),
        P("head"),
        P(),
        P(),
        P("head", None),
        P("ctx", None),
    )
    out_specs = P(("ctx", "head"), None)
    return jax.shard_map(body, mesh=mesh, in_specs=in_specs, out_specs=out_specs, check_vma=False)
```

```python
import functools
import math

import jax
import jax.numpy as jnp
from jax import lax
from jax.experimental import pallas as pl
from jax.experimental.pallas import tpu as pltpu
from jax.sharding import PartitionSpec as P

EPSILON = 1e-06
NEGATIVE = -1e30
LOG2E = math.log2(math.e)
F32 = jnp.float32
BF16 = jnp.bfloat16
MIB = 1024 * 1024


def call(kernel, out_shape, args, in_specs=None, out_specs=None, scratch=(), flops=0, moved=0, limit=6):
    vmem = pl.BlockSpec(memory_space=pltpu.VMEM)
    return pl.pallas_call(
        kernel,
        out_shape=out_shape,
        in_specs=in_specs or [vmem] * len(args),
        out_specs=out_specs or jax.tree.map(lambda _: vmem, out_shape),
        scratch_shapes=list(scratch),
        compiler_params=pltpu.CompilerParams(vmem_limit_bytes=limit * MIB),
        cost_estimate=pl.CostEstimate(flops=flops, bytes_accessed=moved, transcendentals=0),
    )(*args)


def target_of(member, step, group):
    return member ^ step if group & (group - 1) == 0 else (member + step) % group


def source_of(member, step, group):
    return member ^ step if group & (group - 1) == 0 else (member + group - step) % group


def in_hbm(array):
    return pltpu.with_memory_space_constraint(array, pltpu.HBM)


def shaped(shape, dtype):
    return jax.ShapeDtypeStruct(shape, dtype)


def split(value):
    high = value.astype(BF16)
    return high, (value - high.astype(F32)).astype(BF16)


def dot3(left, right, left_dim=1, right_dim=0):
    left_high, left_low = split(left)
    right_high, right_low = split(right)
    return lax.dot_general(
        jnp.concatenate([left_high, left_high, left_low], axis=left_dim),
        jnp.concatenate([right_high, right_low, right_high], axis=right_dim),
        (((left_dim,), (right_dim,)), ((), ())),
        preferred_element_type=F32,
    )


def iota2(shape):
    return lax.broadcasted_iota(jnp.int32, shape, 0), lax.broadcasted_iota(jnp.int32, shape, 1)


def merge_inverse(lower, rows, cols):
    tokens = lower.shape[0]
    block = 16
    inverse = jnp.where(rows == cols, 1.0, 0.0).astype(F32)
    first = rows - rows % block
    for step in range(block - 1):
        column = jnp.sum(jnp.where(cols == first + step, lower, 0.0), axis=1, keepdims=True)
        pivot = inverse.reshape(tokens // block, block, tokens)[:, step : step + 1, :]
        pivot = jnp.broadcast_to(pivot, (tokens // block, block, tokens)).reshape(tokens, tokens)
        inverse = inverse - column * pivot
    while block < tokens:
        corner = (
            (rows // (2 * block) == cols // (2 * block))
            & (rows % (2 * block) >= block)
            & (cols % (2 * block) < block)
        )
        inverse = inverse - dot3(dot3(inverse, jnp.where(corner, lower, 0.0)), inverse)
        block *= 2
    return inverse


def load_kernel(size, key_hbm, dir_hbm, value_hbm, rate_hbm, key_gain_hbm,
                query_gain_hbm, mine_hbm, weight_ref, rate_ref, key_gain_ref, query_gain_ref,
                mine_ref, sems):
    pairs = [
        (hbm, weight_ref.at[:, index * size : (index + 1) * size])
        for index, hbm in enumerate((key_hbm, dir_hbm, value_hbm))
    ]
    pairs += [(rate_hbm, rate_ref), (key_gain_hbm, key_gain_ref)]
    pairs += [(query_gain_hbm, query_gain_ref), (mine_hbm, mine_ref)]
    copies = [pltpu.make_async_copy(*pair, sems.at[n]) for n, pair in enumerate(pairs)]
    for copy in copies:
        copy.start()
    for copy in copies:
        copy.wait()


def prepare_kernel(core_ref, mine_ref, other_ref, weight_ref, rate_ref, bias_ref, gain_ref,
                   rows_ref, kn_ref, val_ref, dirs_ref, coeff_ref, solved_ref, exit_ref, turn_ref):
    core = core_ref[0]
    half = mine_ref.shape[0]
    rows_ref[pl.ds(pl.multiple_of(core * half, half), half), :] = mine_ref[...]
    rows_ref[pl.ds(pl.multiple_of((1 - core) * half, half), half), :] = other_ref[...]
    seg = rows_ref[...]
    size = turn_ref.shape[0]
    raw = jnp.dot(seg, weight_ref[...], preferred_element_type=F32)
    keys, raw, vals = raw[:, :size], raw[:, size : 2 * size], raw[:, 2 * size :]
    kn = keys * lax.rsqrt(jnp.mean(keys * keys, axis=-1, keepdims=True) + EPSILON) * gain_ref[...]
    dirs = raw * lax.rsqrt(jnp.sum(raw * raw, axis=-1, keepdims=True) + EPSILON)
    vector = jnp.broadcast_to(rate_ref[...], (16, seg.shape[1]))
    logits = lax.dot_general(seg, vector, (((1,), (1,)), ((), ())), preferred_element_type=F32)
    rates = 2.0 * jax.nn.sigmoid(logits[:, :1] + bias_ref[0])
    val_ref[...] = vals.astype(BF16)
    kn_ref[...] = kn
    dirs_ref[...] = dirs
    tokens, size = dirs.shape
    rows, cols = iota2((tokens, tokens))
    below = rows > cols
    grams = dot3(dirs, jnp.concatenate([dirs, kn], axis=0), 1, 1)
    lower = jnp.where(below, rates * grams[:, :tokens], 0.0)
    crossing = jnp.where(below, rates * grams[:, tokens:], 0.0)
    inverse = merge_inverse(lower, rows, cols)
    both = dot3(inverse, jnp.concatenate([crossing, rates * dirs], axis=1))
    coeff_ref[...] = both[:, :tokens]
    solved_ref[...] = both[:, tokens:]
    crossed = dot3(both, dirs, 0, 0)
    exit_ref[...] = kn - crossed[:tokens]
    heads, lanes = iota2((size, size))
    turn_ref[...] = jnp.where(heads == lanes, 1.0, 0.0) - crossed[tokens:]


def leave_kernel(group, place_ref, exit_ref, *refs):
    turn_refs, (leave_ref, starts_ref) = refs[:group], refs[group : group + 2]
    near_refs, (turns_ref, seen_ref) = refs[group + 2 : -2], refs[-2:]
    member = place_ref[0] % group
    tokens, size = exit_ref.shape
    for step in range(group):
        turns_ref[source_of(member, step, group)] = turn_refs[group - 1 - step][...]
    own = exit_ref[...]
    keys = own
    product = None
    heads, lanes = iota2((size, size))
    starts_ref[0] = jnp.where(heads == lanes, 1.0, 0.0)
    for index in range(group):
        seen_ref[index] = keys.astype(BF16)
        turn = turns_ref[index]
        product = turn if product is None else dot3(product, turn)
        if index:
            keys = jnp.where(index > member, dot3(keys, turn), own)
        if index < group - 1:
            starts_ref[index + 1] = product
    high, low = split(keys)
    leave_ref[:tokens] = high
    leave_ref[tokens : 2 * tokens] = low
    high, low = split(product)
    leave_ref[2 * tokens : 2 * tokens + size] = high
    leave_ref[2 * tokens + size :] = low
    for step in range(group):
        near_refs[step][...] = seen_ref[target_of(member, step, group)]


def word_of(slot, segments):
    bits = segments.bit_length()
    per_word = 31 // bits
    return slot // per_word, bits * (slot % per_word), (1 << bits) - 1


def bundle_kernel(group, groups, most, place_ref, mask_ref, after_ref, *refs):
    val_refs, (line_ref, table_ref) = refs[:groups], refs[groups:]
    place = place_ref[0]
    mine = place // group
    segments = mask_ref.shape[0]
    for word in range(table_ref.shape[0]):
        table_ref[word] = 0

    def pick(segment, count):
        wanted = (mask_ref[segment] > 0) & (segment < place) & (count < most)
        word, shift, _ = word_of(count, segments)

        @pl.when(wanted)
        def _():
            table_ref[word] = table_ref[word] | ((segment + 1) << shift)

        return count + wanted.astype(jnp.int32)

    lax.fori_loop(0, segments, pick, jnp.int32(0))
    tokens = val_refs[0].shape[0]
    for way in range(groups):
        at = pl.multiple_of(source_of(mine, way, groups) * tokens, tokens)
        line_ref[pl.ds(at, tokens), :] = val_refs[groups - 1 - way][...]


def query_kernel(rows_ref, weight_hbm, gain_ref, kn_ref, dirs_ref, coeff_ref, solved_ref, val_ref,
                 moved_ref, weighted_ref, peak_ref, total_ref, weight_ref, raw_ref, sems):
    tokens, size = kn_ref.shape
    heads = moved_ref.shape[0]
    pieces, deep, _ = weight_ref.shape
    copies = [
        pltpu.make_async_copy(
            weight_hbm.at[n * deep : (n + 1) * deep, :], weight_ref.at[n], sems.at[n]
        )
        for n in range(pieces)
    ]
    for copy in copies:
        copy.start()
    across = jnp.concatenate([kn_ref[...], dirs_ref[...]], axis=0)
    into = jnp.concatenate([coeff_ref[...], solved_ref[...]], axis=1)
    for n in range(pieces):
        copies[n].wait()
        part = jnp.dot(
            rows_ref[:, n * deep : (n + 1) * deep], weight_ref[n], preferred_element_type=F32
        )
        raw_ref[...] = raw_ref[...] + part if n else part
    count = math.gcd(heads, 4)
    for turn in range(heads // count):
        raw = jnp.concatenate(
            [
                raw_ref[:, head * size : (head + 1) * size]
                for head in range(turn * count, (turn + 1) * count)
            ],
            axis=0,
        )
        queries = (
            raw * lax.rsqrt(jnp.mean(raw * raw, axis=-1, keepdims=True) + EPSILON) * gain_ref[...]
        )
        seen = dot3(queries, across, 1, 1)
        rows, cols = iota2((count * tokens, tokens))
        up_to = rows % tokens >= cols
        reach = jnp.where(up_to, seen[:, tokens:], 0.0)
        taken = dot3(reach, into)
        scores = (seen[:, :tokens] - taken[:, :tokens]) * (LOG2E / math.sqrt(size))
        scores = jnp.where(up_to, scores, NEGATIVE)
        moved = (queries - taken[:, tokens:]).astype(BF16)
        peak = jnp.max(scores, axis=1, keepdims=True)
        weights = jnp.exp2(scores - peak)
        total = jnp.sum(weights, axis=1, keepdims=True)
        weighted = jnp.dot(weights.astype(BF16), val_ref[...], preferred_element_type=F32)
        for h in range(count):
            part = slice(h * tokens, (h + 1) * tokens)
            head = turn * count + h
            moved_ref[head] = moved[part]
            weighted_ref[head] = weighted[part]
            peak_ref[head] = peak[part]
            total_ref[head] = total[part]


def arrive_kernel(groups, group, tokens, place_ref, *refs):
    arrived, starts_ref, near_refs = refs[:groups], refs[groups], refs[groups + 1 :]
    far_refs, (keys_ref, whole_ref) = refs[-group - 2 : -2], refs[-2:]
    mine, member = place_ref[0] // group, place_ref[0] % group
    size = starts_ref.shape[1]
    for step in range(groups):
        index = source_of(mine, step, groups)
        ref = arrived[groups - 1 - step]
        keys_ref[index] = ref[:tokens].astype(F32) + ref[tokens : 2 * tokens].astype(F32)
        whole = ref[2 * tokens : 2 * tokens + size].astype(F32)
        whole_ref[index] = whole + ref[2 * tokens + size :].astype(F32)
    brought = [keys_ref[groups - 2]]
    product = None
    for index in range(groups - 3, -1, -1):
        keys, whole = keys_ref[index], whole_ref[index + 1]
        if product is not None:
            whole = jnp.where(index + 2 < mine, dot3(whole, product), whole)
        product = whole
        brought.append(jnp.where(index + 1 < mine, dot3(keys, product), keys))
    keys = jnp.concatenate(brought[::-1], axis=0)
    count, size = keys.shape
    ways = [starts_ref[target_of(member, step, group)] for step in range(group)]
    spread = dot3(keys, jnp.concatenate(ways, axis=1)).astype(BF16)
    for step in range(group):
        far_refs[step][:count] = spread[:, step * size : (step + 1) * size]
        far_refs[step][count:] = near_refs[step][...]


def attend_kernel(group, segments, most, place_ref, core_ref, table_ref, *refs):
    far_refs, line_refs = refs[:group][::-1], refs[group : 2 * group][::-1]
    (moved_ref, weighted_ref, peak_ref, total_ref, out_ref, away_ref, kept_ref, keys_ref, vals_ref,
     attended_ref) = refs[2 * group :]
    core = core_ref[0]
    mine, member = place_ref[0] // group, place_ref[0] % group
    heads, tokens, size = moved_ref.shape
    groups = far_refs[0].shape[0] // tokens
    scaling = LOG2E / math.sqrt(size)
    chunk = keys_ref.shape[0] // tokens
    lanes = lax.broadcasted_iota(jnp.int32, (1, chunk * tokens), 1)

    def collect(turn):
        found = jnp.int32(0)
        for slot in range(chunk):
            part = slice(slot * tokens, (slot + 1) * tokens)
            word, shift, ones = word_of(turn * chunk + slot, segments)
            code = (table_ref[word] >> shift) & ones
            found = found + (code > 0).astype(jnp.int32)
            segment = jnp.maximum(code - 1, 0)
            whose, source = segment % group, segment // group
            before = jnp.where(source < mine, source, groups - 1)
            before = pl.multiple_of(before * tokens, tokens)
            after = pl.multiple_of(source * tokens, tokens)
            for number in range(group):

                @pl.when(whose == source_of(member, number, group))
                def _():
                    vals_ref[part, :] = line_refs[number][pl.ds(after, tokens), :]
                    keys_ref[part, :] = far_refs[number][pl.ds(before, tokens), :]

        return jnp.where(lanes < found * tokens, 0.0, NEGATIVE)

    def advance(moved, bias, peak, total, weighted):
        scores = lax.dot_general(
            moved, keys_ref[...], (((1,), (1,)), ((), ())), preferred_element_type=F32
        )
        scores = scores * scaling + bias
        new_peak = jnp.maximum(peak, jnp.max(scores, axis=1, keepdims=True))
        fading = jnp.exp2(peak - new_peak)
        weights = jnp.exp2(scores - new_peak)
        total = total * fading + jnp.sum(weights, axis=1, keepdims=True)
        weighted = weighted * fading + jnp.dot(
            weights.astype(BF16), vals_ref[...], preferred_element_type=F32
        )
        return new_peak, total, weighted

    half = kept_ref.shape[0]
    turns = most // chunk
    if turns == 1:
        bias = collect(0)
    stack = math.gcd(heads, 4)
    for first in range(0, heads, stack):
        some = slice(first, first + stack)
        moved = moved_ref[some].reshape(stack * tokens, size)
        state = (
            peak_ref[some].reshape(stack * tokens, 1),
            total_ref[some].reshape(stack * tokens, 1),
            weighted_ref[some].reshape(stack * tokens, size),
        )
        if turns == 1:
            _, total, weighted = advance(moved, bias, *state)
        else:

            def step_of(turn, state, moved=moved):
                return advance(moved, collect(turn), *state)

            _, total, weighted = lax.fori_loop(0, turns, step_of, state)
        done = (weighted * (1.0 / total)).astype(BF16)
        for head in range(first, first + stack):
            for index in range(tokens // half):
                at = pl.multiple_of(jnp.where(index == core, half, 0), half)
                row = (head - first) * tokens + index * half
                attended_ref[pl.ds(at, half), head * size : (head + 1) * size] = done[
                    row : row + half
                ]
    wide = math.gcd(out_ref.shape[1], 4 * size)
    for at in range(0, out_ref.shape[1], wide):
        part = slice(at, at + wide)
        result = jnp.dot(attended_ref[...], out_ref[:, part], preferred_element_type=F32)
        result = result.astype(BF16)
        away_ref[:, part] = result[:half]
        kept_ref[:, part] = result[half:]


def body(
    hidden, w_query, w_key, w_value, w_dir, u_rate, rate_bias, q_gain, k_gain, w_out, block_mask
):
    segments = lax.axis_size("ctx")
    place = lax.axis_index("ctx").astype(jnp.int32).reshape(1)
    core = lax.axis_index("head").astype(jnp.int32).reshape(1)
    group = max(d for d in range(1, math.isqrt(segments) + 1) if segments % d == 0)
    groups = segments // group
    other = lax.ppermute(hidden, "head", [(0, 1), (1, 0)])
    half, width = hidden.shape
    tokens = half * lax.axis_size("head")
    size = w_key.shape[1]
    heads = w_query.shape[1] // size
    smem = pl.BlockSpec(memory_space=pltpu.SMEM)
    vmem = pl.BlockSpec(memory_space=pltpu.VMEM)
    hbm = pl.BlockSpec(memory_space=pltpu.HBM)
    anywhere = pl.BlockSpec(memory_space=pl.ANY)
    square = shaped((tokens, size), F32)

    def swapped(values, count, pairs_of):
        out = [values[0]] * count
        for step in range(count - 1, 0, -1):
            out[step] = lax.ppermute(values[step], "ctx", pairs_of(step))
        return out

    def within_group(values):
        return swapped(values, group, lambda step: [
            (s, s - s % group + target_of(s % group, step, group)) for s in range(segments)
        ])

    def along_line(values):
        return swapped(values, groups, lambda step: [
            (s, s % group + group * target_of(s // group, step, groups)) for s in range(segments)
        ])

    weights, rate_row, key_gain, query_gain, mine = call(
        functools.partial(load_kernel, size),
        (
            shaped((width, 3 * size), BF16), shaped((1, width), BF16), shaped((1, size), F32),
            shaped((1, size), F32), shaped((half, width), BF16),
        ),
        tuple(
            in_hbm(array)
            for array in (
                w_key, w_dir, w_value, u_rate, k_gain.reshape(1, size), q_gain.reshape(1, size),
                hidden,
            )
        ),
        in_specs=[hbm] * 7,
        scratch=(pltpu.SemaphoreType.DMA((7,)),),
        moved=12 * width * size,
    )
    rows, kn, val, dirs, coeff, solved, exit_keys, turn = call(
        prepare_kernel,
        (
            shaped((tokens, width), BF16), square, shaped((tokens, size), BF16), square, square,
            square, square, shaped((size, size), F32),
        ),
        (core, mine, other, weights, rate_row, rate_bias, key_gain),
        in_specs=[smem] + [vmem] * 4 + [smem, vmem],
        flops=6 * tokens * width * size,
        moved=8 * width * size,
    )
    turns = within_group([turn] * group)
    line = along_line([val] * groups)
    leaving, starts, *near = call(
        functools.partial(leave_kernel, group),
        [
            shaped((2 * tokens + 2 * size, size), BF16),
            shaped((group, size, size), F32),
        ]
        + [shaped((tokens, size), BF16)] * group,
        (place, exit_keys, *turns[::-1]),
        in_specs=[smem] + [vmem] * (1 + group),
        scratch=(
            pltpu.VMEM((group, size, size), F32),
            pltpu.VMEM((group, tokens, size), BF16),
        ),
        flops=12 * group * size**3,
        moved=10**6,
    )
    arrived = along_line([leaving] * groups)
    most = segments // 4
    values, table = call(
        functools.partial(bundle_kernel, group, groups, most),
        [
            shaped((groups * tokens, size), BF16),
            shaped((word_of(most - 1, segments)[0] + 1,), jnp.int32),
        ],
        (place, block_mask[0], starts, *line[::-1]),
        in_specs=[smem, smem, anywhere] + [vmem] * groups,
        out_specs=[vmem, smem],
        moved=10**6,
        limit=8 + group * groups // 4,
    )
    values = within_group([values] * group)
    own = call(
        query_kernel,
        (
            shaped((heads, tokens, size), BF16),
            shaped((heads, tokens, size), F32),
            shaped((heads, tokens, 1), F32),
            shaped((heads, tokens, 1), F32),
        ),
        (rows, in_hbm(w_query), query_gain, kn, dirs, coeff, solved, val),
        in_specs=[vmem, hbm] + [vmem] * 6,
        scratch=(
            pltpu.VMEM((2, width // 2, w_query.shape[1]), BF16),
            pltpu.VMEM((tokens, w_query.shape[1]), F32),
            pltpu.SemaphoreType.DMA((2,)),
        ),
        flops=4 * tokens * width * heads * size,
        moved=8 * width * heads * size,
        limit=16,
    )
    far = call(
        functools.partial(arrive_kernel, groups, group, tokens),
        [shaped((groups * tokens, size), BF16)] * group,
        (place, *arrived[::-1], starts, *near),
        in_specs=[smem] + [vmem] * (groups + 1 + group),
        scratch=(
            pltpu.VMEM((groups, tokens, size), F32),
            pltpu.VMEM((groups, size, size), F32),
        ),
        flops=6 * groups * group * size**3,
        moved=10**6,
        limit=8 + group * groups // 4,
    )
    far = within_group(far)
    chunk = math.gcd(most, 4)
    width_out = w_out.shape[1]
    away, kept = call(
        functools.partial(attend_kernel, group, segments, most),
        [shaped((half, width_out), BF16)] * 2,
        (place, core, table, *far[::-1], *values[::-1], *own, w_out),
        in_specs=[smem] * 3 + [vmem] * (2 * group + 5),
        scratch=[
            pltpu.VMEM((chunk * tokens, size), BF16),
            pltpu.VMEM((chunk * tokens, size), BF16),
            pltpu.VMEM((tokens, heads * size), BF16),
        ],
        flops=2 * tokens * width_out * heads * size,
        moved=4 * 10**6,
        limit=14 + group * groups // 4,
    )
    return kept + lax.ppermute(away, "head", [(0, 1), (1, 0)])


def solution(mesh):
    in_specs = (
        P(("ctx", "head"), None),
        P(None, "head"),
        P(None, "head"),
        P(None, "head"),
        P(None, "head"),
        P("head", None),
        P("head"),
        P(),
        P(),
        P("head", None),
        P("ctx", None),
    )
    out_specs = P(("ctx", "head"), None)
    return jax.shard_map(body, mesh=mesh, in_specs=in_specs, out_specs=out_specs, check_vma=False)
```

```python
import functools
import math

import jax
import jax.numpy as jnp
from jax import lax
from jax.experimental import pallas as pl
from jax.experimental.pallas import tpu as pltpu
from jax.sharding import PartitionSpec as P

EPSILON = 1e-06
NEGATIVE = -1e30
LOG2E = math.log2(math.e)
F32 = jnp.float32
BF16 = jnp.bfloat16
MIB = 1024 * 1024


def call(kernel, out_shape, args, in_specs=None, out_specs=None, scratch=(), flops=0, moved=0, limit=6):
    vmem = pl.BlockSpec(memory_space=pltpu.VMEM)
    return pl.pallas_call(
        kernel,
        out_shape=out_shape,
        in_specs=in_specs or [vmem] * len(args),
        out_specs=out_specs or jax.tree.map(lambda _: vmem, out_shape),
        scratch_shapes=list(scratch),
        compiler_params=pltpu.CompilerParams(vmem_limit_bytes=limit * MIB),
        cost_estimate=pl.CostEstimate(flops=flops, bytes_accessed=moved, transcendentals=0),
    )(*args)


def target_of(member, step, group):
    return member ^ step if group & (group - 1) == 0 else (member + step) % group


def source_of(member, step, group):
    return member ^ step if group & (group - 1) == 0 else (member + group - step) % group


def in_hbm(array):
    return pltpu.with_memory_space_constraint(array, pltpu.HBM)


def line_order(groups):
    return [groups // 2] + [step for step in range(groups - 1, 0, -1) if step != groups // 2] + [0]


def shaped(shape, dtype):
    return jax.ShapeDtypeStruct(shape, dtype)


def split(value):
    high = value.astype(BF16)
    return high, (value - high.astype(F32)).astype(BF16)


def dot3(left, right, left_dim=1, right_dim=0):
    left_high, left_low = split(left)
    right_high, right_low = split(right)
    return lax.dot_general(
        jnp.concatenate([left_high, left_high, left_low], axis=left_dim),
        jnp.concatenate([right_high, right_low, right_high], axis=right_dim),
        (((left_dim,), (right_dim,)), ((), ())),
        preferred_element_type=F32,
    )


def iota2(shape):
    return lax.broadcasted_iota(jnp.int32, shape, 0), lax.broadcasted_iota(jnp.int32, shape, 1)


def merge_inverse(lower, rows, cols):
    tokens = lower.shape[0]
    block = 16
    inverse = jnp.where(rows == cols, 1.0, 0.0).astype(F32)
    first = rows - rows % block
    for step in range(block - 1):
        column = jnp.sum(jnp.where(cols == first + step, lower, 0.0), axis=1, keepdims=True)
        pivot = inverse.reshape(tokens // block, block, tokens)[:, step : step + 1, :]
        pivot = jnp.broadcast_to(pivot, (tokens // block, block, tokens)).reshape(tokens, tokens)
        inverse = inverse - column * pivot
    while block < tokens:
        corner = (
            (rows // (2 * block) == cols // (2 * block))
            & (rows % (2 * block) >= block)
            & (cols % (2 * block) < block)
        )
        inverse = inverse - dot3(dot3(inverse, jnp.where(corner, lower, 0.0)), inverse)
        block *= 2
    return inverse


def load_kernel(size, key_hbm, dir_hbm, value_hbm, rate_hbm, key_gain_hbm,
                query_gain_hbm, mine_hbm, weight_ref, rate_ref, key_gain_ref, query_gain_ref,
                mine_ref, sems):
    pairs = [
        (hbm, weight_ref.at[:, index * size : (index + 1) * size])
        for index, hbm in enumerate((key_hbm, dir_hbm, value_hbm))
    ]
    pairs += [(rate_hbm, rate_ref), (key_gain_hbm, key_gain_ref)]
    pairs += [(query_gain_hbm, query_gain_ref), (mine_hbm, mine_ref)]
    copies = [pltpu.make_async_copy(*pair, sems.at[n]) for n, pair in enumerate(pairs)]
    for copy in copies:
        copy.start()
    for copy in copies:
        copy.wait()


def prepare_kernel(core_ref, mine_ref, other_ref, weight_ref, rate_ref, bias_ref, gain_ref,
                   rows_ref, kn_ref, val_ref, dirs_ref, coeff_ref, solved_ref, exit_ref, turn_ref):
    core = core_ref[0]
    half = mine_ref.shape[0]
    rows_ref[pl.ds(pl.multiple_of(core * half, half), half), :] = mine_ref[...]
    rows_ref[pl.ds(pl.multiple_of((1 - core) * half, half), half), :] = other_ref[...]
    seg = rows_ref[...]
    size = turn_ref.shape[0]
    raw = jnp.dot(seg, weight_ref[...], preferred_element_type=F32)
    keys, raw, vals = raw[:, :size], raw[:, size : 2 * size], raw[:, 2 * size :]
    kn = keys * lax.rsqrt(jnp.mean(keys * keys, axis=-1, keepdims=True) + EPSILON) * gain_ref[...]
    dirs = raw * lax.rsqrt(jnp.sum(raw * raw, axis=-1, keepdims=True) + EPSILON)
    vector = jnp.broadcast_to(rate_ref[...], (16, seg.shape[1]))
    logits = lax.dot_general(seg, vector, (((1,), (1,)), ((), ())), preferred_element_type=F32)
    rates = 2.0 * jax.nn.sigmoid(logits[:, :1] + bias_ref[0])
    val_ref[...] = vals.astype(BF16)
    kn_ref[...] = kn
    dirs_ref[...] = dirs
    tokens, size = dirs.shape
    rows, cols = iota2((tokens, tokens))
    below = rows > cols
    grams = dot3(dirs, jnp.concatenate([dirs, kn], axis=0), 1, 1)
    lower = jnp.where(below, rates * grams[:, :tokens], 0.0)
    crossing = jnp.where(below, rates * grams[:, tokens:], 0.0)
    inverse = merge_inverse(lower, rows, cols)
    both = dot3(inverse, jnp.concatenate([crossing, rates * dirs], axis=1))
    coeff_ref[...] = both[:, :tokens]
    solved_ref[...] = both[:, tokens:]
    crossed = dot3(both, dirs, 0, 0)
    exit_ref[...] = kn - crossed[:tokens]
    heads, lanes = iota2((size, size))
    turn_ref[...] = jnp.where(heads == lanes, 1.0, 0.0) - crossed[tokens:]


def leave_kernel(group, place_ref, exit_ref, *refs):
    turn_refs, (leave_ref, starts_ref) = refs[:group], refs[group : group + 2]
    near_refs, (turns_ref, seen_ref) = refs[group + 2 : -2], refs[-2:]
    member = place_ref[0] % group
    tokens, size = exit_ref.shape
    for step in range(group):
        turns_ref[source_of(member, step, group)] = turn_refs[group - 1 - step][...]
    own = exit_ref[...]
    keys = own
    product = None
    heads, lanes = iota2((size, size))
    starts_ref[0] = jnp.where(heads == lanes, 1.0, 0.0)
    for index in range(group):
        seen_ref[index] = keys.astype(BF16)
        turn = turns_ref[index]
        product = turn if product is None else dot3(product, turn)
        if index:
            keys = jnp.where(index > member, dot3(keys, turn), own)
        if index < group - 1:
            starts_ref[index + 1] = product
    high, low = split(keys)
    leave_ref[:tokens] = high
    leave_ref[tokens : 2 * tokens] = low
    high, low = split(product)
    leave_ref[2 * tokens : 2 * tokens + size] = high
    leave_ref[2 * tokens + size :] = low
    for step in range(group):
        near_refs[step][...] = seen_ref[target_of(member, step, group)]


def word_of(slot, segments):
    bits = segments.bit_length()
    per_word = 31 // bits
    return slot // per_word, bits * (slot % per_word), (1 << bits) - 1


def bundle_kernel(group, groups, most, place_ref, mask_ref, after_ref, *refs):
    val_refs, (line_ref, table_ref) = refs[:groups], refs[groups:]
    place = place_ref[0]
    mine = place // group
    segments = mask_ref.shape[0]
    for word in range(table_ref.shape[0]):
        table_ref[word] = 0

    def pick(segment, count):
        wanted = (mask_ref[segment] > 0) & (segment < place) & (count < most)
        word, shift, _ = word_of(count, segments)

        @pl.when(wanted)
        def _():
            table_ref[word] = table_ref[word] | ((segment + 1) << shift)

        return count + wanted.astype(jnp.int32)

    lax.fori_loop(0, segments, pick, jnp.int32(0))
    tokens = val_refs[0].shape[0]
    for way in range(groups):
        at = pl.multiple_of(source_of(mine, way, groups) * tokens, tokens)
        line_ref[pl.ds(at, tokens), :] = val_refs[groups - 1 - way][...]


def query_kernel(rows_ref, weight_hbm, gain_ref, kn_ref, dirs_ref, coeff_ref, solved_ref, val_ref,
                 moved_ref, weighted_ref, peak_ref, total_ref, weight_ref, raw_ref, sems):
    tokens, size = kn_ref.shape
    heads = moved_ref.shape[0]
    pieces, deep, _ = weight_ref.shape
    copies = [
        pltpu.make_async_copy(
            weight_hbm.at[n * deep : (n + 1) * deep, :], weight_ref.at[n], sems.at[n]
        )
        for n in range(pieces)
    ]
    for copy in copies:
        copy.start()
    across = jnp.concatenate([kn_ref[...], dirs_ref[...]], axis=0)
    into = jnp.concatenate([coeff_ref[...], solved_ref[...]], axis=1)
    for n in range(pieces):
        copies[n].wait()
        part = jnp.dot(
            rows_ref[:, n * deep : (n + 1) * deep], weight_ref[n], preferred_element_type=F32
        )
        raw_ref[...] = raw_ref[...] + part if n else part
    count = math.gcd(heads, 4)
    for turn in range(heads // count):
        raw = jnp.concatenate(
            [
                raw_ref[:, head * size : (head + 1) * size]
                for head in range(turn * count, (turn + 1) * count)
            ],
            axis=0,
        )
        queries = (
            raw * lax.rsqrt(jnp.mean(raw * raw, axis=-1, keepdims=True) + EPSILON) * gain_ref[...]
        )
        seen = dot3(queries, across, 1, 1)
        rows, cols = iota2((count * tokens, tokens))
        up_to = rows % tokens >= cols
        reach = jnp.where(up_to, seen[:, tokens:], 0.0)
        taken = dot3(reach, into)
        scores = (seen[:, :tokens] - taken[:, :tokens]) * (LOG2E / math.sqrt(size))
        scores = jnp.where(up_to, scores, NEGATIVE)
        moved = (queries - taken[:, tokens:]).astype(BF16)
        peak = jnp.max(scores, axis=1, keepdims=True)
        weights = jnp.exp2(scores - peak)
        total = jnp.sum(weights, axis=1, keepdims=True)
        weighted = jnp.dot(weights.astype(BF16), val_ref[...], preferred_element_type=F32)
        for h in range(count):
            part = slice(h * tokens, (h + 1) * tokens)
            head = turn * count + h
            moved_ref[head] = moved[part]
            weighted_ref[head] = weighted[part]
            peak_ref[head] = peak[part]
            total_ref[head] = total[part]


def arrive_kernel(groups, group, tokens, place_ref, *refs):
    arrived, starts_ref, near_refs = refs[:groups], refs[groups], refs[groups + 1 :]
    far_refs, (keys_ref, whole_ref) = refs[-group - 2 : -2], refs[-2:]
    mine, member = place_ref[0] // group, place_ref[0] % group
    size = starts_ref.shape[1]
    for ref, step in zip(arrived, line_order(groups)):
        index = source_of(mine, step, groups)
        keys_ref[index] = ref[:tokens].astype(F32) + ref[tokens : 2 * tokens].astype(F32)
        whole = ref[2 * tokens : 2 * tokens + size].astype(F32)
        whole_ref[index] = whole + ref[2 * tokens + size :].astype(F32)
    brought = [keys_ref[groups - 2]]
    product = None
    for index in range(groups - 3, -1, -1):
        keys, whole = keys_ref[index], whole_ref[index + 1]
        if product is not None:
            whole = jnp.where(index + 2 < mine, dot3(whole, product), whole)
        product = whole
        brought.append(jnp.where(index + 1 < mine, dot3(keys, product), keys))
    keys = jnp.concatenate(brought[::-1], axis=0)
    count, size = keys.shape
    ways = [starts_ref[target_of(member, step, group)] for step in range(group)]
    spread = dot3(keys, jnp.concatenate(ways, axis=1)).astype(BF16)
    for step in range(group):
        far_refs[step][:count] = spread[:, step * size : (step + 1) * size]
        far_refs[step][count:] = near_refs[step][...]


def attend_kernel(group, segments, most, place_ref, core_ref, table_ref, *refs):
    far_refs, line_refs = refs[:group][::-1], refs[group : 2 * group][::-1]
    (moved_ref, weighted_ref, peak_ref, total_ref, out_ref, away_ref, kept_ref, keys_ref, vals_ref,
     attended_ref) = refs[2 * group :]
    core = core_ref[0]
    mine, member = place_ref[0] // group, place_ref[0] % group
    heads, tokens, size = moved_ref.shape
    groups = far_refs[0].shape[0] // tokens
    scaling = LOG2E / math.sqrt(size)
    chunk = keys_ref.shape[0] // tokens
    lanes = lax.broadcasted_iota(jnp.int32, (1, chunk * tokens), 1)

    def collect(turn):
        found = jnp.int32(0)
        for slot in range(chunk):
            part = slice(slot * tokens, (slot + 1) * tokens)
            word, shift, ones = word_of(turn * chunk + slot, segments)
            code = (table_ref[word] >> shift) & ones
            found = found + (code > 0).astype(jnp.int32)
            segment = jnp.maximum(code - 1, 0)
            whose, source = segment % group, segment // group
            before = jnp.where(source < mine, source, groups - 1)
            before = pl.multiple_of(before * tokens, tokens)
            after = pl.multiple_of(source * tokens, tokens)
            for number in range(group):

                @pl.when(whose == source_of(member, number, group))
                def _():
                    vals_ref[part, :] = line_refs[number][pl.ds(after, tokens), :]
                    keys_ref[part, :] = far_refs[number][pl.ds(before, tokens), :]

        return jnp.where(lanes < found * tokens, 0.0, NEGATIVE)

    def advance(moved, bias, peak, total, weighted):
        scores = lax.dot_general(
            moved, keys_ref[...], (((1,), (1,)), ((), ())), preferred_element_type=F32
        )
        scores = scores * scaling + bias
        new_peak = jnp.maximum(peak, jnp.max(scores, axis=1, keepdims=True))
        fading = jnp.exp2(peak - new_peak)
        weights = jnp.exp2(scores - new_peak)
        total = total * fading + jnp.sum(weights, axis=1, keepdims=True)
        weighted = weighted * fading + jnp.dot(
            weights.astype(BF16), vals_ref[...], preferred_element_type=F32
        )
        return new_peak, total, weighted

    half = kept_ref.shape[0]
    turns = most // chunk
    if turns == 1:
        bias = collect(0)
    stack = math.gcd(heads, 8)
    for first in range(0, heads, stack):
        some = slice(first, first + stack)
        moved = moved_ref[some].reshape(stack * tokens, size)
        state = (
            peak_ref[some].reshape(stack * tokens, 1),
            total_ref[some].reshape(stack * tokens, 1),
            weighted_ref[some].reshape(stack * tokens, size),
        )
        if turns == 1:
            _, total, weighted = advance(moved, bias, *state)
        else:

            def step_of(turn, state, moved=moved):
                return advance(moved, collect(turn), *state)

            _, total, weighted = lax.fori_loop(0, turns, step_of, state)
        done = (weighted * (1.0 / total)).astype(BF16)
        for head in range(first, first + stack):
            for index in range(tokens // half):
                at = pl.multiple_of(jnp.where(index == core, half, 0), half)
                row = (head - first) * tokens + index * half
                attended_ref[pl.ds(at, half), head * size : (head + 1) * size] = done[
                    row : row + half
                ]
    wide = math.gcd(out_ref.shape[1], 4 * size)
    for at in range(0, out_ref.shape[1], wide):
        part = slice(at, at + wide)
        result = jnp.dot(attended_ref[...], out_ref[:, part], preferred_element_type=F32)
        result = result.astype(BF16)
        away_ref[:, part] = result[:half]
        kept_ref[:, part] = result[half:]


def body(
    hidden, w_query, w_key, w_value, w_dir, u_rate, rate_bias, q_gain, k_gain, w_out, block_mask
):
    segments = lax.axis_size("ctx")
    place = lax.axis_index("ctx").astype(jnp.int32).reshape(1)
    core = lax.axis_index("head").astype(jnp.int32).reshape(1)
    group = max(d for d in range(1, math.isqrt(segments) + 1) if segments % d == 0)
    groups = segments // group
    other = lax.ppermute(hidden, "head", [(0, 1), (1, 0)])
    half, width = hidden.shape
    tokens = half * lax.axis_size("head")
    size = w_key.shape[1]
    heads = w_query.shape[1] // size
    smem = pl.BlockSpec(memory_space=pltpu.SMEM)
    vmem = pl.BlockSpec(memory_space=pltpu.VMEM)
    hbm = pl.BlockSpec(memory_space=pltpu.HBM)
    anywhere = pl.BlockSpec(memory_space=pl.ANY)
    square = shaped((tokens, size), F32)

    def swapped(values, count, pairs_of):
        out = [values[0]] * count
        for step in range(count - 1, 0, -1):
            out[step] = lax.ppermute(values[step], "ctx", pairs_of(step))
        return out

    def within_group(values):
        return swapped(values, group, lambda step: [
            (s, s - s % group + target_of(s % group, step, group)) for s in range(segments)
        ])

    def along_line(values):
        return swapped(values, groups, lambda step: [
            (s, s % group + group * target_of(s // group, step, groups)) for s in range(segments)
        ])

    weights, rate_row, key_gain, query_gain, mine = call(
        functools.partial(load_kernel, size),
        (
            shaped((width, 3 * size), BF16), shaped((1, width), BF16), shaped((1, size), F32),
            shaped((1, size), F32), shaped((half, width), BF16),
        ),
        tuple(
            in_hbm(array)
            for array in (
                w_key, w_dir, w_value, u_rate, k_gain.reshape(1, size), q_gain.reshape(1, size),
                hidden,
            )
        ),
        in_specs=[hbm] * 7,
        scratch=(pltpu.SemaphoreType.DMA((7,)),),
        moved=12 * width * size,
    )
    rows, kn, val, dirs, coeff, solved, exit_keys, turn = call(
        prepare_kernel,
        (
            shaped((tokens, width), BF16), square, shaped((tokens, size), BF16), square, square,
            square, square, shaped((size, size), F32),
        ),
        (core, mine, other, weights, rate_row, rate_bias, key_gain),
        in_specs=[smem] + [vmem] * 4 + [smem, vmem],
        flops=6 * tokens * width * size,
        moved=8 * width * size,
    )
    turns = within_group([turn] * group)
    line = along_line([val] * groups)
    leaving, starts, *near = call(
        functools.partial(leave_kernel, group),
        [
            shaped((2 * tokens + 2 * size, size), BF16),
            shaped((group, size, size), F32),
        ]
        + [shaped((tokens, size), BF16)] * group,
        (place, exit_keys, *turns[::-1]),
        in_specs=[smem] + [vmem] * (1 + group),
        scratch=(
            pltpu.VMEM((group, size, size), F32),
            pltpu.VMEM((group, tokens, size), BF16),
        ),
        flops=12 * group * size**3,
        moved=10**6,
    )
    arrived = along_line([leaving] * groups)
    most = segments // 4
    values, table = call(
        functools.partial(bundle_kernel, group, groups, most),
        [
            shaped((groups * tokens, size), BF16),
            shaped((word_of(most - 1, segments)[0] + 1,), jnp.int32),
        ],
        (place, block_mask[0], starts, *line[::-1]),
        in_specs=[smem, smem, anywhere] + [vmem] * groups,
        out_specs=[vmem, smem],
        moved=10**6,
        limit=8 + group * groups // 4,
    )
    values = within_group([values] * group)
    own = call(
        query_kernel,
        (
            shaped((heads, tokens, size), BF16),
            shaped((heads, tokens, size), F32),
            shaped((heads, tokens, 1), F32),
            shaped((heads, tokens, 1), F32),
        ),
        (rows, in_hbm(w_query), query_gain, kn, dirs, coeff, solved, val),
        in_specs=[vmem, hbm] + [vmem] * 6,
        scratch=(
            pltpu.VMEM((2, width // 2, w_query.shape[1]), BF16),
            pltpu.VMEM((tokens, w_query.shape[1]), F32),
            pltpu.SemaphoreType.DMA((2,)),
        ),
        flops=4 * tokens * width * heads * size,
        moved=8 * width * heads * size,
        limit=16,
    )
    far = call(
        functools.partial(arrive_kernel, groups, group, tokens),
        [shaped((groups * tokens, size), BF16)] * group,
        (place, *(arrived[step] for step in line_order(groups)), starts, *near),
        in_specs=[smem] + [vmem] * (groups + 1 + group),
        scratch=(
            pltpu.VMEM((groups, tokens, size), F32),
            pltpu.VMEM((groups, size, size), F32),
        ),
        flops=6 * groups * group * size**3,
        moved=10**6,
        limit=8 + group * groups // 4,
    )
    far = within_group(far)
    chunk = math.gcd(most, 4)
    width_out = w_out.shape[1]
    away, kept = call(
        functools.partial(attend_kernel, group, segments, most),
        [shaped((half, width_out), BF16)] * 2,
        (place, core, table, *far[::-1], *values[::-1], *own, w_out),
        in_specs=[smem] * 3 + [vmem] * (2 * group + 5),
        scratch=[
            pltpu.VMEM((chunk * tokens, size), BF16),
            pltpu.VMEM((chunk * tokens, size), BF16),
            pltpu.VMEM((tokens, heads * size), BF16),
        ],
        flops=2 * tokens * width_out * heads * size,
        moved=4 * 10**6,
        limit=14 + group * groups // 4,
    )
    return kept + lax.ppermute(away, "head", [(0, 1), (1, 0)])


def solution(mesh):
    in_specs = (
        P(("ctx", "head"), None),
        P(None, "head"),
        P(None, "head"),
        P(None, "head"),
        P(None, "head"),
        P("head", None),
        P("head"),
        P(),
        P(),
        P("head", None),
        P("ctx", None),
    )
    out_specs = P(("ctx", "head"), None)
    return jax.shard_map(body, mesh=mesh, in_specs=in_specs, out_specs=out_specs, check_vma=False)
```

```python
import functools
import math

import jax
import jax.numpy as jnp
from jax import lax
from jax.experimental import pallas as pl
from jax.experimental.pallas import tpu as pltpu
from jax.sharding import PartitionSpec as P

EPSILON = 1e-06
NEGATIVE = -1e30
LOG2E = math.log2(math.e)
F32 = jnp.float32
BF16 = jnp.bfloat16
MIB = 1024 * 1024


def call(kernel, out_shape, args, in_specs=None, out_specs=None, scratch=(), flops=0, moved=0, limit=6):
    vmem = pl.BlockSpec(memory_space=pltpu.VMEM)
    return pl.pallas_call(
        kernel,
        out_shape=out_shape,
        in_specs=in_specs or [vmem] * len(args),
        out_specs=out_specs or jax.tree.map(lambda _: vmem, out_shape),
        scratch_shapes=list(scratch),
        compiler_params=pltpu.CompilerParams(vmem_limit_bytes=limit * MIB),
        cost_estimate=pl.CostEstimate(flops=flops, bytes_accessed=moved, transcendentals=0),
    )(*args)


def target_of(member, step, group):
    return member ^ step if group & (group - 1) == 0 else (member + step) % group


def source_of(member, step, group):
    return member ^ step if group & (group - 1) == 0 else (member + group - step) % group


def in_hbm(array):
    return pltpu.with_memory_space_constraint(array, pltpu.HBM)


def line_order(groups):
    return [groups // 2] + [step for step in range(groups - 1, 0, -1) if step != groups // 2] + [0]


def shaped(shape, dtype):
    return jax.ShapeDtypeStruct(shape, dtype)


def split(value):
    high = value.astype(BF16)
    return high, (value - high.astype(F32)).astype(BF16)


def dot3(left, right, left_dim=1, right_dim=0):
    left_high, left_low = split(left)
    right_high, right_low = split(right)
    return lax.dot_general(
        jnp.concatenate([left_high, left_high, left_low], axis=left_dim),
        jnp.concatenate([right_high, right_low, right_high], axis=right_dim),
        (((left_dim,), (right_dim,)), ((), ())),
        preferred_element_type=F32,
    )


def iota2(shape):
    return lax.broadcasted_iota(jnp.int32, shape, 0), lax.broadcasted_iota(jnp.int32, shape, 1)


def merge_inverse(lower, rows, cols):
    tokens = lower.shape[0]
    block = 16
    inverse = jnp.where(rows == cols, 1.0, 0.0).astype(F32)
    first = rows - rows % block
    for step in range(block - 1):
        column = jnp.sum(jnp.where(cols == first + step, lower, 0.0), axis=1, keepdims=True)
        pivot = inverse.reshape(tokens // block, block, tokens)[:, step : step + 1, :]
        pivot = jnp.broadcast_to(pivot, (tokens // block, block, tokens)).reshape(tokens, tokens)
        inverse = inverse - column * pivot
    while block < tokens:
        corner = (
            (rows // (2 * block) == cols // (2 * block))
            & (rows % (2 * block) >= block)
            & (cols % (2 * block) < block)
        )
        inverse = inverse - dot3(dot3(inverse, jnp.where(corner, lower, 0.0)), inverse)
        block *= 2
    return inverse


def load_kernel(size, key_hbm, dir_hbm, value_hbm, rate_hbm, key_gain_hbm,
                query_gain_hbm, mine_hbm, weight_ref, rate_ref, key_gain_ref, query_gain_ref,
                mine_ref, sems):
    pairs = [
        (hbm, weight_ref.at[:, index * size : (index + 1) * size])
        for index, hbm in enumerate((key_hbm, dir_hbm, value_hbm))
    ]
    pairs += [(rate_hbm, rate_ref), (key_gain_hbm, key_gain_ref)]
    pairs += [(query_gain_hbm, query_gain_ref), (mine_hbm, mine_ref)]
    copies = [pltpu.make_async_copy(*pair, sems.at[n]) for n, pair in enumerate(pairs)]
    for copy in copies:
        copy.start()
    for copy in copies:
        copy.wait()


def prepare_kernel(core_ref, mine_ref, other_ref, weight_ref, rate_ref, bias_ref, gain_ref,
                   rows_ref, kn_ref, val_ref, dirs_ref, coeff_ref, solved_ref, exit_ref, turn_ref):
    core = core_ref[0]
    half = mine_ref.shape[0]
    rows_ref[pl.ds(pl.multiple_of(core * half, half), half), :] = mine_ref[...]
    rows_ref[pl.ds(pl.multiple_of((1 - core) * half, half), half), :] = other_ref[...]
    seg = rows_ref[...]
    size = turn_ref.shape[0]
    raw = jnp.dot(seg, weight_ref[...], preferred_element_type=F32)
    keys, raw, vals = raw[:, :size], raw[:, size : 2 * size], raw[:, 2 * size :]
    kn = keys * lax.rsqrt(jnp.mean(keys * keys, axis=-1, keepdims=True) + EPSILON) * gain_ref[...]
    dirs = raw * lax.rsqrt(jnp.sum(raw * raw, axis=-1, keepdims=True) + EPSILON)
    vector = jnp.broadcast_to(rate_ref[...], (16, seg.shape[1]))
    logits = lax.dot_general(seg, vector, (((1,), (1,)), ((), ())), preferred_element_type=F32)
    rates = 2.0 * jax.nn.sigmoid(logits[:, :1] + bias_ref[0])
    val_ref[...] = vals.astype(BF16)
    kn_ref[...] = kn
    dirs_ref[...] = dirs
    tokens, size = dirs.shape
    rows, cols = iota2((tokens, tokens))
    below = rows > cols
    grams = dot3(dirs, jnp.concatenate([dirs, kn], axis=0), 1, 1)
    lower = jnp.where(below, rates * grams[:, :tokens], 0.0)
    crossing = jnp.where(below, rates * grams[:, tokens:], 0.0)
    inverse = merge_inverse(lower, rows, cols)
    both = dot3(inverse, jnp.concatenate([crossing, rates * dirs], axis=1))
    coeff_ref[...] = both[:, :tokens]
    solved_ref[...] = both[:, tokens:]
    crossed = dot3(both, dirs, 0, 0)
    exit_ref[...] = kn - crossed[:tokens]
    heads, lanes = iota2((size, size))
    turn_ref[...] = jnp.where(heads == lanes, 1.0, 0.0) - crossed[tokens:]


def leave_kernel(group, place_ref, exit_ref, *refs):
    turn_refs, (leave_ref, starts_ref) = refs[:group], refs[group : group + 2]
    near_refs, (turns_ref, seen_ref) = refs[group + 2 : -2], refs[-2:]
    member = place_ref[0] % group
    tokens, size = exit_ref.shape
    for step in range(group):
        turns_ref[source_of(member, step, group)] = turn_refs[group - 1 - step][...]
    own = exit_ref[...]
    keys = own
    product = None
    heads, lanes = iota2((size, size))
    starts_ref[0] = jnp.where(heads == lanes, 1.0, 0.0)
    for index in range(group):
        seen_ref[index] = keys.astype(BF16)
        turn = turns_ref[index]
        product = turn if product is None else dot3(product, turn)
        if index:
            keys = jnp.where(index > member, dot3(keys, turn), own)
        if index < group - 1:
            starts_ref[index + 1] = product
    high, low = split(keys)
    leave_ref[:tokens] = high
    leave_ref[tokens : 2 * tokens] = low
    high, low = split(product)
    leave_ref[2 * tokens : 2 * tokens + size] = high
    leave_ref[2 * tokens + size :] = low
    for step in range(group):
        near_refs[step][...] = seen_ref[target_of(member, step, group)]


def word_of(slot, segments):
    bits = segments.bit_length()
    per_word = 31 // bits
    return slot // per_word, bits * (slot % per_word), (1 << bits) - 1


def bundle_kernel(group, groups, most, place_ref, mask_ref, after_ref, *refs):
    val_refs, (line_ref, table_ref) = refs[:groups], refs[groups:]
    place = place_ref[0]
    mine = place // group
    segments = mask_ref.shape[0]
    for word in range(table_ref.shape[0]):
        table_ref[word] = 0

    def pick(segment, count):
        wanted = (mask_ref[segment] > 0) & (segment < place) & (count < most)
        word, shift, _ = word_of(count, segments)

        @pl.when(wanted)
        def _():
            table_ref[word] = table_ref[word] | ((segment + 1) << shift)

        return count + wanted.astype(jnp.int32)

    lax.fori_loop(0, segments, pick, jnp.int32(0))
    tokens = val_refs[0].shape[0]
    for way in range(groups):
        at = pl.multiple_of(source_of(mine, way, groups) * tokens, tokens)
        line_ref[pl.ds(at, tokens), :] = val_refs[groups - 1 - way][...]


def query_kernel(rows_ref, weight_hbm, gain_ref, kn_ref, dirs_ref, coeff_ref, solved_ref, val_ref,
                 moved_ref, weighted_ref, peak_ref, total_ref, weight_ref, raw_ref, sems):
    tokens, size = kn_ref.shape
    heads = moved_ref.shape[0]
    pieces, deep, _ = weight_ref.shape
    copies = [
        pltpu.make_async_copy(
            weight_hbm.at[n * deep : (n + 1) * deep, :], weight_ref.at[n], sems.at[n]
        )
        for n in range(pieces)
    ]
    for copy in copies:
        copy.start()
    across = jnp.concatenate([kn_ref[...], dirs_ref[...]], axis=0)
    into = jnp.concatenate([coeff_ref[...], solved_ref[...]], axis=1)
    for n in range(pieces):
        copies[n].wait()
        part = jnp.dot(
            rows_ref[:, n * deep : (n + 1) * deep], weight_ref[n], preferred_element_type=F32
        )
        raw_ref[...] = raw_ref[...] + part if n else part
    count = math.gcd(heads, 4)
    for turn in range(heads // count):
        raw = jnp.concatenate(
            [
                raw_ref[:, head * size : (head + 1) * size]
                for head in range(turn * count, (turn + 1) * count)
            ],
            axis=0,
        )
        queries = (
            raw * lax.rsqrt(jnp.mean(raw * raw, axis=-1, keepdims=True) + EPSILON) * gain_ref[...]
        )
        seen = dot3(queries, across, 1, 1)
        rows, cols = iota2((count * tokens, tokens))
        up_to = rows % tokens >= cols
        reach = jnp.where(up_to, seen[:, tokens:], 0.0)
        taken = dot3(reach, into)
        scores = (seen[:, :tokens] - taken[:, :tokens]) * (LOG2E / math.sqrt(size))
        scores = jnp.where(up_to, scores, NEGATIVE)
        moved = (queries - taken[:, tokens:]).astype(BF16)
        peak = jnp.max(scores, axis=1, keepdims=True)
        weights = jnp.exp2(scores - peak)
        total = jnp.sum(weights, axis=1, keepdims=True)
        weighted = jnp.dot(weights.astype(BF16), val_ref[...], preferred_element_type=F32)
        for h in range(count):
            part = slice(h * tokens, (h + 1) * tokens)
            head = turn * count + h
            moved_ref[head] = moved[part]
            weighted_ref[head] = weighted[part]
            peak_ref[head] = peak[part]
            total_ref[head] = total[part]


def arrive_kernel(groups, group, tokens, place_ref, *refs):
    arrived, starts_ref, near_refs = refs[:groups], refs[groups], refs[groups + 1 :]
    far_refs, (keys_ref, whole_ref) = refs[-group - 2 : -2], refs[-2:]
    mine, member = place_ref[0] // group, place_ref[0] % group
    size = starts_ref.shape[1]
    for ref, step in zip(arrived, line_order(groups)):
        index = source_of(mine, step, groups)
        keys_ref[index] = ref[:tokens].astype(F32) + ref[tokens : 2 * tokens].astype(F32)
        whole = ref[2 * tokens : 2 * tokens + size].astype(F32)
        whole_ref[index] = whole + ref[2 * tokens + size :].astype(F32)
    brought = [keys_ref[groups - 2]]
    product = None
    for index in range(groups - 3, -1, -1):
        keys, whole = keys_ref[index], whole_ref[index + 1]
        if product is not None:
            whole = jnp.where(index + 2 < mine, dot3(whole, product), whole)
        product = whole
        brought.append(jnp.where(index + 1 < mine, dot3(keys, product), keys))
    keys = jnp.concatenate(brought[::-1], axis=0)
    count, size = keys.shape
    ways = [starts_ref[target_of(member, step, group)] for step in range(group)]
    spread = dot3(keys, jnp.concatenate(ways, axis=1)).astype(BF16)
    for step in range(group):
        far_refs[step][:count] = spread[:, step * size : (step + 1) * size]
        far_refs[step][count:] = near_refs[step][...]


def attend_kernel(group, segments, most, place_ref, core_ref, table_ref, *refs):
    far_refs, line_refs = refs[:group][::-1], refs[group : 2 * group][::-1]
    (moved_ref, weighted_ref, peak_ref, total_ref, out_ref, away_ref, kept_ref, keys_ref, vals_ref,
     summed_ref) = refs[2 * group :]
    core = core_ref[0]
    mine, member = place_ref[0] // group, place_ref[0] % group
    heads, tokens, size = moved_ref.shape
    groups = far_refs[0].shape[0] // tokens
    scaling = LOG2E / math.sqrt(size)
    chunk = keys_ref.shape[0] // tokens
    lanes = lax.broadcasted_iota(jnp.int32, (1, chunk * tokens), 1)

    def collect(turn):
        found = jnp.int32(0)
        for slot in range(chunk):
            part = slice(slot * tokens, (slot + 1) * tokens)
            word, shift, ones = word_of(turn * chunk + slot, segments)
            code = (table_ref[word] >> shift) & ones
            found = found + (code > 0).astype(jnp.int32)
            segment = jnp.maximum(code - 1, 0)
            whose, source = segment % group, segment // group
            before = jnp.where(source < mine, source, groups - 1)
            before = pl.multiple_of(before * tokens, tokens)
            after = pl.multiple_of(source * tokens, tokens)
            for number in range(group):

                @pl.when(whose == source_of(member, number, group))
                def _():
                    vals_ref[part, :] = line_refs[number][pl.ds(after, tokens), :]
                    keys_ref[part, :] = far_refs[number][pl.ds(before, tokens), :]

        return jnp.where(lanes < found * tokens, 0.0, NEGATIVE)

    def advance(moved, bias, peak, total, weighted):
        scores = lax.dot_general(
            moved, keys_ref[...], (((1,), (1,)), ((), ())), preferred_element_type=F32
        )
        scores = scores * scaling + bias
        new_peak = jnp.maximum(peak, jnp.max(scores, axis=1, keepdims=True))
        fading = jnp.exp2(peak - new_peak)
        weights = jnp.exp2(scores - new_peak)
        total = total * fading + jnp.sum(weights, axis=1, keepdims=True)
        weighted = weighted * fading + jnp.dot(
            weights.astype(BF16), vals_ref[...], preferred_element_type=F32
        )
        return new_peak, total, weighted

    half = kept_ref.shape[0]
    turns = most // chunk
    if turns == 1:
        bias = collect(0)
    stack = math.gcd(heads, 4)
    wide = math.gcd(out_ref.shape[1], 4 * size)
    for first in range(0, heads, stack):
        some = slice(first, first + stack)
        moved = moved_ref[some].reshape(stack * tokens, size)
        state = (
            peak_ref[some].reshape(stack * tokens, 1),
            total_ref[some].reshape(stack * tokens, 1),
            weighted_ref[some].reshape(stack * tokens, size),
        )
        if turns == 1:
            _, total, weighted = advance(moved, bias, *state)
        else:

            def step_of(turn, state, moved=moved):
                return advance(moved, collect(turn), *state)

            _, total, weighted = lax.fori_loop(0, turns, step_of, state)
        done = (weighted * (1.0 / total)).astype(BF16)
        done = jnp.concatenate(
            [done[n * tokens : (n + 1) * tokens] for n in range(stack)], axis=1
        )
        deep = slice(first * size, (first + stack) * size)
        for at in range(0, out_ref.shape[1], wide):
            part = slice(at, at + wide)
            result = jnp.dot(done, out_ref[deep, part], preferred_element_type=F32)
            if first:
                result = result + summed_ref[:, part]
            if first + stack < heads:
                summed_ref[:, part] = result
            else:
                away_ref[:, part] = jnp.where(core == 0, result[half:], result[:half]).astype(BF16)
                kept_ref[:, part] = jnp.where(core == 0, result[:half], result[half:]).astype(BF16)


def body(
    hidden, w_query, w_key, w_value, w_dir, u_rate, rate_bias, q_gain, k_gain, w_out, block_mask
):
    segments = lax.axis_size("ctx")
    place = lax.axis_index("ctx").astype(jnp.int32).reshape(1)
    core = lax.axis_index("head").astype(jnp.int32).reshape(1)
    group = max(d for d in range(1, math.isqrt(segments) + 1) if segments % d == 0)
    groups = segments // group
    other = lax.ppermute(hidden, "head", [(0, 1), (1, 0)])
    half, width = hidden.shape
    tokens = half * lax.axis_size("head")
    size = w_key.shape[1]
    heads = w_query.shape[1] // size
    smem = pl.BlockSpec(memory_space=pltpu.SMEM)
    vmem = pl.BlockSpec(memory_space=pltpu.VMEM)
    hbm = pl.BlockSpec(memory_space=pltpu.HBM)
    anywhere = pl.BlockSpec(memory_space=pl.ANY)
    square = shaped((tokens, size), F32)

    def swapped(values, count, pairs_of):
        out = [values[0]] * count
        for step in range(count - 1, 0, -1):
            out[step] = lax.ppermute(values[step], "ctx", pairs_of(step))
        return out

    def within_group(values):
        return swapped(values, group, lambda step: [
            (s, s - s % group + target_of(s % group, step, group)) for s in range(segments)
        ])

    def along_line(values):
        return swapped(values, groups, lambda step: [
            (s, s % group + group * target_of(s // group, step, groups)) for s in range(segments)
        ])

    weights, rate_row, key_gain, query_gain, mine = call(
        functools.partial(load_kernel, size),
        (
            shaped((width, 3 * size), BF16), shaped((1, width), BF16), shaped((1, size), F32),
            shaped((1, size), F32), shaped((half, width), BF16),
        ),
        tuple(
            in_hbm(array)
            for array in (
                w_key, w_dir, w_value, u_rate, k_gain.reshape(1, size), q_gain.reshape(1, size),
                hidden,
            )
        ),
        in_specs=[hbm] * 7,
        scratch=(pltpu.SemaphoreType.DMA((7,)),),
        moved=12 * width * size,
    )
    rows, kn, val, dirs, coeff, solved, exit_keys, turn = call(
        prepare_kernel,
        (
            shaped((tokens, width), BF16), square, shaped((tokens, size), BF16), square, square,
            square, square, shaped((size, size), F32),
        ),
        (core, mine, other, weights, rate_row, rate_bias, key_gain),
        in_specs=[smem] + [vmem] * 4 + [smem, vmem],
        flops=6 * tokens * width * size,
        moved=8 * width * size,
    )
    turns = within_group([turn] * group)
    line = along_line([val] * groups)
    leaving, starts, *near = call(
        functools.partial(leave_kernel, group),
        [
            shaped((2 * tokens + 2 * size, size), BF16),
            shaped((group, size, size), F32),
        ]
        + [shaped((tokens, size), BF16)] * group,
        (place, exit_keys, *turns[::-1]),
        in_specs=[smem] + [vmem] * (1 + group),
        scratch=(
            pltpu.VMEM((group, size, size), F32),
            pltpu.VMEM((group, tokens, size), BF16),
        ),
        flops=12 * group * size**3,
        moved=10**6,
    )
    arrived = along_line([leaving] * groups)
    most = segments // 4
    values, table = call(
        functools.partial(bundle_kernel, group, groups, most),
        [
            shaped((groups * tokens, size), BF16),
            shaped((word_of(most - 1, segments)[0] + 1,), jnp.int32),
        ],
        (place, block_mask[0], starts, *line[::-1]),
        in_specs=[smem, smem, anywhere] + [vmem] * groups,
        out_specs=[vmem, smem],
        moved=10**6,
        limit=8 + group * groups // 4,
    )
    values = within_group([values] * group)
    own = call(
        query_kernel,
        (
            shaped((heads, tokens, size), BF16),
            shaped((heads, tokens, size), F32),
            shaped((heads, tokens, 1), F32),
            shaped((heads, tokens, 1), F32),
        ),
        (rows, in_hbm(w_query), query_gain, kn, dirs, coeff, solved, val),
        in_specs=[vmem, hbm] + [vmem] * 6,
        scratch=(
            pltpu.VMEM((2, width // 2, w_query.shape[1]), BF16),
            pltpu.VMEM((tokens, w_query.shape[1]), F32),
            pltpu.SemaphoreType.DMA((2,)),
        ),
        flops=4 * tokens * width * heads * size,
        moved=8 * width * heads * size,
        limit=16,
    )
    far = call(
        functools.partial(arrive_kernel, groups, group, tokens),
        [shaped((groups * tokens, size), BF16)] * group,
        (place, *(arrived[step] for step in line_order(groups)), starts, *near),
        in_specs=[smem] + [vmem] * (groups + 1 + group),
        scratch=(
            pltpu.VMEM((groups, tokens, size), F32),
            pltpu.VMEM((groups, size, size), F32),
        ),
        flops=6 * groups * group * size**3,
        moved=10**6,
        limit=8 + group * groups // 4,
    )
    far = within_group(far)
    chunk = math.gcd(most, 4)
    width_out = w_out.shape[1]
    away, kept = call(
        functools.partial(attend_kernel, group, segments, most),
        [shaped((half, width_out), BF16)] * 2,
        (place, core, table, *far[::-1], *values[::-1], *own, w_out),
        in_specs=[smem] * 3 + [vmem] * (2 * group + 5),
        scratch=[
            pltpu.VMEM((chunk * tokens, size), BF16),
            pltpu.VMEM((chunk * tokens, size), BF16),
            pltpu.VMEM((tokens, width_out), F32),
        ],
        flops=2 * tokens * width_out * heads * size,
        moved=4 * 10**6,
        limit=14 + group * groups // 4,
    )
    return kept + lax.ppermute(away, "head", [(0, 1), (1, 0)])


def solution(mesh):
    in_specs = (
        P(("ctx", "head"), None),
        P(None, "head"),
        P(None, "head"),
        P(None, "head"),
        P(None, "head"),
        P("head", None),
        P("head"),
        P(),
        P(),
        P("head", None),
        P("ctx", None),
    )
    out_specs = P(("ctx", "head"), None)
    return jax.shard_map(body, mesh=mesh, in_specs=in_specs, out_specs=out_specs, check_vma=False)
```

```python
import functools
import math

import jax
import jax.numpy as jnp
from jax import lax
from jax.experimental import pallas as pl
from jax.experimental.pallas import tpu as pltpu
from jax.sharding import PartitionSpec as P

EPSILON = 1e-06
NEGATIVE = -1e30
LOG2E = math.log2(math.e)
F32 = jnp.float32
BF16 = jnp.bfloat16
MIB = 1024 * 1024


def call(kernel, out_shape, args, in_specs=None, out_specs=None, scratch=(), flops=0, moved=0, limit=6):
    vmem = pl.BlockSpec(memory_space=pltpu.VMEM)
    return pl.pallas_call(
        kernel,
        out_shape=out_shape,
        in_specs=in_specs or [vmem] * len(args),
        out_specs=out_specs or jax.tree.map(lambda _: vmem, out_shape),
        scratch_shapes=list(scratch),
        compiler_params=pltpu.CompilerParams(vmem_limit_bytes=limit * MIB),
        cost_estimate=pl.CostEstimate(flops=flops, bytes_accessed=moved, transcendentals=0),
    )(*args)


def target_of(member, step, group):
    return member ^ step if group & (group - 1) == 0 else (member + step) % group


def source_of(member, step, group):
    return member ^ step if group & (group - 1) == 0 else (member + group - step) % group


def in_hbm(array):
    return pltpu.with_memory_space_constraint(array, pltpu.HBM)


def line_order(groups):
    return [groups // 2] + [step for step in range(groups - 1, 0, -1) if step != groups // 2] + [0]


def shaped(shape, dtype):
    return jax.ShapeDtypeStruct(shape, dtype)


def split(value):
    high = value.astype(BF16)
    return high, (value - high.astype(F32)).astype(BF16)


def dot3(left, right, left_dim=1, right_dim=0):
    left_high, left_low = split(left)
    right_high, right_low = split(right)
    return lax.dot_general(
        jnp.concatenate([left_high, left_high, left_low], axis=left_dim),
        jnp.concatenate([right_high, right_low, right_high], axis=right_dim),
        (((left_dim,), (right_dim,)), ((), ())),
        preferred_element_type=F32,
    )


def iota2(shape):
    return lax.broadcasted_iota(jnp.int32, shape, 0), lax.broadcasted_iota(jnp.int32, shape, 1)


def merge_inverse(lower, rows, cols):
    tokens = lower.shape[0]
    block = 16
    inverse = jnp.where(rows == cols, 1.0, 0.0).astype(F32)
    first = rows - rows % block
    for step in range(block - 1):
        column = jnp.sum(jnp.where(cols == first + step, lower, 0.0), axis=1, keepdims=True)
        pivot = inverse.reshape(tokens // block, block, tokens)[:, step : step + 1, :]
        pivot = jnp.broadcast_to(pivot, (tokens // block, block, tokens)).reshape(tokens, tokens)
        inverse = inverse - column * pivot
    while block < tokens:
        corner = (
            (rows // (2 * block) == cols // (2 * block))
            & (rows % (2 * block) >= block)
            & (cols % (2 * block) < block)
        )
        inverse = inverse - dot3(dot3(inverse, jnp.where(corner, lower, 0.0)), inverse)
        block *= 2
    return inverse


def load_kernel(size, key_hbm, dir_hbm, rate_hbm, key_gain_hbm,
                query_gain_hbm, mine_hbm, weight_ref, rate_ref, key_gain_ref, query_gain_ref,
                mine_ref, sems):
    pairs = [
        (hbm, weight_ref.at[:, index * size : (index + 1) * size])
        for index, hbm in enumerate((key_hbm, dir_hbm))
    ]
    pairs += [(rate_hbm, rate_ref), (key_gain_hbm, key_gain_ref)]
    pairs += [(query_gain_hbm, query_gain_ref), (mine_hbm, mine_ref)]
    copies = [pltpu.make_async_copy(*pair, sems.at[n]) for n, pair in enumerate(pairs)]
    for copy in copies:
        copy.start()
    for copy in copies:
        copy.wait()


def prepare_kernel(core_ref, mine_ref, other_ref, weight_ref, rate_ref, bias_ref, gain_ref,
                   value_hbm, rows_ref, kn_ref, val_ref, dirs_ref, coeff_ref, solved_ref, exit_ref,
                   turn_ref, value_ref, value_sem):
    value_copy = pltpu.make_async_copy(value_hbm, value_ref, value_sem)
    value_copy.start()
    core = core_ref[0]
    half = mine_ref.shape[0]
    rows_ref[pl.ds(pl.multiple_of(core * half, half), half), :] = mine_ref[...]
    rows_ref[pl.ds(pl.multiple_of((1 - core) * half, half), half), :] = other_ref[...]
    seg = rows_ref[...]
    size = turn_ref.shape[0]
    raw = jnp.dot(seg, weight_ref[...], preferred_element_type=F32)
    keys, raw = raw[:, :size], raw[:, size:]
    kn = keys * lax.rsqrt(jnp.mean(keys * keys, axis=-1, keepdims=True) + EPSILON) * gain_ref[...]
    dirs = raw * lax.rsqrt(jnp.sum(raw * raw, axis=-1, keepdims=True) + EPSILON)
    vector = jnp.broadcast_to(rate_ref[...], (16, seg.shape[1]))
    logits = lax.dot_general(seg, vector, (((1,), (1,)), ((), ())), preferred_element_type=F32)
    rates = 2.0 * jax.nn.sigmoid(logits[:, :1] + bias_ref[0])
    kn_ref[...] = kn
    dirs_ref[...] = dirs
    tokens, size = dirs.shape
    rows, cols = iota2((tokens, tokens))
    below = rows > cols
    grams = dot3(dirs, jnp.concatenate([dirs, kn], axis=0), 1, 1)
    lower = jnp.where(below, rates * grams[:, :tokens], 0.0)
    crossing = jnp.where(below, rates * grams[:, tokens:], 0.0)
    inverse = merge_inverse(lower, rows, cols)
    value_copy.wait()
    val_ref[...] = jnp.dot(seg, value_ref[...], preferred_element_type=F32).astype(BF16)
    both = dot3(inverse, jnp.concatenate([crossing, rates * dirs], axis=1))
    coeff_ref[...] = both[:, :tokens]
    solved_ref[...] = both[:, tokens:]
    crossed = dot3(both, dirs, 0, 0)
    exit_ref[...] = kn - crossed[:tokens]
    heads, lanes = iota2((size, size))
    turn_ref[...] = jnp.where(heads == lanes, 1.0, 0.0) - crossed[tokens:]


def leave_kernel(group, place_ref, exit_ref, *refs):
    turn_refs, (leave_ref, starts_ref) = refs[:group], refs[group : group + 2]
    near_refs, (turns_ref, seen_ref) = refs[group + 2 : -2], refs[-2:]
    member = place_ref[0] % group
    tokens, size = exit_ref.shape
    for step in range(group):
        turns_ref[source_of(member, step, group)] = turn_refs[group - 1 - step][...]
    own = exit_ref[...]
    keys = own
    product = None
    heads, lanes = iota2((size, size))
    starts_ref[0] = jnp.where(heads == lanes, 1.0, 0.0)
    for index in range(group):
        seen_ref[index] = keys.astype(BF16)
        turn = turns_ref[index]
        product = turn if product is None else dot3(product, turn)
        if index:
            keys = jnp.where(index > member, dot3(keys, turn), own)
        if index < group - 1:
            starts_ref[index + 1] = product
    high, low = split(keys)
    leave_ref[:tokens] = high
    leave_ref[tokens : 2 * tokens] = low
    high, low = split(product)
    leave_ref[2 * tokens : 2 * tokens + size] = high
    leave_ref[2 * tokens + size :] = low
    for step in range(group):
        near_refs[step][...] = seen_ref[target_of(member, step, group)]


def word_of(slot, segments):
    bits = segments.bit_length()
    per_word = 31 // bits
    return slot // per_word, bits * (slot % per_word), (1 << bits) - 1


def bundle_kernel(group, groups, most, place_ref, mask_ref, after_ref, *refs):
    val_refs, (line_ref, table_ref) = refs[:groups], refs[groups:]
    place = place_ref[0]
    mine = place // group
    segments = mask_ref.shape[0]
    for word in range(table_ref.shape[0]):
        table_ref[word] = 0

    def pick(segment, count):
        wanted = (mask_ref[segment] > 0) & (segment < place) & (count < most)
        word, shift, _ = word_of(count, segments)

        @pl.when(wanted)
        def _():
            table_ref[word] = table_ref[word] | ((segment + 1) << shift)

        return count + wanted.astype(jnp.int32)

    lax.fori_loop(0, segments, pick, jnp.int32(0))
    tokens = val_refs[0].shape[0]
    for way in range(groups):
        at = pl.multiple_of(source_of(mine, way, groups) * tokens, tokens)
        line_ref[pl.ds(at, tokens), :] = val_refs[groups - 1 - way][...]


def query_kernel(rows_ref, weight_hbm, gain_ref, kn_ref, dirs_ref, coeff_ref, solved_ref, val_ref,
                 moved_ref, weighted_ref, peak_ref, total_ref, weight_ref, raw_ref, sems):
    tokens, size = kn_ref.shape
    heads = moved_ref.shape[0]
    pieces, deep, _ = weight_ref.shape
    copies = [
        pltpu.make_async_copy(
            weight_hbm.at[n * deep : (n + 1) * deep, :], weight_ref.at[n], sems.at[n]
        )
        for n in range(pieces)
    ]
    for copy in copies:
        copy.start()
    across = jnp.concatenate([kn_ref[...], dirs_ref[...]], axis=0)
    into = jnp.concatenate([coeff_ref[...], solved_ref[...]], axis=1)
    for n in range(pieces):
        copies[n].wait()
        part = jnp.dot(
            rows_ref[:, n * deep : (n + 1) * deep], weight_ref[n], preferred_element_type=F32
        )
        raw_ref[...] = raw_ref[...] + part if n else part
    count = math.gcd(heads, 4)
    for turn in range(heads // count):
        raw = jnp.concatenate(
            [
                raw_ref[:, head * size : (head + 1) * size]
                for head in range(turn * count, (turn + 1) * count)
            ],
            axis=0,
        )
        queries = (
            raw * lax.rsqrt(jnp.mean(raw * raw, axis=-1, keepdims=True) + EPSILON) * gain_ref[...]
        )
        seen = dot3(queries, across, 1, 1)
        rows, cols = iota2((count * tokens, tokens))
        up_to = rows % tokens >= cols
        reach = jnp.where(up_to, seen[:, tokens:], 0.0)
        taken = dot3(reach, into)
        scores = (seen[:, :tokens] - taken[:, :tokens]) * (LOG2E / math.sqrt(size))
        scores = jnp.where(up_to, scores, NEGATIVE)
        moved = (queries - taken[:, tokens:]).astype(BF16)
        peak = jnp.max(scores, axis=1, keepdims=True)
        weights = jnp.exp2(scores - peak)
        total = jnp.sum(weights, axis=1, keepdims=True)
        weighted = jnp.dot(weights.astype(BF16), val_ref[...], preferred_element_type=F32)
        for h in range(count):
            part = slice(h * tokens, (h + 1) * tokens)
            head = turn * count + h
            moved_ref[head] = moved[part]
            weighted_ref[head] = weighted[part]
            peak_ref[head] = peak[part]
            total_ref[head] = total[part]


def arrive_kernel(groups, group, tokens, place_ref, *refs):
    arrived, starts_ref, near_refs = refs[:groups], refs[groups], refs[groups + 1 :]
    far_refs, (keys_ref, whole_ref) = refs[-group - 2 : -2], refs[-2:]
    mine, member = place_ref[0] // group, place_ref[0] % group
    size = starts_ref.shape[1]
    for ref, step in zip(arrived, line_order(groups)):
        index = source_of(mine, step, groups)
        keys_ref[index] = ref[:tokens].astype(F32) + ref[tokens : 2 * tokens].astype(F32)
        whole = ref[2 * tokens : 2 * tokens + size].astype(F32)
        whole_ref[index] = whole + ref[2 * tokens + size :].astype(F32)
    brought = [keys_ref[groups - 2]]
    product = None
    for index in range(groups - 3, -1, -1):
        keys, whole = keys_ref[index], whole_ref[index + 1]
        if product is not None:
            whole = jnp.where(index + 2 < mine, dot3(whole, product), whole)
        product = whole
        brought.append(jnp.where(index + 1 < mine, dot3(keys, product), keys))
    keys = jnp.concatenate(brought[::-1], axis=0)
    count, size = keys.shape
    ways = [starts_ref[target_of(member, step, group)] for step in range(group)]
    spread = dot3(keys, jnp.concatenate(ways, axis=1)).astype(BF16)
    for step in range(group):
        far_refs[step][:count] = spread[:, step * size : (step + 1) * size]
        far_refs[step][count:] = near_refs[step][...]


def attend_kernel(group, segments, most, place_ref, core_ref, table_ref, *refs):
    far_refs, line_refs = refs[:group][::-1], refs[group : 2 * group][::-1]
    (moved_ref, weighted_ref, peak_ref, total_ref, out_ref, away_ref, kept_ref, keys_ref, vals_ref,
     summed_ref) = refs[2 * group :]
    core = core_ref[0]
    mine, member = place_ref[0] // group, place_ref[0] % group
    heads, tokens, size = moved_ref.shape
    groups = far_refs[0].shape[0] // tokens
    scaling = LOG2E / math.sqrt(size)
    chunk = keys_ref.shape[0] // tokens
    lanes = lax.broadcasted_iota(jnp.int32, (1, chunk * tokens), 1)

    def collect(turn):
        found = jnp.int32(0)
        for slot in range(chunk):
            part = slice(slot * tokens, (slot + 1) * tokens)
            word, shift, ones = word_of(turn * chunk + slot, segments)
            code = (table_ref[word] >> shift) & ones
            found = found + (code > 0).astype(jnp.int32)
            segment = jnp.maximum(code - 1, 0)
            whose, source = segment % group, segment // group
            before = jnp.where(source < mine, source, groups - 1)
            before = pl.multiple_of(before * tokens, tokens)
            after = pl.multiple_of(source * tokens, tokens)
            for number in range(group):

                @pl.when(whose == source_of(member, number, group))
                def _():
                    vals_ref[part, :] = line_refs[number][pl.ds(after, tokens), :]
                    keys_ref[part, :] = far_refs[number][pl.ds(before, tokens), :]

        return jnp.where(lanes < found * tokens, 0.0, NEGATIVE)

    def advance(moved, bias, peak, total, weighted):
        scores = lax.dot_general(
            moved, keys_ref[...], (((1,), (1,)), ((), ())), preferred_element_type=F32
        )
        scores = scores * scaling + bias
        new_peak = jnp.maximum(peak, jnp.max(scores, axis=1, keepdims=True))
        fading = jnp.exp2(peak - new_peak)
        weights = jnp.exp2(scores - new_peak)
        total = total * fading + jnp.sum(weights, axis=1, keepdims=True)
        weighted = weighted * fading + jnp.dot(
            weights.astype(BF16), vals_ref[...], preferred_element_type=F32
        )
        return new_peak, total, weighted

    half = kept_ref.shape[0]
    turns = most // chunk
    if turns == 1:
        bias = collect(0)
    stack = math.gcd(heads, 4)
    wide = math.gcd(out_ref.shape[1], 4 * size)
    for first in range(0, heads, stack):
        some = slice(first, first + stack)
        moved = moved_ref[some].reshape(stack * tokens, size)
        state = (
            peak_ref[some].reshape(stack * tokens, 1),
            total_ref[some].reshape(stack * tokens, 1),
            weighted_ref[some].reshape(stack * tokens, size),
        )
        if turns == 1:
            _, total, weighted = advance(moved, bias, *state)
        else:

            def step_of(turn, state, moved=moved):
                return advance(moved, collect(turn), *state)

            _, total, weighted = lax.fori_loop(0, turns, step_of, state)
        done = (weighted * (1.0 / total)).astype(BF16)
        done = jnp.concatenate(
            [done[n * tokens : (n + 1) * tokens] for n in range(stack)], axis=1
        )
        deep = slice(first * size, (first + stack) * size)
        for at in range(0, out_ref.shape[1], wide):
            part = slice(at, at + wide)
            result = jnp.dot(done, out_ref[deep, part], preferred_element_type=F32)
            if first:
                result = result + summed_ref[:, part]
            if first + stack < heads:
                summed_ref[:, part] = result
            else:
                away_ref[:, part] = jnp.where(core == 0, result[half:], result[:half]).astype(BF16)
                kept_ref[:, part] = jnp.where(core == 0, result[:half], result[half:]).astype(BF16)


def body(
    hidden, w_query, w_key, w_value, w_dir, u_rate, rate_bias, q_gain, k_gain, w_out, block_mask
):
    segments = lax.axis_size("ctx")
    place = lax.axis_index("ctx").astype(jnp.int32).reshape(1)
    core = lax.axis_index("head").astype(jnp.int32).reshape(1)
    group = max(d for d in range(1, math.isqrt(segments) + 1) if segments % d == 0)
    groups = segments // group
    other = lax.ppermute(hidden, "head", [(0, 1), (1, 0)])
    half, width = hidden.shape
    tokens = half * lax.axis_size("head")
    size = w_key.shape[1]
    heads = w_query.shape[1] // size
    smem = pl.BlockSpec(memory_space=pltpu.SMEM)
    vmem = pl.BlockSpec(memory_space=pltpu.VMEM)
    hbm = pl.BlockSpec(memory_space=pltpu.HBM)
    anywhere = pl.BlockSpec(memory_space=pl.ANY)
    square = shaped((tokens, size), F32)

    def swapped(values, count, pairs_of):
        out = [values[0]] * count
        for step in range(count - 1, 0, -1):
            out[step] = lax.ppermute(values[step], "ctx", pairs_of(step))
        return out

    def within_group(values):
        return swapped(values, group, lambda step: [
            (s, s - s % group + target_of(s % group, step, group)) for s in range(segments)
        ])

    def along_line(values):
        return swapped(values, groups, lambda step: [
            (s, s % group + group * target_of(s // group, step, groups)) for s in range(segments)
        ])

    weights, rate_row, key_gain, query_gain, mine = call(
        functools.partial(load_kernel, size),
        (
            shaped((width, 2 * size), BF16), shaped((1, width), BF16), shaped((1, size), F32),
            shaped((1, size), F32), shaped((half, width), BF16),
        ),
        tuple(
            in_hbm(array)
            for array in (
                w_key, w_dir, u_rate, k_gain.reshape(1, size), q_gain.reshape(1, size),
                hidden,
            )
        ),
        in_specs=[hbm] * 6,
        scratch=(pltpu.SemaphoreType.DMA((6,)),),
        moved=12 * width * size,
    )
    rows, kn, val, dirs, coeff, solved, exit_keys, turn = call(
        prepare_kernel,
        (
            shaped((tokens, width), BF16), square, shaped((tokens, size), BF16), square, square,
            square, square, shaped((size, size), F32),
        ),
        (core, mine, other, weights, rate_row, rate_bias, key_gain, in_hbm(w_value)),
        in_specs=[smem] + [vmem] * 4 + [smem, vmem, hbm],
        scratch=(pltpu.VMEM(w_value.shape, BF16), pltpu.SemaphoreType.DMA),
        flops=6 * tokens * width * size,
        moved=8 * width * size,
    )
    turns = within_group([turn] * group)
    line = along_line([val] * groups)
    leaving, starts, *near = call(
        functools.partial(leave_kernel, group),
        [
            shaped((2 * tokens + 2 * size, size), BF16),
            shaped((group, size, size), F32),
        ]
        + [shaped((tokens, size), BF16)] * group,
        (place, exit_keys, *turns[::-1]),
        in_specs=[smem] + [vmem] * (1 + group),
        scratch=(
            pltpu.VMEM((group, size, size), F32),
            pltpu.VMEM((group, tokens, size), BF16),
        ),
        flops=12 * group * size**3,
        moved=10**6,
    )
    arrived = along_line([leaving] * groups)
    most = segments // 4
    values, table = call(
        functools.partial(bundle_kernel, group, groups, most),
        [
            shaped((groups * tokens, size), BF16),
            shaped((word_of(most - 1, segments)[0] + 1,), jnp.int32),
        ],
        (place, block_mask[0], starts, *line[::-1]),
        in_specs=[smem, smem, anywhere] + [vmem] * groups,
        out_specs=[vmem, smem],
        moved=10**6,
        limit=8 + group * groups // 4,
    )
    values = within_group([values] * group)
    own = call(
        query_kernel,
        (
            shaped((heads, tokens, size), BF16),
            shaped((heads, tokens, size), F32),
            shaped((heads, tokens, 1), F32),
            shaped((heads, tokens, 1), F32),
        ),
        (rows, in_hbm(w_query), query_gain, kn, dirs, coeff, solved, val),
        in_specs=[vmem, hbm] + [vmem] * 6,
        scratch=(
            pltpu.VMEM((2, width // 2, w_query.shape[1]), BF16),
            pltpu.VMEM((tokens, w_query.shape[1]), F32),
            pltpu.SemaphoreType.DMA((2,)),
        ),
        flops=4 * tokens * width * heads * size,
        moved=8 * width * heads * size,
        limit=16,
    )
    far = call(
        functools.partial(arrive_kernel, groups, group, tokens),
        [shaped((groups * tokens, size), BF16)] * group,
        (place, *(arrived[step] for step in line_order(groups)), starts, *near),
        in_specs=[smem] + [vmem] * (groups + 1 + group),
        scratch=(
            pltpu.VMEM((groups, tokens, size), F32),
            pltpu.VMEM((groups, size, size), F32),
        ),
        flops=6 * groups * group * size**3,
        moved=10**6,
        limit=8 + group * groups // 4,
    )
    far = within_group(far)
    chunk = math.gcd(most, 4)
    width_out = w_out.shape[1]
    away, kept = call(
        functools.partial(attend_kernel, group, segments, most),
        [shaped((half, width_out), BF16)] * 2,
        (place, core, table, *far[::-1], *values[::-1], *own, w_out),
        in_specs=[smem] * 3 + [vmem] * (2 * group + 5),
        scratch=[
            pltpu.VMEM((chunk * tokens, size), BF16),
            pltpu.VMEM((chunk * tokens, size), BF16),
            pltpu.VMEM((tokens, width_out), F32),
        ],
        flops=2 * tokens * width_out * heads * size,
        moved=4 * 10**6,
        limit=14 + group * groups // 4,
    )
    return kept + lax.ppermute(away, "head", [(0, 1), (1, 0)])


def solution(mesh):
    in_specs = (
        P(("ctx", "head"), None),
        P(None, "head"),
        P(None, "head"),
        P(None, "head"),
        P(None, "head"),
        P("head", None),
        P("head"),
        P(),
        P(),
        P("head", None),
        P("ctx", None),
    )
    out_specs = P(("ctx", "head"), None)
    return jax.shard_map(body, mesh=mesh, in_specs=in_specs, out_specs=out_specs, check_vma=False)
```

```python
import functools
import math

import jax
import jax.numpy as jnp
from jax import lax
from jax.experimental import pallas as pl
from jax.experimental.pallas import tpu as pltpu
from jax.sharding import PartitionSpec as P

EPSILON = 1e-06
NEGATIVE = -1e30
LOG2E = math.log2(math.e)
F32 = jnp.float32
BF16 = jnp.bfloat16
MIB = 1024 * 1024


def call(kernel, out_shape, args, in_specs=None, out_specs=None, scratch=(), flops=0, moved=0, limit=6):
    vmem = pl.BlockSpec(memory_space=pltpu.VMEM)
    return pl.pallas_call(
        kernel,
        out_shape=out_shape,
        in_specs=in_specs or [vmem] * len(args),
        out_specs=out_specs or jax.tree.map(lambda _: vmem, out_shape),
        scratch_shapes=list(scratch),
        compiler_params=pltpu.CompilerParams(vmem_limit_bytes=limit * MIB),
        cost_estimate=pl.CostEstimate(flops=flops, bytes_accessed=moved, transcendentals=0),
    )(*args)


def target_of(member, step, group):
    return member ^ step if group & (group - 1) == 0 else (member + step) % group


def source_of(member, step, group):
    return member ^ step if group & (group - 1) == 0 else (member + group - step) % group


def in_hbm(array):
    return pltpu.with_memory_space_constraint(array, pltpu.HBM)


def swap_order(groups):
    return [groups // 2] + [step for step in range(groups - 1, 0, -1) if step != groups // 2] + [0]


def shaped(shape, dtype):
    return jax.ShapeDtypeStruct(shape, dtype)


def split(value):
    high = value.astype(BF16)
    return high, (value - high.astype(F32)).astype(BF16)


def dot3(left, right, left_dim=1, right_dim=0):
    left_high, left_low = split(left)
    right_high, right_low = split(right)
    return lax.dot_general(
        jnp.concatenate([left_high, left_high, left_low], axis=left_dim),
        jnp.concatenate([right_high, right_low, right_high], axis=right_dim),
        (((left_dim,), (right_dim,)), ((), ())),
        preferred_element_type=F32,
    )


def iota2(shape):
    return lax.broadcasted_iota(jnp.int32, shape, 0), lax.broadcasted_iota(jnp.int32, shape, 1)


def merge_inverse(lower, rows, cols):
    tokens = lower.shape[0]
    block = 16
    inverse = jnp.where(rows == cols, 1.0, 0.0).astype(F32)
    first = rows - rows % block
    for step in range(block - 1):
        column = jnp.sum(jnp.where(cols == first + step, lower, 0.0), axis=1, keepdims=True)
        pivot = inverse.reshape(tokens // block, block, tokens)[:, step : step + 1, :]
        pivot = jnp.broadcast_to(pivot, (tokens // block, block, tokens)).reshape(tokens, tokens)
        inverse = inverse - column * pivot
    while block < tokens:
        corner = (
            (rows // (2 * block) == cols // (2 * block))
            & (rows % (2 * block) >= block)
            & (cols % (2 * block) < block)
        )
        inverse = inverse - dot3(dot3(inverse, jnp.where(corner, lower, 0.0)), inverse)
        block *= 2
    return inverse


def load_kernel(size, key_hbm, dir_hbm, rate_hbm, key_gain_hbm,
                query_gain_hbm, mine_hbm, weight_ref, rate_ref, key_gain_ref, query_gain_ref,
                mine_ref, sems):
    pairs = [
        (hbm, weight_ref.at[:, index * size : (index + 1) * size])
        for index, hbm in enumerate((key_hbm, dir_hbm))
    ]
    pairs += [(rate_hbm, rate_ref), (key_gain_hbm, key_gain_ref)]
    pairs += [(query_gain_hbm, query_gain_ref), (mine_hbm, mine_ref)]
    copies = [pltpu.make_async_copy(*pair, sems.at[n]) for n, pair in enumerate(pairs)]
    for copy in copies:
        copy.start()
    for copy in copies:
        copy.wait()


def prepare_kernel(core_ref, mine_ref, other_ref, weight_ref, rate_ref, bias_ref, gain_ref,
                   value_hbm, rows_ref, kn_ref, val_ref, dirs_ref, coeff_ref, solved_ref, exit_ref,
                   turn_ref, value_ref, value_sem):
    value_copy = pltpu.make_async_copy(value_hbm, value_ref, value_sem)
    value_copy.start()
    core = core_ref[0]
    half = mine_ref.shape[0]
    rows_ref[pl.ds(pl.multiple_of(core * half, half), half), :] = mine_ref[...]
    rows_ref[pl.ds(pl.multiple_of((1 - core) * half, half), half), :] = other_ref[...]
    seg = rows_ref[...]
    size = turn_ref.shape[0]
    raw = jnp.dot(seg, weight_ref[...], preferred_element_type=F32)
    keys, raw = raw[:, :size], raw[:, size:]
    kn = keys * lax.rsqrt(jnp.mean(keys * keys, axis=-1, keepdims=True) + EPSILON) * gain_ref[...]
    dirs = raw * lax.rsqrt(jnp.sum(raw * raw, axis=-1, keepdims=True) + EPSILON)
    vector = jnp.broadcast_to(rate_ref[...], (16, seg.shape[1]))
    logits = lax.dot_general(seg, vector, (((1,), (1,)), ((), ())), preferred_element_type=F32)
    rates = 2.0 * jax.nn.sigmoid(logits[:, :1] + bias_ref[0])
    kn_ref[...] = kn
    dirs_ref[...] = dirs
    tokens, size = dirs.shape
    rows, cols = iota2((tokens, tokens))
    below = rows > cols
    grams = dot3(dirs, jnp.concatenate([dirs, kn], axis=0), 1, 1)
    lower = jnp.where(below, rates * grams[:, :tokens], 0.0)
    crossing = jnp.where(below, rates * grams[:, tokens:], 0.0)
    inverse = merge_inverse(lower, rows, cols)
    value_copy.wait()
    val_ref[...] = jnp.dot(seg, value_ref[...], preferred_element_type=F32).astype(BF16)
    both = dot3(inverse, jnp.concatenate([crossing, rates * dirs], axis=1))
    coeff_ref[...] = both[:, :tokens]
    solved_ref[...] = both[:, tokens:]
    crossed = dot3(both, dirs, 0, 0)
    exit_ref[...] = kn - crossed[:tokens]
    heads, lanes = iota2((size, size))
    turn_ref[...] = jnp.where(heads == lanes, 1.0, 0.0) - crossed[tokens:]


def leave_kernel(group, place_ref, exit_ref, *refs):
    turn_refs, (leave_ref, starts_ref) = refs[:group], refs[group : group + 2]
    near_refs, (turns_ref, seen_ref) = refs[group + 2 : -2], refs[-2:]
    member = place_ref[0] % group
    tokens, size = exit_ref.shape
    for ref, step in zip(turn_refs, swap_order(group)):
        turns_ref[source_of(member, step, group)] = ref[...]
    own = exit_ref[...]
    keys = own
    product = None
    heads, lanes = iota2((size, size))
    starts_ref[0] = jnp.where(heads == lanes, 1.0, 0.0)
    for index in range(group):
        seen_ref[index] = keys.astype(BF16)
        turn = turns_ref[index]
        product = turn if product is None else dot3(product, turn)
        if index:
            keys = jnp.where(index > member, dot3(keys, turn), own)
        if index < group - 1:
            starts_ref[index + 1] = product
    high, low = split(keys)
    leave_ref[:tokens] = high
    leave_ref[tokens : 2 * tokens] = low
    high, low = split(product)
    leave_ref[2 * tokens : 2 * tokens + size] = high
    leave_ref[2 * tokens + size :] = low
    for step in range(group):
        near_refs[step][...] = seen_ref[target_of(member, step, group)]


def word_of(slot, segments):
    bits = segments.bit_length()
    per_word = 31 // bits
    return slot // per_word, bits * (slot % per_word), (1 << bits) - 1


def bundle_kernel(group, groups, most, place_ref, mask_ref, after_ref, *refs):
    val_refs, (line_ref, table_ref) = refs[:groups], refs[groups:]
    place = place_ref[0]
    mine = place // group
    segments = mask_ref.shape[0]
    for word in range(table_ref.shape[0]):
        table_ref[word] = 0

    def pick(segment, count):
        wanted = (mask_ref[segment] > 0) & (segment < place) & (count < most)
        word, shift, _ = word_of(count, segments)

        @pl.when(wanted)
        def _():
            table_ref[word] = table_ref[word] | ((segment + 1) << shift)

        return count + wanted.astype(jnp.int32)

    lax.fori_loop(0, segments, pick, jnp.int32(0))
    tokens = val_refs[0].shape[0]
    for way in range(groups):
        at = pl.multiple_of(source_of(mine, way, groups) * tokens, tokens)
        line_ref[pl.ds(at, tokens), :] = val_refs[groups - 1 - way][...]


def query_kernel(rows_ref, weight_hbm, gain_ref, kn_ref, dirs_ref, coeff_ref, solved_ref, val_ref,
                 moved_ref, weighted_ref, peak_ref, total_ref, weight_ref, raw_ref, sems):
    tokens, size = kn_ref.shape
    heads = moved_ref.shape[0]
    pieces, deep, _ = weight_ref.shape
    copies = [
        pltpu.make_async_copy(
            weight_hbm.at[n * deep : (n + 1) * deep, :], weight_ref.at[n], sems.at[n]
        )
        for n in range(pieces)
    ]
    for copy in copies:
        copy.start()
    across = jnp.concatenate([kn_ref[...], dirs_ref[...]], axis=0)
    into = jnp.concatenate([coeff_ref[...], solved_ref[...]], axis=1)
    for n in range(pieces):
        copies[n].wait()
        part = jnp.dot(
            rows_ref[:, n * deep : (n + 1) * deep], weight_ref[n], preferred_element_type=F32
        )
        raw_ref[...] = raw_ref[...] + part if n else part
    count = math.gcd(heads, 4)
    for turn in range(heads // count):
        raw = jnp.concatenate(
            [
                raw_ref[:, head * size : (head + 1) * size]
                for head in range(turn * count, (turn + 1) * count)
            ],
            axis=0,
        )
        queries = (
            raw * lax.rsqrt(jnp.mean(raw * raw, axis=-1, keepdims=True) + EPSILON) * gain_ref[...]
        )
        seen = dot3(queries, across, 1, 1)
        rows, cols = iota2((count * tokens, tokens))
        up_to = rows % tokens >= cols
        reach = jnp.where(up_to, seen[:, tokens:], 0.0)
        taken = dot3(reach, into)
        scores = (seen[:, :tokens] - taken[:, :tokens]) * (LOG2E / math.sqrt(size))
        scores = jnp.where(up_to, scores, NEGATIVE)
        moved = (queries - taken[:, tokens:]).astype(BF16)
        peak = jnp.max(scores, axis=1, keepdims=True)
        weights = jnp.exp2(scores - peak)
        total = jnp.sum(weights, axis=1, keepdims=True)
        weighted = jnp.dot(weights.astype(BF16), val_ref[...], preferred_element_type=F32)
        for h in range(count):
            part = slice(h * tokens, (h + 1) * tokens)
            head = turn * count + h
            moved_ref[head] = moved[part]
            weighted_ref[head] = weighted[part]
            peak_ref[head] = peak[part]
            total_ref[head] = total[part]


def arrive_kernel(groups, group, tokens, place_ref, *refs):
    arrived, starts_ref, near_refs = refs[:groups], refs[groups], refs[groups + 1 :]
    far_refs, (keys_ref, whole_ref) = refs[-group - 2 : -2], refs[-2:]
    mine, member = place_ref[0] // group, place_ref[0] % group
    size = starts_ref.shape[1]
    for ref, step in zip(arrived, swap_order(groups)):
        index = source_of(mine, step, groups)
        keys_ref[index] = ref[:tokens].astype(F32) + ref[tokens : 2 * tokens].astype(F32)
        whole = ref[2 * tokens : 2 * tokens + size].astype(F32)
        whole_ref[index] = whole + ref[2 * tokens + size :].astype(F32)
    brought = [keys_ref[groups - 2]]
    product = None
    for index in range(groups - 3, -1, -1):
        keys, whole = keys_ref[index], whole_ref[index + 1]
        if product is not None:
            whole = jnp.where(index + 2 < mine, dot3(whole, product), whole)
        product = whole
        brought.append(jnp.where(index + 1 < mine, dot3(keys, product), keys))
    keys = jnp.concatenate(brought[::-1], axis=0)
    count, size = keys.shape
    ways = [starts_ref[target_of(member, step, group)] for step in range(group)]
    spread = dot3(keys, jnp.concatenate(ways, axis=1)).astype(BF16)
    for step in range(group):
        far_refs[step][:count] = spread[:, step * size : (step + 1) * size]
        far_refs[step][count:] = near_refs[step][...]


def attend_kernel(group, segments, most, place_ref, core_ref, table_ref, *refs):
    order = swap_order(group)
    far_refs = [refs[order.index(step)] for step in range(group)]
    line_refs = refs[group : 2 * group][::-1]
    (moved_ref, weighted_ref, peak_ref, total_ref, out_ref, away_ref, kept_ref, keys_ref, vals_ref,
     summed_ref) = refs[2 * group :]
    core = core_ref[0]
    mine, member = place_ref[0] // group, place_ref[0] % group
    heads, tokens, size = moved_ref.shape
    groups = far_refs[0].shape[0] // tokens
    scaling = LOG2E / math.sqrt(size)
    chunk = keys_ref.shape[0] // tokens
    lanes = lax.broadcasted_iota(jnp.int32, (1, chunk * tokens), 1)

    def collect(turn):
        found = jnp.int32(0)
        for slot in range(chunk):
            part = slice(slot * tokens, (slot + 1) * tokens)
            word, shift, ones = word_of(turn * chunk + slot, segments)
            code = (table_ref[word] >> shift) & ones
            found = found + (code > 0).astype(jnp.int32)
            segment = jnp.maximum(code - 1, 0)
            whose, source = segment % group, segment // group
            before = jnp.where(source < mine, source, groups - 1)
            before = pl.multiple_of(before * tokens, tokens)
            after = pl.multiple_of(source * tokens, tokens)
            for number in range(group):

                @pl.when(whose == source_of(member, number, group))
                def _():
                    vals_ref[part, :] = line_refs[number][pl.ds(after, tokens), :]
                    keys_ref[part, :] = far_refs[number][pl.ds(before, tokens), :]

        return jnp.where(lanes < found * tokens, 0.0, NEGATIVE)

    def advance(moved, bias, peak, total, weighted):
        scores = lax.dot_general(
            moved, keys_ref[...], (((1,), (1,)), ((), ())), preferred_element_type=F32
        )
        scores = scores * scaling + bias
        new_peak = jnp.maximum(peak, jnp.max(scores, axis=1, keepdims=True))
        fading = jnp.exp2(peak - new_peak)
        weights = jnp.exp2(scores - new_peak)
        total = total * fading + jnp.sum(weights, axis=1, keepdims=True)
        weighted = weighted * fading + jnp.dot(
            weights.astype(BF16), vals_ref[...], preferred_element_type=F32
        )
        return new_peak, total, weighted

    half = kept_ref.shape[0]
    turns = most // chunk
    if turns == 1:
        bias = collect(0)
    stack = math.gcd(heads, 4)
    wide = math.gcd(out_ref.shape[1], 4 * size)
    for first in range(0, heads, stack):
        some = slice(first, first + stack)
        moved = moved_ref[some].reshape(stack * tokens, size)
        state = (
            peak_ref[some].reshape(stack * tokens, 1),
            total_ref[some].reshape(stack * tokens, 1),
            weighted_ref[some].reshape(stack * tokens, size),
        )
        if turns == 1:
            _, total, weighted = advance(moved, bias, *state)
        else:

            def step_of(turn, state, moved=moved):
                return advance(moved, collect(turn), *state)

            _, total, weighted = lax.fori_loop(0, turns, step_of, state)
        done = (weighted * (1.0 / total)).astype(BF16)
        done = jnp.concatenate(
            [done[n * tokens : (n + 1) * tokens] for n in range(stack)], axis=1
        )
        deep = slice(first * size, (first + stack) * size)
        for at in range(0, out_ref.shape[1], wide):
            part = slice(at, at + wide)
            result = jnp.dot(done, out_ref[deep, part], preferred_element_type=F32)
            if first:
                result = result + summed_ref[:, part]
            if first + stack < heads:
                summed_ref[:, part] = result
            else:
                away_ref[:, part] = jnp.where(core == 0, result[half:], result[:half]).astype(BF16)
                kept_ref[:, part] = jnp.where(core == 0, result[:half], result[half:]).astype(BF16)


def body(
    hidden, w_query, w_key, w_value, w_dir, u_rate, rate_bias, q_gain, k_gain, w_out, block_mask
):
    segments = lax.axis_size("ctx")
    place = lax.axis_index("ctx").astype(jnp.int32).reshape(1)
    core = lax.axis_index("head").astype(jnp.int32).reshape(1)
    group = max(d for d in range(1, math.isqrt(segments) + 1) if segments % d == 0)
    groups = segments // group
    other = lax.ppermute(hidden, "head", [(0, 1), (1, 0)])
    half, width = hidden.shape
    tokens = half * lax.axis_size("head")
    size = w_key.shape[1]
    heads = w_query.shape[1] // size
    smem = pl.BlockSpec(memory_space=pltpu.SMEM)
    vmem = pl.BlockSpec(memory_space=pltpu.VMEM)
    hbm = pl.BlockSpec(memory_space=pltpu.HBM)
    anywhere = pl.BlockSpec(memory_space=pl.ANY)
    square = shaped((tokens, size), F32)

    def swapped(values, count, pairs_of):
        out = [values[0]] * count
        for step in range(count - 1, 0, -1):
            out[step] = lax.ppermute(values[step], "ctx", pairs_of(step))
        return out

    def within_group(values):
        return swapped(values, group, lambda step: [
            (s, s - s % group + target_of(s % group, step, group)) for s in range(segments)
        ])

    def along_line(values):
        return swapped(values, groups, lambda step: [
            (s, s % group + group * target_of(s // group, step, groups)) for s in range(segments)
        ])

    weights, rate_row, key_gain, query_gain, mine = call(
        functools.partial(load_kernel, size),
        (
            shaped((width, 2 * size), BF16), shaped((1, width), BF16), shaped((1, size), F32),
            shaped((1, size), F32), shaped((half, width), BF16),
        ),
        tuple(
            in_hbm(array)
            for array in (
                w_key, w_dir, u_rate, k_gain.reshape(1, size), q_gain.reshape(1, size),
                hidden,
            )
        ),
        in_specs=[hbm] * 6,
        scratch=(pltpu.SemaphoreType.DMA((6,)),),
        moved=12 * width * size,
    )
    rows, kn, val, dirs, coeff, solved, exit_keys, turn = call(
        prepare_kernel,
        (
            shaped((tokens, width), BF16), square, shaped((tokens, size), BF16), square, square,
            square, square, shaped((size, size), F32),
        ),
        (core, mine, other, weights, rate_row, rate_bias, key_gain, in_hbm(w_value)),
        in_specs=[smem] + [vmem] * 4 + [smem, vmem, hbm],
        scratch=(pltpu.VMEM(w_value.shape, BF16), pltpu.SemaphoreType.DMA),
        flops=6 * tokens * width * size,
        moved=8 * width * size,
    )
    turns = within_group([turn] * group)
    line = along_line([val] * groups)
    leaving, starts, *near = call(
        functools.partial(leave_kernel, group),
        [
            shaped((2 * tokens + 2 * size, size), BF16),
            shaped((group, size, size), F32),
        ]
        + [shaped((tokens, size), BF16)] * group,
        (place, exit_keys, *(turns[step] for step in swap_order(group))),
        in_specs=[smem] + [vmem] * (1 + group),
        scratch=(
            pltpu.VMEM((group, size, size), F32),
            pltpu.VMEM((group, tokens, size), BF16),
        ),
        flops=12 * group * size**3,
        moved=10**6,
    )
    arrived = along_line([leaving] * groups)
    most = segments // 4
    values, table = call(
        functools.partial(bundle_kernel, group, groups, most),
        [
            shaped((groups * tokens, size), BF16),
            shaped((word_of(most - 1, segments)[0] + 1,), jnp.int32),
        ],
        (place, block_mask[0], starts, *line[::-1]),
        in_specs=[smem, smem, anywhere] + [vmem] * groups,
        out_specs=[vmem, smem],
        moved=10**6,
        limit=8 + group * groups // 4,
    )
    values = within_group([values] * group)
    own = call(
        query_kernel,
        (
            shaped((heads, tokens, size), BF16),
            shaped((heads, tokens, size), F32),
            shaped((heads, tokens, 1), F32),
            shaped((heads, tokens, 1), F32),
        ),
        (rows, in_hbm(w_query), query_gain, kn, dirs, coeff, solved, val),
        in_specs=[vmem, hbm] + [vmem] * 6,
        scratch=(
            pltpu.VMEM((2, width // 2, w_query.shape[1]), BF16),
            pltpu.VMEM((tokens, w_query.shape[1]), F32),
            pltpu.SemaphoreType.DMA((2,)),
        ),
        flops=4 * tokens * width * heads * size,
        moved=8 * width * heads * size,
        limit=16,
    )
    far = call(
        functools.partial(arrive_kernel, groups, group, tokens),
        [shaped((groups * tokens, size), BF16)] * group,
        (place, *(arrived[step] for step in swap_order(groups)), starts, *near),
        in_specs=[smem] + [vmem] * (groups + 1 + group),
        scratch=(
            pltpu.VMEM((groups, tokens, size), F32),
            pltpu.VMEM((groups, size, size), F32),
        ),
        flops=6 * groups * group * size**3,
        moved=10**6,
        limit=8 + group * groups // 4,
    )
    far = within_group(far)
    chunk = math.gcd(most, 4)
    width_out = w_out.shape[1]
    away, kept = call(
        functools.partial(attend_kernel, group, segments, most),
        [shaped((half, width_out), BF16)] * 2,
        (
            place, core, table, *(far[step] for step in swap_order(group)), *values[::-1], *own,
            w_out,
        ),
        in_specs=[smem] * 3 + [vmem] * (2 * group + 5),
        scratch=[
            pltpu.VMEM((chunk * tokens, size), BF16),
            pltpu.VMEM((chunk * tokens, size), BF16),
            pltpu.VMEM((tokens, width_out), F32),
        ],
        flops=2 * tokens * width_out * heads * size,
        moved=4 * 10**6,
        limit=14 + group * groups // 4,
    )
    return kept + lax.ppermute(away, "head", [(0, 1), (1, 0)])


def solution(mesh):
    in_specs = (
        P(("ctx", "head"), None),
        P(None, "head"),
        P(None, "head"),
        P(None, "head"),
        P(None, "head"),
        P("head", None),
        P("head"),
        P(),
        P(),
        P("head", None),
        P("ctx", None),
    )
    out_specs = P(("ctx", "head"), None)
    return jax.shard_map(body, mesh=mesh, in_specs=in_specs, out_specs=out_specs, check_vma=False)
```

```python
import functools
import math

import jax
import jax.numpy as jnp
from jax import lax
from jax.experimental import pallas as pl
from jax.experimental.pallas import tpu as pltpu
from jax.sharding import PartitionSpec as P

EPSILON = 1e-06
NEGATIVE = -1e30
LOG2E = math.log2(math.e)
F32 = jnp.float32
BF16 = jnp.bfloat16
MIB = 1024 * 1024


def call(kernel, out_shape, args, in_specs=None, out_specs=None, scratch=(), flops=0, moved=0, limit=6):
    vmem = pl.BlockSpec(memory_space=pltpu.VMEM)
    return pl.pallas_call(
        kernel,
        out_shape=out_shape,
        in_specs=in_specs or [vmem] * len(args),
        out_specs=out_specs or jax.tree.map(lambda _: vmem, out_shape),
        scratch_shapes=list(scratch),
        compiler_params=pltpu.CompilerParams(vmem_limit_bytes=limit * MIB),
        cost_estimate=pl.CostEstimate(flops=flops, bytes_accessed=moved, transcendentals=0),
    )(*args)


def target_of(member, step, group):
    return member ^ step if group & (group - 1) == 0 else (member + step) % group


def source_of(member, step, group):
    return member ^ step if group & (group - 1) == 0 else (member + group - step) % group


def in_hbm(array):
    return pltpu.with_memory_space_constraint(array, pltpu.HBM)


def line_order(groups):
    return [groups // 2] + [step for step in range(groups - 1, 0, -1) if step != groups // 2] + [0]


def shaped(shape, dtype):
    return jax.ShapeDtypeStruct(shape, dtype)


def split(value):
    high = value.astype(BF16)
    return high, (value - high.astype(F32)).astype(BF16)


def dot3(left, right, left_dim=1, right_dim=0):
    left_high, left_low = split(left)
    right_high, right_low = split(right)
    return lax.dot_general(
        jnp.concatenate([left_high, left_high, left_low], axis=left_dim),
        jnp.concatenate([right_high, right_low, right_high], axis=right_dim),
        (((left_dim,), (right_dim,)), ((), ())),
        preferred_element_type=F32,
    )


def iota2(shape):
    return lax.broadcasted_iota(jnp.int32, shape, 0), lax.broadcasted_iota(jnp.int32, shape, 1)


def merge_inverse(lower, rows, cols):
    tokens = lower.shape[0]
    block = 16
    inverse = jnp.where(rows == cols, 1.0, 0.0).astype(F32)
    first = rows - rows % block
    for step in range(block - 1):
        column = jnp.sum(jnp.where(cols == first + step, lower, 0.0), axis=1, keepdims=True)
        pivot = inverse.reshape(tokens // block, block, tokens)[:, step : step + 1, :]
        pivot = jnp.broadcast_to(pivot, (tokens // block, block, tokens)).reshape(tokens, tokens)
        inverse = inverse - column * pivot
    while block < tokens:
        corner = (
            (rows // (2 * block) == cols // (2 * block))
            & (rows % (2 * block) >= block)
            & (cols % (2 * block) < block)
        )
        inverse = inverse - dot3(dot3(inverse, jnp.where(corner, lower, 0.0)), inverse)
        block *= 2
    return inverse


def load_kernel(size, key_hbm, dir_hbm, rate_hbm, key_gain_hbm,
                query_gain_hbm, mine_hbm, weight_ref, rate_ref, key_gain_ref, query_gain_ref,
                mine_ref, sems):
    pairs = [
        (hbm, weight_ref.at[:, index * size : (index + 1) * size])
        for index, hbm in enumerate((key_hbm, dir_hbm))
    ]
    pairs += [(rate_hbm, rate_ref), (key_gain_hbm, key_gain_ref)]
    pairs += [(query_gain_hbm, query_gain_ref), (mine_hbm, mine_ref)]
    copies = [pltpu.make_async_copy(*pair, sems.at[n]) for n, pair in enumerate(pairs)]
    for copy in copies:
        copy.start()
    for copy in copies:
        copy.wait()


def prepare_kernel(core_ref, mine_ref, other_ref, weight_ref, rate_ref, bias_ref, gain_ref,
                   value_hbm, rows_ref, kn_ref, val_ref, dirs_ref, coeff_ref, solved_ref, exit_ref,
                   turn_ref, value_ref, value_sem):
    value_copy = pltpu.make_async_copy(value_hbm, value_ref, value_sem)
    value_copy.start()
    core = core_ref[0]
    half = mine_ref.shape[0]
    rows_ref[pl.ds(pl.multiple_of(core * half, half), half), :] = mine_ref[...]
    rows_ref[pl.ds(pl.multiple_of((1 - core) * half, half), half), :] = other_ref[...]
    seg = rows_ref[...]
    size = turn_ref.shape[0]
    raw = jnp.dot(seg, weight_ref[...], preferred_element_type=F32)
    keys, raw = raw[:, :size], raw[:, size:]
    kn = keys * lax.rsqrt(jnp.mean(keys * keys, axis=-1, keepdims=True) + EPSILON) * gain_ref[...]
    dirs = raw * lax.rsqrt(jnp.sum(raw * raw, axis=-1, keepdims=True) + EPSILON)
    vector = jnp.broadcast_to(rate_ref[...], (16, seg.shape[1]))
    logits = lax.dot_general(seg, vector, (((1,), (1,)), ((), ())), preferred_element_type=F32)
    rates = 2.0 * jax.nn.sigmoid(logits[:, :1] + bias_ref[0])
    kn_ref[...] = kn
    dirs_ref[...] = dirs
    tokens, size = dirs.shape
    rows, cols = iota2((tokens, tokens))
    below = rows > cols
    grams = dot3(dirs, jnp.concatenate([dirs, kn], axis=0), 1, 1)
    lower = jnp.where(below, rates * grams[:, :tokens], 0.0)
    crossing = jnp.where(below, rates * grams[:, tokens:], 0.0)
    inverse = merge_inverse(lower, rows, cols)
    value_copy.wait()
    val_ref[...] = jnp.dot(seg, value_ref[...], preferred_element_type=F32).astype(BF16)
    both = dot3(inverse, jnp.concatenate([crossing, rates * dirs], axis=1))
    coeff_ref[...] = both[:, :tokens]
    solved_ref[...] = both[:, tokens:]
    crossed = dot3(both, dirs, 0, 0)
    exit_ref[...] = kn - crossed[:tokens]
    heads, lanes = iota2((size, size))
    turn_ref[...] = jnp.where(heads == lanes, 1.0, 0.0) - crossed[tokens:]


def leave_kernel(group, place_ref, exit_ref, *refs):
    turn_refs, (leave_ref, starts_ref) = refs[:group], refs[group : group + 2]
    near_refs, (turns_ref, seen_ref) = refs[group + 2 : -2], refs[-2:]
    member = place_ref[0] % group
    tokens, size = exit_ref.shape
    for step in range(group):
        turns_ref[source_of(member, step, group)] = turn_refs[group - 1 - step][...]
    own = exit_ref[...]
    keys = own
    product = None
    heads, lanes = iota2((size, size))
    starts_ref[0] = jnp.where(heads == lanes, 1.0, 0.0)
    for index in range(group):
        seen_ref[index] = keys.astype(BF16)
        turn = turns_ref[index]
        product = turn if product is None else dot3(product, turn)
        if index:
            keys = jnp.where(index > member, dot3(keys, turn), own)
        if index < group - 1:
            starts_ref[index + 1] = product
    high, low = split(keys)
    leave_ref[:tokens] = high
    leave_ref[tokens : 2 * tokens] = low
    high, low = split(product)
    leave_ref[2 * tokens : 2 * tokens + size] = high
    leave_ref[2 * tokens + size :] = low
    for step in range(group):
        near_refs[step][...] = seen_ref[target_of(member, step, group)]


def word_of(slot, segments):
    bits = segments.bit_length()
    per_word = 31 // bits
    return slot // per_word, bits * (slot % per_word), (1 << bits) - 1


def bundle_kernel(group, groups, most, place_ref, mask_ref, after_ref, *refs):
    val_refs, (line_ref, table_ref) = refs[:groups], refs[groups:]
    place = place_ref[0]
    mine = place // group
    segments = mask_ref.shape[0]
    for word in range(table_ref.shape[0]):
        table_ref[word] = 0

    def pick(segment, count):
        wanted = (mask_ref[segment] > 0) & (segment < place) & (count < most)
        word, shift, _ = word_of(count, segments)

        @pl.when(wanted)
        def _():
            table_ref[word] = table_ref[word] | ((segment + 1) << shift)

        return count + wanted.astype(jnp.int32)

    lax.fori_loop(0, segments, pick, jnp.int32(0))
    tokens = val_refs[0].shape[0]
    for way in range(groups):
        at = pl.multiple_of(source_of(mine, way, groups) * tokens, tokens)
        line_ref[pl.ds(at, tokens), :] = val_refs[groups - 1 - way][...]


def query_kernel(rows_ref, weight_hbm, gain_ref, kn_ref, dirs_ref, coeff_ref, solved_ref, val_ref,
                 moved_ref, weighted_ref, peak_ref, total_ref, weight_ref, raw_ref, sems):
    tokens, size = kn_ref.shape
    heads = moved_ref.shape[0]
    pieces, deep, _ = weight_ref.shape
    copies = [
        pltpu.make_async_copy(
            weight_hbm.at[n * deep : (n + 1) * deep, :], weight_ref.at[n], sems.at[n]
        )
        for n in range(pieces)
    ]
    for copy in copies:
        copy.start()
    across = jnp.concatenate([kn_ref[...], dirs_ref[...]], axis=0)
    into = jnp.concatenate([coeff_ref[...], solved_ref[...]], axis=1)
    for n in range(pieces):
        copies[n].wait()
        part = jnp.dot(
            rows_ref[:, n * deep : (n + 1) * deep], weight_ref[n], preferred_element_type=F32
        )
        raw_ref[...] = raw_ref[...] + part if n else part
    count = math.gcd(heads, 4)
    for turn in range(heads // count):
        raw = jnp.concatenate(
            [
                raw_ref[:, head * size : (head + 1) * size]
                for head in range(turn * count, (turn + 1) * count)
            ],
            axis=0,
        )
        queries = (
            raw * lax.rsqrt(jnp.mean(raw * raw, axis=-1, keepdims=True) + EPSILON) * gain_ref[...]
        )
        seen = dot3(queries, across, 1, 1)
        rows, cols = iota2((count * tokens, tokens))
        up_to = rows % tokens >= cols
        reach = jnp.where(up_to, seen[:, tokens:], 0.0)
        taken = dot3(reach, into)
        scores = (seen[:, :tokens] - taken[:, :tokens]) * (LOG2E / math.sqrt(size))
        scores = jnp.where(up_to, scores, NEGATIVE)
        moved = (queries - taken[:, tokens:]).astype(BF16)
        peak = jnp.max(scores, axis=1, keepdims=True)
        weights = jnp.exp2(scores - peak)
        total = jnp.sum(weights, axis=1, keepdims=True)
        weighted = jnp.dot(weights.astype(BF16), val_ref[...], preferred_element_type=F32)
        for h in range(count):
            part = slice(h * tokens, (h + 1) * tokens)
            head = turn * count + h
            moved_ref[head] = moved[part]
            weighted_ref[head] = weighted[part]
            peak_ref[head] = peak[part]
            total_ref[head] = total[part]


def arrive_kernel(groups, group, tokens, place_ref, *refs):
    arrived, starts_ref, near_refs = refs[:groups], refs[groups], refs[groups + 1 :]
    far_refs, (keys_ref, whole_ref) = refs[-group - 2 : -2], refs[-2:]
    mine, member = place_ref[0] // group, place_ref[0] % group
    size = starts_ref.shape[1]
    for ref, step in zip(arrived, line_order(groups)):
        index = source_of(mine, step, groups)
        keys_ref[index] = ref[:tokens].astype(F32) + ref[tokens : 2 * tokens].astype(F32)
        whole = ref[2 * tokens : 2 * tokens + size].astype(F32)
        whole_ref[index] = whole + ref[2 * tokens + size :].astype(F32)
    brought = [keys_ref[groups - 2]]
    product = None
    for index in range(groups - 3, -1, -1):
        keys, whole = keys_ref[index], whole_ref[index + 1]
        if product is not None:
            whole = jnp.where(index + 2 < mine, dot3(whole, product), whole)
        product = whole
        brought.append(jnp.where(index + 1 < mine, dot3(keys, product), keys))
    keys = jnp.concatenate(brought[::-1], axis=0)
    count, size = keys.shape
    ways = [starts_ref[target_of(member, step, group)] for step in range(group)]
    spread = dot3(keys, jnp.concatenate(ways, axis=1)).astype(BF16)
    for step in range(group):
        far_refs[step][:count] = spread[:, step * size : (step + 1) * size]
        far_refs[step][count:] = near_refs[step][...]


def attend_kernel(group, segments, most, place_ref, core_ref, table_ref, *refs):
    far_refs, line_refs = refs[:group][::-1], refs[group : 2 * group][::-1]
    (moved_ref, weighted_ref, peak_ref, total_ref, out_ref, away_ref, kept_ref, keys_ref, vals_ref,
     summed_ref) = refs[2 * group :]
    core = core_ref[0]
    mine, member = place_ref[0] // group, place_ref[0] % group
    heads, tokens, size = moved_ref.shape
    groups = far_refs[0].shape[0] // tokens
    scaling = LOG2E / math.sqrt(size)
    chunk = keys_ref.shape[0] // tokens
    lanes = lax.broadcasted_iota(jnp.int32, (1, chunk * tokens), 1)

    def collect(turn):
        found = jnp.int32(0)
        for slot in range(chunk):
            part = slice(slot * tokens, (slot + 1) * tokens)
            word, shift, ones = word_of(turn * chunk + slot, segments)
            code = (table_ref[word] >> shift) & ones
            found = found + (code > 0).astype(jnp.int32)
            segment = jnp.maximum(code - 1, 0)
            whose, source = segment % group, segment // group
            before = jnp.where(source < mine, source, groups - 1)
            before = pl.multiple_of(before * tokens, tokens)
            after = pl.multiple_of(source * tokens, tokens)
            for number in range(group):

                @pl.when(whose == source_of(member, number, group))
                def _():
                    vals_ref[part, :] = line_refs[number][pl.ds(after, tokens), :]
                    keys_ref[part, :] = far_refs[number][pl.ds(before, tokens), :]

        return jnp.where(lanes < found * tokens, 0.0, NEGATIVE)

    def advance(moved, bias, peak, total, weighted):
        scores = lax.dot_general(
            moved, keys_ref[...], (((1,), (1,)), ((), ())), preferred_element_type=F32
        )
        scores = scores * scaling + bias
        new_peak = jnp.maximum(peak, jnp.max(scores, axis=1, keepdims=True))
        fading = jnp.exp2(peak - new_peak)
        weights = jnp.exp2(scores - new_peak)
        total = total * fading + jnp.sum(weights, axis=1, keepdims=True)
        weighted = weighted * fading + jnp.dot(
            weights.astype(BF16), vals_ref[...], preferred_element_type=F32
        )
        return new_peak, total, weighted

    half = kept_ref.shape[0]
    turns = most // chunk
    if turns == 1:
        bias = collect(0)
    stack = math.gcd(heads, 4)
    wide = math.gcd(out_ref.shape[1], 4 * size)
    for first in range(0, heads, stack):
        some = slice(first, first + stack)
        moved = moved_ref[some].reshape(stack * tokens, size)
        state = (
            peak_ref[some].reshape(stack * tokens, 1),
            total_ref[some].reshape(stack * tokens, 1),
            weighted_ref[some].reshape(stack * tokens, size),
        )
        if turns == 1:
            _, total, weighted = advance(moved, bias, *state)
        else:

            def step_of(turn, state, moved=moved):
                return advance(moved, collect(turn), *state)

            _, total, weighted = lax.fori_loop(0, turns, step_of, state)
        done = (weighted * (1.0 / total)).astype(BF16)
        done = jnp.concatenate(
            [done[n * tokens : (n + 1) * tokens] for n in range(stack)], axis=1
        )
        deep = slice(first * size, (first + stack) * size)
        for at in range(0, out_ref.shape[1], wide):
            part = slice(at, at + wide)
            result = jnp.dot(done, out_ref[deep, part], preferred_element_type=F32)
            if first:
                result = result + summed_ref[:, part]
            if first + stack < heads:
                summed_ref[:, part] = result
            else:
                away_ref[:, part] = jnp.where(core == 0, result[half:], result[:half]).astype(BF16)
                kept_ref[:, part] = jnp.where(core == 0, result[:half], result[half:]).astype(BF16)


def body(
    hidden, w_query, w_key, w_value, w_dir, u_rate, rate_bias, q_gain, k_gain, w_out, block_mask
):
    segments = lax.axis_size("ctx")
    place = lax.axis_index("ctx").astype(jnp.int32).reshape(1)
    core = lax.axis_index("head").astype(jnp.int32).reshape(1)
    group = max(d for d in range(1, math.isqrt(segments) + 1) if segments % d == 0)
    groups = segments // group
    other = lax.ppermute(hidden, "head", [(0, 1), (1, 0)])
    half, width = hidden.shape
    tokens = half * lax.axis_size("head")
    size = w_key.shape[1]
    heads = w_query.shape[1] // size
    smem = pl.BlockSpec(memory_space=pltpu.SMEM)
    vmem = pl.BlockSpec(memory_space=pltpu.VMEM)
    hbm = pl.BlockSpec(memory_space=pltpu.HBM)
    anywhere = pl.BlockSpec(memory_space=pl.ANY)
    square = shaped((tokens, size), F32)

    def swapped(values, count, pairs_of):
        out = [values[0]] * count
        for step in range(count - 1, 0, -1):
            out[step] = lax.ppermute(values[step], "ctx", pairs_of(step))
        return out

    def within_group(values):
        return swapped(values, group, lambda step: [
            (s, s - s % group + target_of(s % group, step, group)) for s in range(segments)
        ])

    def along_line(values):
        return swapped(values, groups, lambda step: [
            (s, s % group + group * target_of(s // group, step, groups))
            for s in reversed(range(segments))
        ])

    weights, rate_row, key_gain, query_gain, mine = call(
        functools.partial(load_kernel, size),
        (
            shaped((width, 2 * size), BF16), shaped((1, width), BF16), shaped((1, size), F32),
            shaped((1, size), F32), shaped((half, width), BF16),
        ),
        tuple(
            in_hbm(array)
            for array in (
                w_key, w_dir, u_rate, k_gain.reshape(1, size), q_gain.reshape(1, size),
                hidden,
            )
        ),
        in_specs=[hbm] * 6,
        scratch=(pltpu.SemaphoreType.DMA((6,)),),
        moved=12 * width * size,
    )
    rows, kn, val, dirs, coeff, solved, exit_keys, turn = call(
        prepare_kernel,
        (
            shaped((tokens, width), BF16), square, shaped((tokens, size), BF16), square, square,
            square, square, shaped((size, size), F32),
        ),
        (core, mine, other, weights, rate_row, rate_bias, key_gain, in_hbm(w_value)),
        in_specs=[smem] + [vmem] * 4 + [smem, vmem, hbm],
        scratch=(pltpu.VMEM(w_value.shape, BF16), pltpu.SemaphoreType.DMA),
        flops=6 * tokens * width * size,
        moved=8 * width * size,
    )
    turns = within_group([turn] * group)
    line = along_line([val] * groups)
    leaving, starts, *near = call(
        functools.partial(leave_kernel, group),
        [
            shaped((2 * tokens + 2 * size, size), BF16),
            shaped((group, size, size), F32),
        ]
        + [shaped((tokens, size), BF16)] * group,
        (place, exit_keys, *turns[::-1]),
        in_specs=[smem] + [vmem] * (1 + group),
        scratch=(
            pltpu.VMEM((group, size, size), F32),
            pltpu.VMEM((group, tokens, size), BF16),
        ),
        flops=12 * group * size**3,
        moved=10**6,
    )
    arrived = along_line([leaving] * groups)
    most = segments // 4
    values, table = call(
        functools.partial(bundle_kernel, group, groups, most),
        [
            shaped((groups * tokens, size), BF16),
            shaped((word_of(most - 1, segments)[0] + 1,), jnp.int32),
        ],
        (place, block_mask[0], starts, *line[::-1]),
        in_specs=[smem, smem, anywhere] + [vmem] * groups,
        out_specs=[vmem, smem],
        moved=10**6,
        limit=8 + group * groups // 4,
    )
    values = within_group([values] * group)
    own = call(
        query_kernel,
        (
            shaped((heads, tokens, size), BF16),
            shaped((heads, tokens, size), F32),
            shaped((heads, tokens, 1), F32),
            shaped((heads, tokens, 1), F32),
        ),
        (rows, in_hbm(w_query), query_gain, kn, dirs, coeff, solved, val),
        in_specs=[vmem, hbm] + [vmem] * 6,
        scratch=(
            pltpu.VMEM((2, width // 2, w_query.shape[1]), BF16),
            pltpu.VMEM((tokens, w_query.shape[1]), F32),
            pltpu.SemaphoreType.DMA((2,)),
        ),
        flops=4 * tokens * width * heads * size,
        moved=8 * width * heads * size,
        limit=16,
    )
    far = call(
        functools.partial(arrive_kernel, groups, group, tokens),
        [shaped((groups * tokens, size), BF16)] * group,
        (place, *(arrived[step] for step in line_order(groups)), starts, *near),
        in_specs=[smem] + [vmem] * (groups + 1 + group),
        scratch=(
            pltpu.VMEM((groups, tokens, size), F32),
            pltpu.VMEM((groups, size, size), F32),
        ),
        flops=6 * groups * group * size**3,
        moved=10**6,
        limit=8 + group * groups // 4,
    )
    far = within_group(far)
    chunk = math.gcd(most, 4)
    width_out = w_out.shape[1]
    away, kept = call(
        functools.partial(attend_kernel, group, segments, most),
        [shaped((half, width_out), BF16)] * 2,
        (place, core, table, *far[::-1], *values[::-1], *own, w_out),
        in_specs=[smem] * 3 + [vmem] * (2 * group + 5),
        scratch=[
            pltpu.VMEM((chunk * tokens, size), BF16),
            pltpu.VMEM((chunk * tokens, size), BF16),
            pltpu.VMEM((tokens, width_out), F32),
        ],
        flops=2 * tokens * width_out * heads * size,
        moved=4 * 10**6,
        limit=14 + group * groups // 4,
    )
    return kept + lax.ppermute(away, "head", [(0, 1), (1, 0)])


def solution(mesh):
    in_specs = (
        P(("ctx", "head"), None),
        P(None, "head"),
        P(None, "head"),
        P(None, "head"),
        P(None, "head"),
        P("head", None),
        P("head"),
        P(),
        P(),
        P("head", None),
        P("ctx", None),
    )
    out_specs = P(("ctx", "head"), None)
    return jax.shard_map(body, mesh=mesh, in_specs=in_specs, out_specs=out_specs, check_vma=False)
```

```python
import functools
import math

import jax
import jax.numpy as jnp
from jax import lax
from jax.experimental import pallas as pl
from jax.experimental.pallas import tpu as pltpu
from jax.sharding import PartitionSpec as P

EPSILON = 1e-06
NEGATIVE = -1e30
LOG2E = math.log2(math.e)
F32 = jnp.float32
BF16 = jnp.bfloat16
MIB = 1024 * 1024


def call(kernel, out_shape, args, in_specs=None, out_specs=None, scratch=(), flops=0, moved=0, limit=6):
    vmem = pl.BlockSpec(memory_space=pltpu.VMEM)
    return pl.pallas_call(
        kernel,
        out_shape=out_shape,
        in_specs=in_specs or [vmem] * len(args),
        out_specs=out_specs or jax.tree.map(lambda _: vmem, out_shape),
        scratch_shapes=list(scratch),
        compiler_params=pltpu.CompilerParams(vmem_limit_bytes=limit * MIB),
        cost_estimate=pl.CostEstimate(flops=flops, bytes_accessed=moved, transcendentals=0),
    )(*args)


def target_of(member, step, group):
    return member ^ step if group & (group - 1) == 0 else (member + step) % group


def source_of(member, step, group):
    return member ^ step if group & (group - 1) == 0 else (member + group - step) % group


def in_hbm(array):
    return pltpu.with_memory_space_constraint(array, pltpu.HBM)


def line_order(groups):
    return [groups // 2] + [step for step in range(1, groups) if step != groups // 2] + [0]


def shaped(shape, dtype):
    return jax.ShapeDtypeStruct(shape, dtype)


def split(value):
    high = value.astype(BF16)
    return high, (value - high.astype(F32)).astype(BF16)


def dot3(left, right, left_dim=1, right_dim=0):
    left_high, left_low = split(left)
    right_high, right_low = split(right)
    return lax.dot_general(
        jnp.concatenate([left_high, left_high, left_low], axis=left_dim),
        jnp.concatenate([right_high, right_low, right_high], axis=right_dim),
        (((left_dim,), (right_dim,)), ((), ())),
        preferred_element_type=F32,
    )


def iota2(shape):
    return lax.broadcasted_iota(jnp.int32, shape, 0), lax.broadcasted_iota(jnp.int32, shape, 1)


def merge_inverse(lower, rows, cols):
    tokens = lower.shape[0]
    block = 16
    inverse = jnp.where(rows == cols, 1.0, 0.0).astype(F32)
    first = rows - rows % block
    for step in range(block - 1):
        column = jnp.sum(jnp.where(cols == first + step, lower, 0.0), axis=1, keepdims=True)
        pivot = inverse.reshape(tokens // block, block, tokens)[:, step : step + 1, :]
        pivot = jnp.broadcast_to(pivot, (tokens // block, block, tokens)).reshape(tokens, tokens)
        inverse = inverse - column * pivot
    while block < tokens:
        corner = (
            (rows // (2 * block) == cols // (2 * block))
            & (rows % (2 * block) >= block)
            & (cols % (2 * block) < block)
        )
        inverse = inverse - dot3(dot3(inverse, jnp.where(corner, lower, 0.0)), inverse)
        block *= 2
    return inverse


def load_kernel(size, key_hbm, dir_hbm, rate_hbm, key_gain_hbm,
                query_gain_hbm, mine_hbm, weight_ref, rate_ref, key_gain_ref, query_gain_ref,
                mine_ref, sems):
    pairs = [
        (hbm, weight_ref.at[:, index * size : (index + 1) * size])
        for index, hbm in enumerate((key_hbm, dir_hbm))
    ]
    pairs += [(rate_hbm, rate_ref), (key_gain_hbm, key_gain_ref)]
    pairs += [(query_gain_hbm, query_gain_ref), (mine_hbm, mine_ref)]
    copies = [pltpu.make_async_copy(*pair, sems.at[n]) for n, pair in enumerate(pairs)]
    for copy in copies:
        copy.start()
    for copy in copies:
        copy.wait()


def prepare_kernel(core_ref, mine_ref, other_ref, weight_ref, rate_ref, bias_ref, gain_ref,
                   value_hbm, rows_ref, kn_ref, val_ref, dirs_ref, coeff_ref, solved_ref, exit_ref,
                   turn_ref, value_ref, value_sem):
    value_copy = pltpu.make_async_copy(value_hbm, value_ref, value_sem)
    value_copy.start()
    core = core_ref[0]
    half = mine_ref.shape[0]
    rows_ref[pl.ds(pl.multiple_of(core * half, half), half), :] = mine_ref[...]
    rows_ref[pl.ds(pl.multiple_of((1 - core) * half, half), half), :] = other_ref[...]
    seg = rows_ref[...]
    size = turn_ref.shape[0]
    raw = jnp.dot(seg, weight_ref[...], preferred_element_type=F32)
    keys, raw = raw[:, :size], raw[:, size:]
    kn = keys * lax.rsqrt(jnp.mean(keys * keys, axis=-1, keepdims=True) + EPSILON) * gain_ref[...]
    dirs = raw * lax.rsqrt(jnp.sum(raw * raw, axis=-1, keepdims=True) + EPSILON)
    vector = jnp.broadcast_to(rate_ref[...], (16, seg.shape[1]))
    logits = lax.dot_general(seg, vector, (((1,), (1,)), ((), ())), preferred_element_type=F32)
    rates = 2.0 * jax.nn.sigmoid(logits[:, :1] + bias_ref[0])
    kn_ref[...] = kn
    dirs_ref[...] = dirs
    tokens, size = dirs.shape
    rows, cols = iota2((tokens, tokens))
    below = rows > cols
    grams = dot3(dirs, jnp.concatenate([dirs, kn], axis=0), 1, 1)
    lower = jnp.where(below, rates * grams[:, :tokens], 0.0)
    crossing = jnp.where(below, rates * grams[:, tokens:], 0.0)
    inverse = merge_inverse(lower, rows, cols)
    value_copy.wait()
    val_ref[...] = jnp.dot(seg, value_ref[...], preferred_element_type=F32).astype(BF16)
    both = dot3(inverse, jnp.concatenate([crossing, rates * dirs], axis=1))
    coeff_ref[...] = both[:, :tokens]
    solved_ref[...] = both[:, tokens:]
    crossed = dot3(both, dirs, 0, 0)
    exit_ref[...] = kn - crossed[:tokens]
    heads, lanes = iota2((size, size))
    turn_ref[...] = jnp.where(heads == lanes, 1.0, 0.0) - crossed[tokens:]


def leave_kernel(group, place_ref, exit_ref, *refs):
    turn_refs, (leave_ref, starts_ref) = refs[:group], refs[group : group + 2]
    near_refs, (turns_ref, seen_ref) = refs[group + 2 : -2], refs[-2:]
    member = place_ref[0] % group
    tokens, size = exit_ref.shape
    for step in range(group):
        turns_ref[source_of(member, step, group)] = turn_refs[group - 1 - step][...]
    own = exit_ref[...]
    keys = own
    product = None
    heads, lanes = iota2((size, size))
    starts_ref[0] = jnp.where(heads == lanes, 1.0, 0.0)
    for index in range(group):
        seen_ref[index] = keys.astype(BF16)
        turn = turns_ref[index]
        product = turn if product is None else dot3(product, turn)
        if index:
            keys = jnp.where(index > member, dot3(keys, turn), own)
        if index < group - 1:
            starts_ref[index + 1] = product
    high, low = split(keys)
    leave_ref[:tokens] = high
    leave_ref[tokens : 2 * tokens] = low
    high, low = split(product)
    leave_ref[2 * tokens : 2 * tokens + size] = high
    leave_ref[2 * tokens + size :] = low
    for step in range(group):
        near_refs[step][...] = seen_ref[target_of(member, step, group)]


def word_of(slot, segments):
    bits = segments.bit_length()
    per_word = 31 // bits
    return slot // per_word, bits * (slot % per_word), (1 << bits) - 1


def bundle_kernel(group, groups, most, place_ref, mask_ref, after_ref, *refs):
    val_refs, (line_ref, table_ref) = refs[:groups], refs[groups:]
    place = place_ref[0]
    mine = place // group
    segments = mask_ref.shape[0]
    for word in range(table_ref.shape[0]):
        table_ref[word] = 0

    def pick(segment, count):
        wanted = (mask_ref[segment] > 0) & (segment < place) & (count < most)
        word, shift, _ = word_of(count, segments)

        @pl.when(wanted)
        def _():
            table_ref[word] = table_ref[word] | ((segment + 1) << shift)

        return count + wanted.astype(jnp.int32)

    lax.fori_loop(0, segments, pick, jnp.int32(0))
    tokens = val_refs[0].shape[0]
    for way in range(groups):
        at = pl.multiple_of(source_of(mine, way, groups) * tokens, tokens)
        line_ref[pl.ds(at, tokens), :] = val_refs[groups - 1 - way][...]


def query_kernel(rows_ref, weight_hbm, gain_ref, kn_ref, dirs_ref, coeff_ref, solved_ref, val_ref,
                 moved_ref, weighted_ref, peak_ref, total_ref, weight_ref, raw_ref, sems):
    tokens, size = kn_ref.shape
    heads = moved_ref.shape[0]
    pieces, deep, _ = weight_ref.shape
    copies = [
        pltpu.make_async_copy(
            weight_hbm.at[n * deep : (n + 1) * deep, :], weight_ref.at[n], sems.at[n]
        )
        for n in range(pieces)
    ]
    for copy in copies:
        copy.start()
    across = jnp.concatenate([kn_ref[...], dirs_ref[...]], axis=0)
    into = jnp.concatenate([coeff_ref[...], solved_ref[...]], axis=1)
    for n in range(pieces):
        copies[n].wait()
        part = jnp.dot(
            rows_ref[:, n * deep : (n + 1) * deep], weight_ref[n], preferred_element_type=F32
        )
        raw_ref[...] = raw_ref[...] + part if n else part
    count = math.gcd(heads, 4)
    for turn in range(heads // count):
        raw = jnp.concatenate(
            [
                raw_ref[:, head * size : (head + 1) * size]
                for head in range(turn * count, (turn + 1) * count)
            ],
            axis=0,
        )
        queries = (
            raw * lax.rsqrt(jnp.mean(raw * raw, axis=-1, keepdims=True) + EPSILON) * gain_ref[...]
        )
        seen = dot3(queries, across, 1, 1)
        rows, cols = iota2((count * tokens, tokens))
        up_to = rows % tokens >= cols
        reach = jnp.where(up_to, seen[:, tokens:], 0.0)
        taken = dot3(reach, into)
        scores = (seen[:, :tokens] - taken[:, :tokens]) * (LOG2E / math.sqrt(size))
        scores = jnp.where(up_to, scores, NEGATIVE)
        moved = (queries - taken[:, tokens:]).astype(BF16)
        peak = jnp.max(scores, axis=1, keepdims=True)
        weights = jnp.exp2(scores - peak)
        total = jnp.sum(weights, axis=1, keepdims=True)
        weighted = jnp.dot(weights.astype(BF16), val_ref[...], preferred_element_type=F32)
        for h in range(count):
            part = slice(h * tokens, (h + 1) * tokens)
            head = turn * count + h
            moved_ref[head] = moved[part]
            weighted_ref[head] = weighted[part]
            peak_ref[head] = peak[part]
            total_ref[head] = total[part]


def arrive_kernel(groups, group, tokens, place_ref, *refs):
    arrived, starts_ref, near_refs = refs[:groups], refs[groups], refs[groups + 1 :]
    far_refs, (keys_ref, whole_ref) = refs[-group - 2 : -2], refs[-2:]
    mine, member = place_ref[0] // group, place_ref[0] % group
    size = starts_ref.shape[1]
    for ref, step in zip(arrived, line_order(groups)):
        index = source_of(mine, step, groups)
        keys_ref[index] = ref[:tokens].astype(F32) + ref[tokens : 2 * tokens].astype(F32)
        whole = ref[2 * tokens : 2 * tokens + size].astype(F32)
        whole_ref[index] = whole + ref[2 * tokens + size :].astype(F32)
    brought = [keys_ref[groups - 2]]
    product = None
    for index in range(groups - 3, -1, -1):
        keys, whole = keys_ref[index], whole_ref[index + 1]
        if product is not None:
            whole = jnp.where(index + 2 < mine, dot3(whole, product), whole)
        product = whole
        brought.append(jnp.where(index + 1 < mine, dot3(keys, product), keys))
    keys = jnp.concatenate(brought[::-1], axis=0)
    count, size = keys.shape
    ways = [starts_ref[target_of(member, step, group)] for step in range(group)]
    spread = dot3(keys, jnp.concatenate(ways, axis=1)).astype(BF16)
    for step in range(group):
        far_refs[step][:count] = spread[:, step * size : (step + 1) * size]
        far_refs[step][count:] = near_refs[step][...]


def attend_kernel(group, segments, most, place_ref, core_ref, table_ref, *refs):
    far_refs, line_refs = refs[:group][::-1], refs[group : 2 * group][::-1]
    (moved_ref, weighted_ref, peak_ref, total_ref, out_ref, away_ref, kept_ref, keys_ref, vals_ref,
     summed_ref) = refs[2 * group :]
    core = core_ref[0]
    mine, member = place_ref[0] // group, place_ref[0] % group
    heads, tokens, size = moved_ref.shape
    groups = far_refs[0].shape[0] // tokens
    scaling = LOG2E / math.sqrt(size)
    chunk = keys_ref.shape[0] // tokens
    lanes = lax.broadcasted_iota(jnp.int32, (1, chunk * tokens), 1)

    def collect(turn):
        found = jnp.int32(0)
        for slot in range(chunk):
            part = slice(slot * tokens, (slot + 1) * tokens)
            word, shift, ones = word_of(turn * chunk + slot, segments)
            code = (table_ref[word] >> shift) & ones
            found = found + (code > 0).astype(jnp.int32)
            segment = jnp.maximum(code - 1, 0)
            whose, source = segment % group, segment // group
            before = jnp.where(source < mine, source, groups - 1)
            before = pl.multiple_of(before * tokens, tokens)
            after = pl.multiple_of(source * tokens, tokens)
            for number in range(group):

                @pl.when(whose == source_of(member, number, group))
                def _():
                    vals_ref[part, :] = line_refs[number][pl.ds(after, tokens), :]
                    keys_ref[part, :] = far_refs[number][pl.ds(before, tokens), :]

        return jnp.where(lanes < found * tokens, 0.0, NEGATIVE)

    def advance(moved, bias, peak, total, weighted):
        scores = lax.dot_general(
            moved, keys_ref[...], (((1,), (1,)), ((), ())), preferred_element_type=F32
        )
        scores = scores * scaling + bias
        new_peak = jnp.maximum(peak, jnp.max(scores, axis=1, keepdims=True))
        fading = jnp.exp2(peak - new_peak)
        weights = jnp.exp2(scores - new_peak)
        total = total * fading + jnp.sum(weights, axis=1, keepdims=True)
        weighted = weighted * fading + jnp.dot(
            weights.astype(BF16), vals_ref[...], preferred_element_type=F32
        )
        return new_peak, total, weighted

    half = kept_ref.shape[0]
    turns = most // chunk
    if turns == 1:
        bias = collect(0)
    stack = math.gcd(heads, 4)
    wide = math.gcd(out_ref.shape[1], 4 * size)
    for first in range(0, heads, stack):
        some = slice(first, first + stack)
        moved = moved_ref[some].reshape(stack * tokens, size)
        state = (
            peak_ref[some].reshape(stack * tokens, 1),
            total_ref[some].reshape(stack * tokens, 1),
            weighted_ref[some].reshape(stack * tokens, size),
        )
        if turns == 1:
            _, total, weighted = advance(moved, bias, *state)
        else:

            def step_of(turn, state, moved=moved):
                return advance(moved, collect(turn), *state)

            _, total, weighted = lax.fori_loop(0, turns, step_of, state)
        done = (weighted * (1.0 / total)).astype(BF16)
        done = jnp.concatenate(
            [done[n * tokens : (n + 1) * tokens] for n in range(stack)], axis=1
        )
        deep = slice(first * size, (first + stack) * size)
        for at in range(0, out_ref.shape[1], wide):
            part = slice(at, at + wide)
            result = jnp.dot(done, out_ref[deep, part], preferred_element_type=F32)
            if first:
                result = result + summed_ref[:, part]
            if first + stack < heads:
                summed_ref[:, part] = result
            else:
                away_ref[:, part] = jnp.where(core == 0, result[half:], result[:half]).astype(BF16)
                kept_ref[:, part] = jnp.where(core == 0, result[:half], result[half:]).astype(BF16)


def body(
    hidden, w_query, w_key, w_value, w_dir, u_rate, rate_bias, q_gain, k_gain, w_out, block_mask
):
    segments = lax.axis_size("ctx")
    place = lax.axis_index("ctx").astype(jnp.int32).reshape(1)
    core = lax.axis_index("head").astype(jnp.int32).reshape(1)
    group = max(d for d in range(1, math.isqrt(segments) + 1) if segments % d == 0)
    groups = segments // group
    other = lax.ppermute(hidden, "head", [(0, 1), (1, 0)])
    half, width = hidden.shape
    tokens = half * lax.axis_size("head")
    size = w_key.shape[1]
    heads = w_query.shape[1] // size
    smem = pl.BlockSpec(memory_space=pltpu.SMEM)
    vmem = pl.BlockSpec(memory_space=pltpu.VMEM)
    hbm = pl.BlockSpec(memory_space=pltpu.HBM)
    anywhere = pl.BlockSpec(memory_space=pl.ANY)
    square = shaped((tokens, size), F32)

    def swapped(values, count, pairs_of):
        out = [values[0]] * count
        for step in range(count - 1, 0, -1):
            out[step] = lax.ppermute(values[step], "ctx", pairs_of(step))
        return out

    def within_group(values):
        return swapped(values, group, lambda step: [
            (s, s - s % group + target_of(s % group, step, group)) for s in range(segments)
        ])

    def along_line(values):
        return swapped(values, groups, lambda step: [
            (s, s % group + group * target_of(s // group, step, groups)) for s in range(segments)
        ])

    weights, rate_row, key_gain, query_gain, mine = call(
        functools.partial(load_kernel, size),
        (
            shaped((width, 2 * size), BF16), shaped((1, width), BF16), shaped((1, size), F32),
            shaped((1, size), F32), shaped((half, width), BF16),
        ),
        tuple(
            in_hbm(array)
            for array in (
                w_key, w_dir, u_rate, k_gain.reshape(1, size), q_gain.reshape(1, size),
                hidden,
            )
        ),
        in_specs=[hbm] * 6,
        scratch=(pltpu.SemaphoreType.DMA((6,)),),
        moved=12 * width * size,
    )
    rows, kn, val, dirs, coeff, solved, exit_keys, turn = call(
        prepare_kernel,
        (
            shaped((tokens, width), BF16), square, shaped((tokens, size), BF16), square, square,
            square, square, shaped((size, size), F32),
        ),
        (core, mine, other, weights, rate_row, rate_bias, key_gain, in_hbm(w_value)),
        in_specs=[smem] + [vmem] * 4 + [smem, vmem, hbm],
        scratch=(pltpu.VMEM(w_value.shape, BF16), pltpu.SemaphoreType.DMA),
        flops=6 * tokens * width * size,
        moved=8 * width * size,
    )
    turns = within_group([turn] * group)
    line = along_line([val] * groups)
    leaving, starts, *near = call(
        functools.partial(leave_kernel, group),
        [
            shaped((2 * tokens + 2 * size, size), BF16),
            shaped((group, size, size), F32),
        ]
        + [shaped((tokens, size), BF16)] * group,
        (place, exit_keys, *turns[::-1]),
        in_specs=[smem] + [vmem] * (1 + group),
        scratch=(
            pltpu.VMEM((group, size, size), F32),
            pltpu.VMEM((group, tokens, size), BF16),
        ),
        flops=12 * group * size**3,
        moved=10**6,
    )
    arrived = along_line([leaving] * groups)
    most = segments // 4
    values, table = call(
        functools.partial(bundle_kernel, group, groups, most),
        [
            shaped((groups * tokens, size), BF16),
            shaped((word_of(most - 1, segments)[0] + 1,), jnp.int32),
        ],
        (place, block_mask[0], starts, *line[::-1]),
        in_specs=[smem, smem, anywhere] + [vmem] * groups,
        out_specs=[vmem, smem],
        moved=10**6,
        limit=8 + group * groups // 4,
    )
    values = within_group([values] * group)
    own = call(
        query_kernel,
        (
            shaped((heads, tokens, size), BF16),
            shaped((heads, tokens, size), F32),
            shaped((heads, tokens, 1), F32),
            shaped((heads, tokens, 1), F32),
        ),
        (rows, in_hbm(w_query), query_gain, kn, dirs, coeff, solved, val),
        in_specs=[vmem, hbm] + [vmem] * 6,
        scratch=(
            pltpu.VMEM((2, width // 2, w_query.shape[1]), BF16),
            pltpu.VMEM((tokens, w_query.shape[1]), F32),
            pltpu.SemaphoreType.DMA((2,)),
        ),
        flops=4 * tokens * width * heads * size,
        moved=8 * width * heads * size,
        limit=16,
    )
    far = call(
        functools.partial(arrive_kernel, groups, group, tokens),
        [shaped((groups * tokens, size), BF16)] * group,
        (place, *(arrived[step] for step in line_order(groups)), starts, *near),
        in_specs=[smem] + [vmem] * (groups + 1 + group),
        scratch=(
            pltpu.VMEM((groups, tokens, size), F32),
            pltpu.VMEM((groups, size, size), F32),
        ),
        flops=6 * groups * group * size**3,
        moved=10**6,
        limit=8 + group * groups // 4,
    )
    far = within_group(far)
    chunk = math.gcd(most, 4)
    width_out = w_out.shape[1]
    away, kept = call(
        functools.partial(attend_kernel, group, segments, most),
        [shaped((half, width_out), BF16)] * 2,
        (place, core, table, *far[::-1], *values[::-1], *own, w_out),
        in_specs=[smem] * 3 + [vmem] * (2 * group + 5),
        scratch=[
            pltpu.VMEM((chunk * tokens, size), BF16),
            pltpu.VMEM((chunk * tokens, size), BF16),
            pltpu.VMEM((tokens, width_out), F32),
        ],
        flops=2 * tokens * width_out * heads * size,
        moved=4 * 10**6,
        limit=14 + group * groups // 4,
    )
    return kept + lax.ppermute(away, "head", [(0, 1), (1, 0)])


def solution(mesh):
    in_specs = (
        P(("ctx", "head"), None),
        P(None, "head"),
        P(None, "head"),
        P(None, "head"),
        P(None, "head"),
        P("head", None),
        P("head"),
        P(),
        P(),
        P("head", None),
        P("ctx", None),
    )
    out_specs = P(("ctx", "head"), None)
    return jax.shard_map(body, mesh=mesh, in_specs=in_specs, out_specs=out_specs, check_vma=False)
```

```python
import functools
import math

import jax
import jax.numpy as jnp
from jax import lax
from jax.experimental import pallas as pl
from jax.experimental.pallas import tpu as pltpu
from jax.sharding import PartitionSpec as P

EPSILON = 1e-06
NEGATIVE = -1e30
LOG2E = math.log2(math.e)
F32 = jnp.float32
BF16 = jnp.bfloat16
MIB = 1024 * 1024


def call(kernel, out_shape, args, in_specs=None, out_specs=None, scratch=(), flops=0, moved=0, limit=6):
    vmem = pl.BlockSpec(memory_space=pltpu.VMEM)
    return pl.pallas_call(
        kernel,
        out_shape=out_shape,
        in_specs=in_specs or [vmem] * len(args),
        out_specs=out_specs or jax.tree.map(lambda _: vmem, out_shape),
        scratch_shapes=list(scratch),
        compiler_params=pltpu.CompilerParams(vmem_limit_bytes=limit * MIB),
        cost_estimate=pl.CostEstimate(flops=flops, bytes_accessed=moved, transcendentals=0),
    )(*args)


def target_of(member, step, group):
    return member ^ step if group & (group - 1) == 0 else (member + step) % group


def source_of(member, step, group):
    return member ^ step if group & (group - 1) == 0 else (member + group - step) % group


def in_hbm(array):
    return pltpu.with_memory_space_constraint(array, pltpu.HBM)


def line_order(groups):
    return [*range(1, groups), 0]


def shaped(shape, dtype):
    return jax.ShapeDtypeStruct(shape, dtype)


def split(value):
    high = value.astype(BF16)
    return high, (value - high.astype(F32)).astype(BF16)


def dot3(left, right, left_dim=1, right_dim=0):
    left_high, left_low = split(left)
    right_high, right_low = split(right)
    return lax.dot_general(
        jnp.concatenate([left_high, left_high, left_low], axis=left_dim),
        jnp.concatenate([right_high, right_low, right_high], axis=right_dim),
        (((left_dim,), (right_dim,)), ((), ())),
        preferred_element_type=F32,
    )


def iota2(shape):
    return lax.broadcasted_iota(jnp.int32, shape, 0), lax.broadcasted_iota(jnp.int32, shape, 1)


def merge_inverse(lower, rows, cols):
    tokens = lower.shape[0]
    block = 16
    inverse = jnp.where(rows == cols, 1.0, 0.0).astype(F32)
    first = rows - rows % block
    for step in range(block - 1):
        column = jnp.sum(jnp.where(cols == first + step, lower, 0.0), axis=1, keepdims=True)
        pivot = inverse.reshape(tokens // block, block, tokens)[:, step : step + 1, :]
        pivot = jnp.broadcast_to(pivot, (tokens // block, block, tokens)).reshape(tokens, tokens)
        inverse = inverse - column * pivot
    while block < tokens:
        corner = (
            (rows // (2 * block) == cols // (2 * block))
            & (rows % (2 * block) >= block)
            & (cols % (2 * block) < block)
        )
        inverse = inverse - dot3(dot3(inverse, jnp.where(corner, lower, 0.0)), inverse)
        block *= 2
    return inverse


def load_kernel(size, key_hbm, dir_hbm, rate_hbm, key_gain_hbm,
                query_gain_hbm, mine_hbm, weight_ref, rate_ref, key_gain_ref, query_gain_ref,
                mine_ref, sems):
    pairs = [
        (hbm, weight_ref.at[:, index * size : (index + 1) * size])
        for index, hbm in enumerate((key_hbm, dir_hbm))
    ]
    pairs += [(rate_hbm, rate_ref), (key_gain_hbm, key_gain_ref)]
    pairs += [(query_gain_hbm, query_gain_ref), (mine_hbm, mine_ref)]
    copies = [pltpu.make_async_copy(*pair, sems.at[n]) for n, pair in enumerate(pairs)]
    for copy in copies:
        copy.start()
    for copy in copies:
        copy.wait()


def prepare_kernel(core_ref, mine_ref, other_ref, weight_ref, rate_ref, bias_ref, gain_ref,
                   value_hbm, rows_ref, kn_ref, val_ref, dirs_ref, coeff_ref, solved_ref, exit_ref,
                   turn_ref, value_ref, value_sem):
    value_copy = pltpu.make_async_copy(value_hbm, value_ref, value_sem)
    value_copy.start()
    core = core_ref[0]
    half = mine_ref.shape[0]
    rows_ref[pl.ds(pl.multiple_of(core * half, half), half), :] = mine_ref[...]
    rows_ref[pl.ds(pl.multiple_of((1 - core) * half, half), half), :] = other_ref[...]
    seg = rows_ref[...]
    size = turn_ref.shape[0]
    raw = jnp.dot(seg, weight_ref[...], preferred_element_type=F32)
    keys, raw = raw[:, :size], raw[:, size:]
    kn = keys * lax.rsqrt(jnp.mean(keys * keys, axis=-1, keepdims=True) + EPSILON) * gain_ref[...]
    dirs = raw * lax.rsqrt(jnp.sum(raw * raw, axis=-1, keepdims=True) + EPSILON)
    vector = jnp.broadcast_to(rate_ref[...], (16, seg.shape[1]))
    logits = lax.dot_general(seg, vector, (((1,), (1,)), ((), ())), preferred_element_type=F32)
    rates = 2.0 * jax.nn.sigmoid(logits[:, :1] + bias_ref[0])
    kn_ref[...] = kn
    dirs_ref[...] = dirs
    tokens, size = dirs.shape
    rows, cols = iota2((tokens, tokens))
    below = rows > cols
    grams = dot3(dirs, jnp.concatenate([dirs, kn], axis=0), 1, 1)
    lower = jnp.where(below, rates * grams[:, :tokens], 0.0)
    crossing = jnp.where(below, rates * grams[:, tokens:], 0.0)
    inverse = merge_inverse(lower, rows, cols)
    value_copy.wait()
    val_ref[...] = jnp.dot(seg, value_ref[...], preferred_element_type=F32).astype(BF16)
    both = dot3(inverse, jnp.concatenate([crossing, rates * dirs], axis=1))
    coeff_ref[...] = both[:, :tokens]
    solved_ref[...] = both[:, tokens:]
    crossed = dot3(both, dirs, 0, 0)
    exit_ref[...] = kn - crossed[:tokens]
    heads, lanes = iota2((size, size))
    turn_ref[...] = jnp.where(heads == lanes, 1.0, 0.0) - crossed[tokens:]


def leave_kernel(group, place_ref, exit_ref, *refs):
    turn_refs, (leave_ref, starts_ref) = refs[:group], refs[group : group + 2]
    near_refs, (turns_ref, seen_ref) = refs[group + 2 : -2], refs[-2:]
    member = place_ref[0] % group
    tokens, size = exit_ref.shape
    for step in range(group):
        turns_ref[source_of(member, step, group)] = turn_refs[group - 1 - step][...]
    own = exit_ref[...]
    keys = own
    product = None
    heads, lanes = iota2((size, size))
    starts_ref[0] = jnp.where(heads == lanes, 1.0, 0.0)
    for index in range(group):
        seen_ref[index] = keys.astype(BF16)
        turn = turns_ref[index]
        product = turn if product is None else dot3(product, turn)
        if index:
            keys = jnp.where(index > member, dot3(keys, turn), own)
        if index < group - 1:
            starts_ref[index + 1] = product
    high, low = split(keys)
    leave_ref[:tokens] = high
    leave_ref[tokens : 2 * tokens] = low
    high, low = split(product)
    leave_ref[2 * tokens : 2 * tokens + size] = high
    leave_ref[2 * tokens + size :] = low
    for step in range(group):
        near_refs[step][...] = seen_ref[target_of(member, step, group)]


def word_of(slot, segments):
    bits = segments.bit_length()
    per_word = 31 // bits
    return slot // per_word, bits * (slot % per_word), (1 << bits) - 1


def bundle_kernel(group, groups, most, place_ref, mask_ref, after_ref, *refs):
    val_refs, (line_ref, table_ref) = refs[:groups], refs[groups:]
    place = place_ref[0]
    mine = place // group
    segments = mask_ref.shape[0]
    for word in range(table_ref.shape[0]):
        table_ref[word] = 0

    def pick(segment, count):
        wanted = (mask_ref[segment] > 0) & (segment < place) & (count < most)
        word, shift, _ = word_of(count, segments)

        @pl.when(wanted)
        def _():
            table_ref[word] = table_ref[word] | ((segment + 1) << shift)

        return count + wanted.astype(jnp.int32)

    lax.fori_loop(0, segments, pick, jnp.int32(0))
    tokens = val_refs[0].shape[0]
    for way in range(groups):
        at = pl.multiple_of(source_of(mine, way, groups) * tokens, tokens)
        line_ref[pl.ds(at, tokens), :] = val_refs[groups - 1 - way][...]


def query_kernel(rows_ref, weight_hbm, gain_ref, kn_ref, dirs_ref, coeff_ref, solved_ref, val_ref,
                 moved_ref, weighted_ref, peak_ref, total_ref, weight_ref, raw_ref, sems):
    tokens, size = kn_ref.shape
    heads = moved_ref.shape[0]
    pieces, deep, _ = weight_ref.shape
    copies = [
        pltpu.make_async_copy(
            weight_hbm.at[n * deep : (n + 1) * deep, :], weight_ref.at[n], sems.at[n]
        )
        for n in range(pieces)
    ]
    for copy in copies:
        copy.start()
    across = jnp.concatenate([kn_ref[...], dirs_ref[...]], axis=0)
    into = jnp.concatenate([coeff_ref[...], solved_ref[...]], axis=1)
    for n in range(pieces):
        copies[n].wait()
        part = jnp.dot(
            rows_ref[:, n * deep : (n + 1) * deep], weight_ref[n], preferred_element_type=F32
        )
        raw_ref[...] = raw_ref[...] + part if n else part
    count = math.gcd(heads, 4)
    for turn in range(heads // count):
        raw = jnp.concatenate(
            [
                raw_ref[:, head * size : (head + 1) * size]
                for head in range(turn * count, (turn + 1) * count)
            ],
            axis=0,
        )
        queries = (
            raw * lax.rsqrt(jnp.mean(raw * raw, axis=-1, keepdims=True) + EPSILON) * gain_ref[...]
        )
        seen = dot3(queries, across, 1, 1)
        rows, cols = iota2((count * tokens, tokens))
        up_to = rows % tokens >= cols
        reach = jnp.where(up_to, seen[:, tokens:], 0.0)
        taken = dot3(reach, into)
        scores = (seen[:, :tokens] - taken[:, :tokens]) * (LOG2E / math.sqrt(size))
        scores = jnp.where(up_to, scores, NEGATIVE)
        moved = (queries - taken[:, tokens:]).astype(BF16)
        peak = jnp.max(scores, axis=1, keepdims=True)
        weights = jnp.exp2(scores - peak)
        total = jnp.sum(weights, axis=1, keepdims=True)
        weighted = jnp.dot(weights.astype(BF16), val_ref[...], preferred_element_type=F32)
        for h in range(count):
            part = slice(h * tokens, (h + 1) * tokens)
            head = turn * count + h
            moved_ref[head] = moved[part]
            weighted_ref[head] = weighted[part]
            peak_ref[head] = peak[part]
            total_ref[head] = total[part]


def arrive_kernel(groups, group, tokens, place_ref, *refs):
    arrived, starts_ref, near_refs = refs[:groups], refs[groups], refs[groups + 1 :]
    far_refs, (keys_ref, whole_ref) = refs[-group - 2 : -2], refs[-2:]
    mine, member = place_ref[0] // group, place_ref[0] % group
    size = starts_ref.shape[1]
    for ref, step in zip(arrived, line_order(groups)):
        index = source_of(mine, step, groups)
        keys_ref[index] = ref[:tokens].astype(F32) + ref[tokens : 2 * tokens].astype(F32)
        whole = ref[2 * tokens : 2 * tokens + size].astype(F32)
        whole_ref[index] = whole + ref[2 * tokens + size :].astype(F32)
    brought = [keys_ref[groups - 2]]
    product = None
    for index in range(groups - 3, -1, -1):
        keys, whole = keys_ref[index], whole_ref[index + 1]
        if product is not None:
            whole = jnp.where(index + 2 < mine, dot3(whole, product), whole)
        product = whole
        brought.append(jnp.where(index + 1 < mine, dot3(keys, product), keys))
    keys = jnp.concatenate(brought[::-1], axis=0)
    count, size = keys.shape
    ways = [starts_ref[target_of(member, step, group)] for step in range(group)]
    spread = dot3(keys, jnp.concatenate(ways, axis=1)).astype(BF16)
    for step in range(group):
        far_refs[step][:count] = spread[:, step * size : (step + 1) * size]
        far_refs[step][count:] = near_refs[step][...]


def attend_kernel(group, segments, most, place_ref, core_ref, table_ref, *refs):
    far_refs, line_refs = refs[:group][::-1], refs[group : 2 * group][::-1]
    (moved_ref, weighted_ref, peak_ref, total_ref, out_ref, away_ref, kept_ref, keys_ref, vals_ref,
     summed_ref) = refs[2 * group :]
    core = core_ref[0]
    mine, member = place_ref[0] // group, place_ref[0] % group
    heads, tokens, size = moved_ref.shape
    groups = far_refs[0].shape[0] // tokens
    scaling = LOG2E / math.sqrt(size)
    chunk = keys_ref.shape[0] // tokens
    lanes = lax.broadcasted_iota(jnp.int32, (1, chunk * tokens), 1)

    def collect(turn):
        found = jnp.int32(0)
        for slot in range(chunk):
            part = slice(slot * tokens, (slot + 1) * tokens)
            word, shift, ones = word_of(turn * chunk + slot, segments)
            code = (table_ref[word] >> shift) & ones
            found = found + (code > 0).astype(jnp.int32)
            segment = jnp.maximum(code - 1, 0)
            whose, source = segment % group, segment // group
            before = jnp.where(source < mine, source, groups - 1)
            before = pl.multiple_of(before * tokens, tokens)
            after = pl.multiple_of(source * tokens, tokens)
            for number in range(group):

                @pl.when(whose == source_of(member, number, group))
                def _():
                    vals_ref[part, :] = line_refs[number][pl.ds(after, tokens), :]
                    keys_ref[part, :] = far_refs[number][pl.ds(before, tokens), :]

        return jnp.where(lanes < found * tokens, 0.0, NEGATIVE)

    def advance(moved, bias, peak, total, weighted):
        scores = lax.dot_general(
            moved, keys_ref[...], (((1,), (1,)), ((), ())), preferred_element_type=F32
        )
        scores = scores * scaling + bias
        new_peak = jnp.maximum(peak, jnp.max(scores, axis=1, keepdims=True))
        fading = jnp.exp2(peak - new_peak)
        weights = jnp.exp2(scores - new_peak)
        total = total * fading + jnp.sum(weights, axis=1, keepdims=True)
        weighted = weighted * fading + jnp.dot(
            weights.astype(BF16), vals_ref[...], preferred_element_type=F32
        )
        return new_peak, total, weighted

    half = kept_ref.shape[0]
    turns = most // chunk
    if turns == 1:
        bias = collect(0)
    stack = math.gcd(heads, 4)
    wide = math.gcd(out_ref.shape[1], 4 * size)
    for first in range(0, heads, stack):
        some = slice(first, first + stack)
        moved = moved_ref[some].reshape(stack * tokens, size)
        state = (
            peak_ref[some].reshape(stack * tokens, 1),
            total_ref[some].reshape(stack * tokens, 1),
            weighted_ref[some].reshape(stack * tokens, size),
        )
        if turns == 1:
            _, total, weighted = advance(moved, bias, *state)
        else:

            def step_of(turn, state, moved=moved):
                return advance(moved, collect(turn), *state)

            _, total, weighted = lax.fori_loop(0, turns, step_of, state)
        done = (weighted * (1.0 / total)).astype(BF16)
        done = jnp.concatenate(
            [done[n * tokens : (n + 1) * tokens] for n in range(stack)], axis=1
        )
        deep = slice(first * size, (first + stack) * size)
        for at in range(0, out_ref.shape[1], wide):
            part = slice(at, at + wide)
            result = jnp.dot(done, out_ref[deep, part], preferred_element_type=F32)
            if first:
                result = result + summed_ref[:, part]
            if first + stack < heads:
                summed_ref[:, part] = result
            else:
                away_ref[:, part] = jnp.where(core == 0, result[half:], result[:half]).astype(BF16)
                kept_ref[:, part] = jnp.where(core == 0, result[:half], result[half:]).astype(BF16)


def body(
    hidden, w_query, w_key, w_value, w_dir, u_rate, rate_bias, q_gain, k_gain, w_out, block_mask
):
    segments = lax.axis_size("ctx")
    place = lax.axis_index("ctx").astype(jnp.int32).reshape(1)
    core = lax.axis_index("head").astype(jnp.int32).reshape(1)
    group = max(d for d in range(1, math.isqrt(segments) + 1) if segments % d == 0)
    groups = segments // group
    other = lax.ppermute(hidden, "head", [(0, 1), (1, 0)])
    half, width = hidden.shape
    tokens = half * lax.axis_size("head")
    size = w_key.shape[1]
    heads = w_query.shape[1] // size
    smem = pl.BlockSpec(memory_space=pltpu.SMEM)
    vmem = pl.BlockSpec(memory_space=pltpu.VMEM)
    hbm = pl.BlockSpec(memory_space=pltpu.HBM)
    anywhere = pl.BlockSpec(memory_space=pl.ANY)
    square = shaped((tokens, size), F32)

    def swapped(values, count, pairs_of):
        out = [values[0]] * count
        for step in range(count - 1, 0, -1):
            out[step] = lax.ppermute(values[step], "ctx", pairs_of(step))
        return out

    def within_group(values):
        return swapped(values, group, lambda step: [
            (s, s - s % group + target_of(s % group, step, group)) for s in range(segments)
        ])

    def along_line(values):
        return swapped(values, groups, lambda step: [
            (s, s % group + group * target_of(s // group, step, groups)) for s in range(segments)
        ])

    weights, rate_row, key_gain, query_gain, mine = call(
        functools.partial(load_kernel, size),
        (
            shaped((width, 2 * size), BF16), shaped((1, width), BF16), shaped((1, size), F32),
            shaped((1, size), F32), shaped((half, width), BF16),
        ),
        tuple(
            in_hbm(array)
            for array in (
                w_key, w_dir, u_rate, k_gain.reshape(1, size), q_gain.reshape(1, size),
                hidden,
            )
        ),
        in_specs=[hbm] * 6,
        scratch=(pltpu.SemaphoreType.DMA((6,)),),
        moved=12 * width * size,
    )
    rows, kn, val, dirs, coeff, solved, exit_keys, turn = call(
        prepare_kernel,
        (
            shaped((tokens, width), BF16), square, shaped((tokens, size), BF16), square, square,
            square, square, shaped((size, size), F32),
        ),
        (core, mine, other, weights, rate_row, rate_bias, key_gain, in_hbm(w_value)),
        in_specs=[smem] + [vmem] * 4 + [smem, vmem, hbm],
        scratch=(pltpu.VMEM(w_value.shape, BF16), pltpu.SemaphoreType.DMA),
        flops=6 * tokens * width * size,
        moved=8 * width * size,
    )
    turns = within_group([turn] * group)
    line = along_line([val] * groups)
    leaving, starts, *near = call(
        functools.partial(leave_kernel, group),
        [
            shaped((2 * tokens + 2 * size, size), BF16),
            shaped((group, size, size), F32),
        ]
        + [shaped((tokens, size), BF16)] * group,
        (place, exit_keys, *turns[::-1]),
        in_specs=[smem] + [vmem] * (1 + group),
        scratch=(
            pltpu.VMEM((group, size, size), F32),
            pltpu.VMEM((group, tokens, size), BF16),
        ),
        flops=12 * group * size**3,
        moved=10**6,
    )
    arrived = along_line([leaving] * groups)
    most = segments // 4
    values, table = call(
        functools.partial(bundle_kernel, group, groups, most),
        [
            shaped((groups * tokens, size), BF16),
            shaped((word_of(most - 1, segments)[0] + 1,), jnp.int32),
        ],
        (place, block_mask[0], starts, *line[::-1]),
        in_specs=[smem, smem, anywhere] + [vmem] * groups,
        out_specs=[vmem, smem],
        moved=10**6,
        limit=8 + group * groups // 4,
    )
    values = within_group([values] * group)
    own = call(
        query_kernel,
        (
            shaped((heads, tokens, size), BF16),
            shaped((heads, tokens, size), F32),
            shaped((heads, tokens, 1), F32),
            shaped((heads, tokens, 1), F32),
        ),
        (rows, in_hbm(w_query), query_gain, kn, dirs, coeff, solved, val),
        in_specs=[vmem, hbm] + [vmem] * 6,
        scratch=(
            pltpu.VMEM((2, width // 2, w_query.shape[1]), BF16),
            pltpu.VMEM((tokens, w_query.shape[1]), F32),
            pltpu.SemaphoreType.DMA((2,)),
        ),
        flops=4 * tokens * width * heads * size,
        moved=8 * width * heads * size,
        limit=16,
    )
    far = call(
        functools.partial(arrive_kernel, groups, group, tokens),
        [shaped((groups * tokens, size), BF16)] * group,
        (place, *(arrived[step] for step in line_order(groups)), starts, *near),
        in_specs=[smem] + [vmem] * (groups + 1 + group),
        scratch=(
            pltpu.VMEM((groups, tokens, size), F32),
            pltpu.VMEM((groups, size, size), F32),
        ),
        flops=6 * groups * group * size**3,
        moved=10**6,
        limit=8 + group * groups // 4,
    )
    far = within_group(far)
    chunk = math.gcd(most, 4)
    width_out = w_out.shape[1]
    away, kept = call(
        functools.partial(attend_kernel, group, segments, most),
        [shaped((half, width_out), BF16)] * 2,
        (place, core, table, *far[::-1], *values[::-1], *own, w_out),
        in_specs=[smem] * 3 + [vmem] * (2 * group + 5),
        scratch=[
            pltpu.VMEM((chunk * tokens, size), BF16),
            pltpu.VMEM((chunk * tokens, size), BF16),
            pltpu.VMEM((tokens, width_out), F32),
        ],
        flops=2 * tokens * width_out * heads * size,
        moved=4 * 10**6,
        limit=14 + group * groups // 4,
    )
    return kept + lax.ppermute(away, "head", [(0, 1), (1, 0)])


def solution(mesh):
    in_specs = (
        P(("ctx", "head"), None),
        P(None, "head"),
        P(None, "head"),
        P(None, "head"),
        P(None, "head"),
        P("head", None),
        P("head"),
        P(),
        P(),
        P("head", None),
        P("ctx", None),
    )
    out_specs = P(("ctx", "head"), None)
    return jax.shard_map(body, mesh=mesh, in_specs=in_specs, out_specs=out_specs, check_vma=False)
```

```python
import functools
import math

import jax
import jax.numpy as jnp
from jax import lax
from jax.experimental import pallas as pl
from jax.experimental.pallas import tpu as pltpu
from jax.sharding import PartitionSpec as P

EPSILON = 1e-06
NEGATIVE = -1e30
LOG2E = math.log2(math.e)
F32 = jnp.float32
BF16 = jnp.bfloat16
MIB = 1024 * 1024


def call(kernel, out_shape, args, in_specs=None, out_specs=None, scratch=(), flops=0, moved=0, limit=6):
    vmem = pl.BlockSpec(memory_space=pltpu.VMEM)
    return pl.pallas_call(
        kernel,
        out_shape=out_shape,
        in_specs=in_specs or [vmem] * len(args),
        out_specs=out_specs or jax.tree.map(lambda _: vmem, out_shape),
        scratch_shapes=list(scratch),
        compiler_params=pltpu.CompilerParams(vmem_limit_bytes=limit * MIB),
        cost_estimate=pl.CostEstimate(flops=flops, bytes_accessed=moved, transcendentals=0),
    )(*args)


def target_of(member, step, group):
    return member ^ step if group & (group - 1) == 0 else (member + step) % group


def source_of(member, step, group):
    return member ^ step if group & (group - 1) == 0 else (member + group - step) % group


def in_hbm(array):
    return pltpu.with_memory_space_constraint(array, pltpu.HBM)


def line_order(groups):
    return [groups // 2] + [step for step in range(1, groups) if step != groups // 2] + [0]


def shaped(shape, dtype):
    return jax.ShapeDtypeStruct(shape, dtype)


def split(value):
    high = value.astype(BF16)
    return high, (value - high.astype(F32)).astype(BF16)


def dot3(left, right, left_dim=1, right_dim=0):
    left_high, left_low = split(left)
    right_high, right_low = split(right)
    return lax.dot_general(
        jnp.concatenate([left_high, left_high, left_low], axis=left_dim),
        jnp.concatenate([right_high, right_low, right_high], axis=right_dim),
        (((left_dim,), (right_dim,)), ((), ())),
        preferred_element_type=F32,
    )


def iota2(shape):
    return lax.broadcasted_iota(jnp.int32, shape, 0), lax.broadcasted_iota(jnp.int32, shape, 1)


def merge_inverse(lower, rows, cols):
    tokens = lower.shape[0]
    block = 16
    inverse = jnp.where(rows == cols, 1.0, 0.0).astype(F32)
    first = rows - rows % block
    for step in range(block - 1):
        column = jnp.sum(jnp.where(cols == first + step, lower, 0.0), axis=1, keepdims=True)
        pivot = inverse.reshape(tokens // block, block, tokens)[:, step : step + 1, :]
        pivot = jnp.broadcast_to(pivot, (tokens // block, block, tokens)).reshape(tokens, tokens)
        inverse = inverse - column * pivot
    while block < tokens:
        corner = (
            (rows // (2 * block) == cols // (2 * block))
            & (rows % (2 * block) >= block)
            & (cols % (2 * block) < block)
        )
        inverse = inverse - dot3(dot3(inverse, jnp.where(corner, lower, 0.0)), inverse)
        block *= 2
    return inverse


def load_kernel(size, key_hbm, dir_hbm, rate_hbm, key_gain_hbm,
                query_gain_hbm, mine_hbm, weight_ref, rate_ref, key_gain_ref, query_gain_ref,
                mine_ref, sems):
    pairs = [
        (hbm, weight_ref.at[:, index * size : (index + 1) * size])
        for index, hbm in enumerate((key_hbm, dir_hbm))
    ]
    pairs += [(rate_hbm, rate_ref), (key_gain_hbm, key_gain_ref)]
    pairs += [(query_gain_hbm, query_gain_ref), (mine_hbm, mine_ref)]
    copies = [pltpu.make_async_copy(*pair, sems.at[n]) for n, pair in enumerate(pairs)]
    for copy in copies:
        copy.start()
    for copy in copies:
        copy.wait()


def prepare_kernel(core_ref, mine_ref, other_ref, weight_ref, rate_ref, bias_ref, gain_ref,
                   value_hbm, rows_ref, kn_ref, val_ref, dirs_ref, coeff_ref, solved_ref, exit_ref,
                   turn_ref, value_ref, value_sem):
    value_copy = pltpu.make_async_copy(value_hbm, value_ref, value_sem)
    value_copy.start()
    core = core_ref[0]
    half = mine_ref.shape[0]
    rows_ref[pl.ds(pl.multiple_of(core * half, half), half), :] = mine_ref[...]
    rows_ref[pl.ds(pl.multiple_of((1 - core) * half, half), half), :] = other_ref[...]
    seg = rows_ref[...]
    size = turn_ref.shape[0]
    raw = jnp.dot(seg, weight_ref[...], preferred_element_type=F32)
    keys, raw = raw[:, :size], raw[:, size:]
    kn = keys * lax.rsqrt(jnp.mean(keys * keys, axis=-1, keepdims=True) + EPSILON) * gain_ref[...]
    dirs = raw * lax.rsqrt(jnp.sum(raw * raw, axis=-1, keepdims=True) + EPSILON)
    vector = jnp.broadcast_to(rate_ref[...], (16, seg.shape[1]))
    logits = lax.dot_general(seg, vector, (((1,), (1,)), ((), ())), preferred_element_type=F32)
    rates = 2.0 * jax.nn.sigmoid(logits[:, :1] + bias_ref[0])
    kn_ref[...] = kn
    dirs_ref[...] = dirs
    tokens, size = dirs.shape
    rows, cols = iota2((tokens, tokens))
    below = rows > cols
    grams = dot3(dirs, jnp.concatenate([dirs, kn], axis=0), 1, 1)
    lower = jnp.where(below, rates * grams[:, :tokens], 0.0)
    crossing = jnp.where(below, rates * grams[:, tokens:], 0.0)
    inverse = merge_inverse(lower, rows, cols)
    value_copy.wait()
    val_ref[...] = jnp.dot(seg, value_ref[...], preferred_element_type=F32).astype(BF16)
    both = dot3(inverse, jnp.concatenate([crossing, rates * dirs], axis=1))
    coeff_ref[...] = both[:, :tokens]
    solved_ref[...] = both[:, tokens:]
    crossed = dot3(both, dirs, 0, 0)
    exit_ref[...] = kn - crossed[:tokens]
    heads, lanes = iota2((size, size))
    turn_ref[...] = jnp.where(heads == lanes, 1.0, 0.0) - crossed[tokens:]


def leave_kernel(group, place_ref, exit_ref, *refs):
    turn_refs, (leave_ref, starts_ref) = refs[:group], refs[group : group + 2]
    near_refs, (turns_ref, seen_ref) = refs[group + 2 : -2], refs[-2:]
    member = place_ref[0] % group
    tokens, size = exit_ref.shape
    for step in range(group):
        turns_ref[source_of(member, step, group)] = turn_refs[group - 1 - step][...]
    own = exit_ref[...]
    keys = own
    product = None
    heads, lanes = iota2((size, size))
    starts_ref[0] = jnp.where(heads == lanes, 1.0, 0.0)
    for index in range(group):
        seen_ref[index] = keys.astype(BF16)
        turn = turns_ref[index]
        product = turn if product is None else dot3(product, turn)
        if index:
            keys = jnp.where(index > member, dot3(keys, turn), own)
        if index < group - 1:
            starts_ref[index + 1] = product
    high, low = split(keys)
    leave_ref[:tokens] = high
    leave_ref[tokens : 2 * tokens] = low
    high, low = split(product)
    leave_ref[2 * tokens : 2 * tokens + size] = high
    leave_ref[2 * tokens + size :] = low
    for step in range(group):
        near_refs[step][...] = seen_ref[target_of(member, step, group)]


def word_of(slot, segments):
    bits = segments.bit_length()
    per_word = 31 // bits
    return slot // per_word, bits * (slot % per_word), (1 << bits) - 1


def bundle_kernel(group, groups, most, place_ref, mask_ref, after_ref, *refs):
    val_refs, (line_ref, table_ref) = refs[:groups], refs[groups:]
    place = place_ref[0]
    mine = place // group
    segments = mask_ref.shape[0]
    for word in range(table_ref.shape[0]):
        table_ref[word] = 0

    def pick(segment, count):
        wanted = (mask_ref[segment] > 0) & (segment < place) & (count < most)
        word, shift, _ = word_of(count, segments)

        @pl.when(wanted)
        def _():
            table_ref[word] = table_ref[word] | ((segment + 1) << shift)

        return count + wanted.astype(jnp.int32)

    lax.fori_loop(0, segments, pick, jnp.int32(0))
    tokens = val_refs[0].shape[0]
    for ref, way in zip(val_refs, line_order(groups)):
        at = pl.multiple_of(source_of(mine, way, groups) * tokens, tokens)
        line_ref[pl.ds(at, tokens), :] = ref[...]


def query_kernel(rows_ref, weight_hbm, gain_ref, kn_ref, dirs_ref, coeff_ref, solved_ref, val_ref,
                 moved_ref, weighted_ref, peak_ref, total_ref, weight_ref, raw_ref, sems):
    tokens, size = kn_ref.shape
    heads = moved_ref.shape[0]
    pieces, deep, _ = weight_ref.shape
    copies = [
        pltpu.make_async_copy(
            weight_hbm.at[n * deep : (n + 1) * deep, :], weight_ref.at[n], sems.at[n]
        )
        for n in range(pieces)
    ]
    for copy in copies:
        copy.start()
    across = jnp.concatenate([kn_ref[...], dirs_ref[...]], axis=0)
    into = jnp.concatenate([coeff_ref[...], solved_ref[...]], axis=1)
    for n in range(pieces):
        copies[n].wait()
        part = jnp.dot(
            rows_ref[:, n * deep : (n + 1) * deep], weight_ref[n], preferred_element_type=F32
        )
        raw_ref[...] = raw_ref[...] + part if n else part
    count = math.gcd(heads, 4)
    for turn in range(heads // count):
        raw = jnp.concatenate(
            [
                raw_ref[:, head * size : (head + 1) * size]
                for head in range(turn * count, (turn + 1) * count)
            ],
            axis=0,
        )
        queries = (
            raw * lax.rsqrt(jnp.mean(raw * raw, axis=-1, keepdims=True) + EPSILON) * gain_ref[...]
        )
        seen = dot3(queries, across, 1, 1)
        rows, cols = iota2((count * tokens, tokens))
        up_to = rows % tokens >= cols
        reach = jnp.where(up_to, seen[:, tokens:], 0.0)
        taken = dot3(reach, into)
        scores = (seen[:, :tokens] - taken[:, :tokens]) * (LOG2E / math.sqrt(size))
        scores = jnp.where(up_to, scores, NEGATIVE)
        moved = (queries - taken[:, tokens:]).astype(BF16)
        peak = jnp.max(scores, axis=1, keepdims=True)
        weights = jnp.exp2(scores - peak)
        total = jnp.sum(weights, axis=1, keepdims=True)
        weighted = jnp.dot(weights.astype(BF16), val_ref[...], preferred_element_type=F32)
        for h in range(count):
            part = slice(h * tokens, (h + 1) * tokens)
            head = turn * count + h
            moved_ref[head] = moved[part]
            weighted_ref[head] = weighted[part]
            peak_ref[head] = peak[part]
            total_ref[head] = total[part]


def arrive_kernel(groups, group, tokens, place_ref, *refs):
    arrived, starts_ref, near_refs = refs[:groups], refs[groups], refs[groups + 1 :]
    far_refs, (keys_ref, whole_ref) = refs[-group - 2 : -2], refs[-2:]
    mine, member = place_ref[0] // group, place_ref[0] % group
    size = starts_ref.shape[1]
    for ref, step in zip(arrived, line_order(groups)):
        index = source_of(mine, step, groups)
        keys_ref[index] = ref[:tokens].astype(F32) + ref[tokens : 2 * tokens].astype(F32)
        whole = ref[2 * tokens : 2 * tokens + size].astype(F32)
        whole_ref[index] = whole + ref[2 * tokens + size :].astype(F32)
    brought = [keys_ref[groups - 2]]
    product = None
    for index in range(groups - 3, -1, -1):
        keys, whole = keys_ref[index], whole_ref[index + 1]
        if product is not None:
            whole = jnp.where(index + 2 < mine, dot3(whole, product), whole)
        product = whole
        brought.append(jnp.where(index + 1 < mine, dot3(keys, product), keys))
    keys = jnp.concatenate(brought[::-1], axis=0)
    count, size = keys.shape
    ways = [starts_ref[target_of(member, step, group)] for step in range(group)]
    spread = dot3(keys, jnp.concatenate(ways, axis=1)).astype(BF16)
    for step in range(group):
        far_refs[step][:count] = spread[:, step * size : (step + 1) * size]
        far_refs[step][count:] = near_refs[step][...]


def attend_kernel(group, segments, most, place_ref, core_ref, table_ref, *refs):
    far_refs, line_refs = refs[:group][::-1], refs[group : 2 * group][::-1]
    (moved_ref, weighted_ref, peak_ref, total_ref, out_ref, away_ref, kept_ref, keys_ref, vals_ref,
     summed_ref) = refs[2 * group :]
    core = core_ref[0]
    mine, member = place_ref[0] // group, place_ref[0] % group
    heads, tokens, size = moved_ref.shape
    groups = far_refs[0].shape[0] // tokens
    scaling = LOG2E / math.sqrt(size)
    chunk = keys_ref.shape[0] // tokens
    lanes = lax.broadcasted_iota(jnp.int32, (1, chunk * tokens), 1)

    def collect(turn):
        found = jnp.int32(0)
        for slot in range(chunk):
            part = slice(slot * tokens, (slot + 1) * tokens)
            word, shift, ones = word_of(turn * chunk + slot, segments)
            code = (table_ref[word] >> shift) & ones
            found = found + (code > 0).astype(jnp.int32)
            segment = jnp.maximum(code - 1, 0)
            whose, source = segment % group, segment // group
            before = jnp.where(source < mine, source, groups - 1)
            before = pl.multiple_of(before * tokens, tokens)
            after = pl.multiple_of(source * tokens, tokens)
            for number in range(group):

                @pl.when(whose == source_of(member, number, group))
                def _():
                    vals_ref[part, :] = line_refs[number][pl.ds(after, tokens), :]
                    keys_ref[part, :] = far_refs[number][pl.ds(before, tokens), :]

        return jnp.where(lanes < found * tokens, 0.0, NEGATIVE)

    def advance(moved, bias, peak, total, weighted):
        scores = lax.dot_general(
            moved, keys_ref[...], (((1,), (1,)), ((), ())), preferred_element_type=F32
        )
        scores = scores * scaling + bias
        new_peak = jnp.maximum(peak, jnp.max(scores, axis=1, keepdims=True))
        fading = jnp.exp2(peak - new_peak)
        weights = jnp.exp2(scores - new_peak)
        total = total * fading + jnp.sum(weights, axis=1, keepdims=True)
        weighted = weighted * fading + jnp.dot(
            weights.astype(BF16), vals_ref[...], preferred_element_type=F32
        )
        return new_peak, total, weighted

    half = kept_ref.shape[0]
    turns = most // chunk
    if turns == 1:
        bias = collect(0)
    stack = math.gcd(heads, 4)
    wide = math.gcd(out_ref.shape[1], 4 * size)
    for first in range(0, heads, stack):
        some = slice(first, first + stack)
        moved = moved_ref[some].reshape(stack * tokens, size)
        state = (
            peak_ref[some].reshape(stack * tokens, 1),
            total_ref[some].reshape(stack * tokens, 1),
            weighted_ref[some].reshape(stack * tokens, size),
        )
        if turns == 1:
            _, total, weighted = advance(moved, bias, *state)
        else:

            def step_of(turn, state, moved=moved):
                return advance(moved, collect(turn), *state)

            _, total, weighted = lax.fori_loop(0, turns, step_of, state)
        done = (weighted * (1.0 / total)).astype(BF16)
        done = jnp.concatenate(
            [done[n * tokens : (n + 1) * tokens] for n in range(stack)], axis=1
        )
        deep = slice(first * size, (first + stack) * size)
        for at in range(0, out_ref.shape[1], wide):
            part = slice(at, at + wide)
            result = jnp.dot(done, out_ref[deep, part], preferred_element_type=F32)
            if first:
                result = result + summed_ref[:, part]
            if first + stack < heads:
                summed_ref[:, part] = result
            else:
                away_ref[:, part] = jnp.where(core == 0, result[half:], result[:half]).astype(BF16)
                kept_ref[:, part] = jnp.where(core == 0, result[:half], result[half:]).astype(BF16)


def body(
    hidden, w_query, w_key, w_value, w_dir, u_rate, rate_bias, q_gain, k_gain, w_out, block_mask
):
    segments = lax.axis_size("ctx")
    place = lax.axis_index("ctx").astype(jnp.int32).reshape(1)
    core = lax.axis_index("head").astype(jnp.int32).reshape(1)
    group = max(d for d in range(1, math.isqrt(segments) + 1) if segments % d == 0)
    groups = segments // group
    other = lax.ppermute(hidden, "head", [(0, 1), (1, 0)])
    half, width = hidden.shape
    tokens = half * lax.axis_size("head")
    size = w_key.shape[1]
    heads = w_query.shape[1] // size
    smem = pl.BlockSpec(memory_space=pltpu.SMEM)
    vmem = pl.BlockSpec(memory_space=pltpu.VMEM)
    hbm = pl.BlockSpec(memory_space=pltpu.HBM)
    anywhere = pl.BlockSpec(memory_space=pl.ANY)
    square = shaped((tokens, size), F32)

    def swapped(values, count, pairs_of):
        out = [values[0]] * count
        for step in range(count - 1, 0, -1):
            out[step] = lax.ppermute(values[step], "ctx", pairs_of(step))
        return out

    def within_group(values):
        return swapped(values, group, lambda step: [
            (s, s - s % group + target_of(s % group, step, group)) for s in range(segments)
        ])

    def along_line(values):
        return swapped(values, groups, lambda step: [
            (s, s % group + group * target_of(s // group, step, groups)) for s in range(segments)
        ])

    weights, rate_row, key_gain, query_gain, mine = call(
        functools.partial(load_kernel, size),
        (
            shaped((width, 2 * size), BF16), shaped((1, width), BF16), shaped((1, size), F32),
            shaped((1, size), F32), shaped((half, width), BF16),
        ),
        tuple(
            in_hbm(array)
            for array in (
                w_key, w_dir, u_rate, k_gain.reshape(1, size), q_gain.reshape(1, size),
                hidden,
            )
        ),
        in_specs=[hbm] * 6,
        scratch=(pltpu.SemaphoreType.DMA((6,)),),
        moved=12 * width * size,
    )
    rows, kn, val, dirs, coeff, solved, exit_keys, turn = call(
        prepare_kernel,
        (
            shaped((tokens, width), BF16), square, shaped((tokens, size), BF16), square, square,
            square, square, shaped((size, size), F32),
        ),
        (core, mine, other, weights, rate_row, rate_bias, key_gain, in_hbm(w_value)),
        in_specs=[smem] + [vmem] * 4 + [smem, vmem, hbm],
        scratch=(pltpu.VMEM(w_value.shape, BF16), pltpu.SemaphoreType.DMA),
        flops=6 * tokens * width * size,
        moved=8 * width * size,
    )
    turns = within_group([turn] * group)
    line = along_line([val] * groups)
    leaving, starts, *near = call(
        functools.partial(leave_kernel, group),
        [
            shaped((2 * tokens + 2 * size, size), BF16),
            shaped((group, size, size), F32),
        ]
        + [shaped((tokens, size), BF16)] * group,
        (place, exit_keys, *turns[::-1]),
        in_specs=[smem] + [vmem] * (1 + group),
        scratch=(
            pltpu.VMEM((group, size, size), F32),
            pltpu.VMEM((group, tokens, size), BF16),
        ),
        flops=12 * group * size**3,
        moved=10**6,
    )
    arrived = along_line([leaving] * groups)
    most = segments // 4
    values, table = call(
        functools.partial(bundle_kernel, group, groups, most),
        [
            shaped((groups * tokens, size), BF16),
            shaped((word_of(most - 1, segments)[0] + 1,), jnp.int32),
        ],
        (place, block_mask[0], starts, *(line[way] for way in line_order(groups))),
        in_specs=[smem, smem, anywhere] + [vmem] * groups,
        out_specs=[vmem, smem],
        moved=10**6,
        limit=8 + group * groups // 4,
    )
    values = within_group([values] * group)
    own = call(
        query_kernel,
        (
            shaped((heads, tokens, size), BF16),
            shaped((heads, tokens, size), F32),
            shaped((heads, tokens, 1), F32),
            shaped((heads, tokens, 1), F32),
        ),
        (rows, in_hbm(w_query), query_gain, kn, dirs, coeff, solved, val),
        in_specs=[vmem, hbm] + [vmem] * 6,
        scratch=(
            pltpu.VMEM((2, width // 2, w_query.shape[1]), BF16),
            pltpu.VMEM((tokens, w_query.shape[1]), F32),
            pltpu.SemaphoreType.DMA((2,)),
        ),
        flops=4 * tokens * width * heads * size,
        moved=8 * width * heads * size,
        limit=16,
    )
    far = call(
        functools.partial(arrive_kernel, groups, group, tokens),
        [shaped((groups * tokens, size), BF16)] * group,
        (place, *(arrived[step] for step in line_order(groups)), starts, *near),
        in_specs=[smem] + [vmem] * (groups + 1 + group),
        scratch=(
            pltpu.VMEM((groups, tokens, size), F32),
            pltpu.VMEM((groups, size, size), F32),
        ),
        flops=6 * groups * group * size**3,
        moved=10**6,
        limit=8 + group * groups // 4,
    )
    far = within_group(far)
    chunk = math.gcd(most, 4)
    width_out = w_out.shape[1]
    away, kept = call(
        functools.partial(attend_kernel, group, segments, most),
        [shaped((half, width_out), BF16)] * 2,
        (place, core, table, *far[::-1], *values[::-1], *own, w_out),
        in_specs=[smem] * 3 + [vmem] * (2 * group + 5),
        scratch=[
            pltpu.VMEM((chunk * tokens, size), BF16),
            pltpu.VMEM((chunk * tokens, size), BF16),
            pltpu.VMEM((tokens, width_out), F32),
        ],
        flops=2 * tokens * width_out * heads * size,
        moved=4 * 10**6,
        limit=14 + group * groups // 4,
    )
    return kept + lax.ppermute(away, "head", [(0, 1), (1, 0)])


def solution(mesh):
    in_specs = (
        P(("ctx", "head"), None),
        P(None, "head"),
        P(None, "head"),
        P(None, "head"),
        P(None, "head"),
        P("head", None),
        P("head"),
        P(),
        P(),
        P("head", None),
        P("ctx", None),
    )
    out_specs = P(("ctx", "head"), None)
    return jax.shard_map(body, mesh=mesh, in_specs=in_specs, out_specs=out_specs, check_vma=False)
```

```python
import functools
import math

import jax
import jax.numpy as jnp
from jax import lax
from jax.experimental import pallas as pl
from jax.experimental.pallas import tpu as pltpu
from jax.sharding import PartitionSpec as P

EPSILON = 1e-06
NEGATIVE = -1e30
LOG2E = math.log2(math.e)
F32 = jnp.float32
BF16 = jnp.bfloat16
MIB = 1024 * 1024


def call(kernel, out_shape, args, in_specs=None, out_specs=None, scratch=(), flops=0, moved=0, limit=6):
    vmem = pl.BlockSpec(memory_space=pltpu.VMEM)
    return pl.pallas_call(
        kernel,
        out_shape=out_shape,
        in_specs=in_specs or [vmem] * len(args),
        out_specs=out_specs or jax.tree.map(lambda _: vmem, out_shape),
        scratch_shapes=list(scratch),
        compiler_params=pltpu.CompilerParams(vmem_limit_bytes=limit * MIB),
        cost_estimate=pl.CostEstimate(flops=flops, bytes_accessed=moved, transcendentals=0),
    )(*args)


def target_of(member, step, group):
    return member ^ step if group & (group - 1) == 0 else (member + step) % group


def source_of(member, step, group):
    return member ^ step if group & (group - 1) == 0 else (member + group - step) % group


def in_hbm(array):
    return pltpu.with_memory_space_constraint(array, pltpu.HBM)


def line_order(groups):
    return [groups // 2] + [step for step in range(1, groups) if step != groups // 2] + [0]


def shaped(shape, dtype):
    return jax.ShapeDtypeStruct(shape, dtype)


def split(value):
    high = value.astype(BF16)
    return high, (value - high.astype(F32)).astype(BF16)


def dot3(left, right, left_dim=1, right_dim=0):
    left_high, left_low = split(left)
    right_high, right_low = split(right)
    return lax.dot_general(
        jnp.concatenate([left_high, left_high, left_low], axis=left_dim),
        jnp.concatenate([right_high, right_low, right_high], axis=right_dim),
        (((left_dim,), (right_dim,)), ((), ())),
        preferred_element_type=F32,
    )


def iota2(shape):
    return lax.broadcasted_iota(jnp.int32, shape, 0), lax.broadcasted_iota(jnp.int32, shape, 1)


def merge_inverse(lower, rows, cols):
    tokens = lower.shape[0]
    block = 16
    inverse = jnp.where(rows == cols, 1.0, 0.0).astype(F32)
    first = rows - rows % block
    for step in range(block - 1):
        column = jnp.sum(jnp.where(cols == first + step, lower, 0.0), axis=1, keepdims=True)
        pivot = inverse.reshape(tokens // block, block, tokens)[:, step : step + 1, :]
        pivot = jnp.broadcast_to(pivot, (tokens // block, block, tokens)).reshape(tokens, tokens)
        inverse = inverse - column * pivot
    while block < tokens:
        corner = (
            (rows // (2 * block) == cols // (2 * block))
            & (rows % (2 * block) >= block)
            & (cols % (2 * block) < block)
        )
        inverse = inverse - dot3(dot3(inverse, jnp.where(corner, lower, 0.0)), inverse)
        block *= 2
    return inverse


def load_kernel(size, key_hbm, dir_hbm, value_hbm, rate_hbm, key_gain_hbm,
                query_gain_hbm, mine_hbm, weight_ref, rate_ref, key_gain_ref, query_gain_ref,
                mine_ref, sems):
    pairs = [
        (hbm, weight_ref.at[:, index * size : (index + 1) * size])
        for index, hbm in enumerate((key_hbm, dir_hbm, value_hbm))
    ]
    pairs += [(rate_hbm, rate_ref), (key_gain_hbm, key_gain_ref)]
    pairs += [(query_gain_hbm, query_gain_ref), (mine_hbm, mine_ref)]
    copies = [pltpu.make_async_copy(*pair, sems.at[n]) for n, pair in enumerate(pairs)]
    for copy in copies:
        copy.start()
    for copy in copies:
        copy.wait()


def prepare_kernel(core_ref, mine_ref, other_ref, weight_ref, rate_ref, bias_ref, gain_ref,
                   rows_ref, kn_ref, val_ref, dirs_ref, coeff_ref, solved_ref, exit_ref, turn_ref):
    core = core_ref[0]
    half = mine_ref.shape[0]
    rows_ref[pl.ds(pl.multiple_of(core * half, half), half), :] = mine_ref[...]
    rows_ref[pl.ds(pl.multiple_of((1 - core) * half, half), half), :] = other_ref[...]
    seg = rows_ref[...]
    size = turn_ref.shape[0]
    raw = jnp.dot(seg, weight_ref[...], preferred_element_type=F32)
    keys, raw, vals = raw[:, :size], raw[:, size : 2 * size], raw[:, 2 * size :]
    kn = keys * lax.rsqrt(jnp.mean(keys * keys, axis=-1, keepdims=True) + EPSILON) * gain_ref[...]
    dirs = raw * lax.rsqrt(jnp.sum(raw * raw, axis=-1, keepdims=True) + EPSILON)
    vector = jnp.broadcast_to(rate_ref[...], (16, seg.shape[1]))
    logits = lax.dot_general(seg, vector, (((1,), (1,)), ((), ())), preferred_element_type=F32)
    rates = 2.0 * jax.nn.sigmoid(logits[:, :1] + bias_ref[0])
    val_ref[...] = vals.astype(BF16)
    kn_ref[...] = kn
    dirs_ref[...] = dirs
    tokens, size = dirs.shape
    rows, cols = iota2((tokens, tokens))
    below = rows > cols
    grams = dot3(dirs, jnp.concatenate([dirs, kn], axis=0), 1, 1)
    lower = jnp.where(below, rates * grams[:, :tokens], 0.0)
    crossing = jnp.where(below, rates * grams[:, tokens:], 0.0)
    inverse = merge_inverse(lower, rows, cols)
    both = dot3(inverse, jnp.concatenate([crossing, rates * dirs], axis=1))
    coeff_ref[...] = both[:, :tokens]
    solved_ref[...] = both[:, tokens:]
    crossed = dot3(both, dirs, 0, 0)
    exit_ref[...] = kn - crossed[:tokens]
    heads, lanes = iota2((size, size))
    turn_ref[...] = jnp.where(heads == lanes, 1.0, 0.0) - crossed[tokens:]


def leave_kernel(group, place_ref, exit_ref, *refs):
    turn_refs, (leave_ref, starts_ref) = refs[:group], refs[group : group + 2]
    near_refs, (turns_ref, seen_ref) = refs[group + 2 : -2], refs[-2:]
    member = place_ref[0] % group
    tokens, size = exit_ref.shape
    for step in range(group):
        turns_ref[source_of(member, step, group)] = turn_refs[group - 1 - step][...]
    own = exit_ref[...]
    keys = own
    product = None
    heads, lanes = iota2((size, size))
    starts_ref[0] = jnp.where(heads == lanes, 1.0, 0.0)
    for index in range(group):
        seen_ref[index] = keys.astype(BF16)
        turn = turns_ref[index]
        product = turn if product is None else dot3(product, turn)
        if index:
            keys = jnp.where(index > member, dot3(keys, turn), own)
        if index < group - 1:
            starts_ref[index + 1] = product
    high, low = split(keys)
    leave_ref[:tokens] = high
    leave_ref[tokens : 2 * tokens] = low
    high, low = split(product)
    leave_ref[2 * tokens : 2 * tokens + size] = high
    leave_ref[2 * tokens + size :] = low
    for step in range(group):
        near_refs[step][...] = seen_ref[target_of(member, step, group)]


def word_of(slot, segments):
    bits = segments.bit_length()
    per_word = 31 // bits
    return slot // per_word, bits * (slot % per_word), (1 << bits) - 1


def bundle_kernel(group, groups, most, place_ref, mask_ref, after_ref, *refs):
    val_refs, (line_ref, table_ref) = refs[:groups], refs[groups:]
    place = place_ref[0]
    mine = place // group
    segments = mask_ref.shape[0]
    for word in range(table_ref.shape[0]):
        table_ref[word] = 0

    def pick(segment, count):
        wanted = (mask_ref[segment] > 0) & (segment < place) & (count < most)
        word, shift, _ = word_of(count, segments)

        @pl.when(wanted)
        def _():
            table_ref[word] = table_ref[word] | ((segment + 1) << shift)

        return count + wanted.astype(jnp.int32)

    lax.fori_loop(0, segments, pick, jnp.int32(0))
    tokens = val_refs[0].shape[0]
    for way in range(groups):
        at = pl.multiple_of(source_of(mine, way, groups) * tokens, tokens)
        line_ref[pl.ds(at, tokens), :] = val_refs[groups - 1 - way][...]


def query_kernel(rows_ref, weight_hbm, gain_ref, kn_ref, dirs_ref, coeff_ref, solved_ref, val_ref,
                 moved_ref, weighted_ref, peak_ref, total_ref, weight_ref, raw_ref, sems):
    tokens, size = kn_ref.shape
    heads = moved_ref.shape[0]
    pieces, deep, _ = weight_ref.shape
    copies = [
        pltpu.make_async_copy(
            weight_hbm.at[n * deep : (n + 1) * deep, :], weight_ref.at[n], sems.at[n]
        )
        for n in range(pieces)
    ]
    for copy in copies:
        copy.start()
    across = jnp.concatenate([kn_ref[...], dirs_ref[...]], axis=0)
    into = jnp.concatenate([coeff_ref[...], solved_ref[...]], axis=1)
    for n in range(pieces):
        copies[n].wait()
        part = jnp.dot(
            rows_ref[:, n * deep : (n + 1) * deep], weight_ref[n], preferred_element_type=F32
        )
        raw_ref[...] = raw_ref[...] + part if n else part
    count = math.gcd(heads, 4)
    for turn in range(heads // count):
        raw = jnp.concatenate(
            [
                raw_ref[:, head * size : (head + 1) * size]
                for head in range(turn * count, (turn + 1) * count)
            ],
            axis=0,
        )
        queries = (
            raw * lax.rsqrt(jnp.mean(raw * raw, axis=-1, keepdims=True) + EPSILON) * gain_ref[...]
        )
        seen = dot3(queries, across, 1, 1)
        rows, cols = iota2((count * tokens, tokens))
        up_to = rows % tokens >= cols
        reach = jnp.where(up_to, seen[:, tokens:], 0.0)
        taken = dot3(reach, into)
        scores = (seen[:, :tokens] - taken[:, :tokens]) * (LOG2E / math.sqrt(size))
        scores = jnp.where(up_to, scores, NEGATIVE)
        moved = (queries - taken[:, tokens:]).astype(BF16)
        peak = jnp.max(scores, axis=1, keepdims=True)
        weights = jnp.exp2(scores - peak)
        total = jnp.sum(weights, axis=1, keepdims=True)
        weighted = jnp.dot(weights.astype(BF16), val_ref[...], preferred_element_type=F32)
        for h in range(count):
            part = slice(h * tokens, (h + 1) * tokens)
            head = turn * count + h
            moved_ref[head] = moved[part]
            weighted_ref[head] = weighted[part]
            peak_ref[head] = peak[part]
            total_ref[head] = total[part]


def arrive_kernel(groups, group, tokens, place_ref, *refs):
    arrived, starts_ref, near_refs = refs[:groups], refs[groups], refs[groups + 1 :]
    far_refs, (keys_ref, whole_ref) = refs[-group - 2 : -2], refs[-2:]
    mine, member = place_ref[0] // group, place_ref[0] % group
    size = starts_ref.shape[1]
    for ref, step in zip(arrived, line_order(groups)):
        index = source_of(mine, step, groups)
        keys_ref[index] = ref[:tokens].astype(F32) + ref[tokens : 2 * tokens].astype(F32)
        whole = ref[2 * tokens : 2 * tokens + size].astype(F32)
        whole_ref[index] = whole + ref[2 * tokens + size :].astype(F32)
    brought = [keys_ref[groups - 2]]
    product = None
    for index in range(groups - 3, -1, -1):
        keys, whole = keys_ref[index], whole_ref[index + 1]
        if product is not None:
            whole = jnp.where(index + 2 < mine, dot3(whole, product), whole)
        product = whole
        brought.append(jnp.where(index + 1 < mine, dot3(keys, product), keys))
    keys = jnp.concatenate(brought[::-1], axis=0)
    count, size = keys.shape
    ways = [starts_ref[target_of(member, step, group)] for step in range(group)]
    spread = dot3(keys, jnp.concatenate(ways, axis=1)).astype(BF16)
    for step in range(group):
        far_refs[step][:count] = spread[:, step * size : (step + 1) * size]
        far_refs[step][count:] = near_refs[step][...]


def attend_kernel(group, segments, most, place_ref, core_ref, table_ref, *refs):
    far_refs, line_refs = refs[:group][::-1], refs[group : 2 * group][::-1]
    (moved_ref, weighted_ref, peak_ref, total_ref, out_ref, away_ref, kept_ref, keys_ref, vals_ref,
     summed_ref) = refs[2 * group :]
    core = core_ref[0]
    mine, member = place_ref[0] // group, place_ref[0] % group
    heads, tokens, size = moved_ref.shape
    groups = far_refs[0].shape[0] // tokens
    scaling = LOG2E / math.sqrt(size)
    chunk = keys_ref.shape[0] // tokens
    lanes = lax.broadcasted_iota(jnp.int32, (1, chunk * tokens), 1)

    def collect(turn):
        found = jnp.int32(0)
        for slot in range(chunk):
            part = slice(slot * tokens, (slot + 1) * tokens)
            word, shift, ones = word_of(turn * chunk + slot, segments)
            code = (table_ref[word] >> shift) & ones
            found = found + (code > 0).astype(jnp.int32)
            segment = jnp.maximum(code - 1, 0)
            whose, source = segment % group, segment // group
            before = jnp.where(source < mine, source, groups - 1)
            before = pl.multiple_of(before * tokens, tokens)
            after = pl.multiple_of(source * tokens, tokens)
            for number in range(group):

                @pl.when(whose == source_of(member, number, group))
                def _():
                    vals_ref[part, :] = line_refs[number][pl.ds(after, tokens), :]
                    keys_ref[part, :] = far_refs[number][pl.ds(before, tokens), :]

        return jnp.where(lanes < found * tokens, 0.0, NEGATIVE)

    def advance(moved, bias, peak, total, weighted):
        scores = lax.dot_general(
            moved, keys_ref[...], (((1,), (1,)), ((), ())), preferred_element_type=F32
        )
        scores = scores * scaling + bias
        new_peak = jnp.maximum(peak, jnp.max(scores, axis=1, keepdims=True))
        fading = jnp.exp2(peak - new_peak)
        weights = jnp.exp2(scores - new_peak)
        total = total * fading + jnp.sum(weights, axis=1, keepdims=True)
        weighted = weighted * fading + jnp.dot(
            weights.astype(BF16), vals_ref[...], preferred_element_type=F32
        )
        return new_peak, total, weighted

    half = kept_ref.shape[0]
    turns = most // chunk
    if turns == 1:
        bias = collect(0)
    stack = math.gcd(heads, 4)
    wide = math.gcd(out_ref.shape[1], 4 * size)
    for first in range(0, heads, stack):
        some = slice(first, first + stack)
        moved = moved_ref[some].reshape(stack * tokens, size)
        state = (
            peak_ref[some].reshape(stack * tokens, 1),
            total_ref[some].reshape(stack * tokens, 1),
            weighted_ref[some].reshape(stack * tokens, size),
        )
        if turns == 1:
            _, total, weighted = advance(moved, bias, *state)
        else:

            def step_of(turn, state, moved=moved):
                return advance(moved, collect(turn), *state)

            _, total, weighted = lax.fori_loop(0, turns, step_of, state)
        done = (weighted * (1.0 / total)).astype(BF16)
        done = jnp.concatenate(
            [done[n * tokens : (n + 1) * tokens] for n in range(stack)], axis=1
        )
        deep = slice(first * size, (first + stack) * size)
        for at in range(0, out_ref.shape[1], wide):
            part = slice(at, at + wide)
            result = jnp.dot(done, out_ref[deep, part], preferred_element_type=F32)
            if first:
                result = result + summed_ref[:, part]
            if first + stack < heads:
                summed_ref[:, part] = result
            else:
                away_ref[:, part] = jnp.where(core == 0, result[half:], result[:half]).astype(BF16)
                kept_ref[:, part] = jnp.where(core == 0, result[:half], result[half:]).astype(BF16)


def body(
    hidden, w_query, w_key, w_value, w_dir, u_rate, rate_bias, q_gain, k_gain, w_out, block_mask
):
    segments = lax.axis_size("ctx")
    place = lax.axis_index("ctx").astype(jnp.int32).reshape(1)
    core = lax.axis_index("head").astype(jnp.int32).reshape(1)
    group = max(d for d in range(1, math.isqrt(segments) + 1) if segments % d == 0)
    groups = segments // group
    other = lax.ppermute(hidden, "head", [(0, 1), (1, 0)])
    half, width = hidden.shape
    tokens = half * lax.axis_size("head")
    size = w_key.shape[1]
    heads = w_query.shape[1] // size
    smem = pl.BlockSpec(memory_space=pltpu.SMEM)
    vmem = pl.BlockSpec(memory_space=pltpu.VMEM)
    hbm = pl.BlockSpec(memory_space=pltpu.HBM)
    anywhere = pl.BlockSpec(memory_space=pl.ANY)
    square = shaped((tokens, size), F32)

    def swapped(values, count, pairs_of):
        out = [values[0]] * count
        for step in range(count - 1, 0, -1):
            out[step] = lax.ppermute(values[step], "ctx", pairs_of(step))
        return out

    def within_group(values):
        return swapped(values, group, lambda step: [
            (s, s - s % group + target_of(s % group, step, group)) for s in range(segments)
        ])

    def along_line(values):
        return swapped(values, groups, lambda step: [
            (s, s % group + group * target_of(s // group, step, groups)) for s in range(segments)
        ])

    weights, rate_row, key_gain, query_gain, mine = call(
        functools.partial(load_kernel, size),
        (
            shaped((width, 3 * size), BF16), shaped((1, width), BF16), shaped((1, size), F32),
            shaped((1, size), F32), shaped((half, width), BF16),
        ),
        tuple(
            in_hbm(array)
            for array in (
                w_key, w_dir, w_value, u_rate, k_gain.reshape(1, size), q_gain.reshape(1, size),
                hidden,
            )
        ),
        in_specs=[hbm] * 7,
        scratch=(pltpu.SemaphoreType.DMA((7,)),),
        moved=12 * width * size,
    )
    rows, kn, val, dirs, coeff, solved, exit_keys, turn = call(
        prepare_kernel,
        (
            shaped((tokens, width), BF16), square, shaped((tokens, size), BF16), square, square,
            square, square, shaped((size, size), F32),
        ),
        (core, mine, other, weights, rate_row, rate_bias, key_gain),
        in_specs=[smem] + [vmem] * 4 + [smem, vmem],
        flops=6 * tokens * width * size,
        moved=8 * width * size,
    )
    turns = within_group([turn] * group)
    line = along_line([val] * groups)
    leaving, starts, *near = call(
        functools.partial(leave_kernel, group),
        [
            shaped((2 * tokens + 2 * size, size), BF16),
            shaped((group, size, size), F32),
        ]
        + [shaped((tokens, size), BF16)] * group,
        (place, exit_keys, *turns[::-1]),
        in_specs=[smem] + [vmem] * (1 + group),
        scratch=(
            pltpu.VMEM((group, size, size), F32),
            pltpu.VMEM((group, tokens, size), BF16),
        ),
        flops=12 * group * size**3,
        moved=10**6,
    )
    arrived = along_line([leaving] * groups)
    most = segments // 4
    values, table = call(
        functools.partial(bundle_kernel, group, groups, most),
        [
            shaped((groups * tokens, size), BF16),
            shaped((word_of(most - 1, segments)[0] + 1,), jnp.int32),
        ],
        (place, block_mask[0], starts, *line[::-1]),
        in_specs=[smem, smem, anywhere] + [vmem] * groups,
        out_specs=[vmem, smem],
        moved=10**6,
        limit=8 + group * groups // 4,
    )
    values = within_group([values] * group)
    own = call(
        query_kernel,
        (
            shaped((heads, tokens, size), BF16),
            shaped((heads, tokens, size), F32),
            shaped((heads, tokens, 1), F32),
            shaped((heads, tokens, 1), F32),
        ),
        (rows, in_hbm(w_query), query_gain, kn, dirs, coeff, solved, val),
        in_specs=[vmem, hbm] + [vmem] * 6,
        scratch=(
            pltpu.VMEM((2, width // 2, w_query.shape[1]), BF16),
            pltpu.VMEM((tokens, w_query.shape[1]), F32),
            pltpu.SemaphoreType.DMA((2,)),
        ),
        flops=4 * tokens * width * heads * size,
        moved=8 * width * heads * size,
        limit=16,
    )
    far = call(
        functools.partial(arrive_kernel, groups, group, tokens),
        [shaped((groups * tokens, size), BF16)] * group,
        (place, *(arrived[step] for step in line_order(groups)), starts, *near),
        in_specs=[smem] + [vmem] * (groups + 1 + group),
        scratch=(
            pltpu.VMEM((groups, tokens, size), F32),
            pltpu.VMEM((groups, size, size), F32),
        ),
        flops=6 * groups * group * size**3,
        moved=10**6,
        limit=8 + group * groups // 4,
    )
    far = within_group(far)
    chunk = math.gcd(most, 4)
    width_out = w_out.shape[1]
    away, kept = call(
        functools.partial(attend_kernel, group, segments, most),
        [shaped((half, width_out), BF16)] * 2,
        (place, core, table, *far[::-1], *values[::-1], *own, w_out),
        in_specs=[smem] * 3 + [vmem] * (2 * group + 5),
        scratch=[
            pltpu.VMEM((chunk * tokens, size), BF16),
            pltpu.VMEM((chunk * tokens, size), BF16),
            pltpu.VMEM((tokens, width_out), F32),
        ],
        flops=2 * tokens * width_out * heads * size,
        moved=4 * 10**6,
        limit=14 + group * groups // 4,
    )
    return kept + lax.ppermute(away, "head", [(0, 1), (1, 0)])


def solution(mesh):
    in_specs = (
        P(("ctx", "head"), None),
        P(None, "head"),
        P(None, "head"),
        P(None, "head"),
        P(None, "head"),
        P("head", None),
        P("head"),
        P(),
        P(),
        P("head", None),
        P("ctx", None),
    )
    out_specs = P(("ctx", "head"), None)
    return jax.shard_map(body, mesh=mesh, in_specs=in_specs, out_specs=out_specs, check_vma=False)
```

```python
import functools
import math

import jax
import jax.numpy as jnp
from jax import lax
from jax.experimental import pallas as pl
from jax.experimental.pallas import tpu as pltpu
from jax.sharding import PartitionSpec as P

EPSILON = 1e-06
NEGATIVE = -1e30
LOG2E = math.log2(math.e)
F32 = jnp.float32
BF16 = jnp.bfloat16
MIB = 1024 * 1024


def call(kernel, out_shape, args, in_specs=None, out_specs=None, scratch=(), flops=0, moved=0, limit=6):
    vmem = pl.BlockSpec(memory_space=pltpu.VMEM)
    return pl.pallas_call(
        kernel,
        out_shape=out_shape,
        in_specs=in_specs or [vmem] * len(args),
        out_specs=out_specs or jax.tree.map(lambda _: vmem, out_shape),
        scratch_shapes=list(scratch),
        compiler_params=pltpu.CompilerParams(vmem_limit_bytes=limit * MIB),
        cost_estimate=pl.CostEstimate(flops=flops, bytes_accessed=moved, transcendentals=0),
    )(*args)


def target_of(member, step, group):
    return member ^ step if group & (group - 1) == 0 else (member + step) % group


def source_of(member, step, group):
    return member ^ step if group & (group - 1) == 0 else (member + group - step) % group


def in_hbm(array):
    return pltpu.with_memory_space_constraint(array, pltpu.HBM)


def line_order(groups):
    return [groups // 2] + [step for step in range(1, groups) if step != groups // 2] + [0]


def shaped(shape, dtype):
    return jax.ShapeDtypeStruct(shape, dtype)


def split(value):
    high = value.astype(BF16)
    return high, (value - high.astype(F32)).astype(BF16)


def dot3(left, right, left_dim=1, right_dim=0):
    left_high, left_low = split(left)
    right_high, right_low = split(right)
    return lax.dot_general(
        jnp.concatenate([left_high, left_high, left_low], axis=left_dim),
        jnp.concatenate([right_high, right_low, right_high], axis=right_dim),
        (((left_dim,), (right_dim,)), ((), ())),
        preferred_element_type=F32,
    )


def iota2(shape):
    return lax.broadcasted_iota(jnp.int32, shape, 0), lax.broadcasted_iota(jnp.int32, shape, 1)


def merge_inverse(lower, rows, cols):
    tokens = lower.shape[0]
    block = 16
    inverse = jnp.where(rows == cols, 1.0, 0.0).astype(F32)
    first = rows - rows % block
    for step in range(block - 1):
        column = jnp.sum(jnp.where(cols == first + step, lower, 0.0), axis=1, keepdims=True)
        pivot = inverse.reshape(tokens // block, block, tokens)[:, step : step + 1, :]
        pivot = jnp.broadcast_to(pivot, (tokens // block, block, tokens)).reshape(tokens, tokens)
        inverse = inverse - column * pivot
    while block < tokens:
        corner = (
            (rows // (2 * block) == cols // (2 * block))
            & (rows % (2 * block) >= block)
            & (cols % (2 * block) < block)
        )
        inverse = inverse - dot3(dot3(inverse, jnp.where(corner, lower, 0.0)), inverse)
        block *= 2
    return inverse


def load_kernel(size, key_hbm, dir_hbm, rate_hbm, key_gain_hbm,
                query_gain_hbm, mine_hbm, weight_ref, rate_ref, key_gain_ref, query_gain_ref,
                mine_ref, sems):
    pairs = [
        (hbm, weight_ref.at[:, index * size : (index + 1) * size])
        for index, hbm in enumerate((key_hbm, dir_hbm))
    ]
    pairs += [(rate_hbm, rate_ref), (key_gain_hbm, key_gain_ref)]
    pairs += [(query_gain_hbm, query_gain_ref), (mine_hbm, mine_ref)]
    copies = [pltpu.make_async_copy(*pair, sems.at[n]) for n, pair in enumerate(pairs)]
    for copy in copies:
        copy.start()
    for copy in copies:
        copy.wait()


def prepare_kernel(core_ref, mine_ref, other_ref, weight_ref, rate_ref, bias_ref, gain_ref,
                   value_hbm, rows_ref, kn_ref, val_ref, dirs_ref, coeff_ref, solved_ref, exit_ref,
                   turn_ref, value_ref, value_sem):
    value_copy = pltpu.make_async_copy(value_hbm, value_ref, value_sem)
    value_copy.start()
    core = core_ref[0]
    half = mine_ref.shape[0]
    rows_ref[pl.ds(pl.multiple_of(core * half, half), half), :] = mine_ref[...]
    rows_ref[pl.ds(pl.multiple_of((1 - core) * half, half), half), :] = other_ref[...]
    seg = rows_ref[...]
    size = turn_ref.shape[0]
    raw = jnp.dot(seg, weight_ref[...], preferred_element_type=F32)
    keys, raw = raw[:, :size], raw[:, size:]
    kn = keys * lax.rsqrt(jnp.mean(keys * keys, axis=-1, keepdims=True) + EPSILON) * gain_ref[...]
    dirs = raw * lax.rsqrt(jnp.sum(raw * raw, axis=-1, keepdims=True) + EPSILON)
    vector = jnp.broadcast_to(rate_ref[...], (16, seg.shape[1]))
    logits = lax.dot_general(seg, vector, (((1,), (1,)), ((), ())), preferred_element_type=F32)
    rates = 2.0 * jax.nn.sigmoid(logits[:, :1] + bias_ref[0])
    kn_ref[...] = kn
    dirs_ref[...] = dirs
    tokens, size = dirs.shape
    rows, cols = iota2((tokens, tokens))
    below = rows > cols
    grams = dot3(dirs, jnp.concatenate([dirs, kn], axis=0), 1, 1)
    lower = jnp.where(below, rates * grams[:, :tokens], 0.0)
    crossing = jnp.where(below, rates * grams[:, tokens:], 0.0)
    inverse = merge_inverse(lower, rows, cols)
    value_copy.wait()
    val_ref[...] = jnp.dot(seg, value_ref[...], preferred_element_type=F32).astype(BF16)
    both = dot3(inverse, jnp.concatenate([crossing, rates * dirs], axis=1))
    coeff_ref[...] = both[:, :tokens]
    solved_ref[...] = both[:, tokens:]
    crossed = dot3(both, dirs, 0, 0)
    exit_ref[...] = kn - crossed[:tokens]
    heads, lanes = iota2((size, size))
    turn_ref[...] = jnp.where(heads == lanes, 1.0, 0.0) - crossed[tokens:]


def leave_kernel(group, place_ref, exit_ref, *refs):
    turn_refs, (leave_ref, starts_ref) = refs[:group], refs[group : group + 2]
    near_refs, (turns_ref, seen_ref) = refs[group + 2 : -2], refs[-2:]
    member = place_ref[0] % group
    tokens, size = exit_ref.shape
    for step in range(group):
        turns_ref[source_of(member, step, group)] = turn_refs[group - 1 - step][...]
    own = exit_ref[...]
    keys = own
    product = None
    heads, lanes = iota2((size, size))
    starts_ref[0] = jnp.where(heads == lanes, 1.0, 0.0)
    for index in range(group):
        seen_ref[index] = keys.astype(BF16)
        turn = turns_ref[index]
        product = turn if product is None else dot3(product, turn)
        if index:
            keys = jnp.where(index > member, dot3(keys, turn), own)
        if index < group - 1:
            starts_ref[index + 1] = product
    high, low = split(keys)
    leave_ref[:tokens] = high
    leave_ref[tokens : 2 * tokens] = low
    high, low = split(product)
    leave_ref[2 * tokens : 2 * tokens + size] = high
    leave_ref[2 * tokens + size :] = low
    for step in range(group):
        near_refs[step][...] = seen_ref[target_of(member, step, group)]


def word_of(slot, segments):
    bits = segments.bit_length()
    per_word = 31 // bits
    return slot // per_word, bits * (slot % per_word), (1 << bits) - 1


def bundle_kernel(group, groups, most, place_ref, mask_ref, after_ref, *refs):
    val_refs, (line_ref, table_ref) = refs[:groups], refs[groups:]
    place = place_ref[0]
    mine = place // group
    segments = mask_ref.shape[0]
    for word in range(table_ref.shape[0]):
        table_ref[word] = 0

    def pick(segment, count):
        wanted = (mask_ref[segment] > 0) & (segment < place) & (count < most)
        word, shift, _ = word_of(count, segments)

        @pl.when(wanted)
        def _():
            table_ref[word] = table_ref[word] | ((segment + 1) << shift)

        return count + wanted.astype(jnp.int32)

    lax.fori_loop(0, segments, pick, jnp.int32(0))
    tokens = val_refs[0].shape[0]
    for way in range(groups):
        at = pl.multiple_of(source_of(mine, way, groups) * tokens, tokens)
        line_ref[pl.ds(at, tokens), :] = val_refs[groups - 1 - way][...]


def query_kernel(rows_ref, weight_hbm, gain_ref, kn_ref, dirs_ref, coeff_ref, solved_ref, val_ref,
                 moved_ref, weighted_ref, peak_ref, total_ref, weight_ref, raw_ref, sems):
    tokens, size = kn_ref.shape
    heads = moved_ref.shape[0]
    pieces, deep, _ = weight_ref.shape
    copies = [
        pltpu.make_async_copy(
            weight_hbm.at[n * deep : (n + 1) * deep, :], weight_ref.at[n], sems.at[n]
        )
        for n in range(pieces)
    ]
    for copy in copies:
        copy.start()
    across = jnp.concatenate([kn_ref[...], dirs_ref[...]], axis=0)
    into = jnp.concatenate([coeff_ref[...], solved_ref[...]], axis=1)
    for n in range(pieces):
        copies[n].wait()
        part = jnp.dot(
            rows_ref[:, n * deep : (n + 1) * deep], weight_ref[n], preferred_element_type=F32
        )
        raw_ref[...] = raw_ref[...] + part if n else part
    count = math.gcd(heads, 4)
    for turn in range(heads // count):
        raw = jnp.concatenate(
            [
                raw_ref[:, head * size : (head + 1) * size]
                for head in range(turn * count, (turn + 1) * count)
            ],
            axis=0,
        )
        queries = (
            raw * lax.rsqrt(jnp.mean(raw * raw, axis=-1, keepdims=True) + EPSILON) * gain_ref[...]
        )
        seen = dot3(queries, across, 1, 1)
        rows, cols = iota2((count * tokens, tokens))
        up_to = rows % tokens >= cols
        reach = jnp.where(up_to, seen[:, tokens:], 0.0)
        taken = dot3(reach, into)
        scores = (seen[:, :tokens] - taken[:, :tokens]) * (LOG2E / math.sqrt(size))
        scores = jnp.where(up_to, scores, NEGATIVE)
        moved = (queries - taken[:, tokens:]).astype(BF16)
        peak = jnp.max(scores, axis=1, keepdims=True)
        weights = jnp.exp2(scores - peak)
        total = jnp.sum(weights, axis=1, keepdims=True)
        weighted = jnp.dot(weights.astype(BF16), val_ref[...], preferred_element_type=F32)
        for h in range(count):
            part = slice(h * tokens, (h + 1) * tokens)
            head = turn * count + h
            moved_ref[head] = moved[part]
            weighted_ref[head] = weighted[part]
            peak_ref[head] = peak[part]
            total_ref[head] = total[part]


def arrive_kernel(groups, group, tokens, place_ref, *refs):
    arrived, starts_ref, near_refs = refs[:groups], refs[groups], refs[groups + 1 :]
    far_refs, (keys_ref, whole_ref) = refs[-group - 2 : -2], refs[-2:]
    mine, member = place_ref[0] // group, place_ref[0] % group
    size = starts_ref.shape[1]
    for ref, step in zip(arrived, line_order(groups)):
        index = source_of(mine, step, groups)
        keys_ref[index] = ref[:tokens].astype(F32) + ref[tokens : 2 * tokens].astype(F32)
        whole = ref[2 * tokens : 2 * tokens + size].astype(F32)
        whole_ref[index] = whole + ref[2 * tokens + size :].astype(F32)
    brought = [keys_ref[groups - 2]]
    product = None
    for index in range(groups - 3, -1, -1):
        keys, whole = keys_ref[index], whole_ref[index + 1]
        if product is not None:
            whole = jnp.where(index + 2 < mine, dot3(whole, product), whole)
        product = whole
        brought.append(jnp.where(index + 1 < mine, dot3(keys, product), keys))
    keys = jnp.concatenate(brought[::-1], axis=0)
    count, size = keys.shape
    ways = [starts_ref[target_of(member, step, group)] for step in range(group)]
    spread = dot3(keys, jnp.concatenate(ways, axis=1)).astype(BF16)
    for step in range(group):
        far_refs[step][:count] = spread[:, step * size : (step + 1) * size]
        far_refs[step][count:] = near_refs[step][...]


def attend_kernel(group, segments, most, place_ref, core_ref, table_ref, *refs):
    far_refs, line_refs = refs[:group][::-1], refs[group : 2 * group][::-1]
    (moved_ref, weighted_ref, peak_ref, total_ref, out_ref, away_ref, kept_ref, keys_ref, vals_ref,
     summed_ref) = refs[2 * group :]
    core = core_ref[0]
    mine, member = place_ref[0] // group, place_ref[0] % group
    heads, tokens, size = moved_ref.shape
    groups = far_refs[0].shape[0] // tokens
    scaling = LOG2E / math.sqrt(size)
    chunk = keys_ref.shape[0] // tokens
    lanes = lax.broadcasted_iota(jnp.int32, (1, chunk * tokens), 1)

    def collect(turn):
        found = jnp.int32(0)
        for slot in range(chunk):
            part = slice(slot * tokens, (slot + 1) * tokens)
            word, shift, ones = word_of(turn * chunk + slot, segments)
            code = (table_ref[word] >> shift) & ones
            found = found + (code > 0).astype(jnp.int32)
            segment = jnp.maximum(code - 1, 0)
            whose, source = segment % group, segment // group
            before = jnp.where(source < mine, source, groups - 1)
            before = pl.multiple_of(before * tokens, tokens)
            after = pl.multiple_of(source * tokens, tokens)
            for number in range(group):

                @pl.when(whose == source_of(member, number, group))
                def _():
                    vals_ref[part, :] = line_refs[number][pl.ds(after, tokens), :]
                    keys_ref[part, :] = far_refs[number][pl.ds(before, tokens), :]

        return jnp.where(lanes < found * tokens, 0.0, NEGATIVE)

    def advance(moved, bias, peak, total, weighted):
        scores = lax.dot_general(
            moved, keys_ref[...], (((1,), (1,)), ((), ())), preferred_element_type=F32
        )
        scores = scores * scaling + bias
        new_peak = jnp.maximum(peak, jnp.max(scores, axis=1, keepdims=True))
        fading = jnp.exp2(peak - new_peak)
        weights = jnp.exp2(scores - new_peak)
        total = total * fading + jnp.sum(weights, axis=1, keepdims=True)
        weighted = weighted * fading + jnp.dot(
            weights.astype(BF16), vals_ref[...], preferred_element_type=F32
        )
        return new_peak, total, weighted

    half = kept_ref.shape[0]
    turns = most // chunk
    if turns == 1:
        bias = collect(0)
    stack = math.gcd(heads, 4)
    wide = math.gcd(out_ref.shape[1], 8 * size)
    for first in range(0, heads, stack):
        some = slice(first, first + stack)
        moved = moved_ref[some].reshape(stack * tokens, size)
        state = (
            peak_ref[some].reshape(stack * tokens, 1),
            total_ref[some].reshape(stack * tokens, 1),
            weighted_ref[some].reshape(stack * tokens, size),
        )
        if turns == 1:
            _, total, weighted = advance(moved, bias, *state)
        else:

            def step_of(turn, state, moved=moved):
                return advance(moved, collect(turn), *state)

            _, total, weighted = lax.fori_loop(0, turns, step_of, state)
        done = (weighted * (1.0 / total)).astype(BF16)
        done = jnp.concatenate(
            [done[n * tokens : (n + 1) * tokens] for n in range(stack)], axis=1
        )
        deep = slice(first * size, (first + stack) * size)
        for at in range(0, out_ref.shape[1], wide):
            part = slice(at, at + wide)
            result = jnp.dot(done, out_ref[deep, part], preferred_element_type=F32)
            if first:
                result = result + summed_ref[:, part]
            if first + stack < heads:
                summed_ref[:, part] = result
            else:
                away_ref[:, part] = jnp.where(core == 0, result[half:], result[:half]).astype(BF16)
                kept_ref[:, part] = jnp.where(core == 0, result[:half], result[half:]).astype(BF16)


def body(
    hidden, w_query, w_key, w_value, w_dir, u_rate, rate_bias, q_gain, k_gain, w_out, block_mask
):
    segments = lax.axis_size("ctx")
    place = lax.axis_index("ctx").astype(jnp.int32).reshape(1)
    core = lax.axis_index("head").astype(jnp.int32).reshape(1)
    group = max(d for d in range(1, math.isqrt(segments) + 1) if segments % d == 0)
    groups = segments // group
    other = lax.ppermute(hidden, "head", [(0, 1), (1, 0)])
    half, width = hidden.shape
    tokens = half * lax.axis_size("head")
    size = w_key.shape[1]
    heads = w_query.shape[1] // size
    smem = pl.BlockSpec(memory_space=pltpu.SMEM)
    vmem = pl.BlockSpec(memory_space=pltpu.VMEM)
    hbm = pl.BlockSpec(memory_space=pltpu.HBM)
    anywhere = pl.BlockSpec(memory_space=pl.ANY)
    square = shaped((tokens, size), F32)

    def swapped(values, count, pairs_of):
        out = [values[0]] * count
        for step in range(count - 1, 0, -1):
            out[step] = lax.ppermute(values[step], "ctx", pairs_of(step))
        return out

    def within_group(values):
        return swapped(values, group, lambda step: [
            (s, s - s % group + target_of(s % group, step, group)) for s in range(segments)
        ])

    def along_line(values):
        return swapped(values, groups, lambda step: [
            (s, s % group + group * target_of(s // group, step, groups)) for s in range(segments)
        ])

    weights, rate_row, key_gain, query_gain, mine = call(
        functools.partial(load_kernel, size),
        (
            shaped((width, 2 * size), BF16), shaped((1, width), BF16), shaped((1, size), F32),
            shaped((1, size), F32), shaped((half, width), BF16),
        ),
        tuple(
            in_hbm(array)
            for array in (
                w_key, w_dir, u_rate, k_gain.reshape(1, size), q_gain.reshape(1, size),
                hidden,
            )
        ),
        in_specs=[hbm] * 6,
        scratch=(pltpu.SemaphoreType.DMA((6,)),),
        moved=12 * width * size,
    )
    rows, kn, val, dirs, coeff, solved, exit_keys, turn = call(
        prepare_kernel,
        (
            shaped((tokens, width), BF16), square, shaped((tokens, size), BF16), square, square,
            square, square, shaped((size, size), F32),
        ),
        (core, mine, other, weights, rate_row, rate_bias, key_gain, in_hbm(w_value)),
        in_specs=[smem] + [vmem] * 4 + [smem, vmem, hbm],
        scratch=(pltpu.VMEM(w_value.shape, BF16), pltpu.SemaphoreType.DMA),
        flops=6 * tokens * width * size,
        moved=8 * width * size,
    )
    turns = within_group([turn] * group)
    line = along_line([val] * groups)
    leaving, starts, *near = call(
        functools.partial(leave_kernel, group),
        [
            shaped((2 * tokens + 2 * size, size), BF16),
            shaped((group, size, size), F32),
        ]
        + [shaped((tokens, size), BF16)] * group,
        (place, exit_keys, *turns[::-1]),
        in_specs=[smem] + [vmem] * (1 + group),
        scratch=(
            pltpu.VMEM((group, size, size), F32),
            pltpu.VMEM((group, tokens, size), BF16),
        ),
        flops=12 * group * size**3,
        moved=10**6,
    )
    arrived = along_line([leaving] * groups)
    most = segments // 4
    values, table = call(
        functools.partial(bundle_kernel, group, groups, most),
        [
            shaped((groups * tokens, size), BF16),
            shaped((word_of(most - 1, segments)[0] + 1,), jnp.int32),
        ],
        (place, block_mask[0], starts, *line[::-1]),
        in_specs=[smem, smem, anywhere] + [vmem] * groups,
        out_specs=[vmem, smem],
        moved=10**6,
        limit=8 + group * groups // 4,
    )
    values = within_group([values] * group)
    own = call(
        query_kernel,
        (
            shaped((heads, tokens, size), BF16),
            shaped((heads, tokens, size), F32),
            shaped((heads, tokens, 1), F32),
            shaped((heads, tokens, 1), F32),
        ),
        (rows, in_hbm(w_query), query_gain, kn, dirs, coeff, solved, val),
        in_specs=[vmem, hbm] + [vmem] * 6,
        scratch=(
            pltpu.VMEM((2, width // 2, w_query.shape[1]), BF16),
            pltpu.VMEM((tokens, w_query.shape[1]), F32),
            pltpu.SemaphoreType.DMA((2,)),
        ),
        flops=4 * tokens * width * heads * size,
        moved=8 * width * heads * size,
        limit=16,
    )
    far = call(
        functools.partial(arrive_kernel, groups, group, tokens),
        [shaped((groups * tokens, size), BF16)] * group,
        (place, *(arrived[step] for step in line_order(groups)), starts, *near),
        in_specs=[smem] + [vmem] * (groups + 1 + group),
        scratch=(
            pltpu.VMEM((groups, tokens, size), F32),
            pltpu.VMEM((groups, size, size), F32),
        ),
        flops=6 * groups * group * size**3,
        moved=10**6,
        limit=8 + group * groups // 4,
    )
    far = within_group(far)
    chunk = math.gcd(most, 4)
    width_out = w_out.shape[1]
    away, kept = call(
        functools.partial(attend_kernel, group, segments, most),
        [shaped((half, width_out), BF16)] * 2,
        (place, core, table, *far[::-1], *values[::-1], *own, w_out),
        in_specs=[smem] * 3 + [vmem] * (2 * group + 5),
        scratch=[
            pltpu.VMEM((chunk * tokens, size), BF16),
            pltpu.VMEM((chunk * tokens, size), BF16),
            pltpu.VMEM((tokens, width_out), F32),
        ],
        flops=2 * tokens * width_out * heads * size,
        moved=4 * 10**6,
        limit=14 + group * groups // 4,
    )
    return kept + lax.ppermute(away, "head", [(0, 1), (1, 0)])


def solution(mesh):
    in_specs = (
        P(("ctx", "head"), None),
        P(None, "head"),
        P(None, "head"),
        P(None, "head"),
        P(None, "head"),
        P("head", None),
        P("head"),
        P(),
        P(),
        P("head", None),
        P("ctx", None),
    )
    out_specs = P(("ctx", "head"), None)
    return jax.shard_map(body, mesh=mesh, in_specs=in_specs, out_specs=out_specs, check_vma=False)
```
